32 devices in a mesh: groups: 2 (over y), session: 16 (over z, x, core).
Axes of the slice: x: 2, y: 2, z: 4, core: 2. Of those that a mesh axis runs over, the one named last changes fastest.
Arguments:
- hidden: bfloat16 [2, 32, 8192], P(None, ('groups', 'session')), parts along dimension 1, may hold values from -6 to 6
- norm_gain: bfloat16 [8192], replicated, may hold values from 0.5 to 1.5
- query_weight: bfloat16 [8192, 8192], P(None, 'session'), may hold values from -0.0625 to 0.0625
- kv_weight: bfloat16 [8192, 2048], P(None, 'session'), may hold values from -0.25 to 0.25
- out_weight: bfloat16 [8192, 8192], P('session'), may hold values from -0.0625 to 0.0625
- key_factors: bfloat16 [32, 512, 160], P(('groups', 'session')), parts along dimension 0, may hold values from -6 to 6
- key_basis: bfloat16 [32, 160, 1024], P(('groups', 'session')), parts along dimension 0, may hold values from -0.5 to 0.5
- value_store: bfloat16 [1024, 16, 1024], P(('groups', 'session')), parts along dimension 0, may hold values from -6 to 6
- lengths: int32 [32], P(('groups', 'session')), parts along dimension 0, may hold values from 256 to 512, as said below
- block_slot: int32 [32, 32], P(('groups', 'session')), parts along dimension 0, may hold values from 0 to 511, as said below
- selection: int32 [2, 32, 16], P(None, ('groups', 'session')), parts along dimension 1, may hold values from 0 to 31, as said below
Outputs:
- attended: bfloat16 [2, 32, 8192], P(None, ('groups', 'session')), parts along dimension 1
The draws below stay inside these ranges and needn't reach their ends.
There are 2 independent parts, one for each index of `groups`. The reference program is written for one: setup_inputs(seed, part) draws one part's arguments, and reference() takes and returns one part's arrays. A program takes and returns all parts, laid end to end along the dimension named above; an argument that names none is the same for every part. Nothing has to cross between parts.
Inputs may be any that keep to these rules, and one draw needn't show every extreme that they name: `block_slot`: pages 2m and 2m+1 of a session lie in slots of one store device (slot // 32), which holds no other page of that session; no slot is used twice. `selection`: 16 different page numbers for each step and session, all below ceil(lengths / 16) of that session; in every one of them some pair 2m, 2m+1 is picked whole. `lengths`: some session has exactly 512.
All inputs are finite; a program needn't handle non-finite values.
Results may differ from the reference program's by a relative error of at most 0.012.
Values may be sent and summed in bfloat16 or wider, within the bound.
No kernel may reach another device: no remote copies, remote signals or barrier semaphores. Data moves between devices by JAX's collectives and lax.ppermute only.
A program may use at most 128 MiB of HBM per device.

```python
import math
import jax
import jax.numpy as jnp
from jax import lax

D = 8192
HEADS = 64
KV_HEADS = 8
HEAD_DIM = 128
RANK = 160
BLOCK = 16
STEPS = 2
KVD = 1024
SESSIONS = 16
NBLOCK = 32
SEQ = 512
PICKS = 16


def session_lengths(key):
    inner = jax.random.fold_in(key, 31)
    first_key, second_key = jax.random.split(inner)
    drawn = jax.random.randint(first_key, (SESSIONS,), SEQ // 2, SEQ + 1)
    longest = jax.random.randint(second_key, (), 0, SESSIONS)
    return jnp.where(jnp.arange(SESSIONS, dtype=jnp.int32) == longest, SEQ, drawn).astype(jnp.int32)


def draw_lengths(key, part):
    return session_lengths(key)


def draw_block_slot(key, part):
    key = jax.random.fold_in(key, 32)
    session_keys = jax.random.split(key, SESSIONS)
    orders = jax.vmap(lambda single_key: jax.random.permutation(single_key, SESSIONS))(session_keys)
    holders = jnp.repeat(orders.astype(jnp.int32), 2, axis=1)
    within = 2 * jnp.arange(SESSIONS, dtype=jnp.int32)[:, None] + jnp.arange(NBLOCK, dtype=jnp.int32)[None, :] % 2
    return (holders * NBLOCK + within).astype(jnp.int32)


def draw_selection(key, part):
    session_len = session_lengths(key)
    key = jax.random.fold_in(key, 33)
    usable_all = (session_len + BLOCK - 1) // BLOCK

    def single(single_key, usable):
        first_key, second_key = jax.random.split(single_key)
        page = jnp.arange(NBLOCK, dtype=jnp.int32)
        whole_pairs = jnp.maximum((usable - usable % 2) // 2, 1)
        pair_pick = jax.random.randint(second_key, (), 0, NBLOCK // 2) % whole_pairs
        noise = jax.random.randint(first_key, (NBLOCK,), 0, 1 << 20)
        scores = noise * NBLOCK + page
        scores = jnp.where(page >= usable, scores + (1 << 29), scores)
        scores = jnp.where(page // 2 == pair_pick, page - 2 * NBLOCK, scores)
        order = jnp.argsort(scores, stable=True).astype(jnp.int32)
        return order[:PICKS]
    step_keys = jax.random.split(key, STEPS * SESSIONS)
    usable_rep = jnp.tile(usable_all, STEPS)
    return jax.vmap(single)(step_keys, usable_rep).reshape(STEPS, SESSIONS, PICKS).astype(jnp.int32)


def block_levels(stream_key, extent, shards, least, top_value):
    def one(dim, shards_of):
        draws = jax.random.uniform(jax.random.fold_in(jax.random.fold_in(stream_key, 6), dim), (shards_of,), jnp.float32, least / len(shards), top_value / len(shards))
        return jnp.repeat(jnp.exp(draws), extent[dim] // shards_of).reshape((-1,) + (1,) * (len(extent) - dim - 1))

    level = one(*shards[0])
    for cut in shards[1:]:
        level = level * one(*cut)
    return level


def bell_draw(own_key, shape, scale, most, shards=(), held_as=jnp.bfloat16):
    gain = block_levels(own_key, shape, shards, -0.22, 0.18) if shards else 1.0
    array = jax.random.normal(own_key, shape, jnp.float32) * scale * gain
    return jnp.minimum(jnp.maximum(array, -most), most).astype(held_as)


def setup_inputs(seed: int = 0, part: int = 0) -> dict:
    streams_of = jax.random.split(jax.random.key(seed), 12)
    own_keys = jax.random.split(jax.random.fold_in(streams_of[11], part), 12)
    hidden = bell_draw(own_keys[0], (STEPS, SESSIONS, D), 1.0, 6.0, ((1, 16),))
    norm_gain = jnp.clip(1.0 + 0.1 * jax.random.normal(streams_of[1], (D,), jnp.float32), 0.5, 1.5).astype(jnp.bfloat16)
    query_weight = bell_draw(streams_of[2], (D, D), D ** -0.5, 0.0625, ((1, 16),))
    kv_weight = bell_draw(streams_of[3], (D, 2 * KVD), (D // 16) ** -0.5, 0.25, ((1, 16),))
    out_weight = bell_draw(streams_of[4], (D, D), D ** -0.5, 0.0625, ((0, 16),))
    key_factors = bell_draw(own_keys[5], (SESSIONS, SEQ, RANK), 1.0, 6.0, ((0, 16),))
    key_basis = bell_draw(own_keys[6], (SESSIONS, RANK, KVD), RANK ** -0.5, 0.5, ((0, 16),))
    value_store = bell_draw(own_keys[7], (SESSIONS * NBLOCK, BLOCK, KVD), 1.0, 6.0, ((0, 16),))
    lengths = draw_lengths(jax.random.fold_in(jax.random.fold_in(streams_of[11], part), 71), part)
    block_slot = draw_block_slot(jax.random.fold_in(jax.random.fold_in(streams_of[11], part), 71), part)
    selection = draw_selection(jax.random.fold_in(jax.random.fold_in(streams_of[11], part), 71), part)
    return dict(hidden=hidden, norm_gain=norm_gain, query_weight=query_weight, kv_weight=kv_weight, out_weight=out_weight, key_factors=key_factors, key_basis=key_basis, value_store=value_store, lengths=lengths, block_slot=block_slot, selection=selection)


def rotate(vector, angle):
    half = vector.shape[-1] // 2
    cosine = jnp.cos(angle)
    sine = jnp.sin(angle)
    first = vector[..., :half]
    second = vector[..., half:]
    return jnp.concatenate([first * cosine - second * sine, second * cosine + first * sine], axis=-1)

def angles(positions):
    half = HEAD_DIM // 2
    frequency = jnp.exp(-jnp.arange(half, dtype=jnp.float32) * (2.0 * math.log(500000.0) / HEAD_DIM))
    return positions[..., None] * frequency

def reference(hidden, norm_gain, query_weight, kv_weight, out_weight, key_factors, key_basis, value_store, lengths, block_slot, selection):
    group_size = HEADS // KV_HEADS
    score_scale = 1.0 / math.sqrt(HEAD_DIM)
    inputs = hidden.astype(jnp.float32)
    normed = (inputs * lax.rsqrt(lax.optimization_barrier(jnp.mean(inputs * inputs, axis=-1, keepdims=True)) + 1e-05) * norm_gain.astype(jnp.float32)).astype(jnp.bfloat16)
    flat = normed.reshape(-1, D)
    query_heads = jnp.dot(flat, query_weight, preferred_element_type=jnp.float32).astype(jnp.bfloat16).reshape(STEPS, SESSIONS, HEADS, HEAD_DIM)
    fresh = jnp.dot(flat, kv_weight, preferred_element_type=jnp.float32).astype(jnp.bfloat16).reshape(STEPS, SESSIONS, 2, KV_HEADS, HEAD_DIM)
    new_positions = (lengths[None, :] + jnp.arange(STEPS, dtype=jnp.int32)[:, None]).astype(jnp.float32)
    turned_query = rotate(query_heads.astype(jnp.float32), angles(new_positions)[:, :, None, :]).astype(jnp.bfloat16)
    turned_new = rotate(fresh[:, :, 0].astype(jnp.float32), angles(new_positions)[:, :, None, :]).astype(jnp.bfloat16)
    new_values = fresh[:, :, 1]
    results = []
    for step_index in range(STEPS):

        def per_session(session_index):
            chosen = selection[step_index, session_index]
            places = (chosen[:, None] * BLOCK + jnp.arange(BLOCK, dtype=jnp.int32)[None, :]).reshape(-1)
            factors = key_factors[session_index].reshape(NBLOCK, BLOCK, RANK)[chosen].reshape(-1, RANK)
            product = jnp.dot(factors, key_basis[session_index], preferred_element_type=jnp.float32)
            cached_keys = rotate(product.reshape(-1, KV_HEADS, HEAD_DIM), angles(places.astype(jnp.float32))[:, None, :]).astype(jnp.bfloat16)
            page_values = value_store[block_slot[session_index][chosen]].reshape(-1, KV_HEADS, HEAD_DIM)
            grouped = turned_query[step_index, session_index].reshape(KV_HEADS, group_size, HEAD_DIM).astype(jnp.float32)
            scores = jnp.einsum('kgd,mkd->kgm', grouped, cached_keys.astype(jnp.float32)) * score_scale
            scores = jnp.where(places[None, None, :] < lengths[session_index], scores, -1e+30)
            recent_keys = turned_new[:step_index + 1, session_index].astype(jnp.float32)
            recent = jnp.einsum('kgd,nkd->kgn', grouped, recent_keys) * score_scale
            largest = jnp.maximum(lax.optimization_barrier(jnp.max(scores, axis=-1)), lax.optimization_barrier(jnp.max(recent, axis=-1)))
            cache_exp = jnp.exp(scores - largest[..., None])
            recent_exp = jnp.exp(recent - largest[..., None])
            denominator = lax.optimization_barrier(jnp.sum(cache_exp, axis=-1)) + lax.optimization_barrier(jnp.sum(recent_exp, axis=-1))
            weights_cache = (cache_exp / denominator[..., None]).astype(jnp.bfloat16)
            weights_recent = (recent_exp / denominator[..., None]).astype(jnp.bfloat16)
            mixed_heads = jnp.einsum('kgm,mkd->kgd', weights_cache.astype(jnp.float32), page_values.astype(jnp.float32))
            mixed_heads = mixed_heads + jnp.einsum('kgn,nkd->kgd', weights_recent.astype(jnp.float32), new_values[:step_index + 1, session_index].astype(jnp.float32))
            return mixed_heads.reshape(D).astype(jnp.bfloat16)
        heads = lax.map(per_session, jnp.arange(SESSIONS, dtype=jnp.int32))
        results.append(jnp.dot(heads, out_weight, preferred_element_type=jnp.float32).astype(jnp.bfloat16))
    return jnp.stack(results)
```

```python
import functools
import math

import jax
import jax.numpy as jnp
from jax import lax
from jax.experimental import pallas as pl
from jax.experimental.pallas import tpu as pltpu
from jax.sharding import PartitionSpec as P

HEADS = 64
KV_HEADS = 8
HEAD_DIM = 128
STEPS = 2
GROUP = HEADS // KV_HEADS
LANES = 128
AXIS = "session"
VMEM = pltpu.VMEM
SMEM = pltpu.SMEM
F32 = jnp.float32
BF16 = jnp.bfloat16


def angles(positions):
    half = HEAD_DIM // 2
    frequency = jnp.exp(
        -jnp.arange(half, dtype=F32) * (2.0 * math.log(500000.0) / HEAD_DIM)
    )
    return positions[..., None] * frequency


def turn_tables(positions):
    angle = angles(positions)
    cosine, sine = jnp.cos(angle), jnp.sin(angle)
    return (
        jnp.concatenate([cosine, cosine], axis=-1),
        jnp.concatenate([-sine, sine], axis=-1),
    )


def whole(space=VMEM):
    return pl.BlockSpec(memory_space=space)


def keys_kernel(factors_ref, basis_ref, cos_ref, sin_ref, out_ref):
    product = jnp.dot(factors_ref[...], basis_ref[...], preferred_element_type=F32)
    cosine, sine = cos_ref[...], sin_ref[...]
    for head in range(KV_HEADS):
        lanes = slice(head * HEAD_DIM, (head + 1) * HEAD_DIM)
        part = product[:, lanes]
        turned = part * cosine + pltpu.roll(part, HEAD_DIM // 2, 1) * sine
        out_ref[:, lanes] = turned.astype(BF16)


def make_keys(factors, basis, cosine, sine):
    seq, rank = factors.shape
    width = basis.shape[1]
    rows = min(seq, 512)
    return pl.pallas_call(
        keys_kernel,
        grid=(seq // rows,),
        in_specs=[
            pl.BlockSpec((rows, rank), lambda i: (i, 0)),
            pl.BlockSpec((rank, width), lambda i: (0, 0)),
            pl.BlockSpec((rows, HEAD_DIM), lambda i: (i, 0)),
            pl.BlockSpec((rows, HEAD_DIM), lambda i: (i, 0)),
        ],
        out_specs=pl.BlockSpec((rows, width), lambda i: (i, 0)),
        out_shape=jax.ShapeDtypeStruct((seq, width), BF16),
        compiler_params=pltpu.CompilerParams(vmem_limit_bytes=32 * 2**20),
        cost_estimate=pl.CostEstimate(
            flops=2 * seq * rank * width, bytes_accessed=4 * seq * width, transcendentals=0
        ),
        name="turned_keys",
    )(factors, basis, cosine, sine)


def project_kernel(
    order, fast, me_ref, first_ref, second_ref, gain_ref, wq_ref, wk_ref, out_ref,
    x_scr, lhs_scr, wq_buf, wk_buf, out_scr, sems,
):
    depth, q_cols = wq_ref.shape
    k_cols = wk_ref.shape[1]
    chunks = wq_buf.shape[0]
    span = depth // chunks
    pieces = depth // LANES
    copies = []
    for i in range(chunks):
        rows = pl.ds(i * span, span)
        pair = (
            pltpu.make_async_copy(wq_ref.at[rows, :], wq_buf.at[i], sems.at[0, i]),
            pltpu.make_async_copy(wk_ref.at[rows, :], wk_buf.at[i], sems.at[1, i]),
        )
        for copy in pair:
            copy.start()
        copies.append(pair)
    half = first_ref.shape[0]
    x_scr[:half] = first_ref[...].astype(F32)
    x_scr[half:] = second_ref[...].astype(F32)
    count = 2 * half // pieces
    squares = jnp.zeros((count, LANES), F32)
    for c in range(pieces):
        part = x_scr[pl.ds(c, count, stride=pieces), :]
        squares = squares + part * part
    scale = lax.rsqrt(jnp.sum(squares, axis=1, keepdims=True) * (1.0 / depth) + 1e-05)
    for c in range(pieces):
        part = x_scr[pl.ds(c, count, stride=pieces), :]
        gain = gain_ref[pl.ds(c, 1), :].astype(F32)
        lhs_scr[:, c * LANES : (c + 1) * LANES] = (part * scale * gain).astype(BF16)
    q_sum = jnp.zeros((count, q_cols), F32)
    k_sum = jnp.zeros((count, k_cols), F32)
    for i in range(chunks):
        for copy in copies[i]:
            copy.wait()
        lhs = lhs_scr[:, i * span : (i + 1) * span]
        q_sum = q_sum + jnp.dot(lhs, wq_buf[i], preferred_element_type=F32)
        k_sum = k_sum + jnp.dot(lhs, wk_buf[i], preferred_element_type=F32)
    if not fast:
        out_ref[:, :q_cols] = q_sum.astype(BF16)
        out_ref[:, q_cols:] = k_sum.astype(BF16)
        return
    me = me_ref[0]
    per = q_cols // LANES
    out_scr[...] = jnp.zeros_like(out_scr)
    for j, other in enumerate(order):
        target = jnp.bitwise_xor(me, other)
        for step in range(STEPS):
            row = j * STEPS + step
            for c in range(per):
                out_scr[target, pl.ds(step * per + c, 1), :] = q_sum[
                    row : row + 1, c * LANES : (c + 1) * LANES
                ]
            out_scr[target, pl.ds(STEPS * per + step, 1), :] = k_sum[row : row + 1, :]
    out_ref[...] = out_scr[...].astype(BF16)


def project(me, first, second, gain, query_weight, kv_weight, order, fast):
    depth, q_cols = query_weight.shape
    k_cols = kv_weight.shape[1]
    pieces = depth // LANES
    rows = 2 * first.shape[0] // pieces
    devices = rows // STEPS
    chunks = 8
    span = depth // chunks
    shape = (devices, 16, LANES) if fast else (rows, q_cols + k_cols)
    return pl.pallas_call(
        functools.partial(project_kernel, order, fast),
        in_specs=[whole(SMEM), whole(), whole(), whole(), whole(pl.ANY), whole(pl.ANY)],
        out_specs=whole(),
        out_shape=jax.ShapeDtypeStruct(shape, BF16),
        scratch_shapes=[
            VMEM((rows * pieces, LANES), F32),
            VMEM((rows, depth), BF16),
            VMEM((chunks, span, q_cols), BF16),
            VMEM((chunks, span, k_cols), BF16),
            VMEM((devices, 16, LANES) if fast else (8, LANES), F32),
            pltpu.SemaphoreType.DMA((2, chunks)),
        ],
        compiler_params=pltpu.CompilerParams(vmem_limit_bytes=48 * 2**20),
        cost_estimate=pl.CostEstimate(
            flops=2 * rows * depth * (q_cols + k_cols),
            bytes_accessed=2 * depth * (q_cols + k_cols),
            transcendentals=0,
        ),
        name="norm_project",
    )(me, first, second, gain, query_weight, kv_weight)


def attend_kernel(
    holder_ref, columns_ref, keys_ref, bias_ref, cos_ref, sin_ref, pages_ref, out_ref, values_scr
):
    seq = keys_ref.shape[0]
    pairs, pair_rows = pages_ref.shape[0], pages_ref.shape[1]
    score_scale = 1.0 / math.sqrt(HEAD_DIM)
    half = HEAD_DIM // 2
    rows = 2 * GROUP
    for m in range(pairs):
        values_scr[m * pair_rows : (m + 1) * pair_rows, :] = pages_ref[holder_ref[m]]
    columns = columns_ref[...].astype(F32)
    count = columns.shape[0]
    query = columns[:, :8, :].reshape(count * 8, HEAD_DIM)
    fresh = columns[:, 8:, :]
    row_step = lax.rem(lax.broadcasted_iota(jnp.int32, (count * 8, 1), 0) // 4, STEPS)
    later = row_step == 1
    cosine = jnp.where(later, cos_ref[1:2, :], cos_ref[0:1, :])
    sine = jnp.where(later, sin_ref[1:2, :], sin_ref[0:1, :])
    turned = (query * cosine + pltpu.roll(query, half, 1) * sine).astype(BF16)
    turned_wide = turned.astype(F32)
    step_later = later[:rows]
    bias = jnp.where(step_later, bias_ref[1:2, :], bias_ref[0:1, :])
    new_keys = []
    for step in range(STEPS):
        part = fresh[:KV_HEADS, step, :]
        new = part * cos_ref[step : step + 1, :] + pltpu.roll(part, half, 1) * sin_ref[step : step + 1, :]
        new_keys.append(new.astype(BF16).astype(F32))
    for head in range(KV_HEADS):
        lanes = slice(head * HEAD_DIM, (head + 1) * HEAD_DIM)
        mine = slice(head * rows, (head + 1) * rows)
        scores = (
            lax.dot_general(
                turned[mine], keys_ref[:, lanes], (((1,), (1,)), ((), ())),
                preferred_element_type=F32,
            )
            * score_scale
            + bias
        )
        recent0 = (
            jnp.sum(turned_wide[mine] * new_keys[0][head : head + 1, :], axis=1, keepdims=True)
            * score_scale
        )
        recent1 = (
            jnp.sum(turned_wide[mine] * new_keys[1][head : head + 1, :], axis=1, keepdims=True)
            * score_scale
        )
        recent1 = jnp.where(step_later, recent1, -1e30)
        largest = jnp.maximum(
            jnp.max(scores, axis=1, keepdims=True), jnp.maximum(recent0, recent1)
        )
        cache_exp = jnp.exp(scores - largest)
        exp0 = jnp.exp(recent0 - largest)
        exp1 = jnp.exp(recent1 - largest)
        denominator = jnp.sum(cache_exp, axis=1, keepdims=True) + (exp0 + exp1)
        weights = (cache_exp / denominator).astype(BF16)
        weight0 = (exp0 / denominator).astype(BF16).astype(F32)
        weight1 = (exp1 / denominator).astype(BF16).astype(F32)
        mixed = jnp.dot(weights, values_scr[:, lanes], preferred_element_type=F32)
        mixed = mixed + weight0 * fresh[KV_HEADS + head, 0:1, :]
        mixed = mixed + weight1 * fresh[KV_HEADS + head, 1:2, :]
        out_ref[mine, :] = mixed.astype(BF16)


def attend(holder, columns, keys, bias, cosine, sine, pages):
    seq, width = keys.shape
    return pl.pallas_call(
        attend_kernel,
        in_specs=[whole(SMEM)] + [whole()] * 6,
        out_specs=whole(),
        out_shape=jax.ShapeDtypeStruct((STEPS * HEADS, HEAD_DIM), BF16),
        scratch_shapes=[VMEM((seq, width), BF16)],
        compiler_params=pltpu.CompilerParams(vmem_limit_bytes=48 * 2**20),
        cost_estimate=pl.CostEstimate(
            flops=4 * STEPS * HEADS * seq * HEAD_DIM,
            bytes_accessed=4 * seq * width,
            transcendentals=STEPS * HEADS * seq,
        ),
        name="attend",
    )(holder, columns, keys, bias, cosine, sine, pages)


def output_kernel(lhs_ref, weight_ref, out_ref, weight_buf, out_scr, sems):
    chunks, _, span = weight_buf.shape
    rows = lhs_ref.shape[0]
    pieces = chunks * span // LANES
    copies = []
    for i in range(chunks):
        copy = pltpu.make_async_copy(
            weight_ref.at[:, pl.ds(i * span, span)], weight_buf.at[i], sems.at[i]
        )
        copy.start()
        copies.append(copy)
    lhs = lhs_ref[...]
    for i in range(chunks):
        copies[i].wait()
        part = jnp.dot(lhs, weight_buf[i], preferred_element_type=F32)
        for c in range(span // LANES):
            out_scr[pl.ds(i * (span // LANES) + c, rows, stride=pieces), :] = part[
                :, c * LANES : (c + 1) * LANES
            ]
    out_ref[...] = out_scr[...].astype(BF16)


def output(lhs, weight):
    rows, depth = lhs.shape
    width = weight.shape[1]
    chunks = 8
    return pl.pallas_call(
        output_kernel,
        in_specs=[whole(), whole(pl.ANY)],
        out_specs=whole(),
        out_shape=jax.ShapeDtypeStruct((rows * width // LANES, LANES), BF16),
        scratch_shapes=[
            VMEM((chunks, depth, width // chunks), BF16),
            VMEM((rows * width // LANES, LANES), F32),
            pltpu.SemaphoreType.DMA((chunks,)),
        ],
        compiler_params=pltpu.CompilerParams(vmem_limit_bytes=48 * 2**20),
        cost_estimate=pl.CostEstimate(
            flops=2 * rows * depth * width, bytes_accessed=2 * depth * width, transcendentals=0
        ),
        name="output_project",
    )(lhs, weight)


def exchange(blocks):
    return lax.all_to_all(blocks, AXIS, split_axis=0, concat_axis=0, tiled=True)


def local(
    hidden,
    norm_gain,
    query_weight,
    kv_weight,
    out_weight,
    key_factors,
    key_basis,
    value_store,
    lengths,
    block_slot,
    selection,
):
    devices = lax.axis_size(AXIS)
    me = lax.axis_index(AXIS)
    slots_dev, block_len, width = value_store.shape
    seq = key_factors.shape[1]
    pages = block_slot.shape[1]
    model = hidden.shape[2]
    q_cols = query_weight.shape[1]
    k_cols = kv_weight.shape[1]
    fast = q_cols == 4 * HEAD_DIM and k_cols == HEAD_DIM
    pieces = model // LANES

    slots = block_slot[0].reshape(pages // 2, 2)
    holder = slots[:, 0] // slots_dev
    here = holder[None, :] == jnp.arange(devices, dtype=jnp.int32)[:, None]
    asked = jnp.sum(jnp.where(here[:, :, None], (slots % slots_dev)[None], 0), axis=1)
    asked_here = exchange(asked[:, None, :])
    sent_pages = value_store[asked_here.reshape(-1)]
    fetched = exchange(sent_pages.reshape(devices, 2 * block_len, width))

    block = hidden[:, 0].reshape(1, STEPS * pieces, LANES)
    order = [0]
    bit = devices // 2
    while bit:
        links = [(i, i ^ bit) for i in range(devices)]
        other = lax.ppermute(block, AXIS, links)
        order = order + [k ^ bit for k in order]
        bit //= 2
        if bit:
            block = jnp.concatenate([block, other], axis=0)
    columns = project(
        me.astype(jnp.int32).reshape(1),
        block.reshape(-1, LANES),
        other.reshape(-1, LANES),
        norm_gain.reshape(pieces, LANES),
        query_weight,
        kv_weight,
        tuple(order),
        fast,
    )
    if fast:
        columns = exchange(columns)
    else:
        places = jnp.bitwise_xor(me, jnp.array(order, dtype=jnp.int32))
        columns = exchange(columns.reshape(devices, STEPS, q_cols + k_cols)[places])
        query = columns[:, :, :q_cols].transpose(1, 0, 2).reshape(STEPS, HEADS // 4, 4, HEAD_DIM)
        query = query.transpose(1, 0, 2, 3).reshape(HEADS // 4, 8, HEAD_DIM)
        fresh = columns[:, :, q_cols:].transpose(1, 0, 2).reshape(STEPS, HEADS // 4, HEAD_DIM)
        fresh = jnp.pad(fresh.transpose(1, 0, 2), ((0, 0), (0, 8 - STEPS), (0, 0)))
        columns = jnp.concatenate([query, fresh], axis=1)

    cosine, sine = turn_tables(jnp.arange(seq, dtype=jnp.int32).astype(F32))
    keys = make_keys(key_factors[0], key_basis[0], cosine, sine)
    picked = jnp.any(
        selection[:, 0, :, None] == jnp.arange(pages, dtype=jnp.int32)[None, None, :], axis=1
    )
    usable = jnp.repeat(picked, block_len, axis=1) & (
        jnp.arange(seq, dtype=jnp.int32)[None, :] < lengths[0]
    )
    bias = jnp.where(usable, 0.0, -1e30).astype(F32)
    new_cos, new_sin = turn_tables(
        (lengths[0] + jnp.arange(STEPS, dtype=jnp.int32)).astype(F32)
    )
    heads = attend(holder, columns, keys, bias, new_cos, new_sin, fetched)

    if fast:
        rows = exchange(heads.reshape(devices, STEPS * 4, HEAD_DIM))
        lhs = rows.reshape(devices, STEPS, 4 * HEAD_DIM).reshape(devices * STEPS, 4 * HEAD_DIM)
    else:
        flat = heads.reshape(HEADS // 4, STEPS, 4 * HEAD_DIM).transpose(1, 0, 2)
        flat = flat.reshape(STEPS, devices, model // devices).transpose(1, 0, 2)
        lhs = exchange(flat).reshape(devices * STEPS, model // devices)
    partial = output(lhs, out_weight)
    arrived = exchange(partial.reshape(devices, STEPS * pieces, LANES))
    total = jnp.sum(arrived.astype(F32), axis=0).astype(BF16)
    return total.reshape(STEPS, 1, model)


def solution(mesh):
    return jax.shard_map(
        local,
        mesh=mesh,
        in_specs=(
            P(None, ("groups", "session"), None),
            P(),
            P(None, "session"),
            P(None, "session"),
            P("session", None),
            P(("groups", "session"), None, None),
            P(("groups", "session"), None, None),
            P(("groups", "session"), None, None),
            P(("groups", "session")),
            P(("groups", "session"), None),
            P(None, ("groups", "session"), None),
        ),
        out_specs=P(None, ("groups", "session"), None),
        check_vma=False,
    )
```

```python
import functools
import math

import jax
import jax.numpy as jnp
from jax import lax
from jax.experimental import pallas as pl
from jax.experimental.pallas import tpu as pltpu
from jax.sharding import PartitionSpec as P

HEADS = 64
KV_HEADS = 8
HEAD_DIM = 128
STEPS = 2
GROUP = HEADS // KV_HEADS
LANES = 128
AXIS = "session"
VMEM = pltpu.VMEM
SMEM = pltpu.SMEM
F32 = jnp.float32
BF16 = jnp.bfloat16


def angles(positions):
    half = HEAD_DIM // 2
    frequency = jnp.exp(
        -jnp.arange(half, dtype=F32) * (2.0 * math.log(500000.0) / HEAD_DIM)
    )
    return positions[..., None] * frequency


def turn_tables(positions):
    angle = angles(positions)
    cosine, sine = jnp.cos(angle), jnp.sin(angle)
    return (
        jnp.concatenate([cosine, cosine], axis=-1),
        jnp.concatenate([-sine, sine], axis=-1),
    )


def whole(space=VMEM):
    return pl.BlockSpec(memory_space=space)


def ask_kernel(slots_dev, slots_ref, asked_ref, holder_ref):
    for m in range(holder_ref.shape[0]):
        slot = slots_ref[0, 2 * m]
        holder = lax.div(slot, slots_dev)
        holder_ref[m] = holder
        asked_ref[holder, 0, 0] = slot - holder * slots_dev
        asked_ref[holder, 0, 1] = slots_ref[0, 2 * m + 1] - holder * slots_dev


def ask(block_slot, devices, slots_dev):
    return pl.pallas_call(
        functools.partial(ask_kernel, slots_dev),
        in_specs=[whole(SMEM)],
        out_specs=(whole(SMEM), whole(SMEM)),
        out_shape=(
            jax.ShapeDtypeStruct((devices, 1, 2), jnp.int32),
            jax.ShapeDtypeStruct((block_slot.shape[1] // 2,), jnp.int32),
        ),
        name="ask_pages",
    )(block_slot)


def pick_kernel(asked_ref, store_ref, out_ref, sem):
    count = asked_ref.shape[0]
    block_len = store_ref.shape[1]

    def copies(i):
        return [
            pltpu.make_async_copy(
                store_ref.at[asked_ref[i, 0, k]],
                out_ref.at[i, pl.ds(k * block_len, block_len), :],
                sem.at[i, k],
            )
            for k in range(2)
        ]

    for i in range(count):
        for copy in copies(i):
            copy.start()
    for i in range(count):
        for copy in copies(i):
            copy.wait()


def pick_pages(asked, store):
    count = asked.shape[0]
    _, block_len, width = store.shape
    return pl.pallas_call(
        pick_kernel,
        in_specs=[whole(SMEM), whole(pl.ANY)],
        out_specs=whole(pl.ANY),
        out_shape=jax.ShapeDtypeStruct((count, 2 * block_len, width), store.dtype),
        scratch_shapes=[pltpu.SemaphoreType.DMA((count, 2))],
        name="pick_pages",
    )(asked, store)


def keys_kernel(factors_ref, basis_ref, cos_ref, sin_ref, out_ref):
    product = jnp.dot(factors_ref[...], basis_ref[...], preferred_element_type=F32)
    cosine, sine = cos_ref[...], sin_ref[...]
    for head in range(KV_HEADS):
        lanes = slice(head * HEAD_DIM, (head + 1) * HEAD_DIM)
        part = product[:, lanes]
        turned = part * cosine + pltpu.roll(part, HEAD_DIM // 2, 1) * sine
        out_ref[:, lanes] = turned.astype(BF16)


def make_keys(factors, basis, cosine, sine):
    seq, rank = factors.shape
    width = basis.shape[1]
    rows = min(seq, 512)
    return pl.pallas_call(
        keys_kernel,
        grid=(seq // rows,),
        in_specs=[
            pl.BlockSpec((rows, rank), lambda i: (i, 0)),
            pl.BlockSpec((rank, width), lambda i: (0, 0)),
            pl.BlockSpec((rows, HEAD_DIM), lambda i: (i, 0)),
            pl.BlockSpec((rows, HEAD_DIM), lambda i: (i, 0)),
        ],
        out_specs=pl.BlockSpec((rows, width), lambda i: (i, 0)),
        out_shape=jax.ShapeDtypeStruct((seq, width), BF16),
        compiler_params=pltpu.CompilerParams(vmem_limit_bytes=32 * 2**20),
        cost_estimate=pl.CostEstimate(
            flops=2 * seq * rank * width, bytes_accessed=4 * seq * width, transcendentals=0
        ),
        name="turned_keys",
    )(factors, basis, cosine, sine)


def project_kernel(
    order, fast, first_ref, second_ref, gain_ref, wq_ref, wk_ref, *rest
):
    out_refs = rest[: 2 if fast else 1]
    x_scr, lhs_scr, wq_buf, wk_buf, out_scr, sems = rest[len(out_refs) :]
    depth, q_cols = wq_ref.shape
    k_cols = wk_ref.shape[1]
    chunks = wq_buf.shape[0]
    span = depth // chunks
    pieces = depth // LANES
    copies = []
    for i in range(chunks):
        rows = pl.ds(i * span, span)
        pair = (
            pltpu.make_async_copy(wq_ref.at[rows, :], wq_buf.at[i], sems.at[0, i]),
            pltpu.make_async_copy(wk_ref.at[rows, :], wk_buf.at[i], sems.at[1, i]),
        )
        for copy in pair:
            copy.start()
        copies.append(pair)
    half = first_ref.shape[0]
    x_scr[:half] = first_ref[...].astype(F32)
    x_scr[half:] = second_ref[...].astype(F32)
    count = 2 * half // pieces
    squares = jnp.zeros((count, LANES), F32)
    for c in range(pieces):
        part = x_scr[pl.ds(c, count, stride=pieces), :]
        squares = squares + part * part
    scale = lax.rsqrt(jnp.sum(squares, axis=1, keepdims=True) * (1.0 / depth) + 1e-05)
    for c in range(pieces):
        part = x_scr[pl.ds(c, count, stride=pieces), :]
        gain = gain_ref[pl.ds(c, 1), :].astype(F32)
        lhs_scr[:, c * LANES : (c + 1) * LANES] = (part * scale * gain).astype(BF16)
    q_sum = jnp.zeros((count, q_cols), F32)
    k_sum = jnp.zeros((count, k_cols), F32)
    for i in range(chunks):
        for copy in copies[i]:
            copy.wait()
        lhs = lhs_scr[:, i * span : (i + 1) * span]
        q_sum = q_sum + jnp.dot(lhs, wq_buf[i], preferred_element_type=F32)
        k_sum = k_sum + jnp.dot(lhs, wk_buf[i], preferred_element_type=F32)
    if not fast:
        out_refs[0][:, :q_cols] = q_sum.astype(BF16)
        out_refs[0][:, q_cols:] = k_sum.astype(BF16)
        return
    per = q_cols // LANES
    out_scr[...] = jnp.zeros_like(out_scr)
    for j, place in enumerate(order):
        for step in range(STEPS):
            row = j * STEPS + step
            for c in range(per):
                out_scr[place, step * per + c : step * per + c + 1, :] = q_sum[
                    row : row + 1, c * LANES : (c + 1) * LANES
                ]
            out_scr[place, STEPS * per + step : STEPS * per + step + 1, :] = k_sum[
                row : row + 1, :
            ]
    near_ref, far_ref = out_refs
    half = near_ref.shape[0]
    near_ref[...] = out_scr[:half].astype(BF16)
    far_ref[...] = out_scr[half:].astype(BF16)


def project(first, second, gain, query_weight, kv_weight, order, fast):
    depth, q_cols = query_weight.shape
    k_cols = kv_weight.shape[1]
    pieces = depth // LANES
    rows = 2 * first.shape[0] // pieces
    devices = rows // STEPS
    chunks = 8
    span = depth // chunks
    if fast:
        shape = (jax.ShapeDtypeStruct((devices // 2, 16, LANES), BF16),) * 2
        out_specs = (whole(), whole())
    else:
        shape = jax.ShapeDtypeStruct((rows, q_cols + k_cols), BF16)
        out_specs = whole()
    return pl.pallas_call(
        functools.partial(project_kernel, order, fast),
        in_specs=[whole(), whole(), whole(), whole(pl.ANY), whole(pl.ANY)],
        out_specs=out_specs,
        out_shape=shape,
        scratch_shapes=[
            VMEM((rows * pieces, LANES), F32),
            VMEM((rows, depth), BF16),
            VMEM((chunks, span, q_cols), BF16),
            VMEM((chunks, span, k_cols), BF16),
            VMEM((devices, 16, LANES) if fast else (8, LANES), F32),
            pltpu.SemaphoreType.DMA((2, chunks)),
        ],
        compiler_params=pltpu.CompilerParams(vmem_limit_bytes=48 * 2**20),
        cost_estimate=pl.CostEstimate(
            flops=2 * rows * depth * (q_cols + k_cols),
            bytes_accessed=2 * depth * (q_cols + k_cols),
            transcendentals=0,
        ),
        name="norm_project",
    )(first, second, gain, query_weight, kv_weight)


def attend_kernel(
    places, holder_ref, where_ref, keys_ref, bias_ref, cos_ref, sin_ref, pages_ref, *rest
):
    pieces = rest[:-3]
    out_ref, values_scr, columns_scr = rest[-3:]
    for r, (piece, row) in enumerate(places):
        columns_scr[where_ref[r]] = pieces[piece][row, 0].astype(F32)
    seq = keys_ref.shape[0]
    pairs, pair_rows = pages_ref.shape[0], pages_ref.shape[1]
    score_scale = 1.0 / math.sqrt(HEAD_DIM)
    half = HEAD_DIM // 2
    rows = 2 * GROUP
    for m in range(pairs):
        values_scr[m * pair_rows : (m + 1) * pair_rows, :] = pages_ref[holder_ref[m]]
    columns = columns_scr[...]
    count = columns.shape[0]
    query = columns[:, :8, :].reshape(count * 8, HEAD_DIM)
    fresh = columns[:, 8:, :]
    row_step = lax.rem(lax.broadcasted_iota(jnp.int32, (count * 8, 1), 0) // 4, STEPS)
    later = row_step == 1
    cosine = jnp.where(later, cos_ref[1:2, :], cos_ref[0:1, :])
    sine = jnp.where(later, sin_ref[1:2, :], sin_ref[0:1, :])
    turned = (query * cosine + pltpu.roll(query, half, 1) * sine).astype(BF16)
    turned_wide = turned.astype(F32)
    step_later = later[:rows]
    bias = jnp.where(step_later, bias_ref[1:2, :], bias_ref[0:1, :])
    new_keys = []
    for step in range(STEPS):
        part = fresh[:KV_HEADS, step, :]
        new = part * cos_ref[step : step + 1, :] + pltpu.roll(part, half, 1) * sin_ref[step : step + 1, :]
        new_keys.append(new.astype(BF16).astype(F32))
    for head in range(KV_HEADS):
        lanes = slice(head * HEAD_DIM, (head + 1) * HEAD_DIM)
        mine = slice(head * rows, (head + 1) * rows)
        scores = (
            lax.dot_general(
                turned[mine], keys_ref[:, lanes], (((1,), (1,)), ((), ())),
                preferred_element_type=F32,
            )
            * score_scale
            + bias
        )
        recent0 = (
            jnp.sum(turned_wide[mine] * new_keys[0][head : head + 1, :], axis=1, keepdims=True)
            * score_scale
        )
        recent1 = (
            jnp.sum(turned_wide[mine] * new_keys[1][head : head + 1, :], axis=1, keepdims=True)
            * score_scale
        )
        recent1 = jnp.where(step_later, recent1, -1e30)
        largest = jnp.maximum(
            jnp.max(scores, axis=1, keepdims=True), jnp.maximum(recent0, recent1)
        )
        cache_exp = jnp.exp(scores - largest)
        exp0 = jnp.exp(recent0 - largest)
        exp1 = jnp.exp(recent1 - largest)
        denominator = jnp.sum(cache_exp, axis=1, keepdims=True) + (exp0 + exp1)
        weights = (cache_exp / denominator).astype(BF16)
        weight0 = (exp0 / denominator).astype(BF16).astype(F32)
        weight1 = (exp1 / denominator).astype(BF16).astype(F32)
        mixed = jnp.dot(weights, values_scr[:, lanes], preferred_element_type=F32)
        mixed = mixed + weight0 * fresh[KV_HEADS + head, 0:1, :]
        mixed = mixed + weight1 * fresh[KV_HEADS + head, 1:2, :]
        out_ref[mine, :] = mixed.astype(BF16)


def attend(holder, where, keys, bias, cosine, sine, pages, places, pieces):
    seq, width = keys.shape
    return pl.pallas_call(
        functools.partial(attend_kernel, places),
        in_specs=[whole(SMEM)] * 2 + [whole()] * (5 + len(pieces)),
        out_specs=whole(),
        out_shape=jax.ShapeDtypeStruct((STEPS * HEADS, HEAD_DIM), BF16),
        scratch_shapes=[VMEM((seq, width), BF16), VMEM((len(places), 16, LANES), F32)],
        compiler_params=pltpu.CompilerParams(vmem_limit_bytes=48 * 2**20),
        cost_estimate=pl.CostEstimate(
            flops=4 * STEPS * HEADS * seq * HEAD_DIM,
            bytes_accessed=4 * seq * width,
            transcendentals=STEPS * HEADS * seq,
        ),
        name="attend",
    )(holder, where, keys, bias, cosine, sine, pages, *pieces)


def output_kernel(lhs_ref, weight_ref, out_ref, weight_buf, out_scr, sems):
    chunks, _, span = weight_buf.shape
    rows = lhs_ref.shape[0]
    pieces = chunks * span // LANES
    copies = []
    for i in range(chunks):
        copy = pltpu.make_async_copy(
            weight_ref.at[:, pl.ds(i * span, span)], weight_buf.at[i], sems.at[i]
        )
        copy.start()
        copies.append(copy)
    lhs = lhs_ref[...]
    for i in range(chunks):
        copies[i].wait()
        part = jnp.dot(lhs, weight_buf[i], preferred_element_type=F32)
        for c in range(span // LANES):
            out_scr[pl.ds(i * (span // LANES) + c, rows, stride=pieces), :] = part[
                :, c * LANES : (c + 1) * LANES
            ]
    out_ref[...] = out_scr[...].astype(BF16)


def output(lhs, weight):
    rows, depth = lhs.shape
    width = weight.shape[1]
    chunks = 8
    return pl.pallas_call(
        output_kernel,
        in_specs=[whole(), whole(pl.ANY)],
        out_specs=whole(),
        out_shape=jax.ShapeDtypeStruct((rows * width // LANES, LANES), BF16),
        scratch_shapes=[
            VMEM((chunks, depth, width // chunks), BF16),
            VMEM((rows * width // LANES, LANES), F32),
            pltpu.SemaphoreType.DMA((chunks,)),
        ],
        compiler_params=pltpu.CompilerParams(vmem_limit_bytes=48 * 2**20),
        cost_estimate=pl.CostEstimate(
            flops=2 * rows * depth * width, bytes_accessed=2 * depth * width, transcendentals=0
        ),
        name="output_project",
    )(lhs, weight)


def swap(block, bit, devices):
    return lax.ppermute(block, AXIS, [(i, i ^ bit) for i in range(devices)])


def exchange(blocks):
    return lax.all_to_all(blocks, AXIS, split_axis=0, concat_axis=0, tiled=True)


def local(
    hidden,
    norm_gain,
    query_weight,
    kv_weight,
    out_weight,
    key_factors,
    key_basis,
    value_store,
    lengths,
    block_slot,
    selection,
):
    devices = lax.axis_size(AXIS)
    me = lax.axis_index(AXIS)
    slots_dev, block_len, width = value_store.shape
    seq = key_factors.shape[1]
    pages = block_slot.shape[1]
    model = hidden.shape[2]
    q_cols = query_weight.shape[1]
    k_cols = kv_weight.shape[1]
    fast = q_cols == 4 * HEAD_DIM and k_cols == HEAD_DIM
    pieces = model // LANES

    asked, holder = ask(block_slot, devices, slots_dev)
    sent_pages = pick_pages(exchange(asked), value_store)
    fetched = exchange(sent_pages)

    block = hidden[:, 0].reshape(1, STEPS * pieces, LANES)
    order = [0]
    bit = devices // 2
    while bit:
        if bit == 2:
            block, sent_pages = lax.optimization_barrier((block, sent_pages))
        other = swap(block, bit, devices)
        order = order + [k ^ bit for k in order]
        bit //= 2
        if bit:
            block = jnp.concatenate([block, other], axis=0)
    if fast:
        bits = devices.bit_length() - 1
        turn = [int(format(k, "b").zfill(bits)[::-1], 2) for k in order]
    else:
        turn = order
    projected = project(
        block.reshape(-1, LANES),
        other.reshape(-1, LANES),
        norm_gain.reshape(pieces, LANES),
        query_weight,
        kv_weight,
        tuple(turn),
        fast,
    )
    if fast:
        near, far = projected
        sent, kept, arrived = far[None], [near[None]], [near[None]]
        places = [(0, 0)]
        bit = 1
        while bit < devices:
            if bit > 1:
                middle = kept[0].shape[1] // 2
                sent = jnp.concatenate([part[:, middle:] for part in kept], axis=0)
                kept = [part[:, :middle] for part in kept]
            part = swap(sent, bit, devices)
            places += [(len(arrived), row) for row in range(part.shape[0])]
            arrived.append(part)
            kept.append(part)
            bit *= 2
        where = jnp.bitwise_xor(me, jnp.arange(devices, dtype=jnp.int32))
    else:
        targets = jnp.bitwise_xor(me, jnp.array(order, dtype=jnp.int32))
        columns = exchange(projected.reshape(devices, STEPS, q_cols + k_cols)[targets])
        query = columns[:, :, :q_cols].transpose(1, 0, 2).reshape(STEPS, HEADS // 4, 4, HEAD_DIM)
        query = query.transpose(1, 0, 2, 3).reshape(HEADS // 4, 8, HEAD_DIM)
        fresh = columns[:, :, q_cols:].transpose(1, 0, 2).reshape(STEPS, HEADS // 4, HEAD_DIM)
        fresh = jnp.pad(fresh.transpose(1, 0, 2), ((0, 0), (0, 8 - STEPS), (0, 0)))
        arrived = [jnp.concatenate([query, fresh], axis=1)[:, None]]
        places = [(0, row) for row in range(HEADS // 4)]
        where = jnp.arange(HEADS // 4, dtype=jnp.int32)

    cosine, sine = turn_tables(jnp.arange(seq, dtype=jnp.int32).astype(F32))
    keys = make_keys(key_factors[0], key_basis[0], cosine, sine)
    picked = jnp.any(
        selection[:, 0, :, None] == jnp.arange(pages, dtype=jnp.int32)[None, None, :], axis=1
    )
    usable = jnp.repeat(picked, block_len, axis=1) & (
        jnp.arange(seq, dtype=jnp.int32)[None, :] < lengths[0]
    )
    bias = jnp.where(usable, 0.0, -1e30).astype(F32)
    new_cos, new_sin = turn_tables(
        (lengths[0] + jnp.arange(STEPS, dtype=jnp.int32)).astype(F32)
    )
    heads = attend(
        holder, where, keys, bias, new_cos, new_sin, fetched, tuple(places), arrived
    )

    if fast:
        rows = exchange(heads.reshape(devices, STEPS * 4, HEAD_DIM))
        lhs = rows.reshape(devices, STEPS, 4 * HEAD_DIM).reshape(devices * STEPS, 4 * HEAD_DIM)
    else:
        flat = heads.reshape(HEADS // 4, STEPS, 4 * HEAD_DIM).transpose(1, 0, 2)
        flat = flat.reshape(STEPS, devices, model // devices).transpose(1, 0, 2)
        lhs = exchange(flat).reshape(devices * STEPS, model // devices)
    partial = output(lhs, out_weight)
    arrived = exchange(partial.reshape(devices, STEPS * pieces, LANES))
    total = jnp.sum(arrived.astype(F32), axis=0).astype(BF16)
    return total.reshape(STEPS, 1, model)


def solution(mesh):
    return jax.shard_map(
        local,
        mesh=mesh,
        in_specs=(
            P(None, ("groups", "session"), None),
            P(),
            P(None, "session"),
            P(None, "session"),
            P("session", None),
            P(("groups", "session"), None, None),
            P(("groups", "session"), None, None),
            P(("groups", "session"), None, None),
            P(("groups", "session")),
            P(("groups", "session"), None),
            P(None, ("groups", "session"), None),
        ),
        out_specs=P(None, ("groups", "session"), None),
        check_vma=False,
    )
```

```python
import functools
import math

import jax
import jax.numpy as jnp
from jax import lax
from jax.experimental import pallas as pl
from jax.experimental.pallas import tpu as pltpu
from jax.sharding import PartitionSpec as P

HEADS = 64
KV_HEADS = 8
HEAD_DIM = 128
STEPS = 2
GROUP = HEADS // KV_HEADS
LANES = 128
AXIS = "session"
VMEM = pltpu.VMEM
SMEM = pltpu.SMEM
F32 = jnp.float32
BF16 = jnp.bfloat16


def angles(positions):
    half = HEAD_DIM // 2
    frequency = jnp.exp(
        -jnp.arange(half, dtype=F32) * (2.0 * math.log(500000.0) / HEAD_DIM)
    )
    return positions[..., None] * frequency


def turn_tables(positions):
    angle = angles(positions)
    cosine, sine = jnp.cos(angle), jnp.sin(angle)
    return (
        jnp.concatenate([cosine, cosine], axis=-1),
        jnp.concatenate([-sine, sine], axis=-1),
    )


def whole(space=VMEM):
    return pl.BlockSpec(memory_space=space)


def ask_kernel(slots_dev, slots_ref, asked_ref, holder_ref):
    for m in range(holder_ref.shape[0]):
        slot = slots_ref[0, 2 * m]
        holder = lax.div(slot, slots_dev)
        holder_ref[m] = holder
        asked_ref[holder, 0, 0] = slot - holder * slots_dev
        asked_ref[holder, 0, 1] = slots_ref[0, 2 * m + 1] - holder * slots_dev


def ask(block_slot, devices, slots_dev):
    return pl.pallas_call(
        functools.partial(ask_kernel, slots_dev),
        in_specs=[whole(SMEM)],
        out_specs=(whole(SMEM), whole(SMEM)),
        out_shape=(
            jax.ShapeDtypeStruct((devices, 1, 2), jnp.int32),
            jax.ShapeDtypeStruct((block_slot.shape[1] // 2,), jnp.int32),
        ),
        name="ask_pages",
    )(block_slot)


def pick_kernel(asked_ref, store_ref, out_ref):
    block_len = store_ref.shape[1]
    for i in range(asked_ref.shape[0]):
        for k in range(2):
            out_ref[i, k * block_len : (k + 1) * block_len, :] = store_ref[asked_ref[i, 0, k]]


def pick_pages(asked, store):
    count = asked.shape[0]
    _, block_len, width = store.shape
    return pl.pallas_call(
        pick_kernel,
        in_specs=[whole(SMEM), whole()],
        out_specs=whole(),
        out_shape=jax.ShapeDtypeStruct((count, 2 * block_len, width), store.dtype),
        compiler_params=pltpu.CompilerParams(vmem_limit_bytes=32 * 2**20),
        name="pick_pages",
    )(asked, store)


def keys_kernel(factors_ref, basis_ref, cos_ref, sin_ref, out_ref):
    product = jnp.dot(factors_ref[...], basis_ref[...], preferred_element_type=F32)
    cosine, sine = cos_ref[...], sin_ref[...]
    for head in range(KV_HEADS):
        lanes = slice(head * HEAD_DIM, (head + 1) * HEAD_DIM)
        part = product[:, lanes]
        turned = part * cosine + pltpu.roll(part, HEAD_DIM // 2, 1) * sine
        out_ref[:, lanes] = turned.astype(BF16)


def make_keys(factors, basis, cosine, sine):
    seq, rank = factors.shape
    width = basis.shape[1]
    rows = min(seq, 512)
    return pl.pallas_call(
        keys_kernel,
        grid=(seq // rows,),
        in_specs=[
            pl.BlockSpec((rows, rank), lambda i: (i, 0)),
            pl.BlockSpec((rank, width), lambda i: (0, 0)),
            pl.BlockSpec((rows, HEAD_DIM), lambda i: (i, 0)),
            pl.BlockSpec((rows, HEAD_DIM), lambda i: (i, 0)),
        ],
        out_specs=pl.BlockSpec((rows, width), lambda i: (i, 0)),
        out_shape=jax.ShapeDtypeStruct((seq, width), BF16),
        compiler_params=pltpu.CompilerParams(vmem_limit_bytes=32 * 2**20),
        cost_estimate=pl.CostEstimate(
            flops=2 * seq * rank * width, bytes_accessed=4 * seq * width, transcendentals=0
        ),
        name="turned_keys",
    )(factors, basis, cosine, sine)


def project_kernel(
    order, fast, first_ref, second_ref, gain_ref, wq_ref, wk_ref, *rest
):
    out_refs = rest[: 2 if fast else 1]
    x_scr, lhs_scr, wq_buf, wk_buf, out_scr, sems = rest[len(out_refs) :]
    depth, q_cols = wq_ref.shape
    k_cols = wk_ref.shape[1]
    chunks = wq_buf.shape[0]
    span = depth // chunks
    pieces = depth // LANES
    copies = []
    for i in range(chunks):
        rows = pl.ds(i * span, span)
        pair = (
            pltpu.make_async_copy(wq_ref.at[rows, :], wq_buf.at[i], sems.at[0, i]),
            pltpu.make_async_copy(wk_ref.at[rows, :], wk_buf.at[i], sems.at[1, i]),
        )
        for copy in pair:
            copy.start()
        copies.append(pair)
    half = first_ref.shape[0]
    x_scr[:half] = first_ref[...].astype(F32)
    x_scr[half:] = second_ref[...].astype(F32)
    count = 2 * half // pieces
    squares = jnp.zeros((count, LANES), F32)
    for c in range(pieces):
        part = x_scr[pl.ds(c, count, stride=pieces), :]
        squares = squares + part * part
    scale = lax.rsqrt(jnp.sum(squares, axis=1, keepdims=True) * (1.0 / depth) + 1e-05)
    for c in range(pieces):
        part = x_scr[pl.ds(c, count, stride=pieces), :]
        gain = gain_ref[pl.ds(c, 1), :].astype(F32)
        lhs_scr[:, c * LANES : (c + 1) * LANES] = (part * scale * gain).astype(BF16)
    q_sum = jnp.zeros((count, q_cols), F32)
    k_sum = jnp.zeros((count, k_cols), F32)
    for i in range(chunks):
        for copy in copies[i]:
            copy.wait()
        lhs = lhs_scr[:, i * span : (i + 1) * span]
        q_sum = q_sum + jnp.dot(lhs, wq_buf[i], preferred_element_type=F32)
        k_sum = k_sum + jnp.dot(lhs, wk_buf[i], preferred_element_type=F32)
    if not fast:
        out_refs[0][:, :q_cols] = q_sum.astype(BF16)
        out_refs[0][:, q_cols:] = k_sum.astype(BF16)
        return
    per = q_cols // LANES
    out_scr[...] = jnp.zeros_like(out_scr)
    for j, place in enumerate(order):
        for step in range(STEPS):
            row = j * STEPS + step
            for c in range(per):
                out_scr[place, step * per + c : step * per + c + 1, :] = q_sum[
                    row : row + 1, c * LANES : (c + 1) * LANES
                ]
            out_scr[place, STEPS * per + step : STEPS * per + step + 1, :] = k_sum[
                row : row + 1, :
            ]
    near_ref, far_ref = out_refs
    half = near_ref.shape[0]
    near_ref[...] = out_scr[:half].astype(BF16)
    far_ref[...] = out_scr[half:].astype(BF16)


def project(first, second, gain, query_weight, kv_weight, order, fast):
    depth, q_cols = query_weight.shape
    k_cols = kv_weight.shape[1]
    pieces = depth // LANES
    rows = 2 * first.shape[0] // pieces
    devices = rows // STEPS
    chunks = 8
    span = depth // chunks
    if fast:
        shape = (jax.ShapeDtypeStruct((devices // 2, 16, LANES), BF16),) * 2
        out_specs = (whole(), whole())
    else:
        shape = jax.ShapeDtypeStruct((rows, q_cols + k_cols), BF16)
        out_specs = whole()
    return pl.pallas_call(
        functools.partial(project_kernel, order, fast),
        in_specs=[whole(), whole(), whole(), whole(pl.ANY), whole(pl.ANY)],
        out_specs=out_specs,
        out_shape=shape,
        scratch_shapes=[
            VMEM((rows * pieces, LANES), F32),
            VMEM((rows, depth), BF16),
            VMEM((chunks, span, q_cols), BF16),
            VMEM((chunks, span, k_cols), BF16),
            VMEM((devices, 16, LANES) if fast else (8, LANES), F32),
            pltpu.SemaphoreType.DMA((2, chunks)),
        ],
        compiler_params=pltpu.CompilerParams(vmem_limit_bytes=48 * 2**20),
        cost_estimate=pl.CostEstimate(
            flops=2 * rows * depth * (q_cols + k_cols),
            bytes_accessed=2 * depth * (q_cols + k_cols),
            transcendentals=0,
        ),
        name="norm_project",
    )(first, second, gain, query_weight, kv_weight)


def attend_kernel(
    places, holder_ref, where_ref, keys_ref, bias_ref, cos_ref, sin_ref, pages_ref, *rest
):
    pieces = rest[:-3]
    out_ref, values_scr, columns_scr = rest[-3:]
    for r, (piece, row) in enumerate(places):
        columns_scr[where_ref[r]] = pieces[piece][row, 0].astype(F32)
    seq = keys_ref.shape[0]
    pairs, pair_rows = pages_ref.shape[0], pages_ref.shape[1]
    score_scale = 1.0 / math.sqrt(HEAD_DIM)
    half = HEAD_DIM // 2
    rows = 2 * GROUP
    for m in range(pairs):
        values_scr[m * pair_rows : (m + 1) * pair_rows, :] = pages_ref[holder_ref[m]]
    columns = columns_scr[...]
    count = columns.shape[0]
    query = columns[:, :8, :].reshape(count * 8, HEAD_DIM)
    fresh = columns[:, 8:, :]
    row_step = lax.rem(lax.broadcasted_iota(jnp.int32, (count * 8, 1), 0) // 4, STEPS)
    later = row_step == 1
    cosine = jnp.where(later, cos_ref[1:2, :], cos_ref[0:1, :])
    sine = jnp.where(later, sin_ref[1:2, :], sin_ref[0:1, :])
    turned = (query * cosine + pltpu.roll(query, half, 1) * sine).astype(BF16)
    turned_wide = turned.astype(F32)
    step_later = later[:rows]
    bias = jnp.where(step_later, bias_ref[1:2, :], bias_ref[0:1, :])
    new_keys = []
    for step in range(STEPS):
        part = fresh[:KV_HEADS, step, :]
        new = part * cos_ref[step : step + 1, :] + pltpu.roll(part, half, 1) * sin_ref[step : step + 1, :]
        new_keys.append(new.astype(BF16).astype(F32))
    for head in range(KV_HEADS):
        lanes = slice(head * HEAD_DIM, (head + 1) * HEAD_DIM)
        mine = slice(head * rows, (head + 1) * rows)
        scores = (
            lax.dot_general(
                turned[mine], keys_ref[:, lanes], (((1,), (1,)), ((), ())),
                preferred_element_type=F32,
            )
            * score_scale
            + bias
        )
        recent0 = (
            jnp.sum(turned_wide[mine] * new_keys[0][head : head + 1, :], axis=1, keepdims=True)
            * score_scale
        )
        recent1 = (
            jnp.sum(turned_wide[mine] * new_keys[1][head : head + 1, :], axis=1, keepdims=True)
            * score_scale
        )
        recent1 = jnp.where(step_later, recent1, -1e30)
        largest = jnp.maximum(
            jnp.max(scores, axis=1, keepdims=True), jnp.maximum(recent0, recent1)
        )
        cache_exp = jnp.exp(scores - largest)
        exp0 = jnp.exp(recent0 - largest)
        exp1 = jnp.exp(recent1 - largest)
        denominator = jnp.sum(cache_exp, axis=1, keepdims=True) + (exp0 + exp1)
        weights = (cache_exp / denominator).astype(BF16)
        weight0 = (exp0 / denominator).astype(BF16).astype(F32)
        weight1 = (exp1 / denominator).astype(BF16).astype(F32)
        mixed = jnp.dot(weights, values_scr[:, lanes], preferred_element_type=F32)
        mixed = mixed + weight0 * fresh[KV_HEADS + head, 0:1, :]
        mixed = mixed + weight1 * fresh[KV_HEADS + head, 1:2, :]
        out_ref[mine, :] = mixed.astype(BF16)


def attend(holder, where, keys, bias, cosine, sine, pages, places, pieces):
    seq, width = keys.shape
    return pl.pallas_call(
        functools.partial(attend_kernel, places),
        in_specs=[whole(SMEM)] * 2 + [whole()] * (5 + len(pieces)),
        out_specs=whole(),
        out_shape=jax.ShapeDtypeStruct((STEPS * HEADS, HEAD_DIM), BF16),
        scratch_shapes=[VMEM((seq, width), BF16), VMEM((len(places), 16, LANES), F32)],
        compiler_params=pltpu.CompilerParams(vmem_limit_bytes=48 * 2**20),
        cost_estimate=pl.CostEstimate(
            flops=4 * STEPS * HEADS * seq * HEAD_DIM,
            bytes_accessed=4 * seq * width,
            transcendentals=STEPS * HEADS * seq,
        ),
        name="attend",
    )(holder, where, keys, bias, cosine, sine, pages, *pieces)


def output_kernel(lhs_ref, weight_ref, out_ref, weight_buf, out_scr, sems):
    chunks, _, span = weight_buf.shape
    rows = lhs_ref.shape[0]
    pieces = chunks * span // LANES
    copies = []
    for i in range(chunks):
        copy = pltpu.make_async_copy(
            weight_ref.at[:, pl.ds(i * span, span)], weight_buf.at[i], sems.at[i]
        )
        copy.start()
        copies.append(copy)
    lhs = lhs_ref[...]
    for i in range(chunks):
        copies[i].wait()
        part = jnp.dot(lhs, weight_buf[i], preferred_element_type=F32)
        for c in range(span // LANES):
            out_scr[pl.ds(i * (span // LANES) + c, rows, stride=pieces), :] = part[
                :, c * LANES : (c + 1) * LANES
            ]
    out_ref[...] = out_scr[...].astype(BF16)


def output(lhs, weight):
    rows, depth = lhs.shape
    width = weight.shape[1]
    chunks = 8
    return pl.pallas_call(
        output_kernel,
        in_specs=[whole(), whole(pl.ANY)],
        out_specs=whole(),
        out_shape=jax.ShapeDtypeStruct((rows * width // LANES, LANES), BF16),
        scratch_shapes=[
            VMEM((chunks, depth, width // chunks), BF16),
            VMEM((rows * width // LANES, LANES), F32),
            pltpu.SemaphoreType.DMA((chunks,)),
        ],
        compiler_params=pltpu.CompilerParams(vmem_limit_bytes=48 * 2**20),
        cost_estimate=pl.CostEstimate(
            flops=2 * rows * depth * width, bytes_accessed=2 * depth * width, transcendentals=0
        ),
        name="output_project",
    )(lhs, weight)


def swap(block, bit, devices):
    return lax.ppermute(block, AXIS, [(i, i ^ bit) for i in range(devices)])


def exchange(blocks):
    return lax.all_to_all(blocks, AXIS, split_axis=0, concat_axis=0, tiled=True)


def local(
    hidden,
    norm_gain,
    query_weight,
    kv_weight,
    out_weight,
    key_factors,
    key_basis,
    value_store,
    lengths,
    block_slot,
    selection,
):
    devices = lax.axis_size(AXIS)
    me = lax.axis_index(AXIS)
    slots_dev, block_len, width = value_store.shape
    seq = key_factors.shape[1]
    pages = block_slot.shape[1]
    model = hidden.shape[2]
    q_cols = query_weight.shape[1]
    k_cols = kv_weight.shape[1]
    fast = q_cols == 4 * HEAD_DIM and k_cols == HEAD_DIM
    pieces = model // LANES

    asked, holder = ask(block_slot, devices, slots_dev)
    asked_here = exchange(asked)

    block = hidden[:, 0].reshape(1, STEPS * pieces, LANES)
    order = [0]
    bit = devices // 2
    while bit:
        if bit == 2:
            block, asked_here = lax.optimization_barrier((block, asked_here))
            sent_pages = pick_pages(asked_here, value_store)
            fetched = exchange(sent_pages)
            block, sent_pages = lax.optimization_barrier((block, sent_pages))
        other = swap(block, bit, devices)
        order = order + [k ^ bit for k in order]
        bit //= 2
        if bit:
            block = jnp.concatenate([block, other], axis=0)
    if fast:
        bits = devices.bit_length() - 1
        turn = [int(format(k, "b").zfill(bits)[::-1], 2) for k in order]
    else:
        turn = order
    projected = project(
        block.reshape(-1, LANES),
        other.reshape(-1, LANES),
        norm_gain.reshape(pieces, LANES),
        query_weight,
        kv_weight,
        tuple(turn),
        fast,
    )
    if fast:
        near, far = projected
        sent, kept, arrived = far[None], [near[None]], [near[None]]
        places = [(0, 0)]
        bit = 1
        while bit < devices:
            if bit > 1:
                middle = kept[0].shape[1] // 2
                sent = jnp.concatenate([part[:, middle:] for part in kept], axis=0)
                kept = [part[:, :middle] for part in kept]
            part = swap(sent, bit, devices)
            places += [(len(arrived), row) for row in range(part.shape[0])]
            arrived.append(part)
            kept.append(part)
            bit *= 2
        where = jnp.bitwise_xor(me, jnp.arange(devices, dtype=jnp.int32))
    else:
        targets = jnp.bitwise_xor(me, jnp.array(order, dtype=jnp.int32))
        columns = exchange(projected.reshape(devices, STEPS, q_cols + k_cols)[targets])
        query = columns[:, :, :q_cols].transpose(1, 0, 2).reshape(STEPS, HEADS // 4, 4, HEAD_DIM)
        query = query.transpose(1, 0, 2, 3).reshape(HEADS // 4, 8, HEAD_DIM)
        fresh = columns[:, :, q_cols:].transpose(1, 0, 2).reshape(STEPS, HEADS // 4, HEAD_DIM)
        fresh = jnp.pad(fresh.transpose(1, 0, 2), ((0, 0), (0, 8 - STEPS), (0, 0)))
        arrived = [jnp.concatenate([query, fresh], axis=1)[:, None]]
        places = [(0, row) for row in range(HEADS // 4)]
        where = jnp.arange(HEADS // 4, dtype=jnp.int32)

    cosine, sine = turn_tables(jnp.arange(seq, dtype=jnp.int32).astype(F32))
    keys = make_keys(key_factors[0], key_basis[0], cosine, sine)
    picked = jnp.any(
        selection[:, 0, :, None] == jnp.arange(pages, dtype=jnp.int32)[None, None, :], axis=1
    )
    usable = jnp.repeat(picked, block_len, axis=1) & (
        jnp.arange(seq, dtype=jnp.int32)[None, :] < lengths[0]
    )
    bias = jnp.where(usable, 0.0, -1e30).astype(F32)
    new_cos, new_sin = turn_tables(
        (lengths[0] + jnp.arange(STEPS, dtype=jnp.int32)).astype(F32)
    )
    heads = attend(
        holder, where, keys, bias, new_cos, new_sin, fetched, tuple(places), arrived
    )

    if fast:
        rows = exchange(heads.reshape(devices, STEPS * 4, HEAD_DIM))
        lhs = rows.reshape(devices, STEPS, 4 * HEAD_DIM).reshape(devices * STEPS, 4 * HEAD_DIM)
    else:
        flat = heads.reshape(HEADS // 4, STEPS, 4 * HEAD_DIM).transpose(1, 0, 2)
        flat = flat.reshape(STEPS, devices, model // devices).transpose(1, 0, 2)
        lhs = exchange(flat).reshape(devices * STEPS, model // devices)
    partial = output(lhs, out_weight)
    arrived = exchange(partial.reshape(devices, STEPS * pieces, LANES))
    total = jnp.sum(arrived.astype(F32), axis=0).astype(BF16)
    return total.reshape(STEPS, 1, model)


def solution(mesh):
    return jax.shard_map(
        local,
        mesh=mesh,
        in_specs=(
            P(None, ("groups", "session"), None),
            P(),
            P(None, "session"),
            P(None, "session"),
            P("session", None),
            P(("groups", "session"), None, None),
            P(("groups", "session"), None, None),
            P(("groups", "session"), None, None),
            P(("groups", "session")),
            P(("groups", "session"), None),
            P(None, ("groups", "session"), None),
        ),
        out_specs=P(None, ("groups", "session"), None),
        check_vma=False,
    )
```

```python
import functools
import math

import jax
import jax.numpy as jnp
from jax import lax
from jax.experimental import pallas as pl
from jax.experimental.pallas import tpu as pltpu
from jax.sharding import PartitionSpec as P

HEADS = 64
KV_HEADS = 8
HEAD_DIM = 128
STEPS = 2
GROUP = HEADS // KV_HEADS
LANES = 128
EXTRA = 16
AXIS = "session"
VMEM = pltpu.VMEM
SMEM = pltpu.SMEM
F32 = jnp.float32
BF16 = jnp.bfloat16


def angles(positions):
    half = HEAD_DIM // 2
    frequency = jnp.exp(
        -jnp.arange(half, dtype=F32) * (2.0 * math.log(500000.0) / HEAD_DIM)
    )
    return positions[..., None] * frequency


def turn_tables(positions):
    angle = angles(positions)
    cosine, sine = jnp.cos(angle), jnp.sin(angle)
    return (
        jnp.concatenate([cosine, cosine], axis=-1),
        jnp.concatenate([-sine, sine], axis=-1),
    )


def whole(space=VMEM):
    return pl.BlockSpec(memory_space=space)


def prepare_kernel(slots_dev, hidden_ref, slots_ref, block_ref, holder_ref, wide_scr):
    steps, model = hidden_ref.shape
    pieces = model // LANES
    wide = hidden_ref[...].astype(F32)
    for step in range(steps):
        for c in range(pieces):
            row = step * pieces + c
            wide_scr[row : row + 1, :] = wide[step : step + 1, c * LANES : (c + 1) * LANES]
    lane = lax.broadcasted_iota(jnp.int32, (EXTRA, LANES), 1)
    parity = lax.broadcasted_iota(jnp.int32, (EXTRA, LANES), 0)
    table = jnp.zeros((EXTRA, LANES), jnp.int32)
    for m in range(holder_ref.shape[0]):
        slot = slots_ref[0, 2 * m]
        holder = lax.div(slot, slots_dev)
        holder_ref[m] = holder
        base = holder * slots_dev
        pair = jnp.where(parity == 0, slot - base, slots_ref[0, 2 * m + 1] - base)
        table = jnp.where(lane == holder, pair, table)
    wide_scr[steps * pieces :, :] = table.astype(F32)
    block_ref[0] = wide_scr[...].astype(BF16)


def prepare(hidden, block_slot, slots_dev):
    assert slots_dev <= 256
    steps, model = hidden.shape
    rows = steps * model // LANES + EXTRA
    return pl.pallas_call(
        functools.partial(prepare_kernel, slots_dev),
        in_specs=[whole(), whole(SMEM)],
        out_specs=(whole(), whole(SMEM)),
        out_shape=(
            jax.ShapeDtypeStruct((1, rows, LANES), BF16),
            jax.ShapeDtypeStruct((block_slot.shape[1] // 2,), jnp.int32),
        ),
        scratch_shapes=[VMEM((rows, LANES), F32)],
        name="prepare",
    )(hidden, block_slot)


def pick_kernel(order, me_ref, first_ref, second_ref, store_ref, out_ref, table_scr, table_smem, sem):
    block_len = store_ref.shape[1]
    half, rows, _ = first_ref.shape
    for j in range(2 * half):
        source = first_ref if j < half else second_ref
        asked = source[j % half, rows - EXTRA :, :].astype(F32)
        table_scr[j] = asked[:8].astype(jnp.int32)
    copy = pltpu.make_async_copy(table_scr, table_smem, sem)
    copy.start()
    copy.wait()
    me = me_ref[0]
    for j in range(2 * half):
        target = jnp.bitwise_xor(me, order[j])
        for k in range(2):
            out_ref[target, k * block_len : (k + 1) * block_len, :] = store_ref[
                table_smem[j, k, me]
            ]


def pick_pages(me, first, second, store, order):
    count = 2 * first.shape[0]
    _, block_len, width = store.shape
    return pl.pallas_call(
        functools.partial(pick_kernel, order),
        in_specs=[whole(SMEM), whole(), whole(), whole()],
        out_specs=whole(),
        out_shape=jax.ShapeDtypeStruct((count, 2 * block_len, width), store.dtype),
        scratch_shapes=[
            VMEM((count, 8, LANES), jnp.int32),
            SMEM((count, 8, LANES), jnp.int32),
            pltpu.SemaphoreType.DMA(()),
        ],
        compiler_params=pltpu.CompilerParams(vmem_limit_bytes=36 * 2**20),
        name="pick_pages",
    )(me, first, second, store)


def keys_kernel(factors_ref, basis_ref, cos_ref, sin_ref, out_ref):
    product = jnp.dot(factors_ref[...], basis_ref[...], preferred_element_type=F32)
    cosine, sine = cos_ref[...], sin_ref[...]
    for head in range(KV_HEADS):
        lanes = slice(head * HEAD_DIM, (head + 1) * HEAD_DIM)
        part = product[:, lanes]
        turned = part * cosine + pltpu.roll(part, HEAD_DIM // 2, 1) * sine
        out_ref[:, lanes] = turned.astype(BF16)


def make_keys(factors, basis, cosine, sine):
    seq, rank = factors.shape
    width = basis.shape[1]
    rows = min(seq, 512)
    return pl.pallas_call(
        keys_kernel,
        grid=(seq // rows,),
        in_specs=[
            pl.BlockSpec((rows, rank), lambda i: (i, 0)),
            pl.BlockSpec((rank, width), lambda i: (0, 0)),
            pl.BlockSpec((rows, HEAD_DIM), lambda i: (i, 0)),
            pl.BlockSpec((rows, HEAD_DIM), lambda i: (i, 0)),
        ],
        out_specs=pl.BlockSpec((rows, width), lambda i: (i, 0)),
        out_shape=jax.ShapeDtypeStruct((seq, width), BF16),
        compiler_params=pltpu.CompilerParams(vmem_limit_bytes=32 * 2**20),
        cost_estimate=pl.CostEstimate(
            flops=2 * seq * rank * width, bytes_accessed=4 * seq * width, transcendentals=0
        ),
        name="turned_keys",
    )(factors, basis, cosine, sine)


def project_kernel(
    order, fast, first_ref, second_ref, gain_ref, wq_ref, wk_ref, *rest
):
    out_refs = rest[: 2 if fast else 1]
    x_scr, lhs_scr, wq_buf, wk_buf, out_scr, sems = rest[len(out_refs) :]
    depth, q_cols = wq_ref.shape
    k_cols = wk_ref.shape[1]
    chunks = wq_buf.shape[0]
    span = depth // chunks
    pieces = depth // LANES
    copies = []
    for i in range(chunks):
        rows = pl.ds(i * span, span)
        pair = (
            pltpu.make_async_copy(wq_ref.at[rows, :], wq_buf.at[i], sems.at[0, i]),
            pltpu.make_async_copy(wk_ref.at[rows, :], wk_buf.at[i], sems.at[1, i]),
        )
        for copy in pair:
            copy.start()
        copies.append(pair)
    half = first_ref.shape[0]
    count = 2 * half * STEPS
    rows = STEPS * pieces
    for j in range(2 * half):
        source = first_ref if j < half else second_ref
        x_scr[j * rows : (j + 1) * rows] = source[j % half, :rows, :].astype(F32)
    squares = jnp.zeros((count, LANES), F32)
    for c in range(pieces):
        part = x_scr[pl.ds(c, count, stride=pieces), :]
        squares = squares + part * part
    scale = lax.rsqrt(jnp.sum(squares, axis=1, keepdims=True) * (1.0 / depth) + 1e-05)
    for c in range(pieces):
        part = x_scr[pl.ds(c, count, stride=pieces), :]
        gain = gain_ref[pl.ds(c, 1), :].astype(F32)
        lhs_scr[:, c * LANES : (c + 1) * LANES] = (part * scale * gain).astype(BF16)
    q_sum = jnp.zeros((count, q_cols), F32)
    k_sum = jnp.zeros((count, k_cols), F32)
    for i in range(chunks):
        for copy in copies[i]:
            copy.wait()
        lhs = lhs_scr[:, i * span : (i + 1) * span]
        q_sum = q_sum + jnp.dot(lhs, wq_buf[i], preferred_element_type=F32)
        k_sum = k_sum + jnp.dot(lhs, wk_buf[i], preferred_element_type=F32)
    if not fast:
        out_refs[0][:, :q_cols] = q_sum.astype(BF16)
        out_refs[0][:, q_cols:] = k_sum.astype(BF16)
        return
    per = q_cols // LANES
    out_scr[...] = jnp.zeros_like(out_scr)
    for j, place in enumerate(order):
        for step in range(STEPS):
            row = j * STEPS + step
            for c in range(per):
                out_scr[place, step * per + c : step * per + c + 1, :] = q_sum[
                    row : row + 1, c * LANES : (c + 1) * LANES
                ]
            out_scr[place, STEPS * per + step : STEPS * per + step + 1, :] = k_sum[
                row : row + 1, :
            ]
    near_ref, far_ref = out_refs
    half = near_ref.shape[0]
    near_ref[...] = out_scr[:half].astype(BF16)
    far_ref[...] = out_scr[half:].astype(BF16)


def project(first, second, gain, query_weight, kv_weight, order, fast):
    depth, q_cols = query_weight.shape
    k_cols = kv_weight.shape[1]
    pieces = depth // LANES
    devices = 2 * first.shape[0]
    rows = devices * STEPS
    chunks = 8
    span = depth // chunks
    if fast:
        shape = (jax.ShapeDtypeStruct((devices // 2, 16, LANES), BF16),) * 2
        out_specs = (whole(), whole())
    else:
        shape = jax.ShapeDtypeStruct((rows, q_cols + k_cols), BF16)
        out_specs = whole()
    return pl.pallas_call(
        functools.partial(project_kernel, order, fast),
        in_specs=[whole(), whole(), whole(), whole(pl.ANY), whole(pl.ANY)],
        out_specs=out_specs,
        out_shape=shape,
        scratch_shapes=[
            VMEM((rows * pieces, LANES), F32),
            VMEM((rows, depth), BF16),
            VMEM((chunks, span, q_cols), BF16),
            VMEM((chunks, span, k_cols), BF16),
            VMEM((devices, 16, LANES) if fast else (8, LANES), F32),
            pltpu.SemaphoreType.DMA((2, chunks)),
        ],
        compiler_params=pltpu.CompilerParams(vmem_limit_bytes=48 * 2**20),
        cost_estimate=pl.CostEstimate(
            flops=2 * rows * depth * (q_cols + k_cols),
            bytes_accessed=2 * depth * (q_cols + k_cols),
            transcendentals=0,
        ),
        name="norm_project",
    )(first, second, gain, query_weight, kv_weight)


def attend_kernel(
    places, holder_ref, where_ref, keys_ref, bias_ref, cos_ref, sin_ref, pages_ref, *rest
):
    pieces = rest[:-3]
    out_ref, values_scr, columns_scr = rest[-3:]
    for r, (piece, row) in enumerate(places):
        columns_scr[where_ref[r]] = pieces[piece][row, 0].astype(F32)
    seq = keys_ref.shape[0]
    pairs, pair_rows = pages_ref.shape[0], pages_ref.shape[1]
    score_scale = 1.0 / math.sqrt(HEAD_DIM)
    half = HEAD_DIM // 2
    rows = 2 * GROUP
    for m in range(pairs):
        values_scr[m * pair_rows : (m + 1) * pair_rows, :] = pages_ref[holder_ref[m]]
    columns = columns_scr[...]
    count = columns.shape[0]
    query = columns[:, :8, :].reshape(count * 8, HEAD_DIM)
    fresh = columns[:, 8:, :]
    row_step = lax.rem(lax.broadcasted_iota(jnp.int32, (count * 8, 1), 0) // 4, STEPS)
    later = row_step == 1
    cosine = jnp.where(later, cos_ref[1:2, :], cos_ref[0:1, :])
    sine = jnp.where(later, sin_ref[1:2, :], sin_ref[0:1, :])
    turned = (query * cosine + pltpu.roll(query, half, 1) * sine).astype(BF16)
    turned_wide = turned.astype(F32)
    step_later = later[:rows]
    bias = jnp.where(step_later, bias_ref[1:2, :], bias_ref[0:1, :])
    new_keys = []
    for step in range(STEPS):
        part = fresh[:KV_HEADS, step, :]
        new = part * cos_ref[step : step + 1, :] + pltpu.roll(part, half, 1) * sin_ref[step : step + 1, :]
        new_keys.append(new.astype(BF16).astype(F32))
    for head in range(KV_HEADS):
        lanes = slice(head * HEAD_DIM, (head + 1) * HEAD_DIM)
        mine = slice(head * rows, (head + 1) * rows)
        scores = (
            lax.dot_general(
                turned[mine], keys_ref[:, lanes], (((1,), (1,)), ((), ())),
                preferred_element_type=F32,
            )
            * score_scale
            + bias
        )
        recent0 = (
            jnp.sum(turned_wide[mine] * new_keys[0][head : head + 1, :], axis=1, keepdims=True)
            * score_scale
        )
        recent1 = (
            jnp.sum(turned_wide[mine] * new_keys[1][head : head + 1, :], axis=1, keepdims=True)
            * score_scale
        )
        recent1 = jnp.where(step_later, recent1, -1e30)
        largest = jnp.maximum(
            jnp.max(scores, axis=1, keepdims=True), jnp.maximum(recent0, recent1)
        )
        cache_exp = jnp.exp(scores - largest)
        exp0 = jnp.exp(recent0 - largest)
        exp1 = jnp.exp(recent1 - largest)
        denominator = jnp.sum(cache_exp, axis=1, keepdims=True) + (exp0 + exp1)
        weights = (cache_exp / denominator).astype(BF16)
        weight0 = (exp0 / denominator).astype(BF16).astype(F32)
        weight1 = (exp1 / denominator).astype(BF16).astype(F32)
        mixed = jnp.dot(weights, values_scr[:, lanes], preferred_element_type=F32)
        mixed = mixed + weight0 * fresh[KV_HEADS + head, 0:1, :]
        mixed = mixed + weight1 * fresh[KV_HEADS + head, 1:2, :]
        out_ref[mine, :] = mixed.astype(BF16)


def attend(holder, where, keys, bias, cosine, sine, pages, places, pieces):
    seq, width = keys.shape
    return pl.pallas_call(
        functools.partial(attend_kernel, places),
        in_specs=[whole(SMEM)] * 2 + [whole()] * (5 + len(pieces)),
        out_specs=whole(),
        out_shape=jax.ShapeDtypeStruct((STEPS * HEADS, HEAD_DIM), BF16),
        scratch_shapes=[VMEM((seq, width), BF16), VMEM((len(places), 16, LANES), F32)],
        compiler_params=pltpu.CompilerParams(vmem_limit_bytes=48 * 2**20),
        cost_estimate=pl.CostEstimate(
            flops=4 * STEPS * HEADS * seq * HEAD_DIM,
            bytes_accessed=4 * seq * width,
            transcendentals=STEPS * HEADS * seq,
        ),
        name="attend",
    )(holder, where, keys, bias, cosine, sine, pages, *pieces)


def output_kernel(lhs_ref, weight_ref, out_ref, weight_buf, out_scr, sems):
    chunks, _, span = weight_buf.shape
    rows = lhs_ref.shape[0]
    pieces = chunks * span // LANES
    copies = []
    for i in range(chunks):
        copy = pltpu.make_async_copy(
            weight_ref.at[:, pl.ds(i * span, span)], weight_buf.at[i], sems.at[i]
        )
        copy.start()
        copies.append(copy)
    lhs = lhs_ref[...]
    for i in range(chunks):
        copies[i].wait()
        part = jnp.dot(lhs, weight_buf[i], preferred_element_type=F32)
        for c in range(span // LANES):
            out_scr[pl.ds(i * (span // LANES) + c, rows, stride=pieces), :] = part[
                :, c * LANES : (c + 1) * LANES
            ]
    out_ref[...] = out_scr[...].astype(BF16)


def output(lhs, weight):
    rows, depth = lhs.shape
    width = weight.shape[1]
    chunks = 8
    return pl.pallas_call(
        output_kernel,
        in_specs=[whole(), whole(pl.ANY)],
        out_specs=whole(),
        out_shape=jax.ShapeDtypeStruct((rows * width // LANES, LANES), BF16),
        scratch_shapes=[
            VMEM((chunks, depth, width // chunks), BF16),
            VMEM((rows * width // LANES, LANES), F32),
            pltpu.SemaphoreType.DMA((chunks,)),
        ],
        compiler_params=pltpu.CompilerParams(vmem_limit_bytes=48 * 2**20),
        cost_estimate=pl.CostEstimate(
            flops=2 * rows * depth * width, bytes_accessed=2 * depth * width, transcendentals=0
        ),
        name="output_project",
    )(lhs, weight)


def swap(block, bit, devices):
    return lax.ppermute(block, AXIS, [(i, i ^ bit) for i in range(devices)])


def exchange(blocks):
    return lax.all_to_all(blocks, AXIS, split_axis=0, concat_axis=0, tiled=True)


def local(
    hidden,
    norm_gain,
    query_weight,
    kv_weight,
    out_weight,
    key_factors,
    key_basis,
    value_store,
    lengths,
    block_slot,
    selection,
):
    devices = lax.axis_size(AXIS)
    me = lax.axis_index(AXIS)
    slots_dev, block_len, width = value_store.shape
    seq = key_factors.shape[1]
    pages = block_slot.shape[1]
    model = hidden.shape[2]
    q_cols = query_weight.shape[1]
    k_cols = kv_weight.shape[1]
    fast = q_cols == 4 * HEAD_DIM and k_cols == HEAD_DIM
    pieces = model // LANES

    block, holder = prepare(hidden[:, 0], block_slot, slots_dev)
    order = [0]
    bit = devices // 2
    while bit:
        other = swap(block, bit, devices)
        order = order + [k ^ bit for k in order]
        bit //= 2
        if bit:
            block = jnp.concatenate([block, other], axis=0)
    me_word = me.astype(jnp.int32).reshape(1)
    sent_pages = pick_pages(me_word, block, other, value_store, tuple(order))
    block, other, sent_pages = lax.optimization_barrier((block, other, sent_pages))
    fetched = exchange(sent_pages)
    if fast:
        bits = devices.bit_length() - 1
        turn = [int(format(k, "b").zfill(bits)[::-1], 2) for k in order]
    else:
        turn = order
    projected = project(
        block,
        other,
        norm_gain.reshape(pieces, LANES),
        query_weight,
        kv_weight,
        tuple(turn),
        fast,
    )
    if fast:
        near, far = projected
        sent, kept, arrived = far[None], [near[None]], [near[None]]
        places = [(0, 0)]
        bit = 1
        while bit < devices:
            if bit > 1:
                middle = kept[0].shape[1] // 2
                sent = jnp.concatenate([part[:, middle:] for part in kept], axis=0)
                kept = [part[:, :middle] for part in kept]
            part = swap(sent, bit, devices)
            places += [(len(arrived), row) for row in range(part.shape[0])]
            arrived.append(part)
            kept.append(part)
            bit *= 2
        where = jnp.bitwise_xor(me, jnp.arange(devices, dtype=jnp.int32))
    else:
        targets = jnp.bitwise_xor(me, jnp.array(order, dtype=jnp.int32))
        columns = exchange(projected.reshape(devices, STEPS, q_cols + k_cols)[targets])
        query = columns[:, :, :q_cols].transpose(1, 0, 2).reshape(STEPS, HEADS // 4, 4, HEAD_DIM)
        query = query.transpose(1, 0, 2, 3).reshape(HEADS // 4, 8, HEAD_DIM)
        fresh = columns[:, :, q_cols:].transpose(1, 0, 2).reshape(STEPS, HEADS // 4, HEAD_DIM)
        fresh = jnp.pad(fresh.transpose(1, 0, 2), ((0, 0), (0, 8 - STEPS), (0, 0)))
        arrived = [jnp.concatenate([query, fresh], axis=1)[:, None]]
        places = [(0, row) for row in range(HEADS // 4)]
        where = jnp.arange(HEADS // 4, dtype=jnp.int32)

    cosine, sine = turn_tables(jnp.arange(seq, dtype=jnp.int32).astype(F32))
    keys = make_keys(key_factors[0], key_basis[0], cosine, sine)
    picked = jnp.any(
        selection[:, 0, :, None] == jnp.arange(pages, dtype=jnp.int32)[None, None, :], axis=1
    )
    usable = jnp.repeat(picked, block_len, axis=1) & (
        jnp.arange(seq, dtype=jnp.int32)[None, :] < lengths[0]
    )
    bias = jnp.where(usable, 0.0, -1e30).astype(F32)
    new_cos, new_sin = turn_tables(
        (lengths[0] + jnp.arange(STEPS, dtype=jnp.int32)).astype(F32)
    )
    heads = attend(
        holder, where, keys, bias, new_cos, new_sin, fetched, tuple(places), arrived
    )

    if fast:
        rows = exchange(heads.reshape(devices, STEPS * 4, HEAD_DIM))
        lhs = rows.reshape(devices, STEPS, 4 * HEAD_DIM).reshape(devices * STEPS, 4 * HEAD_DIM)
    else:
        flat = heads.reshape(HEADS // 4, STEPS, 4 * HEAD_DIM).transpose(1, 0, 2)
        flat = flat.reshape(STEPS, devices, model // devices).transpose(1, 0, 2)
        lhs = exchange(flat).reshape(devices * STEPS, model // devices)
    partial = output(lhs, out_weight)
    arrived = exchange(partial.reshape(devices, STEPS * pieces, LANES))
    total = jnp.sum(arrived.astype(F32), axis=0).astype(BF16)
    return total.reshape(STEPS, 1, model)


def solution(mesh):
    return jax.shard_map(
        local,
        mesh=mesh,
        in_specs=(
            P(None, ("groups", "session"), None),
            P(),
            P(None, "session"),
            P(None, "session"),
            P("session", None),
            P(("groups", "session"), None, None),
            P(("groups", "session"), None, None),
            P(("groups", "session"), None, None),
            P(("groups", "session")),
            P(("groups", "session"), None),
            P(None, ("groups", "session"), None),
        ),
        out_specs=P(None, ("groups", "session"), None),
        check_vma=False,
    )
```

```python
import functools
import math

import jax
import jax.numpy as jnp
from jax import lax
from jax.experimental import pallas as pl
from jax.experimental.pallas import tpu as pltpu
from jax.sharding import PartitionSpec as P

HEADS = 64
KV_HEADS = 8
HEAD_DIM = 128
STEPS = 2
GROUP = HEADS // KV_HEADS
LANES = 128
EXTRA = 16
PLANE = 4
AXIS = "session"
VMEM = pltpu.VMEM
SMEM = pltpu.SMEM
F32 = jnp.float32
BF16 = jnp.bfloat16


def angles(positions):
    half = HEAD_DIM // 2
    frequency = jnp.exp(
        -jnp.arange(half, dtype=F32) * (2.0 * math.log(500000.0) / HEAD_DIM)
    )
    return positions[..., None] * frequency


def turn_tables(positions):
    angle = angles(positions)
    cosine, sine = jnp.cos(angle), jnp.sin(angle)
    return (
        jnp.concatenate([cosine, cosine], axis=-1),
        jnp.concatenate([-sine, sine], axis=-1),
    )


def whole(space=VMEM):
    return pl.BlockSpec(memory_space=space)


def prepare_kernel(slots_dev, hidden_ref, slots_ref, block_ref, holder_ref, pair_ref, wide_scr):
    steps, model = hidden_ref.shape
    pieces = model // LANES
    wide = hidden_ref[...].astype(F32)
    for step in range(steps):
        for c in range(pieces):
            row = step * pieces + c
            wide_scr[row : row + 1, :] = wide[step : step + 1, c * LANES : (c + 1) * LANES]
    lane = lax.broadcasted_iota(jnp.int32, (EXTRA, LANES), 1)
    parity = lax.broadcasted_iota(jnp.int32, (EXTRA, LANES), 0)
    table = jnp.zeros((EXTRA, LANES), jnp.int32)
    for m in range(holder_ref.shape[0]):
        slot = slots_ref[0, 2 * m]
        holder = lax.div(slot, slots_dev)
        holder_ref[m] = holder
        pair_ref[holder] = m
        base = holder * slots_dev
        pair = jnp.where(parity == 0, slot - base, slots_ref[0, 2 * m + 1] - base)
        table = jnp.where(lane == holder, pair, table)
    wide_scr[steps * pieces :, :] = table.astype(F32)
    block_ref[0] = wide_scr[...].astype(BF16)


def prepare(hidden, block_slot, slots_dev):
    assert slots_dev <= 256
    steps, model = hidden.shape
    rows = steps * model // LANES + EXTRA
    return pl.pallas_call(
        functools.partial(prepare_kernel, slots_dev),
        in_specs=[whole(), whole(SMEM)],
        out_specs=(whole(), whole(SMEM), whole(SMEM)),
        out_shape=(
            jax.ShapeDtypeStruct((1, rows, LANES), BF16),
            jax.ShapeDtypeStruct((block_slot.shape[1] // 2,), jnp.int32),
            jax.ShapeDtypeStruct((block_slot.shape[1] // 2,), jnp.int32),
        ),
        scratch_shapes=[VMEM((rows, LANES), F32)],
        name="prepare",
    )(hidden, block_slot)


def pick_kernel(order, me_ref, first_ref, second_ref, store_ref, out_ref, table_scr, table_smem, sem):
    block_len = store_ref.shape[1]
    half, rows, _ = first_ref.shape
    for j in range(2 * half):
        source = first_ref if j < half else second_ref
        asked = source[j % half, rows - EXTRA :, :].astype(F32)
        table_scr[j] = asked[:8].astype(jnp.int32)
    copy = pltpu.make_async_copy(table_scr, table_smem, sem)
    copy.start()
    copy.wait()
    me = me_ref[0]
    for j in range(2 * half):
        target = jnp.bitwise_xor(me, order[j])
        for k in range(2):
            out_ref[target, k * block_len : (k + 1) * block_len, :] = store_ref[
                table_smem[j, k, me]
            ]


def pick_pages(me, first, second, store, order):
    count = 2 * first.shape[0]
    _, block_len, width = store.shape
    return pl.pallas_call(
        functools.partial(pick_kernel, order),
        in_specs=[whole(SMEM), whole(), whole(), whole()],
        out_specs=whole(),
        out_shape=jax.ShapeDtypeStruct((count, 2 * block_len, width), store.dtype),
        scratch_shapes=[
            VMEM((count, 8, LANES), jnp.int32),
            SMEM((count, 8, LANES), jnp.int32),
            pltpu.SemaphoreType.DMA(()),
        ],
        compiler_params=pltpu.CompilerParams(vmem_limit_bytes=36 * 2**20),
        name="pick_pages",
    )(me, first, second, store)


def split_kernel(x_ref, store_ref, keep_ref, send_ref):
    slots, block_len, width = store_ref.shape
    for x in range(2):

        @pl.when(x_ref[0] == x)
        def _():
            for head in range(width // LANES):
                target = keep_ref if head % 2 == x else send_ref
                lanes = slice(head // 2 * LANES, (head // 2 + 1) * LANES)
                part = store_ref[:, :, head * LANES : (head + 1) * LANES]
                target[:, lanes] = part.reshape(slots * block_len, LANES)


def split_values(x, store):
    slots, block_len, width = store.shape
    half = jax.ShapeDtypeStruct((slots * block_len, width // 2), store.dtype)
    return pl.pallas_call(
        split_kernel,
        in_specs=[whole(SMEM), whole()],
        out_specs=(whole(), whole()),
        out_shape=(half, half),
        compiler_params=pltpu.CompilerParams(vmem_limit_bytes=16 * 2**20),
        name="split_values",
    )(x, store)


def rows_kernel(order, me_ref, first_ref, second_ref, out_ref, table_scr, table_smem, sem):
    half, rows, _ = first_ref.shape
    for j in range(2 * half):
        source = first_ref if j < half else second_ref
        asked = source[j % half, rows - EXTRA :, :].astype(F32)
        table_scr[j] = asked[:8].astype(jnp.int32)
    copy = pltpu.make_async_copy(table_scr, table_smem, sem)
    copy.start()
    copy.wait()
    me = me_ref[0]
    plane = jnp.bitwise_and(me, -PLANE)
    for j in range(2 * half):
        session = jnp.bitwise_xor(me, order[j])
        for k in range(2):
            for b in range(PLANE):
                out_ref[session * (2 * PLANE) + k * PLANE + b] = table_smem[j, k, plane + b]


def plane_rows(me, first, second, order):
    count = 2 * first.shape[0]
    return pl.pallas_call(
        functools.partial(rows_kernel, order),
        in_specs=[whole(SMEM), whole(), whole()],
        out_specs=whole(SMEM),
        out_shape=jax.ShapeDtypeStruct((count * 2 * PLANE,), jnp.int32),
        scratch_shapes=[
            VMEM((count, 8, LANES), jnp.int32),
            SMEM((count, 8, LANES), jnp.int32),
            pltpu.SemaphoreType.DMA(()),
        ],
        name="plane_rows",
    )(me, first, second)


def mix_kernel(me_ref, rows_ref, weights_ref, *rest):
    stores, (out_ref, values_scr, sum_scr) = rest[:PLANE], rest[PLANE:]
    me = me_ref[0]
    low = jnp.bitwise_and(me, PLANE - 1)
    z_me = lax.div(me, PLANE)
    sessions = weights_ref.shape[0]
    planes = out_ref.shape[0]
    block_len = values_scr.shape[1] // (2 * PLANE)
    for session in range(sessions):
        for q, store in enumerate(stores):
            device = jnp.bitwise_xor(low, q)
            for k in range(2):
                row = rows_ref[session * (2 * PLANE) + k * PLANE + device]
                source = pl.ds(pl.multiple_of(row * block_len, block_len), block_len)
                target = pl.ds(
                    pl.multiple_of((device * 2 + k) * block_len, block_len), block_len
                )
                values_scr[session, target, :] = store[source, :]
        block = weights_ref[session]
        product = jnp.dot(
            block[: planes * 8], values_scr[session], preferred_element_type=F32
        )
        mine = slice(session * 8, (session + 1) * 8)
        for z in range(planes):
            sum_scr[z, mine, :] = product[z * 8 : (z + 1) * 8, z * LANES : (z + 1) * LANES]
        recent = block[planes * 8 :].astype(F32)
        sum_scr[z_me, mine, :] += recent[:8]
    out_ref[...] = sum_scr[...].astype(BF16)


def mix(me, rows, weights, stores):
    sessions = weights.shape[0]
    planes = stores[0].shape[1] // LANES
    shape = (planes, sessions * 8, LANES)
    return pl.pallas_call(
        mix_kernel,
        in_specs=[whole(SMEM)] * 2 + [whole()] * (1 + PLANE),
        out_specs=whole(),
        out_shape=jax.ShapeDtypeStruct(shape, BF16),
        scratch_shapes=[VMEM((sessions, LANES, planes * LANES), BF16), VMEM(shape, F32)],
        compiler_params=pltpu.CompilerParams(vmem_limit_bytes=16 * 2**20),
        cost_estimate=pl.CostEstimate(
            flops=2 * sessions * 32 * LANES * planes * LANES,
            bytes_accessed=4 * stores[0].size * PLANE,
            transcendentals=0,
        ),
        name="mix_values",
    )(me, rows, weights, *stores)


def keys_kernel(pair_ref, factors_ref, basis_ref, cos_ref, sin_ref, out_ref, rows_scr):
    span = factors_ref.shape[0] // pair_ref.shape[0]
    count = rows_scr.shape[0] // span
    base = pl.program_id(0) * count
    for p in range(count):
        source = pl.ds(pl.multiple_of(pair_ref[base + p] * span, span), span)
        rows_scr[p * span : (p + 1) * span, :] = factors_ref[source, :]
    product = jnp.dot(rows_scr[...], basis_ref[...], preferred_element_type=F32)
    cosine, sine = cos_ref[...], sin_ref[...]
    for head in range(KV_HEADS):
        lanes = slice(head * HEAD_DIM, (head + 1) * HEAD_DIM)
        part = product[:, lanes]
        turned = part * cosine + pltpu.roll(part, HEAD_DIM // 2, 1) * sine
        out_ref[:, lanes] = turned.astype(BF16)


def make_keys(pair, factors, basis, cosine, sine):
    seq, rank = factors.shape
    width = basis.shape[1]
    rows = min(seq, 512)
    return pl.pallas_call(
        keys_kernel,
        grid=(seq // rows,),
        in_specs=[
            whole(SMEM),
            pl.BlockSpec((seq, rank), lambda i: (0, 0)),
            pl.BlockSpec((rank, width), lambda i: (0, 0)),
            pl.BlockSpec((rows, HEAD_DIM), lambda i: (i, 0)),
            pl.BlockSpec((rows, HEAD_DIM), lambda i: (i, 0)),
        ],
        out_specs=pl.BlockSpec((rows, width), lambda i: (i, 0)),
        out_shape=jax.ShapeDtypeStruct((seq, width), BF16),
        scratch_shapes=[VMEM((rows, rank), BF16)],
        compiler_params=pltpu.CompilerParams(vmem_limit_bytes=32 * 2**20),
        cost_estimate=pl.CostEstimate(
            flops=2 * seq * rank * width, bytes_accessed=4 * seq * width, transcendentals=0
        ),
        name="turned_keys",
    )(pair, factors, basis, cosine, sine)


def project_kernel(
    order, fast, me_ref, first_ref, second_ref, gain_ref, wq_ref, wk_ref, out_ref,
    x_scr, lhs_scr, wq_buf, wk_buf, out_scr, sems,
):
    depth, q_cols = wq_ref.shape
    k_cols = wk_ref.shape[1]
    chunks = wq_buf.shape[0]
    span = depth // chunks
    pieces = depth // LANES
    copies = []
    for i in range(chunks):
        rows = pl.ds(i * span, span)
        pair = (
            pltpu.make_async_copy(wq_ref.at[rows, :], wq_buf.at[i], sems.at[0, i]),
            pltpu.make_async_copy(wk_ref.at[rows, :], wk_buf.at[i], sems.at[1, i]),
        )
        for copy in pair:
            copy.start()
        copies.append(pair)
    half = first_ref.shape[0]
    count = 2 * half * STEPS
    rows = STEPS * pieces
    for j in range(2 * half):
        source = first_ref if j < half else second_ref
        x_scr[j * rows : (j + 1) * rows] = source[j % half, :rows, :].astype(F32)
    squares = jnp.zeros((count, LANES), F32)
    for c in range(pieces):
        part = x_scr[pl.ds(c, count, stride=pieces), :]
        squares = squares + part * part
    scale = lax.rsqrt(jnp.sum(squares, axis=1, keepdims=True) * (1.0 / depth) + 1e-05)
    for c in range(pieces):
        part = x_scr[pl.ds(c, count, stride=pieces), :]
        gain = gain_ref[pl.ds(c, 1), :].astype(F32)
        lhs_scr[:, c * LANES : (c + 1) * LANES] = (part * scale * gain).astype(BF16)
    q_sum = jnp.zeros((count, q_cols), F32)
    k_sum = jnp.zeros((count, k_cols), F32)
    for i in range(chunks):
        for copy in copies[i]:
            copy.wait()
        lhs = lhs_scr[:, i * span : (i + 1) * span]
        q_sum = q_sum + jnp.dot(lhs, wq_buf[i], preferred_element_type=F32)
        k_sum = k_sum + jnp.dot(lhs, wk_buf[i], preferred_element_type=F32)
    if not fast:
        out_ref[:, :q_cols] = q_sum.astype(BF16)
        out_ref[:, q_cols:] = k_sum.astype(BF16)
        return
    me = me_ref[0]
    per = q_cols // LANES
    out_scr[...] = jnp.zeros_like(out_scr)
    for j, other in enumerate(order):
        place = jnp.bitwise_xor(me, other)
        for step in range(STEPS):
            row = j * STEPS + step
            for c in range(per):
                out_scr[place, step * per + c : step * per + c + 1, :] = q_sum[
                    row : row + 1, c * LANES : (c + 1) * LANES
                ]
            out_scr[place, STEPS * per + step : STEPS * per + step + 1, :] = k_sum[
                row : row + 1, :
            ]
    out_ref[...] = out_scr[...].astype(BF16)


def project(me, first, second, gain, query_weight, kv_weight, order, fast):
    depth, q_cols = query_weight.shape
    k_cols = kv_weight.shape[1]
    pieces = depth // LANES
    devices = 2 * first.shape[0]
    rows = devices * STEPS
    chunks = 8
    span = depth // chunks
    shape = (devices, 16, LANES) if fast else (rows, q_cols + k_cols)
    return pl.pallas_call(
        functools.partial(project_kernel, order, fast),
        in_specs=[whole(SMEM), whole(), whole(), whole(), whole(pl.ANY), whole(pl.ANY)],
        out_specs=whole(),
        out_shape=jax.ShapeDtypeStruct(shape, BF16),
        scratch_shapes=[
            VMEM((rows * pieces, LANES), F32),
            VMEM((rows, depth), BF16),
            VMEM((chunks, span, q_cols), BF16),
            VMEM((chunks, span, k_cols), BF16),
            VMEM((devices, 16, LANES) if fast else (8, LANES), F32),
            pltpu.SemaphoreType.DMA((2, chunks)),
        ],
        compiler_params=pltpu.CompilerParams(vmem_limit_bytes=48 * 2**20),
        cost_estimate=pl.CostEstimate(
            flops=2 * rows * depth * (q_cols + k_cols),
            bytes_accessed=2 * depth * (q_cols + k_cols),
            transcendentals=0,
        ),
        name="norm_project",
    )(me, first, second, gain, query_weight, kv_weight)


def attend_kernel(fast, columns_ref, keys_ref, bias_ref, cos_ref, sin_ref, *rest):
    pages_ref, out_ref, out_scr = (None, *rest) if fast else rest
    score_scale = 1.0 / math.sqrt(HEAD_DIM)
    half = HEAD_DIM // 2
    rows = 2 * GROUP
    columns = columns_ref[...].astype(F32)
    count = columns.shape[0]
    query = columns[:, :8, :].reshape(count * 8, HEAD_DIM)
    fresh = columns[:, 8:, :]
    if fast:
        planes = count // PLANE
        out_scr[...] = jnp.zeros_like(out_scr)
    row_step = lax.rem(lax.broadcasted_iota(jnp.int32, (count * 8, 1), 0) // 4, STEPS)
    later = row_step == 1
    cosine = jnp.where(later, cos_ref[1:2, :], cos_ref[0:1, :])
    sine = jnp.where(later, sin_ref[1:2, :], sin_ref[0:1, :])
    turned = (query * cosine + pltpu.roll(query, half, 1) * sine).astype(BF16)
    turned_wide = turned.astype(F32)
    step_later = later[:rows]
    bias = jnp.where(step_later, bias_ref[1:2, :], bias_ref[0:1, :])
    new_keys = []
    for step in range(STEPS):
        part = fresh[:KV_HEADS, step, :]
        new = part * cos_ref[step : step + 1, :] + pltpu.roll(part, half, 1) * sin_ref[step : step + 1, :]
        new_keys.append(new.astype(BF16).astype(F32))
    for head in range(KV_HEADS):
        lanes = slice(head * HEAD_DIM, (head + 1) * HEAD_DIM)
        mine = slice(head * rows, (head + 1) * rows)
        scores = (
            lax.dot_general(
                turned[mine], keys_ref[:, lanes], (((1,), (1,)), ((), ())),
                preferred_element_type=F32,
            )
            * score_scale
            + bias
        )
        recent0 = (
            jnp.sum(turned_wide[mine] * new_keys[0][head : head + 1, :], axis=1, keepdims=True)
            * score_scale
        )
        recent1 = (
            jnp.sum(turned_wide[mine] * new_keys[1][head : head + 1, :], axis=1, keepdims=True)
            * score_scale
        )
        recent1 = jnp.where(step_later, recent1, -1e30)
        largest = jnp.maximum(
            jnp.max(scores, axis=1, keepdims=True), jnp.maximum(recent0, recent1)
        )
        cache_exp = jnp.exp(scores - largest)
        exp0 = jnp.exp(recent0 - largest)
        exp1 = jnp.exp(recent1 - largest)
        denominator = jnp.sum(cache_exp, axis=1, keepdims=True) + (exp0 + exp1)
        weights = (cache_exp / denominator).astype(BF16)
        weight0 = (exp0 / denominator).astype(BF16).astype(F32)
        weight1 = (exp1 / denominator).astype(BF16).astype(F32)
        recent = weight0 * fresh[KV_HEADS + head, 0:1, :]
        recent = recent + weight1 * fresh[KV_HEADS + head, 1:2, :]
        if not fast:
            values = pages_ref[:, :, lanes].reshape(keys_ref.shape[0], HEAD_DIM)
            mixed = jnp.dot(weights, values, preferred_element_type=F32)
            out_ref[mine, :] = (mixed + recent).astype(BF16)
            continue
        weights = weights.astype(F32)
        z, x = divmod(head, 2)
        for c in range(2):
            part = slice(c * 8, (c + 1) * 8)
            for plane in range(planes):
                out_scr[plane * PLANE + 2 * x + c, z * 8 : (z + 1) * 8, :] = weights[
                    part, plane * LANES : (plane + 1) * LANES
                ]
            out_scr[z * PLANE + 2 * x + c, planes * 8 : planes * 8 + 8, :] = recent[part]
    if fast:
        out_ref[...] = out_scr[...].astype(BF16)


def attend(columns, keys, bias, cosine, sine, pages, fast):
    seq, width = keys.shape
    count = columns.shape[0]
    if fast:
        shape = (count, count // PLANE * 8 + 16, LANES)
        scratch = [VMEM(shape, F32)]
        operands = (columns, keys, bias, cosine, sine)
    else:
        shape = (STEPS * HEADS, HEAD_DIM)
        scratch = [VMEM((8, LANES), F32)]
        operands = (columns, keys, bias, cosine, sine, pages)
    return pl.pallas_call(
        functools.partial(attend_kernel, fast),
        in_specs=[whole()] * len(operands),
        out_specs=whole(),
        out_shape=jax.ShapeDtypeStruct(shape, BF16),
        scratch_shapes=scratch,
        compiler_params=pltpu.CompilerParams(vmem_limit_bytes=48 * 2**20),
        cost_estimate=pl.CostEstimate(
            flops=4 * STEPS * HEADS * seq * HEAD_DIM,
            bytes_accessed=4 * seq * width,
            transcendentals=STEPS * HEADS * seq,
        ),
        name="attend",
    )(*operands)


def output_kernel(fast, lhs_ref, weight_ref, out_ref, weight_buf, out_scr, heads_scr, sems):
    chunks, _, span = weight_buf.shape
    rows = out_ref.shape[0] * LANES // (chunks * span)
    pieces = chunks * span // LANES
    copies = []
    for i in range(chunks):
        copy = pltpu.make_async_copy(
            weight_ref.at[:, pl.ds(i * span, span)], weight_buf.at[i], sems.at[i]
        )
        copy.start()
        copies.append(copy)
    if fast:
        per = heads_scr.shape[0] // rows
        total = lhs_ref[0].astype(F32)
        for z in range(1, lhs_ref.shape[0]):
            total = total + lhs_ref[z].astype(F32)
        heads_scr[...] = total
        lhs = jnp.concatenate(
            [heads_scr[pl.ds(g, rows, stride=per), :].astype(BF16) for g in range(per)], axis=1
        )
    else:
        lhs = lhs_ref[...]
    for i in range(chunks):
        copies[i].wait()
        part = jnp.dot(lhs, weight_buf[i], preferred_element_type=F32)
        for c in range(span // LANES):
            out_scr[pl.ds(i * (span // LANES) + c, rows, stride=pieces), :] = part[
                :, c * LANES : (c + 1) * LANES
            ]
    out_ref[...] = out_scr[...].astype(BF16)


def output(lhs, weight, rows, fast):
    depth, width = weight.shape
    chunks = 8
    return pl.pallas_call(
        functools.partial(output_kernel, fast),
        in_specs=[whole(), whole(pl.ANY)],
        out_specs=whole(),
        out_shape=jax.ShapeDtypeStruct((rows * width // LANES, LANES), BF16),
        scratch_shapes=[
            VMEM((chunks, depth, width // chunks), BF16),
            VMEM((rows * width // LANES, LANES), F32),
            VMEM(lhs.shape[1:] if fast else (8, LANES), F32),
            pltpu.SemaphoreType.DMA((chunks,)),
        ],
        compiler_params=pltpu.CompilerParams(vmem_limit_bytes=48 * 2**20),
        cost_estimate=pl.CostEstimate(
            flops=2 * rows * depth * width, bytes_accessed=2 * depth * width, transcendentals=0
        ),
        name="output_project",
    )(lhs, weight)


def swap(block, bit, devices):
    return lax.ppermute(block, AXIS, [(i, i ^ bit) for i in range(devices)])


def exchange(blocks, groups=None):
    return lax.all_to_all(
        blocks, AXIS, split_axis=0, concat_axis=0, tiled=True, axis_index_groups=groups
    )


def local(
    hidden,
    norm_gain,
    query_weight,
    kv_weight,
    out_weight,
    key_factors,
    key_basis,
    value_store,
    lengths,
    block_slot,
    selection,
):
    devices = lax.axis_size(AXIS)
    me = lax.axis_index(AXIS)
    slots_dev, block_len, width = value_store.shape
    seq = key_factors.shape[1]
    pages = block_slot.shape[1]
    model = hidden.shape[2]
    q_cols = query_weight.shape[1]
    k_cols = kv_weight.shape[1]
    fast = q_cols == 4 * HEAD_DIM and k_cols == HEAD_DIM
    pieces = model // LANES

    me_word = me.astype(jnp.int32).reshape(1)
    block, holder, pair = prepare(hidden[:, 0], block_slot, slots_dev)
    if fast:
        keep, send = split_values((me_word // 2) % 2, value_store)
        neighbour = swap(send, 2, devices)
        stores = (keep, swap(keep, 1, devices), neighbour, swap(neighbour, 1, devices))
    order = [0]
    bit = devices // 2
    while bit:
        other = swap(block, bit, devices)
        order = order + [k ^ bit for k in order]
        bit //= 2
        if bit:
            block = jnp.concatenate([block, other], axis=0)
    order = tuple(order)
    if not fast:
        sent_pages = pick_pages(me_word, block, other, value_store, order)
        block, other, sent_pages = lax.optimization_barrier((block, other, sent_pages))
        fetched = exchange(sent_pages)
    projected = project(
        me_word, block, other, norm_gain.reshape(pieces, LANES), query_weight, kv_weight, order, fast
    )
    if fast:
        columns = exchange(projected)
        rows = plane_rows(me_word, block, other, order)
    else:
        targets = jnp.bitwise_xor(me, jnp.array(order, dtype=jnp.int32))
        columns = exchange(projected.reshape(devices, STEPS, q_cols + k_cols)[targets])
        query = columns[:, :, :q_cols].transpose(1, 0, 2).reshape(STEPS, HEADS // 4, 4, HEAD_DIM)
        query = query.transpose(1, 0, 2, 3).reshape(HEADS // 4, 8, HEAD_DIM)
        fresh = columns[:, :, q_cols:].transpose(1, 0, 2).reshape(STEPS, HEADS // 4, HEAD_DIM)
        fresh = jnp.pad(fresh.transpose(1, 0, 2), ((0, 0), (0, 8 - STEPS), (0, 0)))
        columns = jnp.concatenate([query, fresh], axis=1)

    span = 2 * block_len
    places = (pair[:, None] * span + jnp.arange(span, dtype=jnp.int32)[None, :]).reshape(-1)
    cosine, sine = turn_tables(places.astype(F32))
    keys = make_keys(pair, key_factors[0], key_basis[0], cosine, sine)
    picked = jnp.any(
        selection[:, 0, :, None] == (places // block_len)[None, None, :], axis=1
    )
    bias = jnp.where(picked & (places < lengths[0])[None, :], 0.0, -1e30).astype(F32)
    new_cos, new_sin = turn_tables(
        (lengths[0] + jnp.arange(STEPS, dtype=jnp.int32)).astype(F32)
    )
    if fast:
        blocks = exchange(attend(columns, keys, bias, new_cos, new_sin, None, True))
        parts = mix(me_word, rows, blocks, stores)
        groups = [list(range(low, devices, PLANE)) for low in range(PLANE)]
        lhs = exchange(parts, groups)
    else:
        heads = attend(columns, keys, bias, new_cos, new_sin, fetched, False)
        flat = heads.reshape(HEADS // 4, STEPS, 4 * HEAD_DIM).transpose(1, 0, 2)
        flat = flat.reshape(STEPS, devices, model // devices).transpose(1, 0, 2)
        lhs = exchange(flat).reshape(devices * STEPS, model // devices)
    partial = output(lhs, out_weight, devices * STEPS, fast)
    arrived = exchange(partial.reshape(devices, STEPS * pieces, LANES))
    total = jnp.sum(arrived.astype(F32), axis=0).astype(BF16)
    return total.reshape(STEPS, 1, model)


def solution(mesh):
    return jax.shard_map(
        local,
        mesh=mesh,
        in_specs=(
            P(None, ("groups", "session"), None),
            P(),
            P(None, "session"),
            P(None, "session"),
            P("session", None),
            P(("groups", "session"), None, None),
            P(("groups", "session"), None, None),
            P(("groups", "session"), None, None),
            P(("groups", "session")),
            P(("groups", "session"), None),
            P(None, ("groups", "session"), None),
        ),
        out_specs=P(None, ("groups", "session"), None),
        check_vma=False,
    )
```

```python
import functools
import math

import jax
import jax.numpy as jnp
from jax import lax
from jax.experimental import pallas as pl
from jax.experimental.pallas import tpu as pltpu
from jax.sharding import PartitionSpec as P

HEADS = 64
KV_HEADS = 8
HEAD_DIM = 128
STEPS = 2
GROUP = HEADS // KV_HEADS
LANES = 128
EXTRA = 16
PLANE = 4
PROJECT_LIMIT = 61 * 2**20
AXIS = "session"
VMEM = pltpu.VMEM
SMEM = pltpu.SMEM
F32 = jnp.float32
BF16 = jnp.bfloat16


def angles(positions):
    half = HEAD_DIM // 2
    frequency = jnp.exp(
        -jnp.arange(half, dtype=F32) * (2.0 * math.log(500000.0) / HEAD_DIM)
    )
    return positions[..., None] * frequency


def turn_tables(positions):
    angle = angles(positions)
    cosine, sine = jnp.cos(angle), jnp.sin(angle)
    return (
        jnp.concatenate([cosine, cosine], axis=-1),
        jnp.concatenate([-sine, sine], axis=-1),
    )


def whole(space=VMEM):
    return pl.BlockSpec(memory_space=space)


def prepare_kernel(
    slots_dev, hidden_ref, gain_ref, slots_ref, block_ref, scale_ref, holder_ref, pair_ref, wide_scr
):
    steps, model = hidden_ref.shape
    scale_ref[...] = gain_ref[...].astype(F32)
    pieces = model // LANES
    wide = hidden_ref[...].astype(F32)
    for step in range(steps):
        for c in range(pieces):
            row = step * pieces + c
            wide_scr[row : row + 1, :] = wide[step : step + 1, c * LANES : (c + 1) * LANES]
    lane = lax.broadcasted_iota(jnp.int32, (EXTRA, LANES), 1)
    parity = lax.broadcasted_iota(jnp.int32, (EXTRA, LANES), 0)
    table = jnp.zeros((EXTRA, LANES), jnp.int32)
    for m in range(holder_ref.shape[0]):
        slot = slots_ref[0, 2 * m]
        holder = lax.div(slot, slots_dev)
        holder_ref[m] = holder
        pair_ref[holder] = m
        base = holder * slots_dev
        pair = jnp.where(parity == 0, slot - base, slots_ref[0, 2 * m + 1] - base)
        table = jnp.where(lane == holder, pair, table)
    wide_scr[steps * pieces :, :] = table.astype(F32)
    block_ref[0] = wide_scr[...].astype(BF16)


def prepare(hidden, gain, block_slot, slots_dev):
    assert slots_dev <= 256
    steps, model = hidden.shape
    rows = steps * model // LANES + EXTRA
    return pl.pallas_call(
        functools.partial(prepare_kernel, slots_dev),
        in_specs=[whole(), whole(), whole(SMEM)],
        out_specs=(whole(), whole(), whole(SMEM), whole(SMEM)),
        out_shape=(
            jax.ShapeDtypeStruct((1, rows, LANES), BF16),
            jax.ShapeDtypeStruct(gain.shape, F32),
            jax.ShapeDtypeStruct((block_slot.shape[1] // 2,), jnp.int32),
            jax.ShapeDtypeStruct((block_slot.shape[1] // 2,), jnp.int32),
        ),
        scratch_shapes=[VMEM((rows, LANES), F32)],
        name="prepare",
    )(hidden, gain, block_slot)


def pick_kernel(order, me_ref, first_ref, second_ref, store_ref, out_ref, table_scr, table_smem, sem):
    block_len = store_ref.shape[1]
    half, rows, _ = first_ref.shape
    for j in range(2 * half):
        source = first_ref if j < half else second_ref
        asked = source[j % half, rows - EXTRA :, :].astype(F32)
        table_scr[j] = asked[:8].astype(jnp.int32)
    copy = pltpu.make_async_copy(table_scr, table_smem, sem)
    copy.start()
    copy.wait()
    me = me_ref[0]
    for j in range(2 * half):
        target = jnp.bitwise_xor(me, order[j])
        for k in range(2):
            out_ref[target, k * block_len : (k + 1) * block_len, :] = store_ref[
                table_smem[j, k, me]
            ]


def pick_pages(me, first, second, store, order):
    count = 2 * first.shape[0]
    _, block_len, width = store.shape
    return pl.pallas_call(
        functools.partial(pick_kernel, order),
        in_specs=[whole(SMEM), whole(), whole(), whole()],
        out_specs=whole(),
        out_shape=jax.ShapeDtypeStruct((count, 2 * block_len, width), store.dtype),
        scratch_shapes=[
            VMEM((count, 8, LANES), jnp.int32),
            SMEM((count, 8, LANES), jnp.int32),
            pltpu.SemaphoreType.DMA(()),
        ],
        compiler_params=pltpu.CompilerParams(vmem_limit_bytes=36 * 2**20),
        name="pick_pages",
    )(me, first, second, store)


def split_kernel(x_ref, store_ref, keep_ref, send_ref):
    slots, block_len, width = store_ref.shape
    for x in range(2):

        @pl.when(x_ref[0] == x)
        def _():
            for head in range(width // LANES):
                target = keep_ref if head % 2 == x else send_ref
                lanes = slice(head // 2 * LANES, (head // 2 + 1) * LANES)
                part = store_ref[:, :, head * LANES : (head + 1) * LANES]
                target[:, lanes] = part.reshape(slots * block_len, LANES)


def split_values(x, store):
    slots, block_len, width = store.shape
    half = jax.ShapeDtypeStruct((slots * block_len, width // 2), store.dtype)
    return pl.pallas_call(
        split_kernel,
        in_specs=[whole(SMEM), whole()],
        out_specs=(whole(), whole()),
        out_shape=(half, half),
        compiler_params=pltpu.CompilerParams(vmem_limit_bytes=16 * 2**20),
        name="split_values",
    )(x, store)


def rows_kernel(order, me_ref, first_ref, second_ref, out_ref, table_scr, table_smem, sem):
    half, rows, _ = first_ref.shape
    for j in range(2 * half):
        source = first_ref if j < half else second_ref
        asked = source[j % half, rows - EXTRA :, :].astype(F32)
        table_scr[j] = asked[:8].astype(jnp.int32)
    copy = pltpu.make_async_copy(table_scr, table_smem, sem)
    copy.start()
    copy.wait()
    me = me_ref[0]
    plane = jnp.bitwise_and(me, -PLANE)
    for j in range(2 * half):
        session = jnp.bitwise_xor(me, order[j])
        for k in range(2):
            for b in range(PLANE):
                out_ref[session * (2 * PLANE) + k * PLANE + b] = table_smem[j, k, plane + b]


def plane_rows(me, first, second, order):
    count = 2 * first.shape[0]
    return pl.pallas_call(
        functools.partial(rows_kernel, order),
        in_specs=[whole(SMEM), whole(), whole()],
        out_specs=whole(SMEM),
        out_shape=jax.ShapeDtypeStruct((count * 2 * PLANE,), jnp.int32),
        scratch_shapes=[
            VMEM((count, 8, LANES), jnp.int32),
            SMEM((count, 8, LANES), jnp.int32),
            pltpu.SemaphoreType.DMA(()),
        ],
        name="plane_rows",
    )(me, first, second)


def mix_kernel(me_ref, rows_ref, weights_ref, *rest):
    stores, (out_ref, values_scr, sum_scr) = rest[:PLANE], rest[PLANE:]
    me = me_ref[0]
    low = jnp.bitwise_and(me, PLANE - 1)
    z_me = lax.div(me, PLANE)
    sessions = weights_ref.shape[0]
    planes = out_ref.shape[0]
    block_len = values_scr.shape[1] // (2 * PLANE)
    for session in range(sessions):
        for q, store in enumerate(stores):
            device = jnp.bitwise_xor(low, q)
            for k in range(2):
                row = rows_ref[session * (2 * PLANE) + k * PLANE + device]
                source = pl.ds(pl.multiple_of(row * block_len, block_len), block_len)
                target = pl.ds(
                    pl.multiple_of((device * 2 + k) * block_len, block_len), block_len
                )
                values_scr[session, target, :] = store[source, :]
        block = weights_ref[session]
        product = jnp.dot(
            block[: planes * 8], values_scr[session], preferred_element_type=F32
        )
        mine = slice(session * 8, (session + 1) * 8)
        for z in range(planes):
            sum_scr[z, mine, :] = product[z * 8 : (z + 1) * 8, z * LANES : (z + 1) * LANES]
        recent = block[planes * 8 :].astype(F32)
        sum_scr[z_me, mine, :] += recent[:8]
    out_ref[...] = sum_scr[...].astype(BF16)


def mix(me, rows, weights, stores):
    sessions = weights.shape[0]
    planes = stores[0].shape[1] // LANES
    shape = (planes, sessions * 8, LANES)
    return pl.pallas_call(
        mix_kernel,
        in_specs=[whole(SMEM)] * 2 + [whole()] * (1 + PLANE),
        out_specs=whole(),
        out_shape=jax.ShapeDtypeStruct(shape, BF16),
        scratch_shapes=[VMEM((sessions, LANES, planes * LANES), BF16), VMEM(shape, F32)],
        compiler_params=pltpu.CompilerParams(vmem_limit_bytes=16 * 2**20),
        cost_estimate=pl.CostEstimate(
            flops=2 * sessions * 32 * LANES * planes * LANES,
            bytes_accessed=4 * stores[0].size * PLANE,
            transcendentals=0,
        ),
        name="mix_values",
    )(me, rows, weights, *stores)


def keys_kernel(pair_ref, factors_ref, basis_ref, cos_ref, sin_ref, out_ref, rows_scr):
    span = factors_ref.shape[0] // pair_ref.shape[0]
    count = rows_scr.shape[0] // span
    base = pl.program_id(0) * count
    for p in range(count):
        source = pl.ds(pl.multiple_of(pair_ref[base + p] * span, span), span)
        rows_scr[p * span : (p + 1) * span, :] = factors_ref[source, :]
    product = jnp.dot(rows_scr[...], basis_ref[...], preferred_element_type=F32)
    cosine, sine = cos_ref[...], sin_ref[...]
    for head in range(KV_HEADS):
        lanes = slice(head * HEAD_DIM, (head + 1) * HEAD_DIM)
        part = product[:, lanes]
        turned = part * cosine + pltpu.roll(part, HEAD_DIM // 2, 1) * sine
        out_ref[:, lanes] = turned.astype(BF16)


def make_keys(pair, factors, basis, cosine, sine):
    seq, rank = factors.shape
    width = basis.shape[1]
    rows = min(seq, 512)
    return pl.pallas_call(
        keys_kernel,
        grid=(seq // rows,),
        in_specs=[
            whole(SMEM),
            pl.BlockSpec((seq, rank), lambda i: (0, 0)),
            pl.BlockSpec((rank, width), lambda i: (0, 0)),
            pl.BlockSpec((rows, HEAD_DIM), lambda i: (i, 0)),
            pl.BlockSpec((rows, HEAD_DIM), lambda i: (i, 0)),
        ],
        out_specs=pl.BlockSpec((rows, width), lambda i: (i, 0)),
        out_shape=jax.ShapeDtypeStruct((seq, width), BF16),
        scratch_shapes=[VMEM((rows, rank), BF16)],
        compiler_params=pltpu.CompilerParams(vmem_limit_bytes=32 * 2**20),
        cost_estimate=pl.CostEstimate(
            flops=2 * seq * rank * width, bytes_accessed=4 * seq * width, transcendentals=0
        ),
        name="turned_keys",
    )(pair, factors, basis, cosine, sine)


def project_kernel(
    order, fast, me_ref, first_ref, second_ref, gain_ref, wq_ref, wk_ref, out_ref,
    x_scr, lhs_scr, wq_buf, wk_buf, out_scr, sems,
):
    depth, q_cols = wq_ref.shape
    k_cols = wk_ref.shape[1]
    chunks = wq_buf.shape[0]
    span = depth // chunks
    pieces = depth // LANES
    copies = []
    for i in range(chunks):
        rows = pl.ds(i * span, span)
        pair = (
            pltpu.make_async_copy(wq_ref.at[rows, :], wq_buf.at[i], sems.at[0, i]),
            pltpu.make_async_copy(wk_ref.at[rows, :], wk_buf.at[i], sems.at[1, i]),
        )
        for copy in pair:
            copy.start()
        copies.append(pair)
    half = first_ref.shape[0]
    count = 2 * half * STEPS
    rows = STEPS * pieces
    for j in range(2 * half):
        source = first_ref if j < half else second_ref
        x_scr[j * rows : (j + 1) * rows] = source[j % half, :rows, :].astype(F32)
    squares = jnp.zeros((count, LANES), F32)
    for c in range(pieces):
        part = x_scr[pl.ds(c, count, stride=pieces), :]
        squares = squares + part * part
    scale = lax.rsqrt(jnp.sum(squares, axis=1, keepdims=True) * (1.0 / depth) + 1e-05)
    for c in range(pieces):
        part = x_scr[pl.ds(c, count, stride=pieces), :]
        gain = gain_ref[c : c + 1, :]
        lhs_scr[:, c * LANES : (c + 1) * LANES] = (part * scale * gain).astype(BF16)
    q_sum = jnp.zeros((count, q_cols), F32)
    k_sum = jnp.zeros((count, k_cols), F32)
    for i in range(chunks):
        for copy in copies[i]:
            copy.wait()
        lhs = lhs_scr[:, i * span : (i + 1) * span]
        q_sum = q_sum + jnp.dot(lhs, wq_buf[i], preferred_element_type=F32)
        k_sum = k_sum + jnp.dot(lhs, wk_buf[i], preferred_element_type=F32)
    if not fast:
        out_ref[:, :q_cols] = q_sum.astype(BF16)
        out_ref[:, q_cols:] = k_sum.astype(BF16)
        return
    me = me_ref[0]
    per = q_cols // LANES
    out_scr[...] = jnp.zeros_like(out_scr)
    for j, other in enumerate(order):
        place = jnp.bitwise_xor(me, other)
        for step in range(STEPS):
            row = j * STEPS + step
            for c in range(per):
                out_scr[place, step * per + c : step * per + c + 1, :] = q_sum[
                    row : row + 1, c * LANES : (c + 1) * LANES
                ]
            out_scr[place, STEPS * per + step : STEPS * per + step + 1, :] = k_sum[
                row : row + 1, :
            ]
    out_ref[...] = out_scr[...].astype(BF16)


def project(me, first, second, gain, query_weight, kv_weight, order, fast):
    depth, q_cols = query_weight.shape
    k_cols = kv_weight.shape[1]
    pieces = depth // LANES
    devices = 2 * first.shape[0]
    rows = devices * STEPS
    chunks = 8
    span = depth // chunks
    shape = (devices, 16, LANES) if fast else (rows, q_cols + k_cols)
    return pl.pallas_call(
        functools.partial(project_kernel, order, fast),
        in_specs=[whole(SMEM), whole(), whole(), whole(), whole(pl.ANY), whole(pl.ANY)],
        out_specs=whole(),
        out_shape=jax.ShapeDtypeStruct(shape, BF16),
        scratch_shapes=[
            VMEM((rows * pieces, LANES), F32),
            VMEM((rows, depth), BF16),
            VMEM((chunks, span, q_cols), BF16),
            VMEM((chunks, span, k_cols), BF16),
            VMEM((devices, 16, LANES) if fast else (8, LANES), F32),
            pltpu.SemaphoreType.DMA((2, chunks)),
        ],
        compiler_params=pltpu.CompilerParams(vmem_limit_bytes=PROJECT_LIMIT),
        cost_estimate=pl.CostEstimate(
            flops=2 * rows * depth * (q_cols + k_cols),
            bytes_accessed=2 * depth * (q_cols + k_cols),
            transcendentals=0,
        ),
        name="norm_project",
    )(me, first, second, gain, query_weight, kv_weight)


def attend_kernel(fast, columns_ref, keys_ref, bias_ref, cos_ref, sin_ref, *rest):
    pages_ref, out_ref, out_scr = (None, *rest) if fast else rest
    score_scale = 1.0 / math.sqrt(HEAD_DIM)
    half = HEAD_DIM // 2
    rows = 2 * GROUP
    columns = columns_ref[...].astype(F32)
    count = columns.shape[0]
    query = columns[:, :8, :].reshape(count * 8, HEAD_DIM)
    fresh = columns[:, 8:, :]
    if fast:
        planes = count // PLANE
        out_scr[...] = jnp.zeros_like(out_scr)
    row_step = lax.rem(lax.broadcasted_iota(jnp.int32, (count * 8, 1), 0) // 4, STEPS)
    later = row_step == 1
    cosine = jnp.where(later, cos_ref[1:2, :], cos_ref[0:1, :])
    sine = jnp.where(later, sin_ref[1:2, :], sin_ref[0:1, :])
    turned = (query * cosine + pltpu.roll(query, half, 1) * sine).astype(BF16)
    turned_wide = turned.astype(F32)
    step_later = later[:rows]
    bias = jnp.where(step_later, bias_ref[1:2, :], bias_ref[0:1, :])
    new_keys = []
    for step in range(STEPS):
        part = fresh[:KV_HEADS, step, :]
        new = part * cos_ref[step : step + 1, :] + pltpu.roll(part, half, 1) * sin_ref[step : step + 1, :]
        new_keys.append(new.astype(BF16).astype(F32))
    for head in range(KV_HEADS):
        lanes = slice(head * HEAD_DIM, (head + 1) * HEAD_DIM)
        mine = slice(head * rows, (head + 1) * rows)
        scores = (
            lax.dot_general(
                turned[mine], keys_ref[:, lanes], (((1,), (1,)), ((), ())),
                preferred_element_type=F32,
            )
            * score_scale
            + bias
        )
        recent0 = (
            jnp.sum(turned_wide[mine] * new_keys[0][head : head + 1, :], axis=1, keepdims=True)
            * score_scale
        )
        recent1 = (
            jnp.sum(turned_wide[mine] * new_keys[1][head : head + 1, :], axis=1, keepdims=True)
            * score_scale
        )
        recent1 = jnp.where(step_later, recent1, -1e30)
        largest = jnp.maximum(
            jnp.max(scores, axis=1, keepdims=True), jnp.maximum(recent0, recent1)
        )
        cache_exp = jnp.exp(scores - largest)
        exp0 = jnp.exp(recent0 - largest)
        exp1 = jnp.exp(recent1 - largest)
        denominator = jnp.sum(cache_exp, axis=1, keepdims=True) + (exp0 + exp1)
        weights = (cache_exp / denominator).astype(BF16)
        weight0 = (exp0 / denominator).astype(BF16).astype(F32)
        weight1 = (exp1 / denominator).astype(BF16).astype(F32)
        recent = weight0 * fresh[KV_HEADS + head, 0:1, :]
        recent = recent + weight1 * fresh[KV_HEADS + head, 1:2, :]
        if not fast:
            values = pages_ref[:, :, lanes].reshape(keys_ref.shape[0], HEAD_DIM)
            mixed = jnp.dot(weights, values, preferred_element_type=F32)
            out_ref[mine, :] = (mixed + recent).astype(BF16)
            continue
        weights = weights.astype(F32)
        z, x = divmod(head, 2)
        for c in range(2):
            part = slice(c * 8, (c + 1) * 8)
            for plane in range(planes):
                out_scr[plane * PLANE + 2 * x + c, z * 8 : (z + 1) * 8, :] = weights[
                    part, plane * LANES : (plane + 1) * LANES
                ]
            out_scr[z * PLANE + 2 * x + c, planes * 8 : planes * 8 + 8, :] = recent[part]
    if fast:
        out_ref[...] = out_scr[...].astype(BF16)


def attend(columns, keys, bias, cosine, sine, pages, fast):
    seq, width = keys.shape
    count = columns.shape[0]
    if fast:
        shape = (count, count // PLANE * 8 + 16, LANES)
        scratch = [VMEM(shape, F32)]
        operands = (columns, keys, bias, cosine, sine)
    else:
        shape = (STEPS * HEADS, HEAD_DIM)
        scratch = [VMEM((8, LANES), F32)]
        operands = (columns, keys, bias, cosine, sine, pages)
    return pl.pallas_call(
        functools.partial(attend_kernel, fast),
        in_specs=[whole()] * len(operands),
        out_specs=whole(),
        out_shape=jax.ShapeDtypeStruct(shape, BF16),
        scratch_shapes=scratch,
        compiler_params=pltpu.CompilerParams(vmem_limit_bytes=48 * 2**20),
        cost_estimate=pl.CostEstimate(
            flops=4 * STEPS * HEADS * seq * HEAD_DIM,
            bytes_accessed=4 * seq * width,
            transcendentals=STEPS * HEADS * seq,
        ),
        name="attend",
    )(*operands)


def output_kernel(fast, lhs_ref, weight_ref, out_ref, weight_buf, out_scr, heads_scr, sems):
    chunks, _, span = weight_buf.shape
    rows = out_ref.shape[0] * LANES // (chunks * span)
    pieces = chunks * span // LANES
    copies = []
    for i in range(chunks):
        copy = pltpu.make_async_copy(
            weight_ref.at[:, pl.ds(i * span, span)], weight_buf.at[i], sems.at[i]
        )
        copy.start()
        copies.append(copy)
    if fast:
        per = heads_scr.shape[0] // rows
        total = lhs_ref[0].astype(F32)
        for z in range(1, lhs_ref.shape[0]):
            total = total + lhs_ref[z].astype(F32)
        heads_scr[...] = total
        lhs = jnp.concatenate(
            [heads_scr[pl.ds(g, rows, stride=per), :].astype(BF16) for g in range(per)], axis=1
        )
    else:
        lhs = lhs_ref[...]
    for i in range(chunks):
        copies[i].wait()
        part = jnp.dot(lhs, weight_buf[i], preferred_element_type=F32)
        for c in range(span // LANES):
            out_scr[pl.ds(i * (span // LANES) + c, rows, stride=pieces), :] = part[
                :, c * LANES : (c + 1) * LANES
            ]
    out_ref[...] = out_scr[...].astype(BF16)


def output(lhs, weight, rows, fast):
    depth, width = weight.shape
    chunks = 8
    return pl.pallas_call(
        functools.partial(output_kernel, fast),
        in_specs=[whole(), whole(pl.ANY)],
        out_specs=whole(),
        out_shape=jax.ShapeDtypeStruct((rows * width // LANES, LANES), BF16),
        scratch_shapes=[
            VMEM((chunks, depth, width // chunks), BF16),
            VMEM((rows * width // LANES, LANES), F32),
            VMEM(lhs.shape[1:] if fast else (8, LANES), F32),
            pltpu.SemaphoreType.DMA((chunks,)),
        ],
        compiler_params=pltpu.CompilerParams(vmem_limit_bytes=48 * 2**20),
        cost_estimate=pl.CostEstimate(
            flops=2 * rows * depth * width, bytes_accessed=2 * depth * width, transcendentals=0
        ),
        name="output_project",
    )(lhs, weight)


def swap(block, bit, devices):
    return lax.ppermute(block, AXIS, [(i, i ^ bit) for i in range(devices)])


def exchange(blocks, groups=None):
    return lax.all_to_all(
        blocks, AXIS, split_axis=0, concat_axis=0, tiled=True, axis_index_groups=groups
    )


def local(
    hidden,
    norm_gain,
    query_weight,
    kv_weight,
    out_weight,
    key_factors,
    key_basis,
    value_store,
    lengths,
    block_slot,
    selection,
):
    devices = lax.axis_size(AXIS)
    me = lax.axis_index(AXIS)
    slots_dev, block_len, width = value_store.shape
    seq = key_factors.shape[1]
    pages = block_slot.shape[1]
    model = hidden.shape[2]
    q_cols = query_weight.shape[1]
    k_cols = kv_weight.shape[1]
    fast = q_cols == 4 * HEAD_DIM and k_cols == HEAD_DIM
    pieces = model // LANES

    me_word = me.astype(jnp.int32).reshape(1)
    block, gain, holder, pair = prepare(
        hidden[:, 0], norm_gain.reshape(pieces, LANES), block_slot, slots_dev
    )
    order = [0]
    bit = devices // 2
    while bit:
        other = swap(block, bit, devices)
        order = order + [k ^ bit for k in order]
        bit //= 2
        if bit:
            block = jnp.concatenate([block, other], axis=0)
        if fast and bit == 2:
            block, value_store = lax.optimization_barrier((block, value_store))
    order = tuple(order)
    if fast:
        x = lax.bitwise_and(lax.shift_right_logical(me_word, 1), 1)
        keep, send = split_values(x, value_store)
        block, other, send = lax.optimization_barrier((block, other, send))
        neighbour = swap(send, 2, devices)
        stores = (keep, swap(keep, 1, devices), neighbour, swap(neighbour, 1, devices))
    if not fast:
        sent_pages = pick_pages(me_word, block, other, value_store, order)
        block, other, sent_pages = lax.optimization_barrier((block, other, sent_pages))
        fetched = exchange(sent_pages)
    projected = project(
        me_word, block, other, gain, query_weight, kv_weight, order, fast
    )
    if fast:
        projected, pair = lax.optimization_barrier((projected, pair))
        columns = exchange(projected)
        rows = plane_rows(me_word, block, other, order)
    else:
        targets = jnp.bitwise_xor(me, jnp.array(order, dtype=jnp.int32))
        columns = exchange(projected.reshape(devices, STEPS, q_cols + k_cols)[targets])
        query = columns[:, :, :q_cols].transpose(1, 0, 2).reshape(STEPS, HEADS // 4, 4, HEAD_DIM)
        query = query.transpose(1, 0, 2, 3).reshape(HEADS // 4, 8, HEAD_DIM)
        fresh = columns[:, :, q_cols:].transpose(1, 0, 2).reshape(STEPS, HEADS // 4, HEAD_DIM)
        fresh = jnp.pad(fresh.transpose(1, 0, 2), ((0, 0), (0, 8 - STEPS), (0, 0)))
        columns = jnp.concatenate([query, fresh], axis=1)

    span = 2 * block_len
    places = (pair[:, None] * span + jnp.arange(span, dtype=jnp.int32)[None, :]).reshape(-1)
    cosine, sine = turn_tables(places.astype(F32))
    keys = make_keys(pair, key_factors[0], key_basis[0], cosine, sine)
    picked = jnp.any(
        selection[:, 0, :, None] == (places // block_len)[None, None, :], axis=1
    )
    bias = jnp.where(picked & (places < lengths[0])[None, :], 0.0, -1e30).astype(F32)
    new_cos, new_sin = turn_tables(
        (lengths[0] + jnp.arange(STEPS, dtype=jnp.int32)).astype(F32)
    )
    if fast:
        blocks = exchange(attend(columns, keys, bias, new_cos, new_sin, None, True))
        parts = mix(me_word, rows, blocks, stores)
        groups = [list(range(low, devices, PLANE)) for low in range(PLANE)]
        lhs = exchange(parts, groups)
    else:
        heads = attend(columns, keys, bias, new_cos, new_sin, fetched, False)
        flat = heads.reshape(HEADS // 4, STEPS, 4 * HEAD_DIM).transpose(1, 0, 2)
        flat = flat.reshape(STEPS, devices, model // devices).transpose(1, 0, 2)
        lhs = exchange(flat).reshape(devices * STEPS, model // devices)
    partial = output(lhs, out_weight, devices * STEPS, fast)
    arrived = exchange(partial.reshape(devices, STEPS * pieces, LANES))
    total = jnp.sum(arrived.astype(F32), axis=0).astype(BF16)
    return total.reshape(STEPS, 1, model)


def solution(mesh):
    return jax.shard_map(
        local,
        mesh=mesh,
        in_specs=(
            P(None, ("groups", "session"), None),
            P(),
            P(None, "session"),
            P(None, "session"),
            P("session", None),
            P(("groups", "session"), None, None),
            P(("groups", "session"), None, None),
            P(("groups", "session"), None, None),
            P(("groups", "session")),
            P(("groups", "session"), None),
            P(None, ("groups", "session"), None),
        ),
        out_specs=P(None, ("groups", "session"), None),
        check_vma=False,
    )
```

```python
import functools
import math

import jax
import jax.numpy as jnp
from jax import lax
from jax.experimental import pallas as pl
from jax.experimental.pallas import tpu as pltpu
from jax.sharding import PartitionSpec as P

HEADS = 64
KV_HEADS = 8
HEAD_DIM = 128
STEPS = 2
GROUP = HEADS // KV_HEADS
LANES = 128
EXTRA = 16
PLANE = 4
PAIRS = 8
PROJECT_LIMIT = 48 * 2**20
AXIS = "session"
VMEM = pltpu.VMEM
SMEM = pltpu.SMEM
F32 = jnp.float32
BF16 = jnp.bfloat16


def angles(positions):
    half = HEAD_DIM // 2
    frequency = jnp.exp(
        -jnp.arange(half, dtype=F32) * (2.0 * math.log(500000.0) / HEAD_DIM)
    )
    return positions[..., None] * frequency


def turn_tables(positions):
    angle = angles(positions)
    cosine, sine = jnp.cos(angle), jnp.sin(angle)
    return (
        jnp.concatenate([cosine, cosine], axis=-1),
        jnp.concatenate([-sine, sine], axis=-1),
    )


def origin(me, order, j):
    if order is None:
        return 2 * (j % PAIRS) + jnp.bitwise_xor(jnp.bitwise_and(me, 1), j // PAIRS)
    return jnp.bitwise_xor(me, order[j])


def whole(space=VMEM):
    return pl.BlockSpec(memory_space=space)


def prepare_kernel(
    slots_dev, hidden_ref, gain_ref, slots_ref, block_ref, scale_ref, holder_ref, pair_ref, wide_scr
):
    steps, model = hidden_ref.shape
    scale_ref[...] = gain_ref[...].astype(F32)
    pieces = model // LANES
    wide = hidden_ref[...].astype(F32)
    for step in range(steps):
        for c in range(pieces):
            row = step * pieces + c
            wide_scr[row : row + 1, :] = wide[step : step + 1, c * LANES : (c + 1) * LANES]
    lane = lax.broadcasted_iota(jnp.int32, (EXTRA, LANES), 1)
    parity = lax.broadcasted_iota(jnp.int32, (EXTRA, LANES), 0)
    table = jnp.zeros((EXTRA, LANES), jnp.int32)
    for m in range(holder_ref.shape[0]):
        slot = slots_ref[0, 2 * m]
        holder = lax.div(slot, slots_dev)
        holder_ref[m] = holder
        pair_ref[holder] = m
        base = holder * slots_dev
        pair = jnp.where(parity == 0, slot - base, slots_ref[0, 2 * m + 1] - base)
        table = jnp.where(lane == holder, pair, table)
    wide_scr[steps * pieces :, :] = table.astype(F32)
    block = wide_scr[...].astype(BF16)
    for copy in range(block_ref.shape[0]):
        block_ref[copy] = block


def prepare(hidden, gain, block_slot, slots_dev, copies):
    assert slots_dev <= 256
    steps, model = hidden.shape
    rows = steps * model // LANES + EXTRA
    return pl.pallas_call(
        functools.partial(prepare_kernel, slots_dev),
        in_specs=[whole(), whole(), whole(SMEM)],
        out_specs=(whole(), whole(), whole(SMEM), whole(SMEM)),
        out_shape=(
            jax.ShapeDtypeStruct((copies, rows, LANES), BF16),
            jax.ShapeDtypeStruct(gain.shape, F32),
            jax.ShapeDtypeStruct((block_slot.shape[1] // 2,), jnp.int32),
            jax.ShapeDtypeStruct((block_slot.shape[1] // 2,), jnp.int32),
        ),
        scratch_shapes=[VMEM((rows, LANES), F32)],
        name="prepare",
    )(hidden, gain, block_slot)


def pick_kernel(order, me_ref, first_ref, second_ref, store_ref, out_ref, table_scr, table_smem, sem):
    block_len = store_ref.shape[1]
    half, rows, _ = first_ref.shape
    for j in range(2 * half):
        source = first_ref if j < half else second_ref
        asked = source[j % half, rows - EXTRA :, :].astype(F32)
        table_scr[j] = asked[:8].astype(jnp.int32)
    copy = pltpu.make_async_copy(table_scr, table_smem, sem)
    copy.start()
    copy.wait()
    me = me_ref[0]
    for j in range(2 * half):
        target = origin(me, order, j)
        for k in range(2):
            out_ref[target, k * block_len : (k + 1) * block_len, :] = store_ref[
                table_smem[j, k, me]
            ]


def pick_pages(me, first, second, store, order):
    count = 2 * first.shape[0]
    _, block_len, width = store.shape
    return pl.pallas_call(
        functools.partial(pick_kernel, order),
        in_specs=[whole(SMEM), whole(), whole(), whole()],
        out_specs=whole(),
        out_shape=jax.ShapeDtypeStruct((count, 2 * block_len, width), store.dtype),
        scratch_shapes=[
            VMEM((count, 8, LANES), jnp.int32),
            SMEM((count, 8, LANES), jnp.int32),
            pltpu.SemaphoreType.DMA(()),
        ],
        compiler_params=pltpu.CompilerParams(vmem_limit_bytes=36 * 2**20),
        name="pick_pages",
    )(me, first, second, store)


def split_kernel(x_ref, store_ref, keep_ref, send_ref):
    slots, block_len, width = store_ref.shape
    for x in range(2):

        @pl.when(x_ref[0] == x)
        def _():
            for head in range(width // LANES):
                target = keep_ref if head % 2 == x else send_ref
                lanes = slice(head // 2 * LANES, (head // 2 + 1) * LANES)
                part = store_ref[:, :, head * LANES : (head + 1) * LANES]
                target[:, lanes] = part.reshape(slots * block_len, LANES)


def split_values(x, store):
    slots, block_len, width = store.shape
    half = jax.ShapeDtypeStruct((slots * block_len, width // 2), store.dtype)
    return pl.pallas_call(
        split_kernel,
        in_specs=[whole(SMEM), whole()],
        out_specs=(whole(), whole()),
        out_shape=(half, half),
        compiler_params=pltpu.CompilerParams(vmem_limit_bytes=16 * 2**20),
        name="split_values",
    )(x, store)


def rows_kernel(order, me_ref, first_ref, second_ref, out_ref, table_scr, table_smem, sem):
    half, rows, _ = first_ref.shape
    for j in range(2 * half):
        source = first_ref if j < half else second_ref
        asked = source[j % half, rows - EXTRA :, :].astype(F32)
        table_scr[j] = asked[:8].astype(jnp.int32)
    copy = pltpu.make_async_copy(table_scr, table_smem, sem)
    copy.start()
    copy.wait()
    me = me_ref[0]
    plane = jnp.bitwise_and(me, -PLANE)
    for j in range(2 * half):
        session = origin(me, order, j)
        for k in range(2):
            for b in range(PLANE):
                out_ref[session * (2 * PLANE) + k * PLANE + b] = table_smem[j, k, plane + b]


def plane_rows(me, first, second, order):
    count = 2 * first.shape[0]
    return pl.pallas_call(
        functools.partial(rows_kernel, order),
        in_specs=[whole(SMEM), whole(), whole()],
        out_specs=whole(SMEM),
        out_shape=jax.ShapeDtypeStruct((count * 2 * PLANE,), jnp.int32),
        scratch_shapes=[
            VMEM((count, 8, LANES), jnp.int32),
            SMEM((count, 8, LANES), jnp.int32),
            pltpu.SemaphoreType.DMA(()),
        ],
        name="plane_rows",
    )(me, first, second)


def mix_kernel(me_ref, rows_ref, weights_ref, *rest):
    stores, (out_ref, values_scr, sum_scr) = rest[:PLANE], rest[PLANE:]
    me = me_ref[0]
    low = jnp.bitwise_and(me, PLANE - 1)
    z_me = lax.div(me, PLANE)
    sessions = weights_ref.shape[0]
    planes = out_ref.shape[0]
    block_len = values_scr.shape[1] // (2 * PLANE)
    for session in range(sessions):
        for q, store in enumerate(stores):
            device = jnp.bitwise_xor(low, q)
            for k in range(2):
                row = rows_ref[session * (2 * PLANE) + k * PLANE + device]
                source = pl.ds(pl.multiple_of(row * block_len, block_len), block_len)
                target = pl.ds(
                    pl.multiple_of((device * 2 + k) * block_len, block_len), block_len
                )
                values_scr[session, target, :] = store[source, :]
        block = weights_ref[session]
        product = jnp.dot(
            block[: planes * 8], values_scr[session], preferred_element_type=F32
        )
        mine = slice(session * 8, (session + 1) * 8)
        for z in range(planes):
            sum_scr[z, mine, :] = product[z * 8 : (z + 1) * 8, z * LANES : (z + 1) * LANES]
        recent = block[planes * 8 :].astype(F32)
        sum_scr[z_me, mine, :] += recent[:8]
    out_ref[...] = sum_scr[...].astype(BF16)


def mix(me, rows, weights, stores):
    sessions = weights.shape[0]
    planes = stores[0].shape[1] // LANES
    shape = (planes, sessions * 8, LANES)
    return pl.pallas_call(
        mix_kernel,
        in_specs=[whole(SMEM)] * 2 + [whole()] * (1 + PLANE),
        out_specs=whole(),
        out_shape=jax.ShapeDtypeStruct(shape, BF16),
        scratch_shapes=[VMEM((sessions, LANES, planes * LANES), BF16), VMEM(shape, F32)],
        compiler_params=pltpu.CompilerParams(vmem_limit_bytes=16 * 2**20),
        cost_estimate=pl.CostEstimate(
            flops=2 * sessions * 32 * LANES * planes * LANES,
            bytes_accessed=4 * stores[0].size * PLANE,
            transcendentals=0,
        ),
        name="mix_values",
    )(me, rows, weights, *stores)


def keys_kernel(pair_ref, factors_ref, basis_ref, cos_ref, sin_ref, out_ref, rows_scr):
    span = factors_ref.shape[0] // pair_ref.shape[0]
    count = rows_scr.shape[0] // span
    base = pl.program_id(0) * count
    for p in range(count):
        source = pl.ds(pl.multiple_of(pair_ref[base + p] * span, span), span)
        rows_scr[p * span : (p + 1) * span, :] = factors_ref[source, :]
    product = jnp.dot(rows_scr[...], basis_ref[...], preferred_element_type=F32)
    cosine, sine = cos_ref[...], sin_ref[...]
    for head in range(KV_HEADS):
        lanes = slice(head * HEAD_DIM, (head + 1) * HEAD_DIM)
        part = product[:, lanes]
        turned = part * cosine + pltpu.roll(part, HEAD_DIM // 2, 1) * sine
        out_ref[:, lanes] = turned.astype(BF16)


def make_keys(pair, factors, basis, cosine, sine):
    seq, rank = factors.shape
    width = basis.shape[1]
    rows = min(seq, 512)
    return pl.pallas_call(
        keys_kernel,
        grid=(seq // rows,),
        in_specs=[
            whole(SMEM),
            pl.BlockSpec((seq, rank), lambda i: (0, 0)),
            pl.BlockSpec((rank, width), lambda i: (0, 0)),
            pl.BlockSpec((rows, HEAD_DIM), lambda i: (i, 0)),
            pl.BlockSpec((rows, HEAD_DIM), lambda i: (i, 0)),
        ],
        out_specs=pl.BlockSpec((rows, width), lambda i: (i, 0)),
        out_shape=jax.ShapeDtypeStruct((seq, width), BF16),
        scratch_shapes=[VMEM((rows, rank), BF16)],
        compiler_params=pltpu.CompilerParams(vmem_limit_bytes=32 * 2**20),
        cost_estimate=pl.CostEstimate(
            flops=2 * seq * rank * width, bytes_accessed=4 * seq * width, transcendentals=0
        ),
        name="turned_keys",
    )(pair, factors, basis, cosine, sine)


def project_kernel(
    order, fast, me_ref, first_ref, second_ref, gain_ref, wq_ref, wk_ref, out_ref,
    x_scr, lhs_scr, wq_buf, wk_buf, out_scr, sems,
):
    depth, q_cols = wq_ref.shape
    k_cols = wk_ref.shape[1]
    chunks = wq_buf.shape[0]
    span = depth // chunks
    pieces = depth // LANES
    copies = []
    for i in range(chunks):
        rows = pl.ds(i * span, span)
        pair = (
            pltpu.make_async_copy(wq_ref.at[rows, :], wq_buf.at[i], sems.at[0, i]),
            pltpu.make_async_copy(wk_ref.at[rows, :], wk_buf.at[i], sems.at[1, i]),
        )
        for copy in pair:
            copy.start()
        copies.append(pair)
    half = first_ref.shape[0]
    count = 2 * half * STEPS
    rows = STEPS * pieces
    for j in range(2 * half):
        source = first_ref if j < half else second_ref
        x_scr[j * rows : (j + 1) * rows] = source[j % half, :rows, :].astype(F32)
    squares = jnp.zeros((count, LANES), F32)
    for c in range(pieces):
        part = x_scr[pl.ds(c, count, stride=pieces), :]
        squares = squares + part * part
    scale = lax.rsqrt(jnp.sum(squares, axis=1, keepdims=True) * (1.0 / depth) + 1e-05)
    for c in range(pieces):
        part = x_scr[pl.ds(c, count, stride=pieces), :]
        gain = gain_ref[c : c + 1, :]
        lhs_scr[:, c * LANES : (c + 1) * LANES] = (part * scale * gain).astype(BF16)
    q_sum = jnp.zeros((count, q_cols), F32)
    k_sum = jnp.zeros((count, k_cols), F32)
    for i in range(chunks):
        for copy in copies[i]:
            copy.wait()
        lhs = lhs_scr[:, i * span : (i + 1) * span]
        q_sum = q_sum + jnp.dot(lhs, wq_buf[i], preferred_element_type=F32)
        k_sum = k_sum + jnp.dot(lhs, wk_buf[i], preferred_element_type=F32)
    if not fast:
        out_ref[:, :q_cols] = q_sum.astype(BF16)
        out_ref[:, q_cols:] = k_sum.astype(BF16)
        return
    me = me_ref[0]
    per = q_cols // LANES
    out_scr[...] = jnp.zeros_like(out_scr)
    for j in range(2 * half):
        place = origin(me, order, j)
        for step in range(STEPS):
            row = j * STEPS + step
            for c in range(per):
                out_scr[place, step * per + c : step * per + c + 1, :] = q_sum[
                    row : row + 1, c * LANES : (c + 1) * LANES
                ]
            out_scr[place, STEPS * per + step : STEPS * per + step + 1, :] = k_sum[
                row : row + 1, :
            ]
    out_ref[...] = out_scr[...].astype(BF16)


def project(me, first, second, gain, query_weight, kv_weight, order, fast):
    depth, q_cols = query_weight.shape
    k_cols = kv_weight.shape[1]
    pieces = depth // LANES
    devices = 2 * first.shape[0]
    rows = devices * STEPS
    chunks = 8
    span = depth // chunks
    shape = (devices, 16, LANES) if fast else (rows, q_cols + k_cols)
    return pl.pallas_call(
        functools.partial(project_kernel, order, fast),
        in_specs=[whole(SMEM), whole(), whole(), whole(), whole(pl.ANY), whole(pl.ANY)],
        out_specs=whole(),
        out_shape=jax.ShapeDtypeStruct(shape, BF16),
        scratch_shapes=[
            VMEM((rows * pieces, LANES), F32),
            VMEM((rows, depth), BF16),
            VMEM((chunks, span, q_cols), BF16),
            VMEM((chunks, span, k_cols), BF16),
            VMEM((devices, 16, LANES) if fast else (8, LANES), F32),
            pltpu.SemaphoreType.DMA((2, chunks)),
        ],
        compiler_params=pltpu.CompilerParams(vmem_limit_bytes=PROJECT_LIMIT),
        cost_estimate=pl.CostEstimate(
            flops=2 * rows * depth * (q_cols + k_cols),
            bytes_accessed=2 * depth * (q_cols + k_cols),
            transcendentals=0,
        ),
        name="norm_project",
    )(me, first, second, gain, query_weight, kv_weight)


def attend_kernel(fast, columns_ref, keys_ref, bias_ref, cos_ref, sin_ref, *rest):
    pages_ref, out_ref, out_scr = (None, *rest) if fast else rest
    score_scale = 1.0 / math.sqrt(HEAD_DIM)
    half = HEAD_DIM // 2
    rows = 2 * GROUP
    columns = columns_ref[...].astype(F32)
    count = columns.shape[0]
    query = columns[:, :8, :].reshape(count * 8, HEAD_DIM)
    fresh = columns[:, 8:, :]
    if fast:
        planes = count // PLANE
        out_scr[...] = jnp.zeros_like(out_scr)
    row_step = lax.rem(lax.broadcasted_iota(jnp.int32, (count * 8, 1), 0) // 4, STEPS)
    later = row_step == 1
    cosine = jnp.where(later, cos_ref[1:2, :], cos_ref[0:1, :])
    sine = jnp.where(later, sin_ref[1:2, :], sin_ref[0:1, :])
    turned = (query * cosine + pltpu.roll(query, half, 1) * sine).astype(BF16)
    turned_wide = turned.astype(F32)
    step_later = later[:rows]
    bias = jnp.where(step_later, bias_ref[1:2, :], bias_ref[0:1, :])
    new_keys = []
    for step in range(STEPS):
        part = fresh[:KV_HEADS, step, :]
        new = part * cos_ref[step : step + 1, :] + pltpu.roll(part, half, 1) * sin_ref[step : step + 1, :]
        new_keys.append(new.astype(BF16).astype(F32))
    for head in range(KV_HEADS):
        lanes = slice(head * HEAD_DIM, (head + 1) * HEAD_DIM)
        mine = slice(head * rows, (head + 1) * rows)
        scores = (
            lax.dot_general(
                turned[mine], keys_ref[:, lanes], (((1,), (1,)), ((), ())),
                preferred_element_type=F32,
            )
            * score_scale
            + bias
        )
        recent0 = (
            jnp.sum(turned_wide[mine] * new_keys[0][head : head + 1, :], axis=1, keepdims=True)
            * score_scale
        )
        recent1 = (
            jnp.sum(turned_wide[mine] * new_keys[1][head : head + 1, :], axis=1, keepdims=True)
            * score_scale
        )
        recent1 = jnp.where(step_later, recent1, -1e30)
        largest = jnp.maximum(
            jnp.max(scores, axis=1, keepdims=True), jnp.maximum(recent0, recent1)
        )
        cache_exp = jnp.exp(scores - largest)
        exp0 = jnp.exp(recent0 - largest)
        exp1 = jnp.exp(recent1 - largest)
        denominator = jnp.sum(cache_exp, axis=1, keepdims=True) + (exp0 + exp1)
        weights = (cache_exp / denominator).astype(BF16)
        weight0 = (exp0 / denominator).astype(BF16).astype(F32)
        weight1 = (exp1 / denominator).astype(BF16).astype(F32)
        recent = weight0 * fresh[KV_HEADS + head, 0:1, :]
        recent = recent + weight1 * fresh[KV_HEADS + head, 1:2, :]
        if not fast:
            values = pages_ref[:, :, lanes].reshape(keys_ref.shape[0], HEAD_DIM)
            mixed = jnp.dot(weights, values, preferred_element_type=F32)
            out_ref[mine, :] = (mixed + recent).astype(BF16)
            continue
        weights = weights.astype(F32)
        z, x = divmod(head, 2)
        for c in range(2):
            part = slice(c * 8, (c + 1) * 8)
            for plane in range(planes):
                out_scr[plane * PLANE + 2 * x + c, z * 8 : (z + 1) * 8, :] = weights[
                    part, plane * LANES : (plane + 1) * LANES
                ]
            out_scr[z * PLANE + 2 * x + c, planes * 8 : planes * 8 + 8, :] = recent[part]
    if fast:
        out_ref[...] = out_scr[...].astype(BF16)


def attend(columns, keys, bias, cosine, sine, pages, fast):
    seq, width = keys.shape
    count = columns.shape[0]
    if fast:
        shape = (count, count // PLANE * 8 + 16, LANES)
        scratch = [VMEM(shape, F32)]
        operands = (columns, keys, bias, cosine, sine)
    else:
        shape = (STEPS * HEADS, HEAD_DIM)
        scratch = [VMEM((8, LANES), F32)]
        operands = (columns, keys, bias, cosine, sine, pages)
    return pl.pallas_call(
        functools.partial(attend_kernel, fast),
        in_specs=[whole()] * len(operands),
        out_specs=whole(),
        out_shape=jax.ShapeDtypeStruct(shape, BF16),
        scratch_shapes=scratch,
        compiler_params=pltpu.CompilerParams(vmem_limit_bytes=48 * 2**20),
        cost_estimate=pl.CostEstimate(
            flops=4 * STEPS * HEADS * seq * HEAD_DIM,
            bytes_accessed=4 * seq * width,
            transcendentals=STEPS * HEADS * seq,
        ),
        name="attend",
    )(*operands)


def output_kernel(fast, me_ref, lhs_ref, weight_ref, *rest):
    out_refs, (weight_buf, out_scr, heads_scr, sems) = rest[:-4], rest[-4:]
    chunks, _, span = weight_buf.shape
    rows = out_scr.shape[0] * LANES // (chunks * span)
    pieces = chunks * span // LANES
    copies = []
    for i in range(chunks):
        copy = pltpu.make_async_copy(
            weight_ref.at[:, pl.ds(i * span, span)], weight_buf.at[i], sems.at[i]
        )
        copy.start()
        copies.append(copy)
    if fast:
        per = heads_scr.shape[0] // rows
        total = lhs_ref[0].astype(F32)
        for z in range(1, lhs_ref.shape[0]):
            total = total + lhs_ref[z].astype(F32)
        heads_scr[...] = total
        lhs = jnp.concatenate(
            [heads_scr[pl.ds(g, rows, stride=per), :].astype(BF16) for g in range(per)], axis=1
        )
    else:
        lhs = lhs_ref[...]
    for i in range(chunks):
        copies[i].wait()
        part = jnp.dot(lhs, weight_buf[i], preferred_element_type=F32)
        for c in range(span // LANES):
            out_scr[pl.ds(i * (span // LANES) + c, rows, stride=pieces), :] = part[
                :, c * LANES : (c + 1) * LANES
            ]
    if not fast:
        out_refs[0][...] = out_scr[...].astype(BF16)
        return
    low = jnp.bitwise_and(me_ref[0], 1)
    for out_ref, core in zip(out_refs, (low, 1 - low)):
        count, size, _ = out_ref.shape
        for j in range(count):
            part = pl.ds(pl.multiple_of((2 * j + core) * size, size), size)
            out_ref[j] = out_scr[part, :].astype(BF16)


def output(me, lhs, weight, rows, fast):
    depth, width = weight.shape
    chunks = 8
    if fast:
        shape = (rows // (2 * STEPS), STEPS * width // LANES, LANES)
        shapes = (jax.ShapeDtypeStruct(shape, BF16),) * 2
    else:
        shapes = (jax.ShapeDtypeStruct((rows * width // LANES, LANES), BF16),)
    return pl.pallas_call(
        functools.partial(output_kernel, fast),
        in_specs=[whole(SMEM), whole(), whole(pl.ANY)],
        out_specs=(whole(),) * len(shapes),
        out_shape=shapes,
        scratch_shapes=[
            VMEM((chunks, depth, width // chunks), BF16),
            VMEM((rows * width // LANES, LANES), F32),
            VMEM(lhs.shape[1:] if fast else (8, LANES), F32),
            pltpu.SemaphoreType.DMA((chunks,)),
        ],
        compiler_params=pltpu.CompilerParams(vmem_limit_bytes=48 * 2**20),
        cost_estimate=pl.CostEstimate(
            flops=2 * rows * depth * width, bytes_accessed=2 * depth * width, transcendentals=0
        ),
        name="output_project",
    )(me, lhs, weight)


def swap(block, bit, devices):
    return lax.ppermute(block, AXIS, [(i, i ^ bit) for i in range(devices)])


def exchange(blocks, groups=None):
    return lax.all_to_all(
        blocks, AXIS, split_axis=0, concat_axis=0, tiled=True, axis_index_groups=groups
    )


def local(
    hidden,
    norm_gain,
    query_weight,
    kv_weight,
    out_weight,
    key_factors,
    key_basis,
    value_store,
    lengths,
    block_slot,
    selection,
):
    devices = lax.axis_size(AXIS)
    me = lax.axis_index(AXIS)
    slots_dev, block_len, width = value_store.shape
    seq = key_factors.shape[1]
    pages = block_slot.shape[1]
    model = hidden.shape[2]
    q_cols = query_weight.shape[1]
    k_cols = kv_weight.shape[1]
    fast = devices == 2 * PAIRS and q_cols == 4 * HEAD_DIM and k_cols == HEAD_DIM
    pieces = model // LANES

    me_word = me.astype(jnp.int32).reshape(1)
    block, gain, holder, pair = prepare(
        hidden[:, 0], norm_gain.reshape(pieces, LANES), block_slot, slots_dev, PAIRS if fast else 1
    )
    if fast:
        same_core = [list(range(core, devices, 2)) for core in range(2)]
        block = exchange(block, same_core)
        other = swap(block, 1, devices)
        order = None
        x = lax.bitwise_and(lax.shift_right_logical(me_word, 1), 1)
        keep, send = split_values(x, value_store)
        neighbour = swap(send, 2, devices)
        stores = (keep, swap(keep, 1, devices), neighbour, swap(neighbour, 1, devices))
    else:
        order = [0]
        bit = devices // 2
        while bit:
            other = swap(block, bit, devices)
            order = order + [k ^ bit for k in order]
            bit //= 2
            if bit:
                block = jnp.concatenate([block, other], axis=0)
        order = tuple(order)
    if not fast:
        sent_pages = pick_pages(me_word, block, other, value_store, order)
        block, other, sent_pages = lax.optimization_barrier((block, other, sent_pages))
        fetched = exchange(sent_pages)
    projected = project(
        me_word, block, other, gain, query_weight, kv_weight, order, fast
    )
    if fast:
        columns = exchange(projected)
        rows = plane_rows(me_word, block, other, order)
    else:
        targets = jnp.bitwise_xor(me, jnp.array(order, dtype=jnp.int32))
        columns = exchange(projected.reshape(devices, STEPS, q_cols + k_cols)[targets])
        query = columns[:, :, :q_cols].transpose(1, 0, 2).reshape(STEPS, HEADS // 4, 4, HEAD_DIM)
        query = query.transpose(1, 0, 2, 3).reshape(HEADS // 4, 8, HEAD_DIM)
        fresh = columns[:, :, q_cols:].transpose(1, 0, 2).reshape(STEPS, HEADS // 4, HEAD_DIM)
        fresh = jnp.pad(fresh.transpose(1, 0, 2), ((0, 0), (0, 8 - STEPS), (0, 0)))
        columns = jnp.concatenate([query, fresh], axis=1)

    span = 2 * block_len
    places = (pair[:, None] * span + jnp.arange(span, dtype=jnp.int32)[None, :]).reshape(-1)
    cosine, sine = turn_tables(places.astype(F32))
    keys = make_keys(pair, key_factors[0], key_basis[0], cosine, sine)
    picked = jnp.any(
        selection[:, 0, :, None] == (places // block_len)[None, None, :], axis=1
    )
    bias = jnp.where(picked & (places < lengths[0])[None, :], 0.0, -1e30).astype(F32)
    new_cos, new_sin = turn_tables(
        (lengths[0] + jnp.arange(STEPS, dtype=jnp.int32)).astype(F32)
    )
    if fast:
        blocks = exchange(attend(columns, keys, bias, new_cos, new_sin, None, True))
        parts = mix(me_word, rows, blocks, stores)
        groups = [list(range(low, devices, PLANE)) for low in range(PLANE)]
        lhs = exchange(parts, groups)
    else:
        heads = attend(columns, keys, bias, new_cos, new_sin, fetched, False)
        flat = heads.reshape(HEADS // 4, STEPS, 4 * HEAD_DIM).transpose(1, 0, 2)
        flat = flat.reshape(STEPS, devices, model // devices).transpose(1, 0, 2)
        lhs = exchange(flat).reshape(devices * STEPS, model // devices)
    partial = output(me_word, lhs, out_weight, devices * STEPS, fast)
    if fast:
        near, far = partial
        both = near.astype(F32) + swap(far, 1, devices).astype(F32)
        arrived = exchange(both.astype(BF16), same_core)
    else:
        arrived = exchange(partial[0].reshape(devices, STEPS * pieces, LANES))
    total = jnp.sum(arrived.astype(F32), axis=0).astype(BF16)
    return total.reshape(STEPS, 1, model)


def solution(mesh):
    return jax.shard_map(
        local,
        mesh=mesh,
        in_specs=(
            P(None, ("groups", "session"), None),
            P(),
            P(None, "session"),
            P(None, "session"),
            P("session", None),
            P(("groups", "session"), None, None),
            P(("groups", "session"), None, None),
            P(("groups", "session"), None, None),
            P(("groups", "session")),
            P(("groups", "session"), None),
            P(None, ("groups", "session"), None),
        ),
        out_specs=P(None, ("groups", "session"), None),
        check_vma=False,
    )
```

```python
import functools
import math

import jax
import jax.numpy as jnp
from jax import lax
from jax.experimental import pallas as pl
from jax.experimental.pallas import tpu as pltpu
from jax.sharding import PartitionSpec as P

HEADS = 64
KV_HEADS = 8
HEAD_DIM = 128
STEPS = 2
GROUP = HEADS // KV_HEADS
LANES = 128
EXTRA = 16
PLANE = 4
PAIRS = 8
PROJECT_LIMIT = 48 * 2**20
AXIS = "session"
VMEM = pltpu.VMEM
SMEM = pltpu.SMEM
F32 = jnp.float32
BF16 = jnp.bfloat16


def angles(positions):
    half = HEAD_DIM // 2
    frequency = jnp.exp(
        -jnp.arange(half, dtype=F32) * (2.0 * math.log(500000.0) / HEAD_DIM)
    )
    return positions[..., None] * frequency


def turn_tables(positions):
    angle = angles(positions)
    cosine, sine = jnp.cos(angle), jnp.sin(angle)
    return (
        jnp.concatenate([cosine, cosine], axis=-1),
        jnp.concatenate([-sine, sine], axis=-1),
    )


def origin(me, order, j):
    if order is None:
        return 2 * (j % PAIRS) + jnp.bitwise_xor(jnp.bitwise_and(me, 1), j // PAIRS)
    return jnp.bitwise_xor(me, order[j])


def whole(space=VMEM):
    return pl.BlockSpec(memory_space=space)


def prepare_kernel(
    slots_dev, hidden_ref, gain_ref, slots_ref, block_ref, holder_ref, pair_ref, wide_scr
):
    steps, model = hidden_ref.shape
    pieces = model // LANES
    wide = hidden_ref[...].astype(F32)
    scale = lax.rsqrt(jnp.mean(wide * wide, axis=1, keepdims=True) + 1e-05)
    wide = wide * scale * gain_ref[...].astype(F32)
    for step in range(steps):
        for c in range(pieces):
            row = step * pieces + c
            wide_scr[row : row + 1, :] = wide[step : step + 1, c * LANES : (c + 1) * LANES]
    lane = lax.broadcasted_iota(jnp.int32, (EXTRA, LANES), 1)
    parity = lax.broadcasted_iota(jnp.int32, (EXTRA, LANES), 0)
    table = jnp.zeros((EXTRA, LANES), jnp.int32)
    for m in range(holder_ref.shape[0]):
        slot = slots_ref[0, 2 * m]
        holder = lax.div(slot, slots_dev)
        holder_ref[m] = holder
        pair_ref[holder] = m
        base = holder * slots_dev
        pair = jnp.where(parity == 0, slot - base, slots_ref[0, 2 * m + 1] - base)
        table = jnp.where(lane == holder, pair, table)
    wide_scr[steps * pieces :, :] = table.astype(F32)
    block = wide_scr[...].astype(BF16)
    for copy in range(block_ref.shape[0]):
        block_ref[copy] = block


def prepare(hidden, gain, block_slot, slots_dev, copies):
    assert slots_dev <= 256
    steps, model = hidden.shape
    rows = steps * model // LANES + EXTRA
    return pl.pallas_call(
        functools.partial(prepare_kernel, slots_dev),
        in_specs=[whole(), whole(), whole(SMEM)],
        out_specs=(whole(), whole(SMEM), whole(SMEM)),
        out_shape=(
            jax.ShapeDtypeStruct((copies, rows, LANES), BF16),
            jax.ShapeDtypeStruct((block_slot.shape[1] // 2,), jnp.int32),
            jax.ShapeDtypeStruct((block_slot.shape[1] // 2,), jnp.int32),
        ),
        scratch_shapes=[VMEM((rows, LANES), F32)],
        name="prepare",
    )(hidden, gain, block_slot)


def pick_kernel(order, me_ref, first_ref, second_ref, store_ref, out_ref, table_scr, table_smem, sem):
    block_len = store_ref.shape[1]
    half, rows, _ = first_ref.shape
    for j in range(2 * half):
        source = first_ref if j < half else second_ref
        asked = source[j % half, rows - EXTRA :, :].astype(F32)
        table_scr[j] = asked[:8].astype(jnp.int32)
    copy = pltpu.make_async_copy(table_scr, table_smem, sem)
    copy.start()
    copy.wait()
    me = me_ref[0]
    for j in range(2 * half):
        target = origin(me, order, j)
        for k in range(2):
            out_ref[target, k * block_len : (k + 1) * block_len, :] = store_ref[
                table_smem[j, k, me]
            ]


def pick_pages(me, first, second, store, order):
    count = 2 * first.shape[0]
    _, block_len, width = store.shape
    return pl.pallas_call(
        functools.partial(pick_kernel, order),
        in_specs=[whole(SMEM), whole(), whole(), whole()],
        out_specs=whole(),
        out_shape=jax.ShapeDtypeStruct((count, 2 * block_len, width), store.dtype),
        scratch_shapes=[
            VMEM((count, 8, LANES), jnp.int32),
            SMEM((count, 8, LANES), jnp.int32),
            pltpu.SemaphoreType.DMA(()),
        ],
        compiler_params=pltpu.CompilerParams(vmem_limit_bytes=36 * 2**20),
        name="pick_pages",
    )(me, first, second, store)


def split_kernel(x_ref, store_ref, keep_ref, send_ref):
    slots, block_len, width = store_ref.shape
    for x in range(2):

        @pl.when(x_ref[0] == x)
        def _():
            for head in range(width // LANES):
                target = keep_ref if head % 2 == x else send_ref
                lanes = slice(head // 2 * LANES, (head // 2 + 1) * LANES)
                part = store_ref[:, :, head * LANES : (head + 1) * LANES]
                target[:, lanes] = part.reshape(slots * block_len, LANES)


def split_values(x, store):
    slots, block_len, width = store.shape
    half = jax.ShapeDtypeStruct((slots * block_len, width // 2), store.dtype)
    return pl.pallas_call(
        split_kernel,
        in_specs=[whole(SMEM), whole()],
        out_specs=(whole(), whole()),
        out_shape=(half, half),
        compiler_params=pltpu.CompilerParams(vmem_limit_bytes=16 * 2**20),
        name="split_values",
    )(x, store)


def mix_kernel(me_ref, rows_ref, weights_ref, *rest):
    stores, (out_ref, values_scr, sum_scr) = rest[:PLANE], rest[PLANE:]
    me = me_ref[0]
    low = jnp.bitwise_and(me, PLANE - 1)
    z_me = lax.div(me, PLANE)
    sessions = weights_ref.shape[0]
    planes = out_ref.shape[0]
    block_len = values_scr.shape[1] // (2 * PLANE)
    for session in range(sessions):
        for q, store in enumerate(stores):
            device = jnp.bitwise_xor(low, q)
            for k in range(2):
                row = rows_ref[session * (2 * PLANE) + k * PLANE + device]
                source = pl.ds(pl.multiple_of(row * block_len, block_len), block_len)
                target = pl.ds(
                    pl.multiple_of((device * 2 + k) * block_len, block_len), block_len
                )
                values_scr[session, target, :] = store[source, :]
        block = weights_ref[session]
        product = jnp.dot(
            block[: planes * 8], values_scr[session], preferred_element_type=F32
        )
        mine = slice(session * 8, (session + 1) * 8)
        for z in range(planes):
            sum_scr[z, mine, :] = product[z * 8 : (z + 1) * 8, z * LANES : (z + 1) * LANES]
        recent = block[planes * 8 :].astype(F32)
        sum_scr[z_me, mine, :] += recent[:8]
    out_ref[...] = sum_scr[...].astype(BF16)


def mix(me, rows, weights, stores):
    sessions = weights.shape[0]
    planes = stores[0].shape[1] // LANES
    shape = (planes, sessions * 8, LANES)
    return pl.pallas_call(
        mix_kernel,
        in_specs=[whole(SMEM)] * 2 + [whole()] * (1 + PLANE),
        out_specs=whole(),
        out_shape=jax.ShapeDtypeStruct(shape, BF16),
        scratch_shapes=[VMEM((sessions, LANES, planes * LANES), BF16), VMEM(shape, F32)],
        compiler_params=pltpu.CompilerParams(vmem_limit_bytes=16 * 2**20),
        cost_estimate=pl.CostEstimate(
            flops=2 * sessions * 32 * LANES * planes * LANES,
            bytes_accessed=4 * stores[0].size * PLANE,
            transcendentals=0,
        ),
        name="mix_values",
    )(me, rows, weights, *stores)


def keys_kernel(pair_ref, factors_ref, basis_ref, cos_ref, sin_ref, out_ref, rows_scr):
    span = factors_ref.shape[0] // pair_ref.shape[0]
    count = rows_scr.shape[0] // span
    base = pl.program_id(0) * count
    for p in range(count):
        source = pl.ds(pl.multiple_of(pair_ref[base + p] * span, span), span)
        rows_scr[p * span : (p + 1) * span, :] = factors_ref[source, :]
    product = jnp.dot(rows_scr[...], basis_ref[...], preferred_element_type=F32)
    cosine, sine = cos_ref[...], sin_ref[...]
    for head in range(KV_HEADS):
        lanes = slice(head * HEAD_DIM, (head + 1) * HEAD_DIM)
        part = product[:, lanes]
        turned = part * cosine + pltpu.roll(part, HEAD_DIM // 2, 1) * sine
        out_ref[:, lanes] = turned.astype(BF16)


def make_keys(pair, factors, basis, cosine, sine):
    seq, rank = factors.shape
    width = basis.shape[1]
    rows = min(seq, 512)
    return pl.pallas_call(
        keys_kernel,
        grid=(seq // rows,),
        in_specs=[
            whole(SMEM),
            pl.BlockSpec((seq, rank), lambda i: (0, 0)),
            pl.BlockSpec((rank, width), lambda i: (0, 0)),
            pl.BlockSpec((rows, HEAD_DIM), lambda i: (i, 0)),
            pl.BlockSpec((rows, HEAD_DIM), lambda i: (i, 0)),
        ],
        out_specs=pl.BlockSpec((rows, width), lambda i: (i, 0)),
        out_shape=jax.ShapeDtypeStruct((seq, width), BF16),
        scratch_shapes=[VMEM((rows, rank), BF16)],
        compiler_params=pltpu.CompilerParams(vmem_limit_bytes=32 * 2**20),
        cost_estimate=pl.CostEstimate(
            flops=2 * seq * rank * width, bytes_accessed=4 * seq * width, transcendentals=0
        ),
        name="turned_keys",
    )(pair, factors, basis, cosine, sine)


def project_kernel(
    order, fast, me_ref, first_ref, second_ref, wq_ref, wk_ref, out_ref, *rest
):
    if fast:
        rows_ref, x_scr, lhs_scr, wq_buf, wk_buf, out_scr, sems, *asked_scr = rest
    else:
        x_scr, lhs_scr, wq_buf, wk_buf, out_scr, sems = rest
    depth, q_cols = wq_ref.shape
    k_cols = wk_ref.shape[1]
    chunks = wq_buf.shape[0]
    span = depth // chunks
    pieces = depth // LANES
    copies = []
    for i in range(chunks):
        rows = pl.ds(i * span, span)
        pair = (
            pltpu.make_async_copy(wq_ref.at[rows, :], wq_buf.at[i], sems.at[0, i]),
            pltpu.make_async_copy(wk_ref.at[rows, :], wk_buf.at[i], sems.at[1, i]),
        )
        for copy in pair:
            copy.start()
        copies.append(pair)
    half = first_ref.shape[0]
    count = 2 * half * STEPS
    rows = STEPS * pieces
    for j in range(2 * half):
        source = first_ref if j < half else second_ref
        x_scr[j * rows : (j + 1) * rows] = source[j % half, :rows, :].astype(F32)
    if fast:
        table_scr, table_smem, table_sem = asked_scr
        for j in range(2 * half):
            source = first_ref if j < half else second_ref
            asked = source[j % half, rows:, :].astype(F32)
            table_scr[2 * j : 2 * j + 2, :] = asked[:2].astype(jnp.int32)
        table_copy = pltpu.make_async_copy(table_scr, table_smem, table_sem)
        table_copy.start()
    for c in range(pieces):
        part = x_scr[pl.ds(c, count, stride=pieces), :]
        lhs_scr[:, c * LANES : (c + 1) * LANES] = part.astype(BF16)
    q_sum = jnp.zeros((count, q_cols), F32)
    k_sum = jnp.zeros((count, k_cols), F32)
    for i in range(chunks):
        for copy in copies[i]:
            copy.wait()
        lhs = lhs_scr[:, i * span : (i + 1) * span]
        q_sum = q_sum + jnp.dot(lhs, wq_buf[i], preferred_element_type=F32)
        k_sum = k_sum + jnp.dot(lhs, wk_buf[i], preferred_element_type=F32)
    if not fast:
        out_ref[:, :q_cols] = q_sum.astype(BF16)
        out_ref[:, q_cols:] = k_sum.astype(BF16)
        return
    me = me_ref[0]
    per = q_cols // LANES
    out_scr[...] = jnp.zeros_like(out_scr)
    for j in range(2 * half):
        place = origin(me, order, j)
        for step in range(STEPS):
            row = j * STEPS + step
            for c in range(per):
                out_scr[place, step * per + c : step * per + c + 1, :] = q_sum[
                    row : row + 1, c * LANES : (c + 1) * LANES
                ]
            out_scr[place, STEPS * per + step : STEPS * per + step + 1, :] = k_sum[
                row : row + 1, :
            ]
    out_ref[...] = out_scr[...].astype(BF16)
    table_copy.wait()
    plane = jnp.bitwise_and(me, -PLANE)
    for j in range(2 * half):
        place = origin(me, order, j) * (2 * PLANE)
        for k in range(2):
            for b in range(PLANE):
                rows_ref[place + k * PLANE + b] = table_smem[2 * j + k, plane + b]


def project(me, first, second, query_weight, kv_weight, order, fast):
    depth, q_cols = query_weight.shape
    k_cols = kv_weight.shape[1]
    pieces = depth // LANES
    devices = 2 * first.shape[0]
    rows = devices * STEPS
    chunks = 8
    span = depth // chunks
    shape = (devices, 16, LANES) if fast else (rows, q_cols + k_cols)
    return pl.pallas_call(
        functools.partial(project_kernel, order, fast),
        in_specs=[whole(SMEM), whole(), whole(), whole(pl.ANY), whole(pl.ANY)],
        out_specs=(whole(), whole(SMEM)) if fast else whole(),
        out_shape=(
            (
                jax.ShapeDtypeStruct(shape, BF16),
                jax.ShapeDtypeStruct((devices * 2 * PLANE,), jnp.int32),
            )
            if fast
            else jax.ShapeDtypeStruct(shape, BF16)
        ),
        scratch_shapes=[
            VMEM((rows * pieces, LANES), F32),
            VMEM((rows, depth), BF16),
            VMEM((chunks, span, q_cols), BF16),
            VMEM((chunks, span, k_cols), BF16),
            VMEM((devices, 16, LANES) if fast else (8, LANES), F32),
            pltpu.SemaphoreType.DMA((2, chunks)),
        ]
        + (
            [
                VMEM((2 * devices, LANES), jnp.int32),
                SMEM((2 * devices, LANES), jnp.int32),
                pltpu.SemaphoreType.DMA(()),
            ]
            if fast
            else []
        ),
        compiler_params=pltpu.CompilerParams(vmem_limit_bytes=PROJECT_LIMIT),
        cost_estimate=pl.CostEstimate(
            flops=2 * rows * depth * (q_cols + k_cols),
            bytes_accessed=2 * depth * (q_cols + k_cols),
            transcendentals=0,
        ),
        name="norm_project",
    )(me, first, second, query_weight, kv_weight)


def attend_kernel(fast, columns_ref, keys_ref, bias_ref, cos_ref, sin_ref, *rest):
    pages_ref, out_ref, out_scr = (None, *rest) if fast else rest
    score_scale = 1.0 / math.sqrt(HEAD_DIM)
    half = HEAD_DIM // 2
    rows = 2 * GROUP
    columns = columns_ref[...].astype(F32)
    count = columns.shape[0]
    query = columns[:, :8, :].reshape(count * 8, HEAD_DIM)
    fresh = columns[:, 8:, :]
    if fast:
        planes = count // PLANE
        out_scr[...] = jnp.zeros_like(out_scr)
    row_step = lax.rem(lax.broadcasted_iota(jnp.int32, (count * 8, 1), 0) // 4, STEPS)
    later = row_step == 1
    cosine = jnp.where(later, cos_ref[1:2, :], cos_ref[0:1, :])
    sine = jnp.where(later, sin_ref[1:2, :], sin_ref[0:1, :])
    turned = (query * cosine + pltpu.roll(query, half, 1) * sine).astype(BF16)
    turned_wide = turned.astype(F32)
    step_later = later[:rows]
    bias = jnp.where(step_later, bias_ref[1:2, :], bias_ref[0:1, :])
    new_keys = []
    for step in range(STEPS):
        part = fresh[:KV_HEADS, step, :]
        new = part * cos_ref[step : step + 1, :] + pltpu.roll(part, half, 1) * sin_ref[step : step + 1, :]
        new_keys.append(new.astype(BF16).astype(F32))
    for head in range(KV_HEADS):
        lanes = slice(head * HEAD_DIM, (head + 1) * HEAD_DIM)
        mine = slice(head * rows, (head + 1) * rows)
        scores = (
            lax.dot_general(
                turned[mine], keys_ref[:, lanes], (((1,), (1,)), ((), ())),
                preferred_element_type=F32,
            )
            * score_scale
            + bias
        )
        recent0 = (
            jnp.sum(turned_wide[mine] * new_keys[0][head : head + 1, :], axis=1, keepdims=True)
            * score_scale
        )
        recent1 = (
            jnp.sum(turned_wide[mine] * new_keys[1][head : head + 1, :], axis=1, keepdims=True)
            * score_scale
        )
        recent1 = jnp.where(step_later, recent1, -1e30)
        largest = jnp.maximum(
            jnp.max(scores, axis=1, keepdims=True), jnp.maximum(recent0, recent1)
        )
        cache_exp = jnp.exp(scores - largest)
        exp0 = jnp.exp(recent0 - largest)
        exp1 = jnp.exp(recent1 - largest)
        denominator = jnp.sum(cache_exp, axis=1, keepdims=True) + (exp0 + exp1)
        weights = (cache_exp / denominator).astype(BF16)
        weight0 = (exp0 / denominator).astype(BF16).astype(F32)
        weight1 = (exp1 / denominator).astype(BF16).astype(F32)
        recent = weight0 * fresh[KV_HEADS + head, 0:1, :]
        recent = recent + weight1 * fresh[KV_HEADS + head, 1:2, :]
        if not fast:
            values = pages_ref[:, :, lanes].reshape(keys_ref.shape[0], HEAD_DIM)
            mixed = jnp.dot(weights, values, preferred_element_type=F32)
            out_ref[mine, :] = (mixed + recent).astype(BF16)
            continue
        weights = weights.astype(F32)
        z, x = divmod(head, 2)
        for c in range(2):
            part = slice(c * 8, (c + 1) * 8)
            for plane in range(planes):
                out_scr[plane * PLANE + 2 * x + c, z * 8 : (z + 1) * 8, :] = weights[
                    part, plane * LANES : (plane + 1) * LANES
                ]
            out_scr[z * PLANE + 2 * x + c, planes * 8 : planes * 8 + 8, :] = recent[part]
    if fast:
        out_ref[...] = out_scr[...].astype(BF16)


def attend(columns, keys, bias, cosine, sine, pages, fast):
    seq, width = keys.shape
    count = columns.shape[0]
    if fast:
        shape = (count, count // PLANE * 8 + 16, LANES)
        scratch = [VMEM(shape, F32)]
        operands = (columns, keys, bias, cosine, sine)
    else:
        shape = (STEPS * HEADS, HEAD_DIM)
        scratch = [VMEM((8, LANES), F32)]
        operands = (columns, keys, bias, cosine, sine, pages)
    return pl.pallas_call(
        functools.partial(attend_kernel, fast),
        in_specs=[whole()] * len(operands),
        out_specs=whole(),
        out_shape=jax.ShapeDtypeStruct(shape, BF16),
        scratch_shapes=scratch,
        compiler_params=pltpu.CompilerParams(vmem_limit_bytes=48 * 2**20),
        cost_estimate=pl.CostEstimate(
            flops=4 * STEPS * HEADS * seq * HEAD_DIM,
            bytes_accessed=4 * seq * width,
            transcendentals=STEPS * HEADS * seq,
        ),
        name="attend",
    )(*operands)


def output_kernel(fast, me_ref, lhs_ref, weight_ref, *rest):
    out_refs, (weight_buf, out_scr, heads_scr, sems) = rest[:-4], rest[-4:]
    chunks, _, span = weight_buf.shape
    rows = out_scr.shape[0] * LANES // (chunks * span)
    pieces = chunks * span // LANES
    copies = []
    for i in range(chunks):
        copy = pltpu.make_async_copy(
            weight_ref.at[:, pl.ds(i * span, span)], weight_buf.at[i], sems.at[i]
        )
        copy.start()
        copies.append(copy)
    if fast:
        per = heads_scr.shape[0] // rows
        total = lhs_ref[0].astype(F32)
        for z in range(1, lhs_ref.shape[0]):
            total = total + lhs_ref[z].astype(F32)
        heads_scr[...] = total
        lhs = jnp.concatenate(
            [heads_scr[pl.ds(g, rows, stride=per), :].astype(BF16) for g in range(per)], axis=1
        )
    else:
        lhs = lhs_ref[...]
    for i in range(chunks):
        copies[i].wait()
        part = jnp.dot(lhs, weight_buf[i], preferred_element_type=F32)
        for c in range(span // LANES):
            out_scr[pl.ds(i * (span // LANES) + c, rows, stride=pieces), :] = part[
                :, c * LANES : (c + 1) * LANES
            ]
    if not fast:
        out_refs[0][...] = out_scr[...].astype(BF16)
        return
    low = jnp.bitwise_and(me_ref[0], 1)
    for out_ref, core in zip(out_refs, (low, 1 - low)):
        count, size, _ = out_ref.shape
        for j in range(count):
            part = pl.ds(pl.multiple_of((2 * j + core) * size, size), size)
            out_ref[j] = out_scr[part, :].astype(BF16)


def output(me, lhs, weight, rows, fast):
    depth, width = weight.shape
    chunks = 8
    if fast:
        shape = (rows // (2 * STEPS), STEPS * width // LANES, LANES)
        shapes = (jax.ShapeDtypeStruct(shape, BF16),) * 2
    else:
        shapes = (jax.ShapeDtypeStruct((rows * width // LANES, LANES), BF16),)
    return pl.pallas_call(
        functools.partial(output_kernel, fast),
        in_specs=[whole(SMEM), whole(), whole(pl.ANY)],
        out_specs=(whole(),) * len(shapes),
        out_shape=shapes,
        scratch_shapes=[
            VMEM((chunks, depth, width // chunks), BF16),
            VMEM((rows * width // LANES, LANES), F32),
            VMEM(lhs.shape[1:] if fast else (8, LANES), F32),
            pltpu.SemaphoreType.DMA((chunks,)),
        ],
        compiler_params=pltpu.CompilerParams(vmem_limit_bytes=48 * 2**20),
        cost_estimate=pl.CostEstimate(
            flops=2 * rows * depth * width, bytes_accessed=2 * depth * width, transcendentals=0
        ),
        name="output_project",
    )(me, lhs, weight)


def swap(block, bit, devices):
    return lax.ppermute(block, AXIS, [(i, i ^ bit) for i in range(devices)])


def exchange(blocks, groups=None):
    return lax.all_to_all(
        blocks, AXIS, split_axis=0, concat_axis=0, tiled=True, axis_index_groups=groups
    )


def local(
    hidden,
    norm_gain,
    query_weight,
    kv_weight,
    out_weight,
    key_factors,
    key_basis,
    value_store,
    lengths,
    block_slot,
    selection,
):
    devices = lax.axis_size(AXIS)
    me = lax.axis_index(AXIS)
    slots_dev, block_len, width = value_store.shape
    seq = key_factors.shape[1]
    pages = block_slot.shape[1]
    model = hidden.shape[2]
    q_cols = query_weight.shape[1]
    k_cols = kv_weight.shape[1]
    fast = devices == 2 * PAIRS and q_cols == 4 * HEAD_DIM and k_cols == HEAD_DIM
    pieces = model // LANES

    me_word = me.astype(jnp.int32).reshape(1)
    block, holder, pair = prepare(
        hidden[:, 0], norm_gain.reshape(1, model), block_slot, slots_dev, PAIRS if fast else 1
    )
    if fast:
        same_core = [list(range(core, devices, 2)) for core in range(2)]
        block = exchange(block, same_core)
        other = swap(block, 1, devices)
        order = None
        x = lax.bitwise_and(lax.shift_right_logical(me_word, 1), 1)
        keep, send = split_values(x, value_store)
        neighbour = swap(send, 2, devices)
    else:
        order = [0]
        bit = devices // 2
        while bit:
            other = swap(block, bit, devices)
            order = order + [k ^ bit for k in order]
            bit //= 2
            if bit:
                block = jnp.concatenate([block, other], axis=0)
        order = tuple(order)
    if not fast:
        sent_pages = pick_pages(me_word, block, other, value_store, order)
        block, other, sent_pages = lax.optimization_barrier((block, other, sent_pages))
        fetched = exchange(sent_pages)
    projected = project(
        me_word, block, other, query_weight, kv_weight, order, fast
    )
    if fast:
        projected, rows = projected
        projected, neighbour, pair = lax.optimization_barrier((projected, neighbour, pair))
        stores = (keep, swap(keep, 1, devices), neighbour, swap(neighbour, 1, devices))
        columns = exchange(projected)
    else:
        targets = jnp.bitwise_xor(me, jnp.array(order, dtype=jnp.int32))
        columns = exchange(projected.reshape(devices, STEPS, q_cols + k_cols)[targets])
        query = columns[:, :, :q_cols].transpose(1, 0, 2).reshape(STEPS, HEADS // 4, 4, HEAD_DIM)
        query = query.transpose(1, 0, 2, 3).reshape(HEADS // 4, 8, HEAD_DIM)
        fresh = columns[:, :, q_cols:].transpose(1, 0, 2).reshape(STEPS, HEADS // 4, HEAD_DIM)
        fresh = jnp.pad(fresh.transpose(1, 0, 2), ((0, 0), (0, 8 - STEPS), (0, 0)))
        columns = jnp.concatenate([query, fresh], axis=1)

    span = 2 * block_len
    places = (pair[:, None] * span + jnp.arange(span, dtype=jnp.int32)[None, :]).reshape(-1)
    cosine, sine = turn_tables(places.astype(F32))
    keys = make_keys(pair, key_factors[0], key_basis[0], cosine, sine)
    picked = jnp.any(
        selection[:, 0, :, None] == (places // block_len)[None, None, :], axis=1
    )
    bias = jnp.where(picked & (places < lengths[0])[None, :], 0.0, -1e30).astype(F32)
    new_cos, new_sin = turn_tables(
        (lengths[0] + jnp.arange(STEPS, dtype=jnp.int32)).astype(F32)
    )
    if fast:
        blocks = exchange(attend(columns, keys, bias, new_cos, new_sin, None, True))
        parts = mix(me_word, rows, blocks, stores)
        groups = [list(range(low, devices, PLANE)) for low in range(PLANE)]
        lhs = exchange(parts, groups)
    else:
        heads = attend(columns, keys, bias, new_cos, new_sin, fetched, False)
        flat = heads.reshape(HEADS // 4, STEPS, 4 * HEAD_DIM).transpose(1, 0, 2)
        flat = flat.reshape(STEPS, devices, model // devices).transpose(1, 0, 2)
        lhs = exchange(flat).reshape(devices * STEPS, model // devices)
    partial = output(me_word, lhs, out_weight, devices * STEPS, fast)
    if fast:
        near, far = partial
        both = near.astype(F32) + swap(far, 1, devices).astype(F32)
        arrived = exchange(both.astype(BF16), same_core)
    else:
        arrived = exchange(partial[0].reshape(devices, STEPS * pieces, LANES))
    total = jnp.sum(arrived.astype(F32), axis=0).astype(BF16)
    return total.reshape(STEPS, 1, model)


def solution(mesh):
    return jax.shard_map(
        local,
        mesh=mesh,
        in_specs=(
            P(None, ("groups", "session"), None),
            P(),
            P(None, "session"),
            P(None, "session"),
            P("session", None),
            P(("groups", "session"), None, None),
            P(("groups", "session"), None, None),
            P(("groups", "session"), None, None),
            P(("groups", "session")),
            P(("groups", "session"), None),
            P(None, ("groups", "session"), None),
        ),
        out_specs=P(None, ("groups", "session"), None),
        check_vma=False,
    )
```

```python
import functools
import math

import jax
import jax.numpy as jnp
from jax import lax
from jax.experimental import pallas as pl
from jax.experimental.pallas import tpu as pltpu
from jax.sharding import PartitionSpec as P

HEADS = 64
KV_HEADS = 8
HEAD_DIM = 128
STEPS = 2
GROUP = HEADS // KV_HEADS
LANES = 128
EXTRA = 16
PLANE = 4
PAIRS = 8
PROJECT_LIMIT = 52 * 2**20
AXIS = "session"
VMEM = pltpu.VMEM
SMEM = pltpu.SMEM
F32 = jnp.float32
BF16 = jnp.bfloat16


def angles(positions):
    half = HEAD_DIM // 2
    frequency = jnp.exp(
        -jnp.arange(half, dtype=F32) * (2.0 * math.log(500000.0) / HEAD_DIM)
    )
    return positions[..., None] * frequency


def turn_tables(positions):
    angle = angles(positions)
    cosine, sine = jnp.cos(angle), jnp.sin(angle)
    return (
        jnp.concatenate([cosine, cosine], axis=-1),
        jnp.concatenate([-sine, sine], axis=-1),
    )


def origin(me, order, j):
    if order is None:
        return 2 * (j % PAIRS) + jnp.bitwise_xor(jnp.bitwise_and(me, 1), j // PAIRS)
    return jnp.bitwise_xor(me, order[j])


def whole(space=VMEM):
    return pl.BlockSpec(memory_space=space)


def prepare_kernel(
    slots_dev, hidden_ref, gain_ref, slots_ref, block_ref, holder_ref, pair_ref, wide_scr
):
    steps, model = hidden_ref.shape
    pieces = model // LANES
    wide = hidden_ref[...].astype(F32)
    scale = lax.rsqrt(jnp.mean(wide * wide, axis=1, keepdims=True) + 1e-05)
    wide = wide * scale
    for step in range(steps):
        for c in range(pieces):
            row = step * pieces + c
            wide_scr[row : row + 1, :] = wide[step : step + 1, c * LANES : (c + 1) * LANES]
    lane = lax.broadcasted_iota(jnp.int32, (EXTRA, LANES), 1)
    parity = lax.broadcasted_iota(jnp.int32, (EXTRA, LANES), 0)
    table = jnp.zeros((EXTRA, LANES), jnp.int32)
    for m in range(holder_ref.shape[0]):
        slot = slots_ref[0, 2 * m]
        holder = lax.div(slot, slots_dev)
        holder_ref[m] = holder
        pair_ref[holder] = m
        base = holder * slots_dev
        pair = jnp.where(parity == 0, slot - base, slots_ref[0, 2 * m + 1] - base)
        table = jnp.where(lane == holder, pair, table)
    wide_scr[steps * pieces :, :] = table.astype(F32)
    gain = gain_ref[...].astype(F32)
    for step in range(steps):
        rows = slice(step * pieces, (step + 1) * pieces)
        wide_scr[rows, :] = wide_scr[rows, :] * gain
    block = wide_scr[...].astype(BF16)
    for copy in range(block_ref.shape[0]):
        block_ref[copy] = block


def prepare(hidden, gain, block_slot, slots_dev, copies):
    assert slots_dev <= 256
    steps, model = hidden.shape
    rows = steps * model // LANES + EXTRA
    return pl.pallas_call(
        functools.partial(prepare_kernel, slots_dev),
        in_specs=[whole(), whole(), whole(SMEM)],
        out_specs=(whole(), whole(SMEM), whole(SMEM)),
        out_shape=(
            jax.ShapeDtypeStruct((copies, rows, LANES), BF16),
            jax.ShapeDtypeStruct((block_slot.shape[1] // 2,), jnp.int32),
            jax.ShapeDtypeStruct((block_slot.shape[1] // 2,), jnp.int32),
        ),
        scratch_shapes=[VMEM((rows, LANES), F32)],
        name="prepare",
    )(hidden, gain, block_slot)


def pick_kernel(order, me_ref, first_ref, second_ref, store_ref, out_ref, table_scr, table_smem, sem):
    block_len = store_ref.shape[1]
    half, rows, _ = first_ref.shape
    for j in range(2 * half):
        source = first_ref if j < half else second_ref
        asked = source[j % half, rows - EXTRA :, :].astype(F32)
        table_scr[j] = asked[:8].astype(jnp.int32)
    copy = pltpu.make_async_copy(table_scr, table_smem, sem)
    copy.start()
    copy.wait()
    me = me_ref[0]
    for j in range(2 * half):
        target = origin(me, order, j)
        for k in range(2):
            out_ref[target, k * block_len : (k + 1) * block_len, :] = store_ref[
                table_smem[j, k, me]
            ]


def pick_pages(me, first, second, store, order):
    count = 2 * first.shape[0]
    _, block_len, width = store.shape
    return pl.pallas_call(
        functools.partial(pick_kernel, order),
        in_specs=[whole(SMEM), whole(), whole(), whole()],
        out_specs=whole(),
        out_shape=jax.ShapeDtypeStruct((count, 2 * block_len, width), store.dtype),
        scratch_shapes=[
            VMEM((count, 8, LANES), jnp.int32),
            SMEM((count, 8, LANES), jnp.int32),
            pltpu.SemaphoreType.DMA(()),
        ],
        compiler_params=pltpu.CompilerParams(vmem_limit_bytes=36 * 2**20),
        name="pick_pages",
    )(me, first, second, store)


def split_kernel(x_ref, store_ref, keep_ref, send_ref):
    slots, block_len, width = store_ref.shape
    for x in range(2):

        @pl.when(x_ref[0] == x)
        def _():
            for head in range(width // LANES):
                target = keep_ref if head % 2 == x else send_ref
                lanes = slice(head // 2 * LANES, (head // 2 + 1) * LANES)
                part = store_ref[:, :, head * LANES : (head + 1) * LANES]
                target[:, lanes] = part.reshape(slots * block_len, LANES)


def split_values(x, store):
    slots, block_len, width = store.shape
    half = jax.ShapeDtypeStruct((slots * block_len, width // 2), store.dtype)
    return pl.pallas_call(
        split_kernel,
        in_specs=[whole(SMEM), whole()],
        out_specs=(whole(), whole()),
        out_shape=(half, half),
        compiler_params=pltpu.CompilerParams(vmem_limit_bytes=16 * 2**20),
        name="split_values",
    )(x, store)


def mix_kernel(me_ref, rows_ref, weights_ref, *rest):
    stores, (out_ref, values_scr, sum_scr) = rest[:PLANE], rest[PLANE:]
    me = me_ref[0]
    low = jnp.bitwise_and(me, PLANE - 1)
    z_me = lax.div(me, PLANE)
    sessions = weights_ref.shape[0]
    planes = out_ref.shape[0]
    block_len = values_scr.shape[1] // (2 * PLANE)
    for session in range(sessions):
        for q, store in enumerate(stores):
            device = jnp.bitwise_xor(low, q)
            for k in range(2):
                row = rows_ref[session * (2 * PLANE) + k * PLANE + device]
                source = pl.ds(pl.multiple_of(row * block_len, block_len), block_len)
                target = pl.ds(
                    pl.multiple_of((device * 2 + k) * block_len, block_len), block_len
                )
                values_scr[session, target, :] = store[source, :]
        block = weights_ref[session]
        product = jnp.dot(
            block[: planes * 8], values_scr[session], preferred_element_type=F32
        )
        mine = slice(session * 8, (session + 1) * 8)
        for z in range(planes):
            sum_scr[z, mine, :] = product[z * 8 : (z + 1) * 8, z * LANES : (z + 1) * LANES]
        recent = block[planes * 8 :].astype(F32)
        sum_scr[z_me, mine, :] += recent[:8]
    out_ref[...] = sum_scr[...].astype(BF16)


def mix(me, rows, weights, stores):
    sessions = weights.shape[0]
    planes = stores[0].shape[1] // LANES
    shape = (planes, sessions * 8, LANES)
    return pl.pallas_call(
        mix_kernel,
        in_specs=[whole(SMEM)] * 2 + [whole()] * (1 + PLANE),
        out_specs=whole(),
        out_shape=jax.ShapeDtypeStruct(shape, BF16),
        scratch_shapes=[VMEM((sessions, LANES, planes * LANES), BF16), VMEM(shape, F32)],
        compiler_params=pltpu.CompilerParams(vmem_limit_bytes=16 * 2**20),
        cost_estimate=pl.CostEstimate(
            flops=2 * sessions * 32 * LANES * planes * LANES,
            bytes_accessed=4 * stores[0].size * PLANE,
            transcendentals=0,
        ),
        name="mix_values",
    )(me, rows, weights, *stores)


def keys_kernel(pair_ref, factors_ref, basis_ref, cos_ref, sin_ref, out_ref, rows_scr):
    span = factors_ref.shape[0] // pair_ref.shape[0]
    count = rows_scr.shape[0] // span
    base = pl.program_id(0) * count
    for p in range(count):
        source = pl.ds(pl.multiple_of(pair_ref[base + p] * span, span), span)
        rows_scr[p * span : (p + 1) * span, :] = factors_ref[source, :]
    product = jnp.dot(rows_scr[...], basis_ref[...], preferred_element_type=F32)
    cosine, sine = cos_ref[...], sin_ref[...]
    for head in range(KV_HEADS):
        lanes = slice(head * HEAD_DIM, (head + 1) * HEAD_DIM)
        part = product[:, lanes]
        turned = part * cosine + pltpu.roll(part, HEAD_DIM // 2, 1) * sine
        out_ref[:, lanes] = turned.astype(BF16)


def make_keys(pair, factors, basis, cosine, sine):
    seq, rank = factors.shape
    width = basis.shape[1]
    rows = min(seq, 512)
    return pl.pallas_call(
        keys_kernel,
        grid=(seq // rows,),
        in_specs=[
            whole(SMEM),
            pl.BlockSpec((seq, rank), lambda i: (0, 0)),
            pl.BlockSpec((rank, width), lambda i: (0, 0)),
            pl.BlockSpec((rows, HEAD_DIM), lambda i: (i, 0)),
            pl.BlockSpec((rows, HEAD_DIM), lambda i: (i, 0)),
        ],
        out_specs=pl.BlockSpec((rows, width), lambda i: (i, 0)),
        out_shape=jax.ShapeDtypeStruct((seq, width), BF16),
        scratch_shapes=[VMEM((rows, rank), BF16)],
        compiler_params=pltpu.CompilerParams(vmem_limit_bytes=32 * 2**20),
        cost_estimate=pl.CostEstimate(
            flops=2 * seq * rank * width, bytes_accessed=4 * seq * width, transcendentals=0
        ),
        name="turned_keys",
    )(pair, factors, basis, cosine, sine)


def project_kernel(
    order, fast, me_ref, first_ref, second_ref, wq_ref, wk_ref, out_ref, *rest
):
    if fast:
        rows_ref, x_scr, lhs_scr, wq_buf, wk_buf, out_scr, sems, *asked_scr = rest
    else:
        x_scr, lhs_scr, wq_buf, wk_buf, out_scr, sems = rest
    depth, q_cols = wq_ref.shape
    k_cols = wk_ref.shape[1]
    chunks = wq_buf.shape[0]
    span = depth // chunks
    pieces = depth // LANES
    copies = []
    for i in range(chunks):
        rows = pl.ds(i * span, span)
        pair = (
            pltpu.make_async_copy(wq_ref.at[rows, :], wq_buf.at[i], sems.at[0, i]),
            pltpu.make_async_copy(wk_ref.at[rows, :], wk_buf.at[i], sems.at[1, i]),
        )
        for copy in pair:
            copy.start()
        copies.append(pair)
    half = first_ref.shape[0]
    count = 2 * half * STEPS
    rows = STEPS * pieces
    for j in range(2 * half):
        source = first_ref if j < half else second_ref
        x_scr[j * rows : (j + 1) * rows] = source[j % half, :rows, :].astype(F32)
    if fast:
        table_scr, table_smem, table_sem = asked_scr
        for j in range(2 * half):
            source = first_ref if j < half else second_ref
            asked = source[j % half, rows:, :].astype(F32)
            table_scr[2 * j : 2 * j + 2, :] = asked[:2].astype(jnp.int32)
        table_copy = pltpu.make_async_copy(table_scr, table_smem, table_sem)
        table_copy.start()
    for c in range(pieces):
        part = x_scr[pl.ds(c, count, stride=pieces), :]
        lhs_scr[:, c * LANES : (c + 1) * LANES] = part.astype(BF16)
    q_sum = jnp.zeros((count, q_cols), F32)
    k_sum = jnp.zeros((count, k_cols), F32)
    for i in range(chunks):
        for copy in copies[i]:
            copy.wait()
        lhs = lhs_scr[:, i * span : (i + 1) * span]
        q_sum = q_sum + jnp.dot(lhs, wq_buf[i], preferred_element_type=F32)
        k_sum = k_sum + jnp.dot(lhs, wk_buf[i], preferred_element_type=F32)
    if not fast:
        out_ref[:, :q_cols] = q_sum.astype(BF16)
        out_ref[:, q_cols:] = k_sum.astype(BF16)
        return
    me = me_ref[0]
    per = q_cols // LANES
    out_scr[...] = jnp.zeros_like(out_scr)
    for j in range(2 * half):
        place = origin(me, order, j)
        for step in range(STEPS):
            row = j * STEPS + step
            for c in range(per):
                out_scr[place, step * per + c : step * per + c + 1, :] = q_sum[
                    row : row + 1, c * LANES : (c + 1) * LANES
                ]
            out_scr[place, STEPS * per + step : STEPS * per + step + 1, :] = k_sum[
                row : row + 1, :
            ]
    out_ref[...] = out_scr[...].astype(BF16)
    table_copy.wait()
    plane = jnp.bitwise_and(me, -PLANE)
    for j in range(2 * half):
        place = origin(me, order, j) * (2 * PLANE)
        for k in range(2):
            for b in range(PLANE):
                rows_ref[place + k * PLANE + b] = table_smem[2 * j + k, plane + b]


def project(me, first, second, query_weight, kv_weight, order, fast):
    depth, q_cols = query_weight.shape
    k_cols = kv_weight.shape[1]
    pieces = depth // LANES
    devices = 2 * first.shape[0]
    rows = devices * STEPS
    chunks = 8
    span = depth // chunks
    shape = (devices, 16, LANES) if fast else (rows, q_cols + k_cols)
    return pl.pallas_call(
        functools.partial(project_kernel, order, fast),
        in_specs=[whole(SMEM), whole(), whole(), whole(pl.ANY), whole(pl.ANY)],
        out_specs=(whole(), whole(SMEM)) if fast else whole(),
        out_shape=(
            (
                jax.ShapeDtypeStruct(shape, BF16),
                jax.ShapeDtypeStruct((devices * 2 * PLANE,), jnp.int32),
            )
            if fast
            else jax.ShapeDtypeStruct(shape, BF16)
        ),
        scratch_shapes=[
            VMEM((rows * pieces, LANES), F32),
            VMEM((rows, depth), BF16),
            VMEM((chunks, span, q_cols), BF16),
            VMEM((chunks, span, k_cols), BF16),
            VMEM((devices, 16, LANES) if fast else (8, LANES), F32),
            pltpu.SemaphoreType.DMA((2, chunks)),
        ]
        + (
            [
                VMEM((2 * devices, LANES), jnp.int32),
                SMEM((2 * devices, LANES), jnp.int32),
                pltpu.SemaphoreType.DMA(()),
            ]
            if fast
            else []
        ),
        compiler_params=pltpu.CompilerParams(vmem_limit_bytes=PROJECT_LIMIT),
        cost_estimate=pl.CostEstimate(
            flops=2 * rows * depth * (q_cols + k_cols),
            bytes_accessed=2 * depth * (q_cols + k_cols),
            transcendentals=0,
        ),
        name="norm_project",
    )(me, first, second, query_weight, kv_weight)


def attend_kernel(fast, columns_ref, keys_ref, bias_ref, cos_ref, sin_ref, *rest):
    pages_ref, out_ref, out_scr = (None, *rest) if fast else rest
    score_scale = 1.0 / math.sqrt(HEAD_DIM)
    half = HEAD_DIM // 2
    rows = 2 * GROUP
    columns = columns_ref[...].astype(F32)
    count = columns.shape[0]
    query = columns[:, :8, :].reshape(count * 8, HEAD_DIM)
    fresh = columns[:, 8:, :]
    if fast:
        planes = count // PLANE
        out_scr[...] = jnp.zeros_like(out_scr)
    row_step = lax.rem(lax.broadcasted_iota(jnp.int32, (count * 8, 1), 0) // 4, STEPS)
    later = row_step == 1
    cosine = jnp.where(later, cos_ref[1:2, :], cos_ref[0:1, :])
    sine = jnp.where(later, sin_ref[1:2, :], sin_ref[0:1, :])
    turned = (query * cosine + pltpu.roll(query, half, 1) * sine).astype(BF16)
    turned_wide = turned.astype(F32)
    step_later = later[:rows]
    bias = jnp.where(step_later, bias_ref[1:2, :], bias_ref[0:1, :])
    new_keys = []
    for step in range(STEPS):
        part = fresh[:KV_HEADS, step, :]
        new = part * cos_ref[step : step + 1, :] + pltpu.roll(part, half, 1) * sin_ref[step : step + 1, :]
        new_keys.append(new.astype(BF16).astype(F32))
    for head in range(KV_HEADS):
        lanes = slice(head * HEAD_DIM, (head + 1) * HEAD_DIM)
        mine = slice(head * rows, (head + 1) * rows)
        scores = (
            lax.dot_general(
                turned[mine], keys_ref[:, lanes], (((1,), (1,)), ((), ())),
                preferred_element_type=F32,
            )
            * score_scale
            + bias
        )
        recent0 = (
            jnp.sum(turned_wide[mine] * new_keys[0][head : head + 1, :], axis=1, keepdims=True)
            * score_scale
        )
        recent1 = (
            jnp.sum(turned_wide[mine] * new_keys[1][head : head + 1, :], axis=1, keepdims=True)
            * score_scale
        )
        recent1 = jnp.where(step_later, recent1, -1e30)
        largest = jnp.maximum(
            jnp.max(scores, axis=1, keepdims=True), jnp.maximum(recent0, recent1)
        )
        cache_exp = jnp.exp(scores - largest)
        exp0 = jnp.exp(recent0 - largest)
        exp1 = jnp.exp(recent1 - largest)
        denominator = jnp.sum(cache_exp, axis=1, keepdims=True) + (exp0 + exp1)
        weights = (cache_exp / denominator).astype(BF16)
        weight0 = (exp0 / denominator).astype(BF16).astype(F32)
        weight1 = (exp1 / denominator).astype(BF16).astype(F32)
        recent = weight0 * fresh[KV_HEADS + head, 0:1, :]
        recent = recent + weight1 * fresh[KV_HEADS + head, 1:2, :]
        if not fast:
            values = pages_ref[:, :, lanes].reshape(keys_ref.shape[0], HEAD_DIM)
            mixed = jnp.dot(weights, values, preferred_element_type=F32)
            out_ref[mine, :] = (mixed + recent).astype(BF16)
            continue
        weights = weights.astype(F32)
        z, x = divmod(head, 2)
        for c in range(2):
            part = slice(c * 8, (c + 1) * 8)
            for plane in range(planes):
                out_scr[plane * PLANE + 2 * x + c, z * 8 : (z + 1) * 8, :] = weights[
                    part, plane * LANES : (plane + 1) * LANES
                ]
            out_scr[z * PLANE + 2 * x + c, planes * 8 : planes * 8 + 8, :] = recent[part]
    if fast:
        out_ref[...] = out_scr[...].astype(BF16)


def attend(columns, keys, bias, cosine, sine, pages, fast):
    seq, width = keys.shape
    count = columns.shape[0]
    if fast:
        shape = (count, count // PLANE * 8 + 16, LANES)
        scratch = [VMEM(shape, F32)]
        operands = (columns, keys, bias, cosine, sine)
    else:
        shape = (STEPS * HEADS, HEAD_DIM)
        scratch = [VMEM((8, LANES), F32)]
        operands = (columns, keys, bias, cosine, sine, pages)
    return pl.pallas_call(
        functools.partial(attend_kernel, fast),
        in_specs=[whole()] * len(operands),
        out_specs=whole(),
        out_shape=jax.ShapeDtypeStruct(shape, BF16),
        scratch_shapes=scratch,
        compiler_params=pltpu.CompilerParams(vmem_limit_bytes=48 * 2**20),
        cost_estimate=pl.CostEstimate(
            flops=4 * STEPS * HEADS * seq * HEAD_DIM,
            bytes_accessed=4 * seq * width,
            transcendentals=STEPS * HEADS * seq,
        ),
        name="attend",
    )(*operands)


def output_kernel(fast, me_ref, lhs_ref, weight_ref, *rest):
    out_refs, (weight_buf, out_scr, heads_scr, sems) = rest[:-4], rest[-4:]
    chunks, _, span = weight_buf.shape
    rows = out_scr.shape[0] * LANES // (chunks * span)
    pieces = chunks * span // LANES
    copies = []
    for i in range(chunks):
        copy = pltpu.make_async_copy(
            weight_ref.at[:, pl.ds(i * span, span)], weight_buf.at[i], sems.at[i]
        )
        copy.start()
        copies.append(copy)
    if fast:
        per = heads_scr.shape[0] // rows
        total = lhs_ref[0].astype(F32)
        for z in range(1, lhs_ref.shape[0]):
            total = total + lhs_ref[z].astype(F32)
        heads_scr[...] = total
        lhs = jnp.concatenate(
            [heads_scr[pl.ds(g, rows, stride=per), :].astype(BF16) for g in range(per)], axis=1
        )
    else:
        lhs = lhs_ref[...]
    for i in range(chunks):
        copies[i].wait()
        part = jnp.dot(lhs, weight_buf[i], preferred_element_type=F32)
        for c in range(span // LANES):
            out_scr[pl.ds(i * (span // LANES) + c, rows, stride=pieces), :] = part[
                :, c * LANES : (c + 1) * LANES
            ]
    if not fast:
        out_refs[0][...] = out_scr[...].astype(BF16)
        return
    low = jnp.bitwise_and(me_ref[0], 1)
    for out_ref, core in zip(out_refs, (low, 1 - low)):
        count, size, _ = out_ref.shape
        for j in range(count):
            part = pl.ds(pl.multiple_of((2 * j + core) * size, size), size)
            out_ref[j] = out_scr[part, :].astype(BF16)


def output(me, lhs, weight, rows, fast):
    depth, width = weight.shape
    chunks = 8
    if fast:
        shape = (rows // (2 * STEPS), STEPS * width // LANES, LANES)
        shapes = (jax.ShapeDtypeStruct(shape, BF16),) * 2
    else:
        shapes = (jax.ShapeDtypeStruct((rows * width // LANES, LANES), BF16),)
    return pl.pallas_call(
        functools.partial(output_kernel, fast),
        in_specs=[whole(SMEM), whole(), whole(pl.ANY)],
        out_specs=(whole(),) * len(shapes),
        out_shape=shapes,
        scratch_shapes=[
            VMEM((chunks, depth, width // chunks), BF16),
            VMEM((rows * width // LANES, LANES), F32),
            VMEM(lhs.shape[1:] if fast else (8, LANES), F32),
            pltpu.SemaphoreType.DMA((chunks,)),
        ],
        compiler_params=pltpu.CompilerParams(vmem_limit_bytes=48 * 2**20),
        cost_estimate=pl.CostEstimate(
            flops=2 * rows * depth * width, bytes_accessed=2 * depth * width, transcendentals=0
        ),
        name="output_project",
    )(me, lhs, weight)


def swap(block, bit, devices):
    return lax.ppermute(block, AXIS, [(i, i ^ bit) for i in range(devices)])


def exchange(blocks, groups=None):
    return lax.all_to_all(
        blocks, AXIS, split_axis=0, concat_axis=0, tiled=True, axis_index_groups=groups
    )


def local(
    hidden,
    norm_gain,
    query_weight,
    kv_weight,
    out_weight,
    key_factors,
    key_basis,
    value_store,
    lengths,
    block_slot,
    selection,
):
    devices = lax.axis_size(AXIS)
    me = lax.axis_index(AXIS)
    slots_dev, block_len, width = value_store.shape
    seq = key_factors.shape[1]
    pages = block_slot.shape[1]
    model = hidden.shape[2]
    q_cols = query_weight.shape[1]
    k_cols = kv_weight.shape[1]
    fast = devices == 2 * PAIRS and q_cols == 4 * HEAD_DIM and k_cols == HEAD_DIM
    pieces = model // LANES

    me_word = me.astype(jnp.int32).reshape(1)
    block, holder, pair = prepare(
        hidden[:, 0], norm_gain.reshape(pieces, LANES), block_slot, slots_dev, PAIRS if fast else 1
    )
    if fast:
        same_core = [list(range(core, devices, 2)) for core in range(2)]
        block = exchange(block, same_core)
        other = swap(block, 1, devices)
        order = None
        x = lax.bitwise_and(lax.shift_right_logical(me_word, 1), 1)
        keep, send = split_values(x, value_store)
        neighbour = swap(send, 2, devices)
    else:
        order = [0]
        bit = devices // 2
        while bit:
            other = swap(block, bit, devices)
            order = order + [k ^ bit for k in order]
            bit //= 2
            if bit:
                block = jnp.concatenate([block, other], axis=0)
        order = tuple(order)
    if not fast:
        sent_pages = pick_pages(me_word, block, other, value_store, order)
        block, other, sent_pages = lax.optimization_barrier((block, other, sent_pages))
        fetched = exchange(sent_pages)
    projected = project(
        me_word, block, other, query_weight, kv_weight, order, fast
    )
    if fast:
        projected, rows = projected
        projected, neighbour, pair = lax.optimization_barrier((projected, neighbour, pair))
        stores = (keep, swap(keep, 1, devices), neighbour, swap(neighbour, 1, devices))
        columns = exchange(projected)
    else:
        targets = jnp.bitwise_xor(me, jnp.array(order, dtype=jnp.int32))
        columns = exchange(projected.reshape(devices, STEPS, q_cols + k_cols)[targets])
        query = columns[:, :, :q_cols].transpose(1, 0, 2).reshape(STEPS, HEADS // 4, 4, HEAD_DIM)
        query = query.transpose(1, 0, 2, 3).reshape(HEADS // 4, 8, HEAD_DIM)
        fresh = columns[:, :, q_cols:].transpose(1, 0, 2).reshape(STEPS, HEADS // 4, HEAD_DIM)
        fresh = jnp.pad(fresh.transpose(1, 0, 2), ((0, 0), (0, 8 - STEPS), (0, 0)))
        columns = jnp.concatenate([query, fresh], axis=1)

    span = 2 * block_len
    places = (pair[:, None] * span + jnp.arange(span, dtype=jnp.int32)[None, :]).reshape(-1)
    cosine, sine = turn_tables(places.astype(F32))
    keys = make_keys(pair, key_factors[0], key_basis[0], cosine, sine)
    picked = jnp.any(
        selection[:, 0, :, None] == (places // block_len)[None, None, :], axis=1
    )
    bias = jnp.where(picked & (places < lengths[0])[None, :], 0.0, -1e30).astype(F32)
    new_cos, new_sin = turn_tables(
        (lengths[0] + jnp.arange(STEPS, dtype=jnp.int32)).astype(F32)
    )
    if fast:
        blocks = exchange(attend(columns, keys, bias, new_cos, new_sin, None, True))
        parts = mix(me_word, rows, blocks, stores)
        groups = [list(range(low, devices, PLANE)) for low in range(PLANE)]
        lhs = exchange(parts, groups)
    else:
        heads = attend(columns, keys, bias, new_cos, new_sin, fetched, False)
        flat = heads.reshape(HEADS // 4, STEPS, 4 * HEAD_DIM).transpose(1, 0, 2)
        flat = flat.reshape(STEPS, devices, model // devices).transpose(1, 0, 2)
        lhs = exchange(flat).reshape(devices * STEPS, model // devices)
    partial = output(me_word, lhs, out_weight, devices * STEPS, fast)
    if fast:
        near, far = partial
        both = near.astype(F32) + swap(far, 1, devices).astype(F32)
        arrived = exchange(both.astype(BF16), same_core)
    else:
        arrived = exchange(partial[0].reshape(devices, STEPS * pieces, LANES))
    total = jnp.sum(arrived.astype(F32), axis=0).astype(BF16)
    return total.reshape(STEPS, 1, model)


def solution(mesh):
    return jax.shard_map(
        local,
        mesh=mesh,
        in_specs=(
            P(None, ("groups", "session"), None),
            P(),
            P(None, "session"),
            P(None, "session"),
            P("session", None),
            P(("groups", "session"), None, None),
            P(("groups", "session"), None, None),
            P(("groups", "session"), None, None),
            P(("groups", "session")),
            P(("groups", "session"), None),
            P(None, ("groups", "session"), None),
        ),
        out_specs=P(None, ("groups", "session"), None),
        check_vma=False,
    )
```

```python
import functools
import math

import jax
import jax.numpy as jnp
from jax import lax
from jax.experimental import pallas as pl
from jax.experimental.pallas import tpu as pltpu
from jax.sharding import PartitionSpec as P

HEADS = 64
KV_HEADS = 8
HEAD_DIM = 128
STEPS = 2
GROUP = HEADS // KV_HEADS
LANES = 128
EXTRA = 16
PLANE = 4
PAIRS = 8
PROJECT_LIMIT = 48 * 2**20
AXIS = "session"
VMEM = pltpu.VMEM
SMEM = pltpu.SMEM
F32 = jnp.float32
BF16 = jnp.bfloat16


def angles(positions):
    half = HEAD_DIM // 2
    frequency = jnp.exp(
        -jnp.arange(half, dtype=F32) * (2.0 * math.log(500000.0) / HEAD_DIM)
    )
    return positions[..., None] * frequency


def turn_tables(positions):
    angle = angles(positions)
    cosine, sine = jnp.cos(angle), jnp.sin(angle)
    return (
        jnp.concatenate([cosine, cosine], axis=-1),
        jnp.concatenate([-sine, sine], axis=-1),
    )


def origin(me, order, j):
    if order is None:
        return 2 * (j % PAIRS) + jnp.bitwise_xor(jnp.bitwise_and(me, 1), j // PAIRS)
    return jnp.bitwise_xor(me, order[j])


def whole(space=VMEM):
    return pl.BlockSpec(memory_space=space)


def prepare_kernel(
    slots_dev, hidden_ref, gain_ref, slots_ref, block_ref, holder_ref, pair_ref, wide_scr
):
    steps, model = hidden_ref.shape
    pieces = model // LANES
    wide = hidden_ref[...].astype(F32)
    scale = lax.rsqrt(jnp.mean(wide * wide, axis=1, keepdims=True) + 1e-05)
    wide = wide * scale
    for step in range(steps):
        for c in range(pieces):
            row = step * pieces + c
            wide_scr[row : row + 1, :] = wide[step : step + 1, c * LANES : (c + 1) * LANES]
    lane = lax.broadcasted_iota(jnp.int32, (EXTRA, LANES), 1)
    parity = lax.broadcasted_iota(jnp.int32, (EXTRA, LANES), 0)
    table = jnp.zeros((EXTRA, LANES), jnp.int32)
    for m in range(holder_ref.shape[0]):
        slot = slots_ref[0, 2 * m]
        holder = lax.div(slot, slots_dev)
        holder_ref[m] = holder
        pair_ref[holder] = m
        base = holder * slots_dev
        pair = jnp.where(parity == 0, slot - base, slots_ref[0, 2 * m + 1] - base)
        table = jnp.where(lane == holder, pair, table)
    wide_scr[steps * pieces :, :] = table.astype(F32)
    gain = gain_ref[...].astype(F32)
    for step in range(steps):
        rows = slice(step * pieces, (step + 1) * pieces)
        wide_scr[rows, :] = wide_scr[rows, :] * gain
    block = wide_scr[...].astype(BF16)
    for copy in range(block_ref.shape[0]):
        block_ref[copy] = block


def prepare(hidden, gain, block_slot, slots_dev, copies):
    assert slots_dev <= 256
    steps, model = hidden.shape
    rows = steps * model // LANES + EXTRA
    return pl.pallas_call(
        functools.partial(prepare_kernel, slots_dev),
        in_specs=[whole(), whole(), whole(SMEM)],
        out_specs=(whole(), whole(SMEM), whole(SMEM)),
        out_shape=(
            jax.ShapeDtypeStruct((copies, rows, LANES), BF16),
            jax.ShapeDtypeStruct((block_slot.shape[1] // 2,), jnp.int32),
            jax.ShapeDtypeStruct((block_slot.shape[1] // 2,), jnp.int32),
        ),
        scratch_shapes=[VMEM((rows, LANES), F32)],
        name="prepare",
    )(hidden, gain, block_slot)


def pick_kernel(order, me_ref, first_ref, second_ref, store_ref, out_ref, table_scr, table_smem, sem):
    block_len = store_ref.shape[1]
    half, rows, _ = first_ref.shape
    for j in range(2 * half):
        source = first_ref if j < half else second_ref
        asked = source[j % half, rows - EXTRA :, :].astype(F32)
        table_scr[j] = asked[:8].astype(jnp.int32)
    copy = pltpu.make_async_copy(table_scr, table_smem, sem)
    copy.start()
    copy.wait()
    me = me_ref[0]
    for j in range(2 * half):
        target = origin(me, order, j)
        for k in range(2):
            out_ref[target, k * block_len : (k + 1) * block_len, :] = store_ref[
                table_smem[j, k, me]
            ]


def pick_pages(me, first, second, store, order):
    count = 2 * first.shape[0]
    _, block_len, width = store.shape
    return pl.pallas_call(
        functools.partial(pick_kernel, order),
        in_specs=[whole(SMEM), whole(), whole(), whole()],
        out_specs=whole(),
        out_shape=jax.ShapeDtypeStruct((count, 2 * block_len, width), store.dtype),
        scratch_shapes=[
            VMEM((count, 8, LANES), jnp.int32),
            SMEM((count, 8, LANES), jnp.int32),
            pltpu.SemaphoreType.DMA(()),
        ],
        compiler_params=pltpu.CompilerParams(vmem_limit_bytes=36 * 2**20),
        name="pick_pages",
    )(me, first, second, store)


def split_kernel(x_ref, store_ref, keep_ref, send_ref):
    slots, block_len, width = store_ref.shape
    for x in range(2):

        @pl.when(x_ref[0] == x)
        def _():
            for head in range(width // LANES):
                target = keep_ref if head % 2 == x else send_ref
                lanes = slice(head // 2 * LANES, (head // 2 + 1) * LANES)
                part = store_ref[:, :, head * LANES : (head + 1) * LANES]
                target[:, lanes] = part.reshape(slots * block_len, LANES)


def split_values(x, store):
    slots, block_len, width = store.shape
    half = jax.ShapeDtypeStruct((slots * block_len, width // 2), store.dtype)
    return pl.pallas_call(
        split_kernel,
        in_specs=[whole(SMEM), whole()],
        out_specs=(whole(), whole()),
        out_shape=(half, half),
        compiler_params=pltpu.CompilerParams(vmem_limit_bytes=16 * 2**20),
        name="split_values",
    )(x, store)


def mix_kernel(me_ref, rows_ref, weights_ref, *rest):
    stores, (values_scr, sum_scr) = rest[:PLANE], rest[-2:]
    out_refs = rest[PLANE:-2]
    me = me_ref[0]
    low = jnp.bitwise_and(me, PLANE - 1)
    z_me = lax.div(me, PLANE)
    sessions = weights_ref.shape[0]
    planes = len(out_refs)
    block_len = values_scr.shape[1] // (2 * PLANE)
    for session in range(sessions):
        for q, store in enumerate(stores):
            device = jnp.bitwise_xor(low, q)
            for k in range(2):
                row = rows_ref[session * (2 * PLANE) + k * PLANE + device]
                source = pl.ds(pl.multiple_of(row * block_len, block_len), block_len)
                target = pl.ds(
                    pl.multiple_of((device * 2 + k) * block_len, block_len), block_len
                )
                values_scr[session, target, :] = store[source, :]
        block = weights_ref[session]
        product = jnp.dot(
            block[: planes * 8], values_scr[session], preferred_element_type=F32
        )
        mine = slice(session * 8, (session + 1) * 8)
        for z in range(planes):
            sum_scr[z, mine, :] = product[z * 8 : (z + 1) * 8, z * LANES : (z + 1) * LANES]
        recent = block[planes * 8 :].astype(F32)
        sum_scr[z_me, mine, :] += recent[:8]
    for q, out_ref in enumerate(out_refs):
        out_ref[...] = sum_scr[jnp.bitwise_xor(z_me, q)].astype(BF16)


def mix(me, rows, weights, stores):
    sessions = weights.shape[0]
    planes = stores[0].shape[1] // LANES
    shape = (planes, sessions * 8, LANES)
    return pl.pallas_call(
        mix_kernel,
        in_specs=[whole(SMEM)] * 2 + [whole()] * (1 + PLANE),
        out_specs=(whole(),) * planes,
        out_shape=(jax.ShapeDtypeStruct(shape[1:], BF16),) * planes,
        scratch_shapes=[VMEM((sessions, LANES, planes * LANES), BF16), VMEM(shape, F32)],
        compiler_params=pltpu.CompilerParams(vmem_limit_bytes=16 * 2**20),
        cost_estimate=pl.CostEstimate(
            flops=2 * sessions * 32 * LANES * planes * LANES,
            bytes_accessed=4 * stores[0].size * PLANE,
            transcendentals=0,
        ),
        name="mix_values",
    )(me, rows, weights, *stores)


def keys_kernel(pair_ref, factors_ref, basis_ref, cos_ref, sin_ref, out_ref, rows_scr):
    span = factors_ref.shape[0] // pair_ref.shape[0]
    count = rows_scr.shape[0] // span
    base = pl.program_id(0) * count
    for p in range(count):
        source = pl.ds(pl.multiple_of(pair_ref[base + p] * span, span), span)
        rows_scr[p * span : (p + 1) * span, :] = factors_ref[source, :]
    product = jnp.dot(rows_scr[...], basis_ref[...], preferred_element_type=F32)
    cosine, sine = cos_ref[...], sin_ref[...]
    for head in range(KV_HEADS):
        lanes = slice(head * HEAD_DIM, (head + 1) * HEAD_DIM)
        part = product[:, lanes]
        turned = part * cosine + pltpu.roll(part, HEAD_DIM // 2, 1) * sine
        out_ref[:, lanes] = turned.astype(BF16)


def make_keys(pair, factors, basis, cosine, sine):
    seq, rank = factors.shape
    width = basis.shape[1]
    rows = min(seq, 512)
    return pl.pallas_call(
        keys_kernel,
        grid=(seq // rows,),
        in_specs=[
            whole(SMEM),
            pl.BlockSpec((seq, rank), lambda i: (0, 0)),
            pl.BlockSpec((rank, width), lambda i: (0, 0)),
            pl.BlockSpec((rows, HEAD_DIM), lambda i: (i, 0)),
            pl.BlockSpec((rows, HEAD_DIM), lambda i: (i, 0)),
        ],
        out_specs=pl.BlockSpec((rows, width), lambda i: (i, 0)),
        out_shape=jax.ShapeDtypeStruct((seq, width), BF16),
        scratch_shapes=[VMEM((rows, rank), BF16)],
        compiler_params=pltpu.CompilerParams(vmem_limit_bytes=32 * 2**20),
        cost_estimate=pl.CostEstimate(
            flops=2 * seq * rank * width, bytes_accessed=4 * seq * width, transcendentals=0
        ),
        name="turned_keys",
    )(pair, factors, basis, cosine, sine)


def fetch_kernel(source_ref, target_ref, sems):
    parts = sems.shape[0]
    span = source_ref.shape[0] // parts
    copies = []
    for part in range(parts):
        rows = pl.ds(part * span, span)
        copies.append(
            pltpu.make_async_copy(source_ref.at[rows, :], target_ref.at[rows, :], sems.at[part])
        )
        copies[-1].start()
    for copy in copies:
        copy.wait()


def fetch(weight, limit):
    return pl.pallas_call(
        fetch_kernel,
        in_specs=[whole(pl.ANY)],
        out_specs=whole(pl.ANY),
        out_shape=jax.ShapeDtypeStruct(weight.shape, weight.dtype),
        scratch_shapes=[pltpu.SemaphoreType.DMA((4,))],
        compiler_params=pltpu.CompilerParams(vmem_limit_bytes=limit * 2**20),
        cost_estimate=pl.CostEstimate(
            flops=0, bytes_accessed=2 * weight.size, transcendentals=0
        ),
        name="fetch_weight",
    )(weight)


def project_kernel(
    order, fast, me_ref, first_ref, second_ref, wq_ref, wk_ref, out_ref, *rest
):
    if fast:
        rows_ref, x_scr, lhs_scr, wq_buf, wk_buf, out_scr, sems, *asked_scr = rest
    else:
        x_scr, lhs_scr, wq_buf, wk_buf, out_scr, sems = rest
    depth, q_cols = wq_ref.shape
    k_cols = wk_ref.shape[1]
    chunks = wq_buf.shape[0]
    span = depth // chunks
    pieces = depth // LANES
    copies = []
    for i in range(chunks):
        rows = pl.ds(i * span, span)
        pair = (
            pltpu.make_async_copy(wq_ref.at[rows, :], wq_buf.at[i], sems.at[0, i]),
            pltpu.make_async_copy(wk_ref.at[rows, :], wk_buf.at[i], sems.at[1, i]),
        )
        for copy in pair:
            copy.start()
        copies.append(pair)
    half = first_ref.shape[0]
    count = 2 * half * STEPS
    rows = STEPS * pieces
    for j in range(2 * half):
        source = first_ref if j < half else second_ref
        x_scr[j * rows : (j + 1) * rows] = source[j % half, :rows, :].astype(F32)
    if fast:
        table_scr, table_smem, table_sem = asked_scr
        for j in range(2 * half):
            source = first_ref if j < half else second_ref
            asked = source[j % half, rows:, :].astype(F32)
            table_scr[2 * j : 2 * j + 2, :] = asked[:2].astype(jnp.int32)
        table_copy = pltpu.make_async_copy(table_scr, table_smem, table_sem)
        table_copy.start()
    for c in range(pieces):
        part = x_scr[pl.ds(c, count, stride=pieces), :]
        lhs_scr[:, c * LANES : (c + 1) * LANES] = part.astype(BF16)
    q_sum = jnp.zeros((count, q_cols), F32)
    k_sum = jnp.zeros((count, k_cols), F32)
    for i in range(chunks):
        for copy in copies[i]:
            copy.wait()
        lhs = lhs_scr[:, i * span : (i + 1) * span]
        q_sum = q_sum + jnp.dot(lhs, wq_buf[i], preferred_element_type=F32)
        k_sum = k_sum + jnp.dot(lhs, wk_buf[i], preferred_element_type=F32)
    if not fast:
        out_ref[:, :q_cols] = q_sum.astype(BF16)
        out_ref[:, q_cols:] = k_sum.astype(BF16)
        return
    me = me_ref[0]
    per = q_cols // LANES
    out_scr[...] = jnp.zeros_like(out_scr)
    for j in range(2 * half):
        place = origin(me, order, j)
        for step in range(STEPS):
            row = j * STEPS + step
            for c in range(per):
                out_scr[place, step * per + c : step * per + c + 1, :] = q_sum[
                    row : row + 1, c * LANES : (c + 1) * LANES
                ]
            out_scr[place, STEPS * per + step : STEPS * per + step + 1, :] = k_sum[
                row : row + 1, :
            ]
    out_ref[...] = out_scr[...].astype(BF16)
    table_copy.wait()
    plane = jnp.bitwise_and(me, -PLANE)
    for j in range(2 * half):
        place = origin(me, order, j) * (2 * PLANE)
        for k in range(2):
            for b in range(PLANE):
                rows_ref[place + k * PLANE + b] = table_smem[2 * j + k, plane + b]


def project(me, first, second, query_weight, kv_weight, order, fast):
    depth, q_cols = query_weight.shape
    k_cols = kv_weight.shape[1]
    pieces = depth // LANES
    devices = 2 * first.shape[0]
    rows = devices * STEPS
    chunks = 8
    span = depth // chunks
    shape = (devices, 16, LANES) if fast else (rows, q_cols + k_cols)
    return pl.pallas_call(
        functools.partial(project_kernel, order, fast),
        in_specs=[whole(SMEM), whole(), whole(), whole(pl.ANY), whole(pl.ANY)],
        out_specs=(whole(), whole(SMEM)) if fast else whole(),
        out_shape=(
            (
                jax.ShapeDtypeStruct(shape, BF16),
                jax.ShapeDtypeStruct((devices * 2 * PLANE,), jnp.int32),
            )
            if fast
            else jax.ShapeDtypeStruct(shape, BF16)
        ),
        scratch_shapes=[
            VMEM((rows * pieces, LANES), F32),
            VMEM((rows, depth), BF16),
            VMEM((chunks, span, q_cols), BF16),
            VMEM((chunks, span, k_cols), BF16),
            VMEM((devices, 16, LANES) if fast else (8, LANES), F32),
            pltpu.SemaphoreType.DMA((2, chunks)),
        ]
        + (
            [
                VMEM((2 * devices, LANES), jnp.int32),
                SMEM((2 * devices, LANES), jnp.int32),
                pltpu.SemaphoreType.DMA(()),
            ]
            if fast
            else []
        ),
        compiler_params=pltpu.CompilerParams(vmem_limit_bytes=PROJECT_LIMIT),
        cost_estimate=pl.CostEstimate(
            flops=2 * rows * depth * (q_cols + k_cols),
            bytes_accessed=2 * depth * (q_cols + k_cols),
            transcendentals=0,
        ),
        name="norm_project",
    )(me, first, second, query_weight, kv_weight)


def attend_kernel(fast, columns_ref, keys_ref, bias_ref, cos_ref, sin_ref, *rest):
    pages_ref, out_ref, out_scr = (None, *rest) if fast else rest
    score_scale = 1.0 / math.sqrt(HEAD_DIM)
    half = HEAD_DIM // 2
    rows = 2 * GROUP
    columns = columns_ref[...].astype(F32)
    count = columns.shape[0]
    query = columns[:, :8, :].reshape(count * 8, HEAD_DIM)
    fresh = columns[:, 8:, :]
    if fast:
        planes = count // PLANE
        out_scr[...] = jnp.zeros_like(out_scr)
    row_step = lax.rem(lax.broadcasted_iota(jnp.int32, (count * 8, 1), 0) // 4, STEPS)
    later = row_step == 1
    cosine = jnp.where(later, cos_ref[1:2, :], cos_ref[0:1, :])
    sine = jnp.where(later, sin_ref[1:2, :], sin_ref[0:1, :])
    turned = (query * cosine + pltpu.roll(query, half, 1) * sine).astype(BF16)
    turned_wide = turned.astype(F32)
    step_later = later[:rows]
    bias = jnp.where(step_later, bias_ref[1:2, :], bias_ref[0:1, :])
    new_keys = []
    for step in range(STEPS):
        part = fresh[:KV_HEADS, step, :]
        new = part * cos_ref[step : step + 1, :] + pltpu.roll(part, half, 1) * sin_ref[step : step + 1, :]
        new_keys.append(new.astype(BF16).astype(F32))
    for head in range(KV_HEADS):
        lanes = slice(head * HEAD_DIM, (head + 1) * HEAD_DIM)
        mine = slice(head * rows, (head + 1) * rows)
        scores = (
            lax.dot_general(
                turned[mine], keys_ref[:, lanes], (((1,), (1,)), ((), ())),
                preferred_element_type=F32,
            )
            * score_scale
            + bias
        )
        recent0 = (
            jnp.sum(turned_wide[mine] * new_keys[0][head : head + 1, :], axis=1, keepdims=True)
            * score_scale
        )
        recent1 = (
            jnp.sum(turned_wide[mine] * new_keys[1][head : head + 1, :], axis=1, keepdims=True)
            * score_scale
        )
        recent1 = jnp.where(step_later, recent1, -1e30)
        largest = jnp.maximum(
            jnp.max(scores, axis=1, keepdims=True), jnp.maximum(recent0, recent1)
        )
        cache_exp = jnp.exp(scores - largest)
        exp0 = jnp.exp(recent0 - largest)
        exp1 = jnp.exp(recent1 - largest)
        denominator = jnp.sum(cache_exp, axis=1, keepdims=True) + (exp0 + exp1)
        weights = (cache_exp / denominator).astype(BF16)
        weight0 = (exp0 / denominator).astype(BF16).astype(F32)
        weight1 = (exp1 / denominator).astype(BF16).astype(F32)
        recent = weight0 * fresh[KV_HEADS + head, 0:1, :]
        recent = recent + weight1 * fresh[KV_HEADS + head, 1:2, :]
        if not fast:
            values = pages_ref[:, :, lanes].reshape(keys_ref.shape[0], HEAD_DIM)
            mixed = jnp.dot(weights, values, preferred_element_type=F32)
            out_ref[mine, :] = (mixed + recent).astype(BF16)
            continue
        weights = weights.astype(F32)
        z, x = divmod(head, 2)
        for c in range(2):
            part = slice(c * 8, (c + 1) * 8)
            for plane in range(planes):
                out_scr[plane * PLANE + 2 * x + c, z * 8 : (z + 1) * 8, :] = weights[
                    part, plane * LANES : (plane + 1) * LANES
                ]
            out_scr[z * PLANE + 2 * x + c, planes * 8 : planes * 8 + 8, :] = recent[part]
    if fast:
        out_ref[...] = out_scr[...].astype(BF16)


def attend(columns, keys, bias, cosine, sine, pages, fast):
    seq, width = keys.shape
    count = columns.shape[0]
    if fast:
        shape = (count, count // PLANE * 8 + 16, LANES)
        scratch = [VMEM(shape, F32)]
        operands = (columns, keys, bias, cosine, sine)
    else:
        shape = (STEPS * HEADS, HEAD_DIM)
        scratch = [VMEM((8, LANES), F32)]
        operands = (columns, keys, bias, cosine, sine, pages)
    return pl.pallas_call(
        functools.partial(attend_kernel, fast),
        in_specs=[whole()] * len(operands),
        out_specs=whole(),
        out_shape=jax.ShapeDtypeStruct(shape, BF16),
        scratch_shapes=scratch,
        compiler_params=pltpu.CompilerParams(vmem_limit_bytes=48 * 2**20),
        cost_estimate=pl.CostEstimate(
            flops=4 * STEPS * HEADS * seq * HEAD_DIM,
            bytes_accessed=4 * seq * width,
            transcendentals=STEPS * HEADS * seq,
        ),
        name="attend",
    )(*operands)


def output_kernel(fast, count, me_ref, weight_ref, *rest):
    lhs_refs, rest = rest[:count], rest[count:]
    out_refs, (out_scr, heads_scr) = rest[:-2], rest[-2:]
    chunks = 8
    span = weight_ref.shape[1] // chunks
    rows = out_scr.shape[0] * LANES // (chunks * span)
    pieces = chunks * span // LANES
    if fast:
        per = heads_scr.shape[0] // rows
        total = lhs_refs[0][...].astype(F32)
        for lhs_ref in lhs_refs[1:]:
            total = total + lhs_ref[...].astype(F32)
        heads_scr[...] = total
        lhs = jnp.concatenate(
            [heads_scr[pl.ds(g, rows, stride=per), :].astype(BF16) for g in range(per)], axis=1
        )
    else:
        lhs = lhs_refs[0][...]
    for i in range(chunks):
        part = jnp.dot(
            lhs, weight_ref[:, i * span : (i + 1) * span], preferred_element_type=F32
        )
        for c in range(span // LANES):
            out_scr[pl.ds(i * (span // LANES) + c, rows, stride=pieces), :] = part[
                :, c * LANES : (c + 1) * LANES
            ]
    if not fast:
        out_refs[0][...] = out_scr[...].astype(BF16)
        return
    low = jnp.bitwise_and(me_ref[0], 1)
    for out_ref, core in zip(out_refs, (low, 1 - low)):
        count, size, _ = out_ref.shape
        for j in range(count):
            part = pl.ds(pl.multiple_of((2 * j + core) * size, size), size)
            out_ref[j] = out_scr[part, :].astype(BF16)


def output(me, lhs, weight, rows, fast):
    depth, width = weight.shape
    if fast:
        shape = (rows // (2 * STEPS), STEPS * width // LANES, LANES)
        shapes = (jax.ShapeDtypeStruct(shape, BF16),) * 2
    else:
        shapes = (jax.ShapeDtypeStruct((rows * width // LANES, LANES), BF16),)
    return pl.pallas_call(
        functools.partial(output_kernel, fast, len(lhs)),
        in_specs=[whole(SMEM)] + [whole()] * (1 + len(lhs)),
        out_specs=(whole(),) * len(shapes),
        out_shape=shapes,
        scratch_shapes=[
            VMEM((rows * width // LANES, LANES), F32),
            VMEM(lhs[0].shape if fast else (8, LANES), F32),
        ],
        compiler_params=pltpu.CompilerParams(vmem_limit_bytes=24 * 2**20),
        cost_estimate=pl.CostEstimate(
            flops=2 * rows * depth * width, bytes_accessed=2 * depth * width, transcendentals=0
        ),
        name="output_project",
    )(me, weight, *lhs)


def swap(block, bit, devices):
    return lax.ppermute(block, AXIS, [(i, i ^ bit) for i in range(devices)])


def exchange(blocks, groups=None):
    return lax.all_to_all(
        blocks, AXIS, split_axis=0, concat_axis=0, tiled=True, axis_index_groups=groups
    )


def local(
    hidden,
    norm_gain,
    query_weight,
    kv_weight,
    out_weight,
    key_factors,
    key_basis,
    value_store,
    lengths,
    block_slot,
    selection,
):
    devices = lax.axis_size(AXIS)
    me = lax.axis_index(AXIS)
    slots_dev, block_len, width = value_store.shape
    seq = key_factors.shape[1]
    pages = block_slot.shape[1]
    model = hidden.shape[2]
    q_cols = query_weight.shape[1]
    k_cols = kv_weight.shape[1]
    fast = devices == 2 * PAIRS and q_cols == 4 * HEAD_DIM and k_cols == HEAD_DIM
    pieces = model // LANES

    me_word = me.astype(jnp.int32).reshape(1)
    block, holder, pair = prepare(
        hidden[:, 0], norm_gain.reshape(pieces, LANES), block_slot, slots_dev, PAIRS if fast else 1
    )
    if fast:
        same_core = [list(range(core, devices, 2)) for core in range(2)]
        block = exchange(block, same_core)
        block, kv_weight = lax.optimization_barrier((block, kv_weight))
        kv_weight = fetch(kv_weight, 50)
        other = swap(block, 1, devices)
        order = None
        x = lax.bitwise_and(lax.shift_right_logical(me_word, 1), 1)
        keep, send = split_values(x, value_store)
        neighbour = swap(send, 2, devices)
    else:
        order = [0]
        bit = devices // 2
        while bit:
            other = swap(block, bit, devices)
            order = order + [k ^ bit for k in order]
            bit //= 2
            if bit:
                block = jnp.concatenate([block, other], axis=0)
        order = tuple(order)
    span = 2 * block_len
    places = (pair[:, None] * span + jnp.arange(span, dtype=jnp.int32)[None, :]).reshape(-1)
    if not fast:
        sent_pages = pick_pages(me_word, block, other, value_store, order)
        block, other, sent_pages = lax.optimization_barrier((block, other, sent_pages))
        fetched = exchange(sent_pages)
    projected = project(
        me_word, block, other, query_weight, kv_weight, order, fast
    )
    if fast:
        projected, rows = projected
        projected, places = lax.optimization_barrier((projected, places))
        columns = exchange(projected)
    else:
        targets = jnp.bitwise_xor(me, jnp.array(order, dtype=jnp.int32))
        columns = exchange(projected.reshape(devices, STEPS, q_cols + k_cols)[targets])
        query = columns[:, :, :q_cols].transpose(1, 0, 2).reshape(STEPS, HEADS // 4, 4, HEAD_DIM)
        query = query.transpose(1, 0, 2, 3).reshape(HEADS // 4, 8, HEAD_DIM)
        fresh = columns[:, :, q_cols:].transpose(1, 0, 2).reshape(STEPS, HEADS // 4, HEAD_DIM)
        fresh = jnp.pad(fresh.transpose(1, 0, 2), ((0, 0), (0, 8 - STEPS), (0, 0)))
        columns = jnp.concatenate([query, fresh], axis=1)

    cosine, sine = turn_tables(places.astype(F32))
    keys = make_keys(pair, key_factors[0], key_basis[0], cosine, sine)
    picked = jnp.any(
        selection[:, 0, :, None] == (places // block_len)[None, None, :], axis=1
    )
    bias = jnp.where(picked & (places < lengths[0])[None, :], 0.0, -1e30).astype(F32)
    new_cos, new_sin = turn_tables(
        (lengths[0] + jnp.arange(STEPS, dtype=jnp.int32)).astype(F32)
    )
    if fast:
        blocks = attend(columns, keys, bias, new_cos, new_sin, None, True)
        blocks, neighbour = lax.optimization_barrier((blocks, neighbour))
        stores = (keep, swap(keep, 1, devices), neighbour, swap(neighbour, 1, devices))
        blocks = exchange(blocks)
        parts = mix(me_word, rows, blocks, stores)
        (*parts, out_weight) = lax.optimization_barrier((*parts, out_weight))
        out_weight = fetch(out_weight, 43)
        lhs = [parts[0]] + [swap(parts[q], q * PLANE, devices) for q in range(1, len(parts))]
    else:
        heads = attend(columns, keys, bias, new_cos, new_sin, fetched, False)
        flat = heads.reshape(HEADS // 4, STEPS, 4 * HEAD_DIM).transpose(1, 0, 2)
        flat = flat.reshape(STEPS, devices, model // devices).transpose(1, 0, 2)
        lhs = [exchange(flat).reshape(devices * STEPS, model // devices)]
    partial = output(me_word, lhs, out_weight, devices * STEPS, fast)
    if fast:
        near, far = partial
        both = near.astype(F32) + swap(far, 1, devices).astype(F32)
        arrived = exchange(both.astype(BF16), same_core)
    else:
        arrived = exchange(partial[0].reshape(devices, STEPS * pieces, LANES))
    total = jnp.sum(arrived.astype(F32), axis=0).astype(BF16)
    return total.reshape(STEPS, 1, model)


def solution(mesh):
    return jax.shard_map(
        local,
        mesh=mesh,
        in_specs=(
            P(None, ("groups", "session"), None),
            P(),
            P(None, "session"),
            P(None, "session"),
            P("session", None),
            P(("groups", "session"), None, None),
            P(("groups", "session"), None, None),
            P(("groups", "session"), None, None),
            P(("groups", "session")),
            P(("groups", "session"), None),
            P(None, ("groups", "session"), None),
        ),
        out_specs=P(None, ("groups", "session"), None),
        check_vma=False,
    )
```

```python
import functools
import math

import jax
import jax.numpy as jnp
from jax import lax
from jax.experimental import pallas as pl
from jax.experimental.pallas import tpu as pltpu
from jax.sharding import PartitionSpec as P

HEADS = 64
KV_HEADS = 8
HEAD_DIM = 128
STEPS = 2
GROUP = HEADS // KV_HEADS
LANES = 128
EXTRA = 16
PLANE = 4
PAIRS = 8
PROJECT_LIMIT = 48 * 2**20
AXIS = "session"
VMEM = pltpu.VMEM
SMEM = pltpu.SMEM
F32 = jnp.float32
BF16 = jnp.bfloat16


def angles(positions):
    half = HEAD_DIM // 2
    frequency = jnp.exp(
        -jnp.arange(half, dtype=F32) * (2.0 * math.log(500000.0) / HEAD_DIM)
    )
    return positions[..., None] * frequency


def turn_tables(positions):
    angle = angles(positions)
    cosine, sine = jnp.cos(angle), jnp.sin(angle)
    return (
        jnp.concatenate([cosine, cosine], axis=-1),
        jnp.concatenate([-sine, sine], axis=-1),
    )


def origin(me, order, j):
    if order is None:
        return 2 * (j % PAIRS) + jnp.bitwise_xor(jnp.bitwise_and(me, 1), j // PAIRS)
    return jnp.bitwise_xor(me, order[j])


def whole(space=VMEM):
    return pl.BlockSpec(memory_space=space)


def prepare_kernel(
    slots_dev, hidden_ref, gain_ref, slots_ref, block_ref, holder_ref, pair_ref, wide_scr
):
    steps, model = hidden_ref.shape
    pieces = model // LANES
    wide = hidden_ref[...].astype(F32)
    scale = lax.rsqrt(jnp.mean(wide * wide, axis=1, keepdims=True) + 1e-05)
    wide = wide * scale
    for step in range(steps):
        for c in range(pieces):
            row = step * pieces + c
            wide_scr[row : row + 1, :] = wide[step : step + 1, c * LANES : (c + 1) * LANES]
    lane = lax.broadcasted_iota(jnp.int32, (EXTRA, LANES), 1)
    parity = lax.broadcasted_iota(jnp.int32, (EXTRA, LANES), 0)
    table = jnp.zeros((EXTRA, LANES), jnp.int32)
    for m in range(holder_ref.shape[0]):
        slot = slots_ref[0, 2 * m]
        holder = lax.div(slot, slots_dev)
        holder_ref[m] = holder
        pair_ref[holder] = m
        base = holder * slots_dev
        pair = jnp.where(parity == 0, slot - base, slots_ref[0, 2 * m + 1] - base)
        table = jnp.where(lane == holder, pair, table)
    wide_scr[steps * pieces :, :] = table.astype(F32)
    gain = gain_ref[...].astype(F32)
    for step in range(steps):
        rows = slice(step * pieces, (step + 1) * pieces)
        wide_scr[rows, :] = wide_scr[rows, :] * gain
    block = wide_scr[...].astype(BF16)
    for copy in range(block_ref.shape[0]):
        block_ref[copy] = block


def prepare(hidden, gain, block_slot, slots_dev, copies):
    assert slots_dev <= 256
    steps, model = hidden.shape
    rows = steps * model // LANES + EXTRA
    return pl.pallas_call(
        functools.partial(prepare_kernel, slots_dev),
        in_specs=[whole(), whole(), whole(SMEM)],
        out_specs=(whole(), whole(SMEM), whole(SMEM)),
        out_shape=(
            jax.ShapeDtypeStruct((copies, rows, LANES), BF16),
            jax.ShapeDtypeStruct((block_slot.shape[1] // 2,), jnp.int32),
            jax.ShapeDtypeStruct((block_slot.shape[1] // 2,), jnp.int32),
        ),
        scratch_shapes=[VMEM((rows, LANES), F32)],
        name="prepare",
    )(hidden, gain, block_slot)


def pick_kernel(order, me_ref, first_ref, second_ref, store_ref, out_ref, table_scr, table_smem, sem):
    block_len = store_ref.shape[1]
    half, rows, _ = first_ref.shape
    for j in range(2 * half):
        source = first_ref if j < half else second_ref
        asked = source[j % half, rows - EXTRA :, :].astype(F32)
        table_scr[j] = asked[:8].astype(jnp.int32)
    copy = pltpu.make_async_copy(table_scr, table_smem, sem)
    copy.start()
    copy.wait()
    me = me_ref[0]
    for j in range(2 * half):
        target = origin(me, order, j)
        for k in range(2):
            out_ref[target, k * block_len : (k + 1) * block_len, :] = store_ref[
                table_smem[j, k, me]
            ]


def pick_pages(me, first, second, store, order):
    count = 2 * first.shape[0]
    _, block_len, width = store.shape
    return pl.pallas_call(
        functools.partial(pick_kernel, order),
        in_specs=[whole(SMEM), whole(), whole(), whole()],
        out_specs=whole(),
        out_shape=jax.ShapeDtypeStruct((count, 2 * block_len, width), store.dtype),
        scratch_shapes=[
            VMEM((count, 8, LANES), jnp.int32),
            SMEM((count, 8, LANES), jnp.int32),
            pltpu.SemaphoreType.DMA(()),
        ],
        compiler_params=pltpu.CompilerParams(vmem_limit_bytes=36 * 2**20),
        name="pick_pages",
    )(me, first, second, store)


def split_kernel(x_ref, store_ref, keep_ref, send_ref):
    slots, block_len, width = store_ref.shape
    for x in range(2):

        @pl.when(x_ref[0] == x)
        def _():
            for head in range(width // LANES):
                target = keep_ref if head % 2 == x else send_ref
                lanes = slice(head // 2 * LANES, (head // 2 + 1) * LANES)
                part = store_ref[:, :, head * LANES : (head + 1) * LANES]
                target[:, lanes] = part.reshape(slots * block_len, LANES)


def split_values(x, store):
    slots, block_len, width = store.shape
    half = jax.ShapeDtypeStruct((slots * block_len, width // 2), store.dtype)
    return pl.pallas_call(
        split_kernel,
        in_specs=[whole(SMEM), whole()],
        out_specs=(whole(), whole()),
        out_shape=(half, half),
        compiler_params=pltpu.CompilerParams(vmem_limit_bytes=16 * 2**20),
        name="split_values",
    )(x, store)


def mix_kernel(me_ref, rows_ref, weights_ref, matrix_ref, *rest):
    stores, (head_ref, values_scr, sum_scr, sem) = rest[:PLANE], rest[-4:]
    out_refs = rest[PLANE:-4]
    columns = pl.ds(0, head_ref.shape[1])
    copy = pltpu.make_async_copy(matrix_ref.at[:, columns], head_ref, sem)
    copy.start()
    me = me_ref[0]
    low = jnp.bitwise_and(me, PLANE - 1)
    z_me = lax.div(me, PLANE)
    sessions = weights_ref.shape[0]
    planes = len(out_refs)
    block_len = values_scr.shape[1] // (2 * PLANE)
    for session in range(sessions):
        for q, store in enumerate(stores):
            device = jnp.bitwise_xor(low, q)
            for k in range(2):
                row = rows_ref[session * (2 * PLANE) + k * PLANE + device]
                source = pl.ds(pl.multiple_of(row * block_len, block_len), block_len)
                target = pl.ds(
                    pl.multiple_of((device * 2 + k) * block_len, block_len), block_len
                )
                values_scr[session, target, :] = store[source, :]
        block = weights_ref[session]
        product = jnp.dot(
            block[: planes * 8], values_scr[session], preferred_element_type=F32
        )
        mine = slice(session * 8, (session + 1) * 8)
        for z in range(planes):
            sum_scr[z, mine, :] = product[z * 8 : (z + 1) * 8, z * LANES : (z + 1) * LANES]
        recent = block[planes * 8 :].astype(F32)
        sum_scr[z_me, mine, :] += recent[:8]
    for q, out_ref in enumerate(out_refs):
        out_ref[...] = sum_scr[jnp.bitwise_xor(z_me, q)].astype(BF16)
    copy.wait()


def mix(me, rows, weights, matrix, stores):
    sessions = weights.shape[0]
    planes = stores[0].shape[1] // LANES
    shape = (planes, sessions * 8, LANES)
    head = jax.ShapeDtypeStruct((matrix.shape[0], matrix.shape[1] // 4), matrix.dtype)
    return pl.pallas_call(
        mix_kernel,
        in_specs=[whole(SMEM)] * 2 + [whole(), whole(pl.ANY)] + [whole()] * PLANE,
        out_specs=(whole(),) * planes + (whole(pl.ANY),),
        out_shape=(jax.ShapeDtypeStruct(shape[1:], BF16),) * planes + (head,),
        scratch_shapes=[
            VMEM((sessions, LANES, planes * LANES), BF16),
            VMEM(shape, F32),
            pltpu.SemaphoreType.DMA(()),
        ],
        compiler_params=pltpu.CompilerParams(vmem_limit_bytes=46 * 2**20),
        cost_estimate=pl.CostEstimate(
            flops=2 * sessions * 32 * LANES * planes * LANES,
            bytes_accessed=4 * stores[0].size * PLANE,
            transcendentals=0,
        ),
        name="mix_values",
    )(me, rows, weights, matrix, *stores)


def keys_kernel(pair_ref, factors_ref, basis_ref, cos_ref, sin_ref, out_ref, rows_scr):
    span = factors_ref.shape[0] // pair_ref.shape[0]
    count = rows_scr.shape[0] // span
    base = pl.program_id(0) * count
    for p in range(count):
        source = pl.ds(pl.multiple_of(pair_ref[base + p] * span, span), span)
        rows_scr[p * span : (p + 1) * span, :] = factors_ref[source, :]
    product = jnp.dot(rows_scr[...], basis_ref[...], preferred_element_type=F32)
    cosine, sine = cos_ref[...], sin_ref[...]
    for head in range(KV_HEADS):
        lanes = slice(head * HEAD_DIM, (head + 1) * HEAD_DIM)
        part = product[:, lanes]
        turned = part * cosine + pltpu.roll(part, HEAD_DIM // 2, 1) * sine
        out_ref[:, lanes] = turned.astype(BF16)


def make_keys(pair, factors, basis, cosine, sine):
    seq, rank = factors.shape
    width = basis.shape[1]
    rows = min(seq, 512)
    return pl.pallas_call(
        keys_kernel,
        grid=(seq // rows,),
        in_specs=[
            whole(SMEM),
            pl.BlockSpec((seq, rank), lambda i: (0, 0)),
            pl.BlockSpec((rank, width), lambda i: (0, 0)),
            pl.BlockSpec((rows, HEAD_DIM), lambda i: (i, 0)),
            pl.BlockSpec((rows, HEAD_DIM), lambda i: (i, 0)),
        ],
        out_specs=pl.BlockSpec((rows, width), lambda i: (i, 0)),
        out_shape=jax.ShapeDtypeStruct((seq, width), BF16),
        scratch_shapes=[VMEM((rows, rank), BF16)],
        compiler_params=pltpu.CompilerParams(vmem_limit_bytes=32 * 2**20),
        cost_estimate=pl.CostEstimate(
            flops=2 * seq * rank * width, bytes_accessed=4 * seq * width, transcendentals=0
        ),
        name="turned_keys",
    )(pair, factors, basis, cosine, sine)


def fetch_kernel(source_ref, target_ref, sems):
    parts = sems.shape[0]
    rows, width = target_ref.shape
    columns = pl.ds(source_ref.shape[1] - width, width)
    copies = []
    for part in range(parts):
        mine = pl.ds(part * (rows // parts), rows // parts)
        copies.append(
            pltpu.make_async_copy(
                source_ref.at[mine, columns], target_ref.at[mine, :], sems.at[part]
            )
        )
        copies[-1].start()
    for copy in copies:
        copy.wait()


def fetch(weight, limit, width):
    return pl.pallas_call(
        fetch_kernel,
        in_specs=[whole(pl.ANY)],
        out_specs=whole(pl.ANY),
        out_shape=jax.ShapeDtypeStruct((weight.shape[0], width), weight.dtype),
        scratch_shapes=[pltpu.SemaphoreType.DMA((4,))],
        compiler_params=pltpu.CompilerParams(vmem_limit_bytes=limit * 2**20),
        cost_estimate=pl.CostEstimate(
            flops=0, bytes_accessed=2 * weight.shape[0] * width, transcendentals=0
        ),
        name="fetch_weight",
    )(weight)


def project_kernel(
    order, fast, me_ref, first_ref, second_ref, wq_ref, wk_ref, out_ref, *rest
):
    if fast:
        rows_ref, x_scr, lhs_scr, wq_buf, out_scr, sems, *asked_scr = rest
    else:
        x_scr, lhs_scr, wq_buf, out_scr, sems = rest
    depth, q_cols = wq_ref.shape
    k_cols = wk_ref.shape[1]
    chunks = wq_buf.shape[0]
    span = depth // chunks
    pieces = depth // LANES
    copies = []
    for i in range(chunks):
        rows = pl.ds(i * span, span)
        copies.append(pltpu.make_async_copy(wq_ref.at[rows, :], wq_buf.at[i], sems.at[i]))
        copies[-1].start()
    half = first_ref.shape[0]
    count = 2 * half * STEPS
    rows = STEPS * pieces
    for j in range(2 * half):
        source = first_ref if j < half else second_ref
        x_scr[j * rows : (j + 1) * rows] = source[j % half, :rows, :].astype(F32)
    if fast:
        table_scr, table_smem, table_sem = asked_scr
        for j in range(2 * half):
            source = first_ref if j < half else second_ref
            asked = source[j % half, rows:, :].astype(F32)
            table_scr[2 * j : 2 * j + 2, :] = asked[:2].astype(jnp.int32)
        table_copy = pltpu.make_async_copy(table_scr, table_smem, table_sem)
        table_copy.start()
    for c in range(pieces):
        part = x_scr[pl.ds(c, count, stride=pieces), :]
        lhs_scr[:, c * LANES : (c + 1) * LANES] = part.astype(BF16)
    q_sum = jnp.zeros((count, q_cols), F32)
    k_sum = jnp.zeros((count, k_cols), F32)
    for i in range(chunks):
        copies[i].wait()
        lhs = lhs_scr[:, i * span : (i + 1) * span]
        q_sum = q_sum + jnp.dot(lhs, wq_buf[i], preferred_element_type=F32)
        k_sum = k_sum + jnp.dot(
            lhs, wk_ref[i * span : (i + 1) * span, :], preferred_element_type=F32
        )
    if not fast:
        out_ref[:, :q_cols] = q_sum.astype(BF16)
        out_ref[:, q_cols:] = k_sum.astype(BF16)
        return
    me = me_ref[0]
    per = q_cols // LANES
    out_scr[...] = jnp.zeros_like(out_scr)
    for j in range(2 * half):
        place = origin(me, order, j)
        for step in range(STEPS):
            row = j * STEPS + step
            for c in range(per):
                out_scr[place, step * per + c : step * per + c + 1, :] = q_sum[
                    row : row + 1, c * LANES : (c + 1) * LANES
                ]
            out_scr[place, STEPS * per + step : STEPS * per + step + 1, :] = k_sum[
                row : row + 1, :
            ]
    out_ref[...] = out_scr[...].astype(BF16)
    table_copy.wait()
    plane = jnp.bitwise_and(me, -PLANE)
    for j in range(2 * half):
        place = origin(me, order, j) * (2 * PLANE)
        for k in range(2):
            for b in range(PLANE):
                rows_ref[place + k * PLANE + b] = table_smem[2 * j + k, plane + b]


def project(me, first, second, query_weight, kv_weight, order, fast):
    depth, q_cols = query_weight.shape
    k_cols = kv_weight.shape[1]
    pieces = depth // LANES
    devices = 2 * first.shape[0]
    rows = devices * STEPS
    chunks = 8
    span = depth // chunks
    shape = (devices, 16, LANES) if fast else (rows, q_cols + k_cols)
    return pl.pallas_call(
        functools.partial(project_kernel, order, fast),
        in_specs=[whole(SMEM), whole(), whole(), whole(pl.ANY), whole()],
        out_specs=(whole(), whole(SMEM)) if fast else whole(),
        out_shape=(
            (
                jax.ShapeDtypeStruct(shape, BF16),
                jax.ShapeDtypeStruct((devices * 2 * PLANE,), jnp.int32),
            )
            if fast
            else jax.ShapeDtypeStruct(shape, BF16)
        ),
        scratch_shapes=[
            VMEM((rows * pieces, LANES), F32),
            VMEM((rows, depth), BF16),
            VMEM((chunks, span, q_cols), BF16),
            VMEM((devices, 16, LANES) if fast else (8, LANES), F32),
            pltpu.SemaphoreType.DMA((chunks,)),
        ]
        + (
            [
                VMEM((2 * devices, LANES), jnp.int32),
                SMEM((2 * devices, LANES), jnp.int32),
                pltpu.SemaphoreType.DMA(()),
            ]
            if fast
            else []
        ),
        compiler_params=pltpu.CompilerParams(vmem_limit_bytes=PROJECT_LIMIT),
        cost_estimate=pl.CostEstimate(
            flops=2 * rows * depth * (q_cols + k_cols),
            bytes_accessed=2 * depth * (q_cols + k_cols),
            transcendentals=0,
        ),
        name="norm_project",
    )(me, first, second, query_weight, kv_weight)


def attend_kernel(fast, columns_ref, keys_ref, bias_ref, cos_ref, sin_ref, *rest):
    pages_ref, out_ref, out_scr = (None, *rest) if fast else rest
    score_scale = 1.0 / math.sqrt(HEAD_DIM)
    half = HEAD_DIM // 2
    rows = 2 * GROUP
    columns = columns_ref[...].astype(F32)
    count = columns.shape[0]
    query = columns[:, :8, :].reshape(count * 8, HEAD_DIM)
    fresh = columns[:, 8:, :]
    if fast:
        planes = count // PLANE
        out_scr[...] = jnp.zeros_like(out_scr)
    row_step = lax.rem(lax.broadcasted_iota(jnp.int32, (count * 8, 1), 0) // 4, STEPS)
    later = row_step == 1
    cosine = jnp.where(later, cos_ref[1:2, :], cos_ref[0:1, :])
    sine = jnp.where(later, sin_ref[1:2, :], sin_ref[0:1, :])
    turned = (query * cosine + pltpu.roll(query, half, 1) * sine).astype(BF16)
    turned_wide = turned.astype(F32)
    step_later = later[:rows]
    bias = jnp.where(step_later, bias_ref[1:2, :], bias_ref[0:1, :])
    new_keys = []
    for step in range(STEPS):
        part = fresh[:KV_HEADS, step, :]
        new = part * cos_ref[step : step + 1, :] + pltpu.roll(part, half, 1) * sin_ref[step : step + 1, :]
        new_keys.append(new.astype(BF16).astype(F32))
    for head in range(KV_HEADS):
        lanes = slice(head * HEAD_DIM, (head + 1) * HEAD_DIM)
        mine = slice(head * rows, (head + 1) * rows)
        scores = (
            lax.dot_general(
                turned[mine], keys_ref[:, lanes], (((1,), (1,)), ((), ())),
                preferred_element_type=F32,
            )
            * score_scale
            + bias
        )
        recent0 = (
            jnp.sum(turned_wide[mine] * new_keys[0][head : head + 1, :], axis=1, keepdims=True)
            * score_scale
        )
        recent1 = (
            jnp.sum(turned_wide[mine] * new_keys[1][head : head + 1, :], axis=1, keepdims=True)
            * score_scale
        )
        recent1 = jnp.where(step_later, recent1, -1e30)
        largest = jnp.maximum(
            jnp.max(scores, axis=1, keepdims=True), jnp.maximum(recent0, recent1)
        )
        cache_exp = jnp.exp(scores - largest)
        exp0 = jnp.exp(recent0 - largest)
        exp1 = jnp.exp(recent1 - largest)
        denominator = jnp.sum(cache_exp, axis=1, keepdims=True) + (exp0 + exp1)
        weights = (cache_exp / denominator).astype(BF16)
        weight0 = (exp0 / denominator).astype(BF16).astype(F32)
        weight1 = (exp1 / denominator).astype(BF16).astype(F32)
        recent = weight0 * fresh[KV_HEADS + head, 0:1, :]
        recent = recent + weight1 * fresh[KV_HEADS + head, 1:2, :]
        if not fast:
            values = pages_ref[:, :, lanes].reshape(keys_ref.shape[0], HEAD_DIM)
            mixed = jnp.dot(weights, values, preferred_element_type=F32)
            out_ref[mine, :] = (mixed + recent).astype(BF16)
            continue
        weights = weights.astype(F32)
        z, x = divmod(head, 2)
        for c in range(2):
            part = slice(c * 8, (c + 1) * 8)
            for plane in range(planes):
                out_scr[plane * PLANE + 2 * x + c, z * 8 : (z + 1) * 8, :] = weights[
                    part, plane * LANES : (plane + 1) * LANES
                ]
            out_scr[z * PLANE + 2 * x + c, planes * 8 : planes * 8 + 8, :] = recent[part]
    if fast:
        out_ref[...] = out_scr[...].astype(BF16)


def attend(columns, keys, bias, cosine, sine, pages, fast):
    seq, width = keys.shape
    count = columns.shape[0]
    if fast:
        shape = (count, count // PLANE * 8 + 16, LANES)
        scratch = [VMEM(shape, F32)]
        operands = (columns, keys, bias, cosine, sine)
    else:
        shape = (STEPS * HEADS, HEAD_DIM)
        scratch = [VMEM((8, LANES), F32)]
        operands = (columns, keys, bias, cosine, sine, pages)
    return pl.pallas_call(
        functools.partial(attend_kernel, fast),
        in_specs=[whole()] * len(operands),
        out_specs=whole(),
        out_shape=jax.ShapeDtypeStruct(shape, BF16),
        scratch_shapes=scratch,
        compiler_params=pltpu.CompilerParams(vmem_limit_bytes=48 * 2**20),
        cost_estimate=pl.CostEstimate(
            flops=4 * STEPS * HEADS * seq * HEAD_DIM,
            bytes_accessed=4 * seq * width,
            transcendentals=STEPS * HEADS * seq,
        ),
        name="attend",
    )(*operands)


def output_kernel(fast, count, parts, me_ref, *rest):
    lhs_refs, weight_refs, rest = rest[:count], rest[count : count + parts], rest[count + parts :]
    out_refs, (out_scr, heads_scr) = rest[:-2], rest[-2:]
    chunks = 8
    span = sum(weight_ref.shape[1] for weight_ref in weight_refs) // chunks
    places = [(w, c) for w in weight_refs for c in range(0, w.shape[1], span)]
    rows = out_scr.shape[0] * LANES // (chunks * span)
    pieces = chunks * span // LANES
    if fast:
        per = heads_scr.shape[0] // rows
        total = lhs_refs[0][...].astype(F32)
        for lhs_ref in lhs_refs[1:]:
            total = total + lhs_ref[...].astype(F32)
        heads_scr[...] = total
        lhs = jnp.concatenate(
            [heads_scr[pl.ds(g, rows, stride=per), :].astype(BF16) for g in range(per)], axis=1
        )
    else:
        lhs = lhs_refs[0][...]
    for i in range(chunks):
        weight_ref, first = places[i]
        part = jnp.dot(lhs, weight_ref[:, first : first + span], preferred_element_type=F32)
        for c in range(span // LANES):
            out_scr[pl.ds(i * (span // LANES) + c, rows, stride=pieces), :] = part[
                :, c * LANES : (c + 1) * LANES
            ]
    if not fast:
        out_refs[0][...] = out_scr[...].astype(BF16)
        return
    low = jnp.bitwise_and(me_ref[0], 1)
    for out_ref, core in zip(out_refs, (low, 1 - low)):
        count, size, _ = out_ref.shape
        for j in range(count):
            part = pl.ds(pl.multiple_of((2 * j + core) * size, size), size)
            out_ref[j] = out_scr[part, :].astype(BF16)


def output(me, lhs, weights, rows, fast):
    depth = weights[0].shape[0]
    width = sum(weight.shape[1] for weight in weights)
    if fast:
        shape = (rows // (2 * STEPS), STEPS * width // LANES, LANES)
        shapes = (jax.ShapeDtypeStruct(shape, BF16),) * 2
    else:
        shapes = (jax.ShapeDtypeStruct((rows * width // LANES, LANES), BF16),)
    return pl.pallas_call(
        functools.partial(output_kernel, fast, len(lhs), len(weights)),
        in_specs=[whole(SMEM)] + [whole()] * (len(weights) + len(lhs)),
        out_specs=(whole(),) * len(shapes),
        out_shape=shapes,
        scratch_shapes=[
            VMEM((rows * width // LANES, LANES), F32),
            VMEM(lhs[0].shape if fast else (8, LANES), F32),
        ],
        compiler_params=pltpu.CompilerParams(vmem_limit_bytes=24 * 2**20),
        cost_estimate=pl.CostEstimate(
            flops=2 * rows * depth * width, bytes_accessed=2 * depth * width, transcendentals=0
        ),
        name="output_project",
    )(me, *lhs, *weights)


def swap(block, bit, devices):
    return lax.ppermute(block, AXIS, [(i, i ^ bit) for i in range(devices)])


def exchange(blocks, groups=None):
    return lax.all_to_all(
        blocks, AXIS, split_axis=0, concat_axis=0, tiled=True, axis_index_groups=groups
    )


def local(
    hidden,
    norm_gain,
    query_weight,
    kv_weight,
    out_weight,
    key_factors,
    key_basis,
    value_store,
    lengths,
    block_slot,
    selection,
):
    devices = lax.axis_size(AXIS)
    me = lax.axis_index(AXIS)
    slots_dev, block_len, width = value_store.shape
    seq = key_factors.shape[1]
    pages = block_slot.shape[1]
    model = hidden.shape[2]
    q_cols = query_weight.shape[1]
    k_cols = kv_weight.shape[1]
    fast = devices == 2 * PAIRS and q_cols == 4 * HEAD_DIM and k_cols == HEAD_DIM
    pieces = model // LANES

    me_word = me.astype(jnp.int32).reshape(1)
    block, holder, pair = prepare(
        hidden[:, 0], norm_gain.reshape(pieces, LANES), block_slot, slots_dev, PAIRS if fast else 1
    )
    if fast:
        same_core = [list(range(core, devices, 2)) for core in range(2)]
        block = exchange(block, same_core)
        block, kv_weight = lax.optimization_barrier((block, kv_weight))
        kv_weight = fetch(kv_weight, 50, k_cols)
        other = swap(block, 1, devices)
        order = None
        x = lax.bitwise_and(lax.shift_right_logical(me_word, 1), 1)
        keep, send = split_values(x, value_store)
        neighbour = swap(send, 2, devices)
    else:
        order = [0]
        bit = devices // 2
        while bit:
            other = swap(block, bit, devices)
            order = order + [k ^ bit for k in order]
            bit //= 2
            if bit:
                block = jnp.concatenate([block, other], axis=0)
        order = tuple(order)
    span = 2 * block_len
    places = (pair[:, None] * span + jnp.arange(span, dtype=jnp.int32)[None, :]).reshape(-1)
    if not fast:
        sent_pages = pick_pages(me_word, block, other, value_store, order)
        block, other, sent_pages = lax.optimization_barrier((block, other, sent_pages))
        fetched = exchange(sent_pages)
    projected = project(
        me_word, block, other, query_weight, kv_weight, order, fast
    )
    if fast:
        projected, rows = projected
        projected, places = lax.optimization_barrier((projected, places))
        columns = exchange(projected)
    else:
        targets = jnp.bitwise_xor(me, jnp.array(order, dtype=jnp.int32))
        columns = exchange(projected.reshape(devices, STEPS, q_cols + k_cols)[targets])
        query = columns[:, :, :q_cols].transpose(1, 0, 2).reshape(STEPS, HEADS // 4, 4, HEAD_DIM)
        query = query.transpose(1, 0, 2, 3).reshape(HEADS // 4, 8, HEAD_DIM)
        fresh = columns[:, :, q_cols:].transpose(1, 0, 2).reshape(STEPS, HEADS // 4, HEAD_DIM)
        fresh = jnp.pad(fresh.transpose(1, 0, 2), ((0, 0), (0, 8 - STEPS), (0, 0)))
        columns = jnp.concatenate([query, fresh], axis=1)

    cosine, sine = turn_tables(places.astype(F32))
    keys = make_keys(pair, key_factors[0], key_basis[0], cosine, sine)
    picked = jnp.any(
        selection[:, 0, :, None] == (places // block_len)[None, None, :], axis=1
    )
    bias = jnp.where(picked & (places < lengths[0])[None, :], 0.0, -1e30).astype(F32)
    new_cos, new_sin = turn_tables(
        (lengths[0] + jnp.arange(STEPS, dtype=jnp.int32)).astype(F32)
    )
    if fast:
        blocks = attend(columns, keys, bias, new_cos, new_sin, None, True)
        blocks, neighbour = lax.optimization_barrier((blocks, neighbour))
        stores = (keep, swap(keep, 1, devices), neighbour, swap(neighbour, 1, devices))
        blocks = exchange(blocks)
        (*parts, first_weight) = mix(me_word, rows, blocks, out_weight, stores)
        (*parts, out_weight) = lax.optimization_barrier((*parts, out_weight))
        out_weight = [first_weight, fetch(out_weight, 43, model - first_weight.shape[1])]
        lhs = [parts[0]] + [swap(parts[q], q * PLANE, devices) for q in range(1, len(parts))]
    else:
        heads = attend(columns, keys, bias, new_cos, new_sin, fetched, False)
        flat = heads.reshape(HEADS // 4, STEPS, 4 * HEAD_DIM).transpose(1, 0, 2)
        flat = flat.reshape(STEPS, devices, model // devices).transpose(1, 0, 2)
        lhs = [exchange(flat).reshape(devices * STEPS, model // devices)]
        out_weight = [out_weight]
    partial = output(me_word, lhs, out_weight, devices * STEPS, fast)
    if fast:
        near, far = partial
        both = near.astype(F32) + swap(far, 1, devices).astype(F32)
        arrived = exchange(both.astype(BF16), same_core)
    else:
        arrived = exchange(partial[0].reshape(devices, STEPS * pieces, LANES))
    total = jnp.sum(arrived.astype(F32), axis=0).astype(BF16)
    return total.reshape(STEPS, 1, model)


def solution(mesh):
    return jax.shard_map(
        local,
        mesh=mesh,
        in_specs=(
            P(None, ("groups", "session"), None),
            P(),
            P(None, "session"),
            P(None, "session"),
            P("session", None),
            P(("groups", "session"), None, None),
            P(("groups", "session"), None, None),
            P(("groups", "session"), None, None),
            P(("groups", "session")),
            P(("groups", "session"), None),
            P(None, ("groups", "session"), None),
        ),
        out_specs=P(None, ("groups", "session"), None),
        check_vma=False,
    )
```

```python
import functools
import math

import jax
import jax.numpy as jnp
from jax import lax
from jax.experimental import pallas as pl
from jax.experimental.pallas import tpu as pltpu
from jax.sharding import PartitionSpec as P

HEADS = 64
KV_HEADS = 8
HEAD_DIM = 128
STEPS = 2
GROUP = HEADS // KV_HEADS
LANES = 128
EXTRA = 16
PLANE = 4
PAIRS = 8
PROJECT_LIMIT = 48 * 2**20
AXIS = "session"
VMEM = pltpu.VMEM
SMEM = pltpu.SMEM
F32 = jnp.float32
BF16 = jnp.bfloat16


def angles(positions):
    half = HEAD_DIM // 2
    frequency = jnp.exp(
        -jnp.arange(half, dtype=F32) * (2.0 * math.log(500000.0) / HEAD_DIM)
    )
    return positions[..., None] * frequency


def turn_tables(positions):
    angle = angles(positions)
    cosine, sine = jnp.cos(angle), jnp.sin(angle)
    return (
        jnp.concatenate([cosine, cosine], axis=-1),
        jnp.concatenate([-sine, sine], axis=-1),
    )


def origin(me, order, j):
    if order is None:
        return 2 * (j % PAIRS) + jnp.bitwise_xor(jnp.bitwise_and(me, 1), j // PAIRS)
    return jnp.bitwise_xor(me, order[j])


def whole(space=VMEM):
    return pl.BlockSpec(memory_space=space)


def prepare_kernel(
    slots_dev, hidden_ref, gain_ref, slots_ref, block_ref, holder_ref, pair_ref, wide_scr
):
    steps, model = hidden_ref.shape
    pieces = model // LANES
    wide = hidden_ref[...].astype(F32)
    scale = lax.rsqrt(jnp.mean(wide * wide, axis=1, keepdims=True) + 1e-05)
    wide = wide * scale
    for step in range(steps):
        for c in range(pieces):
            row = step * pieces + c
            wide_scr[row : row + 1, :] = wide[step : step + 1, c * LANES : (c + 1) * LANES]
    lane = lax.broadcasted_iota(jnp.int32, (EXTRA, LANES), 1)
    parity = lax.broadcasted_iota(jnp.int32, (EXTRA, LANES), 0)
    table = jnp.zeros((EXTRA, LANES), jnp.int32)
    for m in range(holder_ref.shape[0]):
        slot = slots_ref[0, 2 * m]
        holder = lax.div(slot, slots_dev)
        holder_ref[m] = holder
        pair_ref[holder] = m
        base = holder * slots_dev
        pair = jnp.where(parity == 0, slot - base, slots_ref[0, 2 * m + 1] - base)
        table = jnp.where(lane == holder, pair, table)
    wide_scr[steps * pieces :, :] = table.astype(F32)
    gain = gain_ref[...].astype(F32)
    for step in range(steps):
        rows = slice(step * pieces, (step + 1) * pieces)
        wide_scr[rows, :] = wide_scr[rows, :] * gain
    block = wide_scr[...].astype(BF16)
    for copy in range(block_ref.shape[0]):
        block_ref[copy] = block


def prepare(hidden, gain, block_slot, slots_dev, copies):
    assert slots_dev <= 256
    steps, model = hidden.shape
    rows = steps * model // LANES + EXTRA
    return pl.pallas_call(
        functools.partial(prepare_kernel, slots_dev),
        in_specs=[whole(), whole(), whole(SMEM)],
        out_specs=(whole(), whole(SMEM), whole(SMEM)),
        out_shape=(
            jax.ShapeDtypeStruct((copies, rows, LANES), BF16),
            jax.ShapeDtypeStruct((block_slot.shape[1] // 2,), jnp.int32),
            jax.ShapeDtypeStruct((block_slot.shape[1] // 2,), jnp.int32),
        ),
        scratch_shapes=[VMEM((rows, LANES), F32)],
        name="prepare",
    )(hidden, gain, block_slot)


def pick_kernel(order, me_ref, first_ref, second_ref, store_ref, out_ref, table_scr, table_smem, sem):
    block_len = store_ref.shape[1]
    half, rows, _ = first_ref.shape
    for j in range(2 * half):
        source = first_ref if j < half else second_ref
        asked = source[j % half, rows - EXTRA :, :].astype(F32)
        table_scr[j] = asked[:8].astype(jnp.int32)
    copy = pltpu.make_async_copy(table_scr, table_smem, sem)
    copy.start()
    copy.wait()
    me = me_ref[0]
    for j in range(2 * half):
        target = origin(me, order, j)
        for k in range(2):
            out_ref[target, k * block_len : (k + 1) * block_len, :] = store_ref[
                table_smem[j, k, me]
            ]


def pick_pages(me, first, second, store, order):
    count = 2 * first.shape[0]
    _, block_len, width = store.shape
    return pl.pallas_call(
        functools.partial(pick_kernel, order),
        in_specs=[whole(SMEM), whole(), whole(), whole()],
        out_specs=whole(),
        out_shape=jax.ShapeDtypeStruct((count, 2 * block_len, width), store.dtype),
        scratch_shapes=[
            VMEM((count, 8, LANES), jnp.int32),
            SMEM((count, 8, LANES), jnp.int32),
            pltpu.SemaphoreType.DMA(()),
        ],
        compiler_params=pltpu.CompilerParams(vmem_limit_bytes=36 * 2**20),
        name="pick_pages",
    )(me, first, second, store)


def split_kernel(x_ref, store_ref, keep_ref, send_ref):
    slots, block_len, width = store_ref.shape
    for x in range(2):

        @pl.when(x_ref[0] == x)
        def _():
            for head in range(width // LANES):
                target = keep_ref if head % 2 == x else send_ref
                lanes = slice(head // 2 * LANES, (head // 2 + 1) * LANES)
                part = store_ref[:, :, head * LANES : (head + 1) * LANES]
                target[:, lanes] = part.reshape(slots * block_len, LANES)


def split_values(x, store):
    slots, block_len, width = store.shape
    half = jax.ShapeDtypeStruct((slots * block_len, width // 2), store.dtype)
    return pl.pallas_call(
        split_kernel,
        in_specs=[whole(SMEM), whole()],
        out_specs=(whole(), whole()),
        out_shape=(half, half),
        compiler_params=pltpu.CompilerParams(vmem_limit_bytes=16 * 2**20),
        name="split_values",
    )(x, store)


def mix_kernel(me_ref, rows_ref, weights_ref, *rest):
    stores, (values_scr, sum_scr) = rest[:PLANE], rest[-2:]
    out_refs = rest[PLANE:-2]
    me = me_ref[0]
    low = jnp.bitwise_and(me, PLANE - 1)
    z_me = lax.div(me, PLANE)
    sessions = weights_ref.shape[0]
    planes = len(out_refs)
    block_len = values_scr.shape[1] // (2 * PLANE)
    for session in range(sessions):
        for q, store in enumerate(stores):
            device = jnp.bitwise_xor(low, q)
            for k in range(2):
                row = rows_ref[session * (2 * PLANE) + k * PLANE + device]
                source = pl.ds(pl.multiple_of(row * block_len, block_len), block_len)
                target = pl.ds(
                    pl.multiple_of((device * 2 + k) * block_len, block_len), block_len
                )
                values_scr[session, target, :] = store[source, :]
        block = weights_ref[session]
        product = jnp.dot(
            block[: planes * 8], values_scr[session], preferred_element_type=F32
        )
        mine = slice(session * 8, (session + 1) * 8)
        for z in range(planes):
            sum_scr[z, mine, :] = product[z * 8 : (z + 1) * 8, z * LANES : (z + 1) * LANES]
        recent = block[planes * 8 :].astype(F32)
        sum_scr[z_me, mine, :] += recent[:8]
    for q, out_ref in enumerate(out_refs):
        out_ref[...] = sum_scr[jnp.bitwise_xor(z_me, q)].astype(BF16)


def mix(me, rows, weights, stores):
    sessions = weights.shape[0]
    planes = stores[0].shape[1] // LANES
    shape = (planes, sessions * 8, LANES)
    return pl.pallas_call(
        mix_kernel,
        in_specs=[whole(SMEM)] * 2 + [whole()] * (1 + PLANE),
        out_specs=(whole(),) * planes,
        out_shape=(jax.ShapeDtypeStruct(shape[1:], BF16),) * planes,
        scratch_shapes=[VMEM((sessions, LANES, planes * LANES), BF16), VMEM(shape, F32)],
        compiler_params=pltpu.CompilerParams(vmem_limit_bytes=16 * 2**20),
        cost_estimate=pl.CostEstimate(
            flops=2 * sessions * 32 * LANES * planes * LANES,
            bytes_accessed=4 * stores[0].size * PLANE,
            transcendentals=0,
        ),
        name="mix_values",
    )(me, rows, weights, *stores)


def keys_kernel(pair_ref, factors_ref, basis_ref, cos_ref, sin_ref, out_ref, rows_scr):
    span = factors_ref.shape[0] // pair_ref.shape[0]
    count = rows_scr.shape[0] // span
    base = pl.program_id(0) * count
    for p in range(count):
        source = pl.ds(pl.multiple_of(pair_ref[base + p] * span, span), span)
        rows_scr[p * span : (p + 1) * span, :] = factors_ref[source, :]
    product = jnp.dot(rows_scr[...], basis_ref[...], preferred_element_type=F32)
    cosine, sine = cos_ref[...], sin_ref[...]
    for head in range(KV_HEADS):
        lanes = slice(head * HEAD_DIM, (head + 1) * HEAD_DIM)
        part = product[:, lanes]
        turned = part * cosine + pltpu.roll(part, HEAD_DIM // 2, 1) * sine
        out_ref[:, lanes] = turned.astype(BF16)


def make_keys(pair, factors, basis, cosine, sine):
    seq, rank = factors.shape
    width = basis.shape[1]
    rows = min(seq, 512)
    return pl.pallas_call(
        keys_kernel,
        grid=(seq // rows,),
        in_specs=[
            whole(SMEM),
            pl.BlockSpec((seq, rank), lambda i: (0, 0)),
            pl.BlockSpec((rank, width), lambda i: (0, 0)),
            pl.BlockSpec((rows, HEAD_DIM), lambda i: (i, 0)),
            pl.BlockSpec((rows, HEAD_DIM), lambda i: (i, 0)),
        ],
        out_specs=pl.BlockSpec((rows, width), lambda i: (i, 0)),
        out_shape=jax.ShapeDtypeStruct((seq, width), BF16),
        scratch_shapes=[VMEM((rows, rank), BF16)],
        compiler_params=pltpu.CompilerParams(vmem_limit_bytes=32 * 2**20),
        cost_estimate=pl.CostEstimate(
            flops=2 * seq * rank * width, bytes_accessed=4 * seq * width, transcendentals=0
        ),
        name="turned_keys",
    )(pair, factors, basis, cosine, sine)


def fetch_kernel(source_ref, target_ref, sems):
    parts = sems.shape[0]
    rows, width = target_ref.shape
    columns = pl.ds(source_ref.shape[1] - width, width)
    copies = []
    for part in range(parts):
        mine = pl.ds(part * (rows // parts), rows // parts)
        copies.append(
            pltpu.make_async_copy(
                source_ref.at[mine, columns], target_ref.at[mine, :], sems.at[part]
            )
        )
        copies[-1].start()
    for copy in copies:
        copy.wait()


def fetch(weight, limit, width):
    return pl.pallas_call(
        fetch_kernel,
        in_specs=[whole(pl.ANY)],
        out_specs=whole(pl.ANY),
        out_shape=jax.ShapeDtypeStruct((weight.shape[0], width), weight.dtype),
        scratch_shapes=[pltpu.SemaphoreType.DMA((4,))],
        compiler_params=pltpu.CompilerParams(vmem_limit_bytes=limit * 2**20),
        cost_estimate=pl.CostEstimate(
            flops=0, bytes_accessed=2 * weight.shape[0] * width, transcendentals=0
        ),
        name="fetch_weight",
    )(weight)


def project_kernel(
    order, fast, me_ref, first_ref, second_ref, wq_ref, wk_ref, out_ref, *rest
):
    if fast:
        rows_ref, x_scr, lhs_scr, wq_buf, out_scr, sems, *asked_scr = rest
    else:
        x_scr, lhs_scr, wq_buf, out_scr, sems = rest
    depth, q_cols = wq_ref.shape
    k_cols = wk_ref.shape[1]
    chunks = wq_buf.shape[0]
    span = depth // chunks
    pieces = depth // LANES
    copies = []
    for i in range(chunks):
        rows = pl.ds(i * span, span)
        copies.append(pltpu.make_async_copy(wq_ref.at[rows, :], wq_buf.at[i], sems.at[i]))
        copies[-1].start()
    half = first_ref.shape[0]
    count = 2 * half * STEPS
    rows = STEPS * pieces
    for j in range(2 * half):
        source = first_ref if j < half else second_ref
        x_scr[j * rows : (j + 1) * rows] = source[j % half, :rows, :].astype(F32)
    if fast:
        table_scr, table_smem, table_sem = asked_scr
        for j in range(2 * half):
            source = first_ref if j < half else second_ref
            asked = source[j % half, rows:, :].astype(F32)
            table_scr[2 * j : 2 * j + 2, :] = asked[:2].astype(jnp.int32)
        table_copy = pltpu.make_async_copy(table_scr, table_smem, table_sem)
        table_copy.start()
    for c in range(pieces):
        part = x_scr[pl.ds(c, count, stride=pieces), :]
        lhs_scr[:, c * LANES : (c + 1) * LANES] = part.astype(BF16)
    q_sum = jnp.zeros((count, q_cols), F32)
    k_sum = jnp.zeros((count, k_cols), F32)
    for i in range(chunks):
        copies[i].wait()
        lhs = lhs_scr[:, i * span : (i + 1) * span]
        q_sum = q_sum + jnp.dot(lhs, wq_buf[i], preferred_element_type=F32)
        k_sum = k_sum + jnp.dot(
            lhs, wk_ref[i * span : (i + 1) * span, :], preferred_element_type=F32
        )
    if not fast:
        out_ref[:, :q_cols] = q_sum.astype(BF16)
        out_ref[:, q_cols:] = k_sum.astype(BF16)
        return
    me = me_ref[0]
    per = q_cols // LANES
    out_scr[...] = jnp.zeros_like(out_scr)
    for j in range(2 * half):
        place = origin(me, order, j)
        for step in range(STEPS):
            row = j * STEPS + step
            for c in range(per):
                out_scr[place, step * per + c : step * per + c + 1, :] = q_sum[
                    row : row + 1, c * LANES : (c + 1) * LANES
                ]
            out_scr[place, STEPS * per + step : STEPS * per + step + 1, :] = k_sum[
                row : row + 1, :
            ]
    out_ref[...] = out_scr[...].astype(BF16)
    table_copy.wait()
    plane = jnp.bitwise_and(me, -PLANE)
    for j in range(2 * half):
        place = origin(me, order, j) * (2 * PLANE)
        for k in range(2):
            for b in range(PLANE):
                rows_ref[place + k * PLANE + b] = table_smem[2 * j + k, plane + b]


def project(me, first, second, query_weight, kv_weight, order, fast):
    depth, q_cols = query_weight.shape
    k_cols = kv_weight.shape[1]
    pieces = depth // LANES
    devices = 2 * first.shape[0]
    rows = devices * STEPS
    chunks = 8
    span = depth // chunks
    shape = (devices, 16, LANES) if fast else (rows, q_cols + k_cols)
    return pl.pallas_call(
        functools.partial(project_kernel, order, fast),
        in_specs=[whole(SMEM), whole(), whole(), whole(pl.ANY), whole()],
        out_specs=(whole(), whole(SMEM)) if fast else whole(),
        out_shape=(
            (
                jax.ShapeDtypeStruct(shape, BF16),
                jax.ShapeDtypeStruct((devices * 2 * PLANE,), jnp.int32),
            )
            if fast
            else jax.ShapeDtypeStruct(shape, BF16)
        ),
        scratch_shapes=[
            VMEM((rows * pieces, LANES), F32),
            VMEM((rows, depth), BF16),
            VMEM((chunks, span, q_cols), BF16),
            VMEM((devices, 16, LANES) if fast else (8, LANES), F32),
            pltpu.SemaphoreType.DMA((chunks,)),
        ]
        + (
            [
                VMEM((2 * devices, LANES), jnp.int32),
                SMEM((2 * devices, LANES), jnp.int32),
                pltpu.SemaphoreType.DMA(()),
            ]
            if fast
            else []
        ),
        compiler_params=pltpu.CompilerParams(vmem_limit_bytes=PROJECT_LIMIT),
        cost_estimate=pl.CostEstimate(
            flops=2 * rows * depth * (q_cols + k_cols),
            bytes_accessed=2 * depth * (q_cols + k_cols),
            transcendentals=0,
        ),
        name="norm_project",
    )(me, first, second, query_weight, kv_weight)


def attend_kernel(fast, columns_ref, keys_ref, bias_ref, cos_ref, sin_ref, *rest):
    pages_ref, out_ref, out_scr = (None, *rest) if fast else rest
    score_scale = 1.0 / math.sqrt(HEAD_DIM)
    half = HEAD_DIM // 2
    rows = 2 * GROUP
    columns = columns_ref[...].astype(F32)
    count = columns.shape[0]
    query = columns[:, :8, :].reshape(count * 8, HEAD_DIM)
    fresh = columns[:, 8:, :]
    if fast:
        planes = count // PLANE
        out_scr[...] = jnp.zeros_like(out_scr)
    row_step = lax.rem(lax.broadcasted_iota(jnp.int32, (count * 8, 1), 0) // 4, STEPS)
    later = row_step == 1
    cosine = jnp.where(later, cos_ref[1:2, :], cos_ref[0:1, :])
    sine = jnp.where(later, sin_ref[1:2, :], sin_ref[0:1, :])
    turned = (query * cosine + pltpu.roll(query, half, 1) * sine).astype(BF16)
    turned_wide = turned.astype(F32)
    step_later = later[:rows]
    bias = jnp.where(step_later, bias_ref[1:2, :], bias_ref[0:1, :])
    new_keys = []
    for step in range(STEPS):
        part = fresh[:KV_HEADS, step, :]
        new = part * cos_ref[step : step + 1, :] + pltpu.roll(part, half, 1) * sin_ref[step : step + 1, :]
        new_keys.append(new.astype(BF16).astype(F32))
    for head in range(KV_HEADS):
        lanes = slice(head * HEAD_DIM, (head + 1) * HEAD_DIM)
        mine = slice(head * rows, (head + 1) * rows)
        scores = (
            lax.dot_general(
                turned[mine], keys_ref[:, lanes], (((1,), (1,)), ((), ())),
                preferred_element_type=F32,
            )
            * score_scale
            + bias
        )
        recent0 = (
            jnp.sum(turned_wide[mine] * new_keys[0][head : head + 1, :], axis=1, keepdims=True)
            * score_scale
        )
        recent1 = (
            jnp.sum(turned_wide[mine] * new_keys[1][head : head + 1, :], axis=1, keepdims=True)
            * score_scale
        )
        recent1 = jnp.where(step_later, recent1, -1e30)
        largest = jnp.maximum(
            jnp.max(scores, axis=1, keepdims=True), jnp.maximum(recent0, recent1)
        )
        cache_exp = jnp.exp(scores - largest)
        exp0 = jnp.exp(recent0 - largest)
        exp1 = jnp.exp(recent1 - largest)
        denominator = jnp.sum(cache_exp, axis=1, keepdims=True) + (exp0 + exp1)
        weights = (cache_exp / denominator).astype(BF16)
        weight0 = (exp0 / denominator).astype(BF16).astype(F32)
        weight1 = (exp1 / denominator).astype(BF16).astype(F32)
        recent = weight0 * fresh[KV_HEADS + head, 0:1, :]
        recent = recent + weight1 * fresh[KV_HEADS + head, 1:2, :]
        if not fast:
            values = pages_ref[:, :, lanes].reshape(keys_ref.shape[0], HEAD_DIM)
            mixed = jnp.dot(weights, values, preferred_element_type=F32)
            out_ref[mine, :] = (mixed + recent).astype(BF16)
            continue
        weights = weights.astype(F32)
        z, x = divmod(head, 2)
        for c in range(2):
            part = slice(c * 8, (c + 1) * 8)
            for plane in range(planes):
                out_scr[plane * PLANE + 2 * x + c, z * 8 : (z + 1) * 8, :] = weights[
                    part, plane * LANES : (plane + 1) * LANES
                ]
            out_scr[z * PLANE + 2 * x + c, planes * 8 : planes * 8 + 8, :] = recent[part]
    if fast:
        out_ref[...] = out_scr[...].astype(BF16)


def attend(columns, keys, bias, cosine, sine, pages, fast):
    seq, width = keys.shape
    count = columns.shape[0]
    if fast:
        shape = (count, count // PLANE * 8 + 16, LANES)
        scratch = [VMEM(shape, F32)]
        operands = (columns, keys, bias, cosine, sine)
    else:
        shape = (STEPS * HEADS, HEAD_DIM)
        scratch = [VMEM((8, LANES), F32)]
        operands = (columns, keys, bias, cosine, sine, pages)
    return pl.pallas_call(
        functools.partial(attend_kernel, fast),
        in_specs=[whole()] * len(operands),
        out_specs=whole(),
        out_shape=jax.ShapeDtypeStruct(shape, BF16),
        scratch_shapes=scratch,
        compiler_params=pltpu.CompilerParams(vmem_limit_bytes=48 * 2**20),
        cost_estimate=pl.CostEstimate(
            flops=4 * STEPS * HEADS * seq * HEAD_DIM,
            bytes_accessed=4 * seq * width,
            transcendentals=STEPS * HEADS * seq,
        ),
        name="attend",
    )(*operands)


def output_kernel(fast, count, me_ref, weight_ref, last_ref, *rest):
    lhs_refs, rest = rest[:count], rest[count:]
    out_refs, (head_buf, out_scr, heads_scr, sem) = rest[:-4], rest[-4:]
    width = head_buf.shape[1]
    head_copy = pltpu.make_async_copy(weight_ref.at[:, pl.ds(0, width)], head_buf, sem)
    head_copy.start()
    chunks = 8
    span = weight_ref.shape[1] // chunks
    rows = out_scr.shape[0] * LANES // (chunks * span)
    pieces = chunks * span // LANES
    if fast:
        per = heads_scr.shape[0] // rows
        total = lhs_refs[0][...].astype(F32)
        for lhs_ref in lhs_refs[1:]:
            total = total + lhs_ref[...].astype(F32)
        heads_scr[...] = total
        lhs = jnp.concatenate(
            [heads_scr[pl.ds(g, rows, stride=per), :].astype(BF16) for g in range(per)], axis=1
        )
    else:
        lhs = lhs_refs[0][...]
    first = width // span
    for i in (*range(first, chunks), *range(first)):
        if i == 0:
            head_copy.wait()
        source, place = (last_ref, i - first) if i >= first else (head_buf, i)
        part = jnp.dot(
            lhs, source[:, place * span : (place + 1) * span], preferred_element_type=F32
        )
        for c in range(span // LANES):
            out_scr[pl.ds(i * (span // LANES) + c, rows, stride=pieces), :] = part[
                :, c * LANES : (c + 1) * LANES
            ]
    if not fast:
        out_refs[0][...] = out_scr[...].astype(BF16)
        return
    low = jnp.bitwise_and(me_ref[0], 1)
    for out_ref, core in zip(out_refs, (low, 1 - low)):
        count, size, _ = out_ref.shape
        for j in range(count):
            part = pl.ds(pl.multiple_of((2 * j + core) * size, size), size)
            out_ref[j] = out_scr[part, :].astype(BF16)


def output(me, lhs, weight, last, rows, fast):
    depth, width = weight.shape
    if fast:
        shape = (rows // (2 * STEPS), STEPS * width // LANES, LANES)
        shapes = (jax.ShapeDtypeStruct(shape, BF16),) * 2
    else:
        shapes = (jax.ShapeDtypeStruct((rows * width // LANES, LANES), BF16),)
    return pl.pallas_call(
        functools.partial(output_kernel, fast, len(lhs)),
        in_specs=[whole(SMEM), whole(pl.ANY)] + [whole()] * (1 + len(lhs)),
        out_specs=(whole(),) * len(shapes),
        out_shape=shapes,
        scratch_shapes=[
            VMEM((depth, width - last.shape[1]), BF16),
            VMEM((rows * width // LANES, LANES), F32),
            VMEM(lhs[0].shape if fast else (8, LANES), F32),
            pltpu.SemaphoreType.DMA(()),
        ],
        compiler_params=pltpu.CompilerParams(vmem_limit_bytes=46 * 2**20),
        cost_estimate=pl.CostEstimate(
            flops=2 * rows * depth * width, bytes_accessed=2 * depth * width, transcendentals=0
        ),
        name="output_project",
    )(me, weight, last, *lhs)


def swap(block, bit, devices):
    return lax.ppermute(block, AXIS, [(i, i ^ bit) for i in range(devices)])


def exchange(blocks, groups=None):
    return lax.all_to_all(
        blocks, AXIS, split_axis=0, concat_axis=0, tiled=True, axis_index_groups=groups
    )


def local(
    hidden,
    norm_gain,
    query_weight,
    kv_weight,
    out_weight,
    key_factors,
    key_basis,
    value_store,
    lengths,
    block_slot,
    selection,
):
    devices = lax.axis_size(AXIS)
    me = lax.axis_index(AXIS)
    slots_dev, block_len, width = value_store.shape
    seq = key_factors.shape[1]
    pages = block_slot.shape[1]
    model = hidden.shape[2]
    q_cols = query_weight.shape[1]
    k_cols = kv_weight.shape[1]
    fast = devices == 2 * PAIRS and q_cols == 4 * HEAD_DIM and k_cols == HEAD_DIM
    pieces = model // LANES

    me_word = me.astype(jnp.int32).reshape(1)
    block, holder, pair = prepare(
        hidden[:, 0], norm_gain.reshape(pieces, LANES), block_slot, slots_dev, PAIRS if fast else 1
    )
    if fast:
        same_core = [list(range(core, devices, 2)) for core in range(2)]
        block = exchange(block, same_core)
        block, kv_weight = lax.optimization_barrier((block, kv_weight))
        kv_weight = fetch(kv_weight, 50, k_cols)
        other = swap(block, 1, devices)
        order = None
        x = lax.bitwise_and(lax.shift_right_logical(me_word, 1), 1)
        keep, send = split_values(x, value_store)
        neighbour = swap(send, 2, devices)
    else:
        order = [0]
        bit = devices // 2
        while bit:
            other = swap(block, bit, devices)
            order = order + [k ^ bit for k in order]
            bit //= 2
            if bit:
                block = jnp.concatenate([block, other], axis=0)
        order = tuple(order)
    span = 2 * block_len
    places = (pair[:, None] * span + jnp.arange(span, dtype=jnp.int32)[None, :]).reshape(-1)
    if not fast:
        sent_pages = pick_pages(me_word, block, other, value_store, order)
        block, other, sent_pages = lax.optimization_barrier((block, other, sent_pages))
        fetched = exchange(sent_pages)
    projected = project(
        me_word, block, other, query_weight, kv_weight, order, fast
    )
    if fast:
        projected, rows = projected
        projected, places = lax.optimization_barrier((projected, places))
        columns = exchange(projected)
    else:
        targets = jnp.bitwise_xor(me, jnp.array(order, dtype=jnp.int32))
        columns = exchange(projected.reshape(devices, STEPS, q_cols + k_cols)[targets])
        query = columns[:, :, :q_cols].transpose(1, 0, 2).reshape(STEPS, HEADS // 4, 4, HEAD_DIM)
        query = query.transpose(1, 0, 2, 3).reshape(HEADS // 4, 8, HEAD_DIM)
        fresh = columns[:, :, q_cols:].transpose(1, 0, 2).reshape(STEPS, HEADS // 4, HEAD_DIM)
        fresh = jnp.pad(fresh.transpose(1, 0, 2), ((0, 0), (0, 8 - STEPS), (0, 0)))
        columns = jnp.concatenate([query, fresh], axis=1)

    cosine, sine = turn_tables(places.astype(F32))
    keys = make_keys(pair, key_factors[0], key_basis[0], cosine, sine)
    picked = jnp.any(
        selection[:, 0, :, None] == (places // block_len)[None, None, :], axis=1
    )
    bias = jnp.where(picked & (places < lengths[0])[None, :], 0.0, -1e30).astype(F32)
    new_cos, new_sin = turn_tables(
        (lengths[0] + jnp.arange(STEPS, dtype=jnp.int32)).astype(F32)
    )
    if fast:
        blocks = attend(columns, keys, bias, new_cos, new_sin, None, True)
        blocks, neighbour = lax.optimization_barrier((blocks, neighbour))
        stores = (keep, swap(keep, 1, devices), neighbour, swap(neighbour, 1, devices))
        blocks = exchange(blocks)
        parts = mix(me_word, rows, blocks, stores)
        (*parts, out_weight) = lax.optimization_barrier((*parts, out_weight))
        last_weight = fetch(out_weight, 43, model - model // 4)
        lhs = [parts[0]] + [swap(parts[q], q * PLANE, devices) for q in range(1, len(parts))]
    else:
        heads = attend(columns, keys, bias, new_cos, new_sin, fetched, False)
        flat = heads.reshape(HEADS // 4, STEPS, 4 * HEAD_DIM).transpose(1, 0, 2)
        flat = flat.reshape(STEPS, devices, model // devices).transpose(1, 0, 2)
        lhs = [exchange(flat).reshape(devices * STEPS, model // devices)]
        last_weight = out_weight[:, model // 4 :]
    partial = output(me_word, lhs, out_weight, last_weight, devices * STEPS, fast)
    if fast:
        near, far = partial
        both = near.astype(F32) + swap(far, 1, devices).astype(F32)
        arrived = exchange(both.astype(BF16), same_core)
    else:
        arrived = exchange(partial[0].reshape(devices, STEPS * pieces, LANES))
    total = jnp.sum(arrived.astype(F32), axis=0).astype(BF16)
    return total.reshape(STEPS, 1, model)


def solution(mesh):
    return jax.shard_map(
        local,
        mesh=mesh,
        in_specs=(
            P(None, ("groups", "session"), None),
            P(),
            P(None, "session"),
            P(None, "session"),
            P("session", None),
            P(("groups", "session"), None, None),
            P(("groups", "session"), None, None),
            P(("groups", "session"), None, None),
            P(("groups", "session")),
            P(("groups", "session"), None),
            P(None, ("groups", "session"), None),
        ),
        out_specs=P(None, ("groups", "session"), None),
        check_vma=False,
    )
```

```python
import functools
import math

import jax
import jax.numpy as jnp
from jax import lax
from jax.experimental import pallas as pl
from jax.experimental.pallas import tpu as pltpu
from jax.sharding import PartitionSpec as P

HEADS = 64
KV_HEADS = 8
HEAD_DIM = 128
STEPS = 2
GROUP = HEADS // KV_HEADS
LANES = 128
EXTRA = 16
PLANE = 4
PAIRS = 8
PROJECT_LIMIT = 48 * 2**20
AXIS = "session"
VMEM = pltpu.VMEM
SMEM = pltpu.SMEM
F32 = jnp.float32
BF16 = jnp.bfloat16


def angles(positions):
    half = HEAD_DIM // 2
    frequency = jnp.exp(
        -jnp.arange(half, dtype=F32) * (2.0 * math.log(500000.0) / HEAD_DIM)
    )
    return positions[..., None] * frequency


def turn_tables(positions):
    angle = angles(positions)
    cosine, sine = jnp.cos(angle), jnp.sin(angle)
    return (
        jnp.concatenate([cosine, cosine], axis=-1),
        jnp.concatenate([-sine, sine], axis=-1),
    )


def origin(me, order, j):
    if order is None:
        return 2 * (j % PAIRS) + jnp.bitwise_xor(jnp.bitwise_and(me, 1), j // PAIRS)
    return jnp.bitwise_xor(me, order[j])


def whole(space=VMEM):
    return pl.BlockSpec(memory_space=space)


def prepare_kernel(
    slots_dev, hidden_ref, gain_ref, slots_ref, block_ref, holder_ref, pair_ref, wide_scr
):
    steps, model = hidden_ref.shape
    pieces = model // LANES
    wide = hidden_ref[...].astype(F32)
    scale = lax.rsqrt(jnp.mean(wide * wide, axis=1, keepdims=True) + 1e-05)
    wide = wide * scale
    for step in range(steps):
        for c in range(pieces):
            row = step * pieces + c
            wide_scr[row : row + 1, :] = wide[step : step + 1, c * LANES : (c + 1) * LANES]
    lane = lax.broadcasted_iota(jnp.int32, (EXTRA, LANES), 1)
    parity = lax.broadcasted_iota(jnp.int32, (EXTRA, LANES), 0)
    table = jnp.zeros((EXTRA, LANES), jnp.int32)
    for m in range(holder_ref.shape[0]):
        slot = slots_ref[0, 2 * m]
        holder = lax.div(slot, slots_dev)
        holder_ref[m] = holder
        pair_ref[holder] = m
        base = holder * slots_dev
        pair = jnp.where(parity == 0, slot - base, slots_ref[0, 2 * m + 1] - base)
        table = jnp.where(lane == holder, pair, table)
    wide_scr[steps * pieces :, :] = table.astype(F32)
    gain = gain_ref[...].astype(F32)
    for step in range(steps):
        rows = slice(step * pieces, (step + 1) * pieces)
        wide_scr[rows, :] = wide_scr[rows, :] * gain
    block = wide_scr[...].astype(BF16)
    for copy in range(block_ref.shape[0]):
        block_ref[copy] = block


def prepare(hidden, gain, block_slot, slots_dev, copies):
    assert slots_dev <= 256
    steps, model = hidden.shape
    rows = steps * model // LANES + EXTRA
    return pl.pallas_call(
        functools.partial(prepare_kernel, slots_dev),
        in_specs=[whole(), whole(), whole(SMEM)],
        out_specs=(whole(), whole(SMEM), whole(SMEM)),
        out_shape=(
            jax.ShapeDtypeStruct((copies, rows, LANES), BF16),
            jax.ShapeDtypeStruct((block_slot.shape[1] // 2,), jnp.int32),
            jax.ShapeDtypeStruct((block_slot.shape[1] // 2,), jnp.int32),
        ),
        scratch_shapes=[VMEM((rows, LANES), F32)],
        name="prepare",
    )(hidden, gain, block_slot)


def pick_kernel(order, me_ref, first_ref, second_ref, store_ref, out_ref, table_scr, table_smem, sem):
    block_len = store_ref.shape[1]
    half, rows, _ = first_ref.shape
    for j in range(2 * half):
        source = first_ref if j < half else second_ref
        asked = source[j % half, rows - EXTRA :, :].astype(F32)
        table_scr[j] = asked[:8].astype(jnp.int32)
    copy = pltpu.make_async_copy(table_scr, table_smem, sem)
    copy.start()
    copy.wait()
    me = me_ref[0]
    for j in range(2 * half):
        target = origin(me, order, j)
        for k in range(2):
            out_ref[target, k * block_len : (k + 1) * block_len, :] = store_ref[
                table_smem[j, k, me]
            ]


def pick_pages(me, first, second, store, order):
    count = 2 * first.shape[0]
    _, block_len, width = store.shape
    return pl.pallas_call(
        functools.partial(pick_kernel, order),
        in_specs=[whole(SMEM), whole(), whole(), whole()],
        out_specs=whole(),
        out_shape=jax.ShapeDtypeStruct((count, 2 * block_len, width), store.dtype),
        scratch_shapes=[
            VMEM((count, 8, LANES), jnp.int32),
            SMEM((count, 8, LANES), jnp.int32),
            pltpu.SemaphoreType.DMA(()),
        ],
        compiler_params=pltpu.CompilerParams(vmem_limit_bytes=36 * 2**20),
        name="pick_pages",
    )(me, first, second, store)


def split_kernel(x_ref, store_ref, keep_ref, send_ref):
    slots, block_len, width = store_ref.shape
    for x in range(2):

        @pl.when(x_ref[0] == x)
        def _():
            for head in range(width // LANES):
                target = keep_ref if head % 2 == x else send_ref
                lanes = slice(head // 2 * LANES, (head // 2 + 1) * LANES)
                part = store_ref[:, :, head * LANES : (head + 1) * LANES]
                target[:, lanes] = part.reshape(slots * block_len, LANES)


def split_values(x, store):
    slots, block_len, width = store.shape
    half = jax.ShapeDtypeStruct((slots * block_len, width // 2), store.dtype)
    return pl.pallas_call(
        split_kernel,
        in_specs=[whole(SMEM), whole()],
        out_specs=(whole(), whole()),
        out_shape=(half, half),
        compiler_params=pltpu.CompilerParams(vmem_limit_bytes=16 * 2**20),
        name="split_values",
    )(x, store)


def mix_kernel(me_ref, rows_ref, weights_ref, *rest):
    stores, (values_scr, sum_scr) = rest[:PLANE], rest[-2:]
    out_refs = rest[PLANE:-2]
    me = me_ref[0]
    low = jnp.bitwise_and(me, PLANE - 1)
    z_me = lax.div(me, PLANE)
    sessions = weights_ref.shape[0]
    planes = len(out_refs)
    block_len = values_scr.shape[1] // (2 * PLANE)
    for session in range(sessions):
        for q, store in enumerate(stores):
            device = jnp.bitwise_xor(low, q)
            for k in range(2):
                row = rows_ref[session * (2 * PLANE) + k * PLANE + device]
                source = pl.ds(pl.multiple_of(row * block_len, block_len), block_len)
                target = pl.ds(
                    pl.multiple_of((device * 2 + k) * block_len, block_len), block_len
                )
                values_scr[session, target, :] = store[source, :]
        block = weights_ref[session]
        product = jnp.dot(
            block[: planes * 8], values_scr[session], preferred_element_type=F32
        )
        mine = slice(session * 8, (session + 1) * 8)
        for z in range(planes):
            sum_scr[z, mine, :] = product[z * 8 : (z + 1) * 8, z * LANES : (z + 1) * LANES]
        recent = block[planes * 8 :].astype(F32)
        sum_scr[z_me, mine, :] += recent[:8]
    for q, out_ref in enumerate(out_refs):
        out_ref[...] = sum_scr[jnp.bitwise_xor(z_me, q)].astype(BF16)


def mix(me, rows, weights, stores):
    sessions = weights.shape[0]
    planes = stores[0].shape[1] // LANES
    shape = (planes, sessions * 8, LANES)
    return pl.pallas_call(
        mix_kernel,
        in_specs=[whole(SMEM)] * 2 + [whole()] * (1 + PLANE),
        out_specs=(whole(),) * planes,
        out_shape=(jax.ShapeDtypeStruct(shape[1:], BF16),) * planes,
        scratch_shapes=[VMEM((sessions, LANES, planes * LANES), BF16), VMEM(shape, F32)],
        compiler_params=pltpu.CompilerParams(vmem_limit_bytes=16 * 2**20),
        cost_estimate=pl.CostEstimate(
            flops=2 * sessions * 32 * LANES * planes * LANES,
            bytes_accessed=4 * stores[0].size * PLANE,
            transcendentals=0,
        ),
        name="mix_values",
    )(me, rows, weights, *stores)


def keys_kernel(pair_ref, factors_ref, basis_ref, cos_ref, sin_ref, out_ref, rows_scr):
    span = factors_ref.shape[0] // pair_ref.shape[0]
    count = rows_scr.shape[0] // span
    base = pl.program_id(0) * count
    for p in range(count):
        source = pl.ds(pl.multiple_of(pair_ref[base + p] * span, span), span)
        rows_scr[p * span : (p + 1) * span, :] = factors_ref[source, :]
    product = jnp.dot(rows_scr[...], basis_ref[...], preferred_element_type=F32)
    cosine, sine = cos_ref[...], sin_ref[...]
    for head in range(KV_HEADS):
        lanes = slice(head * HEAD_DIM, (head + 1) * HEAD_DIM)
        part = product[:, lanes]
        turned = part * cosine + pltpu.roll(part, HEAD_DIM // 2, 1) * sine
        out_ref[:, lanes] = turned.astype(BF16)


def make_keys(pair, factors, basis, cosine, sine):
    seq, rank = factors.shape
    width = basis.shape[1]
    rows = min(seq, 512)
    return pl.pallas_call(
        keys_kernel,
        grid=(seq // rows,),
        in_specs=[
            whole(SMEM),
            pl.BlockSpec((seq, rank), lambda i: (0, 0)),
            pl.BlockSpec((rank, width), lambda i: (0, 0)),
            pl.BlockSpec((rows, HEAD_DIM), lambda i: (i, 0)),
            pl.BlockSpec((rows, HEAD_DIM), lambda i: (i, 0)),
        ],
        out_specs=pl.BlockSpec((rows, width), lambda i: (i, 0)),
        out_shape=jax.ShapeDtypeStruct((seq, width), BF16),
        scratch_shapes=[VMEM((rows, rank), BF16)],
        compiler_params=pltpu.CompilerParams(vmem_limit_bytes=32 * 2**20),
        cost_estimate=pl.CostEstimate(
            flops=2 * seq * rank * width, bytes_accessed=4 * seq * width, transcendentals=0
        ),
        name="turned_keys",
    )(pair, factors, basis, cosine, sine)


def fetch_kernel(source_ref, target_ref, sems):
    parts = sems.shape[0]
    rows, width = target_ref.shape
    columns = pl.ds(source_ref.shape[1] - width, width)
    copies = []
    for part in range(parts):
        mine = pl.ds(part * (rows // parts), rows // parts)
        copies.append(
            pltpu.make_async_copy(
                source_ref.at[mine, columns], target_ref.at[mine, :], sems.at[part]
            )
        )
        copies[-1].start()
    for copy in copies:
        copy.wait()


def fetch(weight, limit, width):
    return pl.pallas_call(
        fetch_kernel,
        in_specs=[whole(pl.ANY)],
        out_specs=whole(pl.ANY),
        out_shape=jax.ShapeDtypeStruct((weight.shape[0], width), weight.dtype),
        scratch_shapes=[pltpu.SemaphoreType.DMA((4,))],
        compiler_params=pltpu.CompilerParams(vmem_limit_bytes=limit * 2**20),
        cost_estimate=pl.CostEstimate(
            flops=0, bytes_accessed=2 * weight.shape[0] * width, transcendentals=0
        ),
        name="fetch_weight",
    )(weight)


def project_kernel(
    order, fast, me_ref, first_ref, second_ref, wq_ref, wk_ref, out_ref, *rest
):
    if fast:
        rows_ref, x_scr, lhs_scr, wq_buf, out_scr, sems, *asked_scr = rest
    else:
        x_scr, lhs_scr, wq_buf, out_scr, sems = rest
    depth, q_cols = wq_ref.shape
    k_cols = wk_ref.shape[1]
    chunks = wq_buf.shape[0]
    span = depth // chunks
    pieces = depth // LANES
    copies = []
    for i in range(chunks):
        rows = pl.ds(i * span, span)
        copies.append(pltpu.make_async_copy(wq_ref.at[rows, :], wq_buf.at[i], sems.at[i]))
        copies[-1].start()
    half = first_ref.shape[0]
    count = 2 * half * STEPS
    rows = STEPS * pieces
    for j in range(2 * half):
        source = first_ref if j < half else second_ref
        x_scr[j * rows : (j + 1) * rows] = source[j % half, :rows, :].astype(F32)
    if fast:
        table_scr, table_smem, table_sem = asked_scr
        for j in range(2 * half):
            source = first_ref if j < half else second_ref
            asked = source[j % half, rows:, :].astype(F32)
            table_scr[2 * j : 2 * j + 2, :] = asked[:2].astype(jnp.int32)
        table_copy = pltpu.make_async_copy(table_scr, table_smem, table_sem)
        table_copy.start()
    for c in range(pieces):
        part = x_scr[pl.ds(c, count, stride=pieces), :]
        lhs_scr[:, c * LANES : (c + 1) * LANES] = part.astype(BF16)
    q_sum = jnp.zeros((count, q_cols), F32)
    k_sum = jnp.zeros((count, k_cols), F32)
    for i in range(chunks):
        copies[i].wait()
        lhs = lhs_scr[:, i * span : (i + 1) * span]
        q_sum = q_sum + jnp.dot(lhs, wq_buf[i], preferred_element_type=F32)
        k_sum = k_sum + jnp.dot(
            lhs, wk_ref[i * span : (i + 1) * span, :], preferred_element_type=F32
        )
    if not fast:
        out_ref[:, :q_cols] = q_sum.astype(BF16)
        out_ref[:, q_cols:] = k_sum.astype(BF16)
        return
    me = me_ref[0]
    per = q_cols // LANES
    out_scr[...] = jnp.zeros_like(out_scr)
    for j in range(2 * half):
        place = origin(me, order, j)
        for step in range(STEPS):
            row = j * STEPS + step
            for c in range(per):
                out_scr[place, step * per + c : step * per + c + 1, :] = q_sum[
                    row : row + 1, c * LANES : (c + 1) * LANES
                ]
            out_scr[place, STEPS * per + step : STEPS * per + step + 1, :] = k_sum[
                row : row + 1, :
            ]
    out_ref[...] = out_scr[...].astype(BF16)
    table_copy.wait()
    plane = jnp.bitwise_and(me, -PLANE)
    for j in range(2 * half):
        place = origin(me, order, j) * (2 * PLANE)
        for k in range(2):
            for b in range(PLANE):
                rows_ref[place + k * PLANE + b] = table_smem[2 * j + k, plane + b]


def project(me, first, second, query_weight, kv_weight, order, fast):
    depth, q_cols = query_weight.shape
    k_cols = kv_weight.shape[1]
    pieces = depth // LANES
    devices = 2 * first.shape[0]
    rows = devices * STEPS
    chunks = 8
    span = depth // chunks
    shape = (devices, 16, LANES) if fast else (rows, q_cols + k_cols)
    return pl.pallas_call(
        functools.partial(project_kernel, order, fast),
        in_specs=[whole(SMEM), whole(), whole(), whole(pl.ANY), whole()],
        out_specs=(whole(), whole(SMEM)) if fast else whole(),
        out_shape=(
            (
                jax.ShapeDtypeStruct(shape, BF16),
                jax.ShapeDtypeStruct((devices * 2 * PLANE,), jnp.int32),
            )
            if fast
            else jax.ShapeDtypeStruct(shape, BF16)
        ),
        scratch_shapes=[
            VMEM((rows * pieces, LANES), F32),
            VMEM((rows, depth), BF16),
            VMEM((chunks, span, q_cols), BF16),
            VMEM((devices, 16, LANES) if fast else (8, LANES), F32),
            pltpu.SemaphoreType.DMA((chunks,)),
        ]
        + (
            [
                VMEM((2 * devices, LANES), jnp.int32),
                SMEM((2 * devices, LANES), jnp.int32),
                pltpu.SemaphoreType.DMA(()),
            ]
            if fast
            else []
        ),
        compiler_params=pltpu.CompilerParams(vmem_limit_bytes=PROJECT_LIMIT),
        cost_estimate=pl.CostEstimate(
            flops=2 * rows * depth * (q_cols + k_cols),
            bytes_accessed=2 * depth * (q_cols + k_cols),
            transcendentals=0,
        ),
        name="norm_project",
    )(me, first, second, query_weight, kv_weight)


def attend_kernel(fast, columns_ref, keys_ref, bias_ref, cos_ref, sin_ref, *rest):
    pages_ref, out_ref, out_scr = (None, *rest) if fast else rest
    score_scale = 1.0 / math.sqrt(HEAD_DIM)
    half = HEAD_DIM // 2
    rows = 2 * GROUP
    columns = columns_ref[...].astype(F32)
    count = columns.shape[0]
    query = columns[:, :8, :].reshape(count * 8, HEAD_DIM)
    fresh = columns[:, 8:, :]
    if fast:
        planes = count // PLANE
        out_scr[...] = jnp.zeros_like(out_scr)
    row_step = lax.rem(lax.broadcasted_iota(jnp.int32, (count * 8, 1), 0) // 4, STEPS)
    later = row_step == 1
    cosine = jnp.where(later, cos_ref[1:2, :], cos_ref[0:1, :])
    sine = jnp.where(later, sin_ref[1:2, :], sin_ref[0:1, :])
    turned = (query * cosine + pltpu.roll(query, half, 1) * sine).astype(BF16)
    turned_wide = turned.astype(F32)
    step_later = later[:rows]
    bias = jnp.where(step_later, bias_ref[1:2, :], bias_ref[0:1, :])
    new_keys = []
    for step in range(STEPS):
        part = fresh[:KV_HEADS, step, :]
        new = part * cos_ref[step : step + 1, :] + pltpu.roll(part, half, 1) * sin_ref[step : step + 1, :]
        new_keys.append(new.astype(BF16).astype(F32))
    for head in range(KV_HEADS):
        lanes = slice(head * HEAD_DIM, (head + 1) * HEAD_DIM)
        mine = slice(head * rows, (head + 1) * rows)
        scores = (
            lax.dot_general(
                turned[mine], keys_ref[:, lanes], (((1,), (1,)), ((), ())),
                preferred_element_type=F32,
            )
            * score_scale
            + bias
        )
        recent0 = (
            jnp.sum(turned_wide[mine] * new_keys[0][head : head + 1, :], axis=1, keepdims=True)
            * score_scale
        )
        recent1 = (
            jnp.sum(turned_wide[mine] * new_keys[1][head : head + 1, :], axis=1, keepdims=True)
            * score_scale
        )
        recent1 = jnp.where(step_later, recent1, -1e30)
        largest = jnp.maximum(
            jnp.max(scores, axis=1, keepdims=True), jnp.maximum(recent0, recent1)
        )
        cache_exp = jnp.exp(scores - largest)
        exp0 = jnp.exp(recent0 - largest)
        exp1 = jnp.exp(recent1 - largest)
        denominator = jnp.sum(cache_exp, axis=1, keepdims=True) + (exp0 + exp1)
        weights = (cache_exp / denominator).astype(BF16)
        weight0 = (exp0 / denominator).astype(BF16).astype(F32)
        weight1 = (exp1 / denominator).astype(BF16).astype(F32)
        recent = weight0 * fresh[KV_HEADS + head, 0:1, :]
        recent = recent + weight1 * fresh[KV_HEADS + head, 1:2, :]
        if not fast:
            values = pages_ref[:, :, lanes].reshape(keys_ref.shape[0], HEAD_DIM)
            mixed = jnp.dot(weights, values, preferred_element_type=F32)
            out_ref[mine, :] = (mixed + recent).astype(BF16)
            continue
        weights = weights.astype(F32)
        z, x = divmod(head, 2)
        for c in range(2):
            part = slice(c * 8, (c + 1) * 8)
            for plane in range(planes):
                out_scr[plane * PLANE + 2 * x + c, z * 8 : (z + 1) * 8, :] = weights[
                    part, plane * LANES : (plane + 1) * LANES
                ]
            out_scr[z * PLANE + 2 * x + c, planes * 8 : planes * 8 + 8, :] = recent[part]
    if fast:
        out_ref[...] = out_scr[...].astype(BF16)


def attend(columns, keys, bias, cosine, sine, pages, fast):
    seq, width = keys.shape
    count = columns.shape[0]
    if fast:
        shape = (count, count // PLANE * 8 + 16, LANES)
        scratch = [VMEM(shape, F32)]
        operands = (columns, keys, bias, cosine, sine)
    else:
        shape = (STEPS * HEADS, HEAD_DIM)
        scratch = [VMEM((8, LANES), F32)]
        operands = (columns, keys, bias, cosine, sine, pages)
    return pl.pallas_call(
        functools.partial(attend_kernel, fast),
        in_specs=[whole()] * len(operands),
        out_specs=whole(),
        out_shape=jax.ShapeDtypeStruct(shape, BF16),
        scratch_shapes=scratch,
        compiler_params=pltpu.CompilerParams(vmem_limit_bytes=48 * 2**20),
        cost_estimate=pl.CostEstimate(
            flops=4 * STEPS * HEADS * seq * HEAD_DIM,
            bytes_accessed=4 * seq * width,
            transcendentals=STEPS * HEADS * seq,
        ),
        name="attend",
    )(*operands)


def output_kernel(fast, count, me_ref, weight_ref, last_ref, *rest):
    lhs_refs, rest = rest[:count], rest[count:]
    out_refs, (head_buf, out_scr, heads_scr, sem) = rest[:-4], rest[-4:]
    width = head_buf.shape[1]
    depth = head_buf.shape[0] // sem.shape[0]
    head_copies = []
    for i in range(sem.shape[0]):
        mine = pl.ds(i * depth, depth)
        head_copies.append(
            pltpu.make_async_copy(
                weight_ref.at[mine, pl.ds(0, width)], head_buf.at[mine, :], sem.at[i]
            )
        )
        head_copies[-1].start()
    chunks = 8
    span = weight_ref.shape[1] // chunks
    rows = out_scr.shape[0] * LANES // (chunks * span)
    pieces = chunks * span // LANES
    if fast:
        per = heads_scr.shape[0] // rows
        total = lhs_refs[0][...].astype(F32)
        for lhs_ref in lhs_refs[1:]:
            total = total + lhs_ref[...].astype(F32)
        heads_scr[...] = total
        lhs = jnp.concatenate(
            [heads_scr[pl.ds(g, rows, stride=per), :].astype(BF16) for g in range(per)], axis=1
        )
    else:
        lhs = lhs_refs[0][...]
    first = width // span
    for i in (*range(first, chunks), *range(first)):
        if i == 0:
            for copy in head_copies:
                copy.wait()
        source, place = (last_ref, i - first) if i >= first else (head_buf, i)
        part = jnp.dot(
            lhs, source[:, place * span : (place + 1) * span], preferred_element_type=F32
        )
        for c in range(span // LANES):
            out_scr[pl.ds(i * (span // LANES) + c, rows, stride=pieces), :] = part[
                :, c * LANES : (c + 1) * LANES
            ]
    if not fast:
        out_refs[0][...] = out_scr[...].astype(BF16)
        return
    low = jnp.bitwise_and(me_ref[0], 1)
    for out_ref, core in zip(out_refs, (low, 1 - low)):
        count, size, _ = out_ref.shape
        for j in range(count):
            part = pl.ds(pl.multiple_of((2 * j + core) * size, size), size)
            out_ref[j] = out_scr[part, :].astype(BF16)


def output(me, lhs, weight, last, rows, fast):
    depth, width = weight.shape
    if fast:
        shape = (rows // (2 * STEPS), STEPS * width // LANES, LANES)
        shapes = (jax.ShapeDtypeStruct(shape, BF16),) * 2
    else:
        shapes = (jax.ShapeDtypeStruct((rows * width // LANES, LANES), BF16),)
    return pl.pallas_call(
        functools.partial(output_kernel, fast, len(lhs)),
        in_specs=[whole(SMEM), whole(pl.ANY)] + [whole()] * (1 + len(lhs)),
        out_specs=(whole(),) * len(shapes),
        out_shape=shapes,
        scratch_shapes=[
            VMEM((depth, width - last.shape[1]), BF16),
            VMEM((rows * width // LANES, LANES), F32),
            VMEM(lhs[0].shape if fast else (8, LANES), F32),
            pltpu.SemaphoreType.DMA((4 if fast else 1,)),
        ],
        compiler_params=pltpu.CompilerParams(vmem_limit_bytes=46 * 2**20),
        cost_estimate=pl.CostEstimate(
            flops=2 * rows * depth * width, bytes_accessed=2 * depth * width, transcendentals=0
        ),
        name="output_project",
    )(me, weight, last, *lhs)


def swap(block, bit, devices):
    return lax.ppermute(block, AXIS, [(i, i ^ bit) for i in range(devices)])


def exchange(blocks, groups=None):
    return lax.all_to_all(
        blocks, AXIS, split_axis=0, concat_axis=0, tiled=True, axis_index_groups=groups
    )


def local(
    hidden,
    norm_gain,
    query_weight,
    kv_weight,
    out_weight,
    key_factors,
    key_basis,
    value_store,
    lengths,
    block_slot,
    selection,
):
    devices = lax.axis_size(AXIS)
    me = lax.axis_index(AXIS)
    slots_dev, block_len, width = value_store.shape
    seq = key_factors.shape[1]
    pages = block_slot.shape[1]
    model = hidden.shape[2]
    q_cols = query_weight.shape[1]
    k_cols = kv_weight.shape[1]
    fast = devices == 2 * PAIRS and q_cols == 4 * HEAD_DIM and k_cols == HEAD_DIM
    pieces = model // LANES

    me_word = me.astype(jnp.int32).reshape(1)
    block, holder, pair = prepare(
        hidden[:, 0], norm_gain.reshape(pieces, LANES), block_slot, slots_dev, PAIRS if fast else 1
    )
    if fast:
        same_core = [list(range(core, devices, 2)) for core in range(2)]
        block = exchange(block, same_core)
        block, kv_weight = lax.optimization_barrier((block, kv_weight))
        kv_weight = fetch(kv_weight, 50, k_cols)
        other = swap(block, 1, devices)
        order = None
        x = lax.bitwise_and(lax.shift_right_logical(me_word, 1), 1)
        keep, send = split_values(x, value_store)
        neighbour = swap(send, 2, devices)
    else:
        order = [0]
        bit = devices // 2
        while bit:
            other = swap(block, bit, devices)
            order = order + [k ^ bit for k in order]
            bit //= 2
            if bit:
                block = jnp.concatenate([block, other], axis=0)
        order = tuple(order)
    span = 2 * block_len
    places = (pair[:, None] * span + jnp.arange(span, dtype=jnp.int32)[None, :]).reshape(-1)
    if not fast:
        sent_pages = pick_pages(me_word, block, other, value_store, order)
        block, other, sent_pages = lax.optimization_barrier((block, other, sent_pages))
        fetched = exchange(sent_pages)
    projected = project(
        me_word, block, other, query_weight, kv_weight, order, fast
    )
    if fast:
        projected, rows = projected
        projected, places = lax.optimization_barrier((projected, places))
        columns = exchange(projected)
    else:
        targets = jnp.bitwise_xor(me, jnp.array(order, dtype=jnp.int32))
        columns = exchange(projected.reshape(devices, STEPS, q_cols + k_cols)[targets])
        query = columns[:, :, :q_cols].transpose(1, 0, 2).reshape(STEPS, HEADS // 4, 4, HEAD_DIM)
        query = query.transpose(1, 0, 2, 3).reshape(HEADS // 4, 8, HEAD_DIM)
        fresh = columns[:, :, q_cols:].transpose(1, 0, 2).reshape(STEPS, HEADS // 4, HEAD_DIM)
        fresh = jnp.pad(fresh.transpose(1, 0, 2), ((0, 0), (0, 8 - STEPS), (0, 0)))
        columns = jnp.concatenate([query, fresh], axis=1)

    cosine, sine = turn_tables(places.astype(F32))
    keys = make_keys(pair, key_factors[0], key_basis[0], cosine, sine)
    picked = jnp.any(
        selection[:, 0, :, None] == (places // block_len)[None, None, :], axis=1
    )
    bias = jnp.where(picked & (places < lengths[0])[None, :], 0.0, -1e30).astype(F32)
    new_cos, new_sin = turn_tables(
        (lengths[0] + jnp.arange(STEPS, dtype=jnp.int32)).astype(F32)
    )
    if fast:
        blocks = attend(columns, keys, bias, new_cos, new_sin, None, True)
        blocks, neighbour = lax.optimization_barrier((blocks, neighbour))
        stores = (keep, swap(keep, 1, devices), neighbour, swap(neighbour, 1, devices))
        blocks = exchange(blocks)
        parts = mix(me_word, rows, blocks, stores)
        (*parts, out_weight) = lax.optimization_barrier((*parts, out_weight))
        last_weight = fetch(out_weight, 43, model - model // 4)
        lhs = [parts[0]] + [swap(parts[q], q * PLANE, devices) for q in range(1, len(parts))]
    else:
        heads = attend(columns, keys, bias, new_cos, new_sin, fetched, False)
        flat = heads.reshape(HEADS // 4, STEPS, 4 * HEAD_DIM).transpose(1, 0, 2)
        flat = flat.reshape(STEPS, devices, model // devices).transpose(1, 0, 2)
        lhs = [exchange(flat).reshape(devices * STEPS, model // devices)]
        last_weight = out_weight[:, model // 4 :]
    partial = output(me_word, lhs, out_weight, last_weight, devices * STEPS, fast)
    if fast:
        near, far = partial
        both = near.astype(F32) + swap(far, 1, devices).astype(F32)
        arrived = exchange(both.astype(BF16), same_core)
    else:
        arrived = exchange(partial[0].reshape(devices, STEPS * pieces, LANES))
    total = jnp.sum(arrived.astype(F32), axis=0).astype(BF16)
    return total.reshape(STEPS, 1, model)


def solution(mesh):
    return jax.shard_map(
        local,
        mesh=mesh,
        in_specs=(
            P(None, ("groups", "session"), None),
            P(),
            P(None, "session"),
            P(None, "session"),
            P("session", None),
            P(("groups", "session"), None, None),
            P(("groups", "session"), None, None),
            P(("groups", "session"), None, None),
            P(("groups", "session")),
            P(("groups", "session"), None),
            P(None, ("groups", "session"), None),
        ),
        out_specs=P(None, ("groups", "session"), None),
        check_vma=False,
    )
```

```python
import functools
import math

import jax
import jax.numpy as jnp
from jax import lax
from jax.experimental import pallas as pl
from jax.experimental.pallas import tpu as pltpu
from jax.sharding import PartitionSpec as P

HEADS = 64
KV_HEADS = 8
HEAD_DIM = 128
STEPS = 2
GROUP = HEADS // KV_HEADS
LANES = 128
EXTRA = 16
PLANE = 4
PAIRS = 8
PROJECT_LIMIT = 48 * 2**20
AXIS = "session"
VMEM = pltpu.VMEM
SMEM = pltpu.SMEM
F32 = jnp.float32
BF16 = jnp.bfloat16


def angles(positions):
    half = HEAD_DIM // 2
    frequency = jnp.exp(
        -jnp.arange(half, dtype=F32) * (2.0 * math.log(500000.0) / HEAD_DIM)
    )
    return positions[..., None] * frequency


def turn_tables(positions):
    angle = angles(positions)
    cosine, sine = jnp.cos(angle), jnp.sin(angle)
    return (
        jnp.concatenate([cosine, cosine], axis=-1),
        jnp.concatenate([-sine, sine], axis=-1),
    )


def origin(me, order, j):
    if order is None:
        return 2 * (j % PAIRS) + jnp.bitwise_xor(jnp.bitwise_and(me, 1), j // PAIRS)
    return jnp.bitwise_xor(me, order[j])


def whole(space=VMEM):
    return pl.BlockSpec(memory_space=space)


def prepare_kernel(
    slots_dev, hidden_ref, gain_ref, slots_ref, block_ref, holder_ref, pair_ref, wide_scr
):
    steps, model = hidden_ref.shape
    pieces = model // LANES
    wide = hidden_ref[...].astype(F32)
    scale = lax.rsqrt(jnp.mean(wide * wide, axis=1, keepdims=True) + 1e-05)
    wide = wide * scale
    for step in range(steps):
        for c in range(pieces):
            row = step * pieces + c
            wide_scr[row : row + 1, :] = wide[step : step + 1, c * LANES : (c + 1) * LANES]
    lane = lax.broadcasted_iota(jnp.int32, (EXTRA, LANES), 1)
    parity = lax.broadcasted_iota(jnp.int32, (EXTRA, LANES), 0)
    table = jnp.zeros((EXTRA, LANES), jnp.int32)
    for m in range(holder_ref.shape[0]):
        slot = slots_ref[0, 2 * m]
        holder = lax.div(slot, slots_dev)
        holder_ref[m] = holder
        pair_ref[holder] = m
        base = holder * slots_dev
        pair = jnp.where(parity == 0, slot - base, slots_ref[0, 2 * m + 1] - base)
        table = jnp.where(lane == holder, pair, table)
    wide_scr[steps * pieces :, :] = table.astype(F32)
    gain = gain_ref[...].astype(F32)
    for step in range(steps):
        rows = slice(step * pieces, (step + 1) * pieces)
        wide_scr[rows, :] = wide_scr[rows, :] * gain
    block = wide_scr[...].astype(BF16)
    for copy in range(block_ref.shape[0]):
        block_ref[copy] = block


def prepare(hidden, gain, block_slot, slots_dev, copies):
    assert slots_dev <= 256
    steps, model = hidden.shape
    rows = steps * model // LANES + EXTRA
    return pl.pallas_call(
        functools.partial(prepare_kernel, slots_dev),
        in_specs=[whole(), whole(), whole(SMEM)],
        out_specs=(whole(), whole(SMEM), whole(SMEM)),
        out_shape=(
            jax.ShapeDtypeStruct((copies, rows, LANES), BF16),
            jax.ShapeDtypeStruct((block_slot.shape[1] // 2,), jnp.int32),
            jax.ShapeDtypeStruct((block_slot.shape[1] // 2,), jnp.int32),
        ),
        scratch_shapes=[VMEM((rows, LANES), F32)],
        name="prepare",
    )(hidden, gain, block_slot)


def pick_kernel(order, me_ref, first_ref, second_ref, store_ref, out_ref, table_scr, table_smem, sem):
    block_len = store_ref.shape[1]
    half, rows, _ = first_ref.shape
    for j in range(2 * half):
        source = first_ref if j < half else second_ref
        asked = source[j % half, rows - EXTRA :, :].astype(F32)
        table_scr[j] = asked[:8].astype(jnp.int32)
    copy = pltpu.make_async_copy(table_scr, table_smem, sem)
    copy.start()
    copy.wait()
    me = me_ref[0]
    for j in range(2 * half):
        target = origin(me, order, j)
        for k in range(2):
            out_ref[target, k * block_len : (k + 1) * block_len, :] = store_ref[
                table_smem[j, k, me]
            ]


def pick_pages(me, first, second, store, order):
    count = 2 * first.shape[0]
    _, block_len, width = store.shape
    return pl.pallas_call(
        functools.partial(pick_kernel, order),
        in_specs=[whole(SMEM), whole(), whole(), whole()],
        out_specs=whole(),
        out_shape=jax.ShapeDtypeStruct((count, 2 * block_len, width), store.dtype),
        scratch_shapes=[
            VMEM((count, 8, LANES), jnp.int32),
            SMEM((count, 8, LANES), jnp.int32),
            pltpu.SemaphoreType.DMA(()),
        ],
        compiler_params=pltpu.CompilerParams(vmem_limit_bytes=36 * 2**20),
        name="pick_pages",
    )(me, first, second, store)


def split_kernel(x_ref, store_ref, keep_ref, send_ref):
    slots, block_len, width = store_ref.shape
    for x in range(2):

        @pl.when(x_ref[0] == x)
        def _():
            for head in range(width // LANES):
                target = keep_ref if head % 2 == x else send_ref
                lanes = slice(head // 2 * LANES, (head // 2 + 1) * LANES)
                part = store_ref[:, :, head * LANES : (head + 1) * LANES]
                target[:, lanes] = part.reshape(slots * block_len, LANES)


def split_values(x, store):
    slots, block_len, width = store.shape
    half = jax.ShapeDtypeStruct((slots * block_len, width // 2), store.dtype)
    return pl.pallas_call(
        split_kernel,
        in_specs=[whole(SMEM), whole()],
        out_specs=(whole(), whole()),
        out_shape=(half, half),
        compiler_params=pltpu.CompilerParams(vmem_limit_bytes=16 * 2**20),
        name="split_values",
    )(x, store)


def mix_kernel(me_ref, rows_ref, weights_ref, *rest):
    stores, (values_scr, sum_scr) = rest[:PLANE], rest[-2:]
    out_refs = rest[PLANE:-2]
    me = me_ref[0]
    low = jnp.bitwise_and(me, PLANE - 1)
    z_me = lax.div(me, PLANE)
    sessions = weights_ref.shape[0]
    planes = len(out_refs)
    block_len = values_scr.shape[1] // (2 * PLANE)
    for session in range(sessions):
        for q, store in enumerate(stores):
            device = jnp.bitwise_xor(low, q)
            for k in range(2):
                row = rows_ref[session * (2 * PLANE) + k * PLANE + device]
                source = pl.ds(pl.multiple_of(row * block_len, block_len), block_len)
                target = pl.ds(
                    pl.multiple_of((device * 2 + k) * block_len, block_len), block_len
                )
                values_scr[session, target, :] = store[source, :]
        block = weights_ref[session]
        product = jnp.dot(
            block[: planes * 8], values_scr[session], preferred_element_type=F32
        )
        mine = slice(session * 8, (session + 1) * 8)
        for z in range(planes):
            sum_scr[z, mine, :] = product[z * 8 : (z + 1) * 8, z * LANES : (z + 1) * LANES]
        recent = block[planes * 8 :].astype(F32)
        sum_scr[z_me, mine, :] += recent[:8]
    for q, out_ref in enumerate(out_refs):
        out_ref[...] = sum_scr[jnp.bitwise_xor(z_me, q)].astype(BF16)


def mix(me, rows, weights, stores):
    sessions = weights.shape[0]
    planes = stores[0].shape[1] // LANES
    shape = (planes, sessions * 8, LANES)
    return pl.pallas_call(
        mix_kernel,
        in_specs=[whole(SMEM)] * 2 + [whole()] * (1 + PLANE),
        out_specs=(whole(),) * planes,
        out_shape=(jax.ShapeDtypeStruct(shape[1:], BF16),) * planes,
        scratch_shapes=[VMEM((sessions, LANES, planes * LANES), BF16), VMEM(shape, F32)],
        compiler_params=pltpu.CompilerParams(vmem_limit_bytes=16 * 2**20),
        cost_estimate=pl.CostEstimate(
            flops=2 * sessions * 32 * LANES * planes * LANES,
            bytes_accessed=4 * stores[0].size * PLANE,
            transcendentals=0,
        ),
        name="mix_values",
    )(me, rows, weights, *stores)


def keys_kernel(pair_ref, factors_ref, basis_ref, cos_ref, sin_ref, out_ref, rows_scr):
    span = factors_ref.shape[0] // pair_ref.shape[0]
    count = rows_scr.shape[0] // span
    base = pl.program_id(0) * count
    for p in range(count):
        source = pl.ds(pl.multiple_of(pair_ref[base + p] * span, span), span)
        rows_scr[p * span : (p + 1) * span, :] = factors_ref[source, :]
    product = jnp.dot(rows_scr[...], basis_ref[...], preferred_element_type=F32)
    cosine, sine = cos_ref[...], sin_ref[...]
    for head in range(KV_HEADS):
        lanes = slice(head * HEAD_DIM, (head + 1) * HEAD_DIM)
        part = product[:, lanes]
        turned = part * cosine + pltpu.roll(part, HEAD_DIM // 2, 1) * sine
        out_ref[:, lanes] = turned.astype(BF16)


def make_keys(pair, factors, basis, cosine, sine):
    seq, rank = factors.shape
    width = basis.shape[1]
    rows = min(seq, 512)
    return pl.pallas_call(
        keys_kernel,
        grid=(seq // rows,),
        in_specs=[
            whole(SMEM),
            pl.BlockSpec((seq, rank), lambda i: (0, 0)),
            pl.BlockSpec((rank, width), lambda i: (0, 0)),
            pl.BlockSpec((rows, HEAD_DIM), lambda i: (i, 0)),
            pl.BlockSpec((rows, HEAD_DIM), lambda i: (i, 0)),
        ],
        out_specs=pl.BlockSpec((rows, width), lambda i: (i, 0)),
        out_shape=jax.ShapeDtypeStruct((seq, width), BF16),
        scratch_shapes=[VMEM((rows, rank), BF16)],
        compiler_params=pltpu.CompilerParams(vmem_limit_bytes=32 * 2**20),
        cost_estimate=pl.CostEstimate(
            flops=2 * seq * rank * width, bytes_accessed=4 * seq * width, transcendentals=0
        ),
        name="turned_keys",
    )(pair, factors, basis, cosine, sine)


def fetch_kernel(source_ref, target_ref, sems):
    parts = sems.shape[0]
    span = source_ref.shape[0] // parts
    copies = []
    for part in range(parts):
        rows = pl.ds(part * span, span)
        copies.append(
            pltpu.make_async_copy(source_ref.at[rows, :], target_ref.at[rows, :], sems.at[part])
        )
        copies[-1].start()
    for copy in copies:
        copy.wait()


def fetch(weight, limit):
    return pl.pallas_call(
        fetch_kernel,
        in_specs=[whole(pl.ANY)],
        out_specs=whole(pl.ANY),
        out_shape=jax.ShapeDtypeStruct(weight.shape, weight.dtype),
        scratch_shapes=[pltpu.SemaphoreType.DMA((4,))],
        compiler_params=pltpu.CompilerParams(vmem_limit_bytes=limit * 2**20),
        cost_estimate=pl.CostEstimate(
            flops=0, bytes_accessed=2 * weight.size, transcendentals=0
        ),
        name="fetch_weight",
    )(weight)


def project_kernel(
    order, fast, me_ref, first_ref, second_ref, wq_ref, wk_ref, out_ref, *rest
):
    if fast:
        rows_ref, x_scr, lhs_scr, wq_buf, out_scr, sems, *asked_scr = rest
    else:
        x_scr, lhs_scr, wq_buf, out_scr, sems = rest
    depth, q_cols = wq_ref.shape
    k_cols = wk_ref.shape[1]
    chunks = wq_buf.shape[0]
    span = depth // chunks
    pieces = depth // LANES
    copies = []
    for i in range(chunks):
        rows = pl.ds(i * span, span)
        copies.append(pltpu.make_async_copy(wq_ref.at[rows, :], wq_buf.at[i], sems.at[i]))
        copies[-1].start()
    half = first_ref.shape[0]
    count = 2 * half * STEPS
    rows = STEPS * pieces
    for j in range(2 * half):
        source = first_ref if j < half else second_ref
        x_scr[j * rows : (j + 1) * rows] = source[j % half, :rows, :].astype(F32)
    if fast:
        table_scr, table_smem, table_sem = asked_scr
        for j in range(2 * half):
            source = first_ref if j < half else second_ref
            asked = source[j % half, rows:, :].astype(F32)
            table_scr[2 * j : 2 * j + 2, :] = asked[:2].astype(jnp.int32)
        table_copy = pltpu.make_async_copy(table_scr, table_smem, table_sem)
        table_copy.start()
    for c in range(pieces):
        part = x_scr[pl.ds(c, count, stride=pieces), :]
        lhs_scr[:, c * LANES : (c + 1) * LANES] = part.astype(BF16)
    q_sum = jnp.zeros((count, q_cols), F32)
    k_sum = jnp.zeros((count, k_cols), F32)
    for i in range(chunks):
        copies[i].wait()
        lhs = lhs_scr[:, i * span : (i + 1) * span]
        q_sum = q_sum + jnp.dot(lhs, wq_buf[i], preferred_element_type=F32)
        k_sum = k_sum + jnp.dot(
            lhs, wk_ref[i * span : (i + 1) * span, :], preferred_element_type=F32
        )
    if not fast:
        out_ref[:, :q_cols] = q_sum.astype(BF16)
        out_ref[:, q_cols:] = k_sum.astype(BF16)
        return
    me = me_ref[0]
    per = q_cols // LANES
    out_scr[...] = jnp.zeros_like(out_scr)
    for j in range(2 * half):
        place = origin(me, order, j)
        for step in range(STEPS):
            row = j * STEPS + step
            for c in range(per):
                out_scr[place, step * per + c : step * per + c + 1, :] = q_sum[
                    row : row + 1, c * LANES : (c + 1) * LANES
                ]
            out_scr[place, STEPS * per + step : STEPS * per + step + 1, :] = k_sum[
                row : row + 1, :
            ]
    out_ref[...] = out_scr[...].astype(BF16)
    table_copy.wait()
    plane = jnp.bitwise_and(me, -PLANE)
    for j in range(2 * half):
        place = origin(me, order, j) * (2 * PLANE)
        for k in range(2):
            for b in range(PLANE):
                rows_ref[place + k * PLANE + b] = table_smem[2 * j + k, plane + b]


def project(me, first, second, query_weight, kv_weight, order, fast):
    depth, q_cols = query_weight.shape
    k_cols = kv_weight.shape[1]
    pieces = depth // LANES
    devices = 2 * first.shape[0]
    rows = devices * STEPS
    chunks = 8
    span = depth // chunks
    shape = (devices, 16, LANES) if fast else (rows, q_cols + k_cols)
    return pl.pallas_call(
        functools.partial(project_kernel, order, fast),
        in_specs=[whole(SMEM), whole(), whole(), whole(pl.ANY), whole()],
        out_specs=(whole(), whole(SMEM)) if fast else whole(),
        out_shape=(
            (
                jax.ShapeDtypeStruct(shape, BF16),
                jax.ShapeDtypeStruct((devices * 2 * PLANE,), jnp.int32),
            )
            if fast
            else jax.ShapeDtypeStruct(shape, BF16)
        ),
        scratch_shapes=[
            VMEM((rows * pieces, LANES), F32),
            VMEM((rows, depth), BF16),
            VMEM((chunks, span, q_cols), BF16),
            VMEM((devices, 16, LANES) if fast else (8, LANES), F32),
            pltpu.SemaphoreType.DMA((chunks,)),
        ]
        + (
            [
                VMEM((2 * devices, LANES), jnp.int32),
                SMEM((2 * devices, LANES), jnp.int32),
                pltpu.SemaphoreType.DMA(()),
            ]
            if fast
            else []
        ),
        compiler_params=pltpu.CompilerParams(vmem_limit_bytes=PROJECT_LIMIT),
        cost_estimate=pl.CostEstimate(
            flops=2 * rows * depth * (q_cols + k_cols),
            bytes_accessed=2 * depth * (q_cols + k_cols),
            transcendentals=0,
        ),
        name="norm_project",
    )(me, first, second, query_weight, kv_weight)


def attend_kernel(fast, columns_ref, keys_ref, bias_ref, cos_ref, sin_ref, *rest):
    pages_ref, out_ref, out_scr = (None, *rest) if fast else rest
    score_scale = 1.0 / math.sqrt(HEAD_DIM)
    half = HEAD_DIM // 2
    rows = 2 * GROUP
    columns = columns_ref[...].astype(F32)
    count = columns.shape[0]
    query = columns[:, :8, :].reshape(count * 8, HEAD_DIM)
    fresh = columns[:, 8:, :]
    if fast:
        planes = count // PLANE
        out_scr[...] = jnp.zeros_like(out_scr)
    row_step = lax.rem(lax.broadcasted_iota(jnp.int32, (count * 8, 1), 0) // 4, STEPS)
    later = row_step == 1
    cosine = jnp.where(later, cos_ref[1:2, :], cos_ref[0:1, :])
    sine = jnp.where(later, sin_ref[1:2, :], sin_ref[0:1, :])
    turned = (query * cosine + pltpu.roll(query, half, 1) * sine).astype(BF16)
    turned_wide = turned.astype(F32)
    step_later = later[:rows]
    bias = jnp.where(step_later, bias_ref[1:2, :], bias_ref[0:1, :])
    new_keys = []
    for step in range(STEPS):
        part = fresh[:KV_HEADS, step, :]
        new = part * cos_ref[step : step + 1, :] + pltpu.roll(part, half, 1) * sin_ref[step : step + 1, :]
        new_keys.append(new.astype(BF16).astype(F32))
    for head in range(KV_HEADS):
        lanes = slice(head * HEAD_DIM, (head + 1) * HEAD_DIM)
        mine = slice(head * rows, (head + 1) * rows)
        scores = (
            lax.dot_general(
                turned[mine], keys_ref[:, lanes], (((1,), (1,)), ((), ())),
                preferred_element_type=F32,
            )
            * score_scale
            + bias
        )
        recent0 = (
            jnp.sum(turned_wide[mine] * new_keys[0][head : head + 1, :], axis=1, keepdims=True)
            * score_scale
        )
        recent1 = (
            jnp.sum(turned_wide[mine] * new_keys[1][head : head + 1, :], axis=1, keepdims=True)
            * score_scale
        )
        recent1 = jnp.where(step_later, recent1, -1e30)
        largest = jnp.maximum(
            jnp.max(scores, axis=1, keepdims=True), jnp.maximum(recent0, recent1)
        )
        cache_exp = jnp.exp(scores - largest)
        exp0 = jnp.exp(recent0 - largest)
        exp1 = jnp.exp(recent1 - largest)
        denominator = jnp.sum(cache_exp, axis=1, keepdims=True) + (exp0 + exp1)
        weights = (cache_exp / denominator).astype(BF16)
        weight0 = (exp0 / denominator).astype(BF16).astype(F32)
        weight1 = (exp1 / denominator).astype(BF16).astype(F32)
        recent = weight0 * fresh[KV_HEADS + head, 0:1, :]
        recent = recent + weight1 * fresh[KV_HEADS + head, 1:2, :]
        if not fast:
            values = pages_ref[:, :, lanes].reshape(keys_ref.shape[0], HEAD_DIM)
            mixed = jnp.dot(weights, values, preferred_element_type=F32)
            out_ref[mine, :] = (mixed + recent).astype(BF16)
            continue
        weights = weights.astype(F32)
        z, x = divmod(head, 2)
        for c in range(2):
            part = slice(c * 8, (c + 1) * 8)
            for plane in range(planes):
                out_scr[plane * PLANE + 2 * x + c, z * 8 : (z + 1) * 8, :] = weights[
                    part, plane * LANES : (plane + 1) * LANES
                ]
            out_scr[z * PLANE + 2 * x + c, planes * 8 : planes * 8 + 8, :] = recent[part]
    if fast:
        out_ref[...] = out_scr[...].astype(BF16)


def attend(columns, keys, bias, cosine, sine, pages, fast):
    seq, width = keys.shape
    count = columns.shape[0]
    if fast:
        shape = (count, count // PLANE * 8 + 16, LANES)
        scratch = [VMEM(shape, F32)]
        operands = (columns, keys, bias, cosine, sine)
    else:
        shape = (STEPS * HEADS, HEAD_DIM)
        scratch = [VMEM((8, LANES), F32)]
        operands = (columns, keys, bias, cosine, sine, pages)
    return pl.pallas_call(
        functools.partial(attend_kernel, fast),
        in_specs=[whole()] * len(operands),
        out_specs=whole(),
        out_shape=jax.ShapeDtypeStruct(shape, BF16),
        scratch_shapes=scratch,
        compiler_params=pltpu.CompilerParams(vmem_limit_bytes=48 * 2**20),
        cost_estimate=pl.CostEstimate(
            flops=4 * STEPS * HEADS * seq * HEAD_DIM,
            bytes_accessed=4 * seq * width,
            transcendentals=STEPS * HEADS * seq,
        ),
        name="attend",
    )(*operands)


def output_kernel(fast, count, me_ref, weight_ref, *rest):
    lhs_refs, rest = rest[:count], rest[count:]
    out_refs, (out_scr, heads_scr) = rest[:-2], rest[-2:]
    chunks = 8
    span = weight_ref.shape[1] // chunks
    rows = out_scr.shape[0] * LANES // (chunks * span)
    pieces = chunks * span // LANES
    if fast:
        per = heads_scr.shape[0] // rows
        total = lhs_refs[0][...].astype(F32)
        for lhs_ref in lhs_refs[1:]:
            total = total + lhs_ref[...].astype(F32)
        heads_scr[...] = total
        lhs = jnp.concatenate(
            [heads_scr[pl.ds(g, rows, stride=per), :].astype(BF16) for g in range(per)], axis=1
        )
    else:
        lhs = lhs_refs[0][...]
    for i in range(chunks):
        part = jnp.dot(
            lhs, weight_ref[:, i * span : (i + 1) * span], preferred_element_type=F32
        )
        for c in range(span // LANES):
            out_scr[pl.ds(i * (span // LANES) + c, rows, stride=pieces), :] = part[
                :, c * LANES : (c + 1) * LANES
            ]
    if not fast:
        out_refs[0][...] = out_scr[...].astype(BF16)
        return
    low = jnp.bitwise_and(me_ref[0], 1)
    for out_ref, core in zip(out_refs, (low, 1 - low)):
        count, size, _ = out_ref.shape
        for j in range(count):
            part = pl.ds(pl.multiple_of((2 * j + core) * size, size), size)
            out_ref[j] = out_scr[part, :].astype(BF16)


def output(me, lhs, weight, rows, fast):
    depth, width = weight.shape
    if fast:
        shape = (rows // (2 * STEPS), STEPS * width // LANES, LANES)
        shapes = (jax.ShapeDtypeStruct(shape, BF16),) * 2
    else:
        shapes = (jax.ShapeDtypeStruct((rows * width // LANES, LANES), BF16),)
    return pl.pallas_call(
        functools.partial(output_kernel, fast, len(lhs)),
        in_specs=[whole(SMEM)] + [whole()] * (1 + len(lhs)),
        out_specs=(whole(),) * len(shapes),
        out_shape=shapes,
        scratch_shapes=[
            VMEM((rows * width // LANES, LANES), F32),
            VMEM(lhs[0].shape if fast else (8, LANES), F32),
        ],
        compiler_params=pltpu.CompilerParams(vmem_limit_bytes=24 * 2**20),
        cost_estimate=pl.CostEstimate(
            flops=2 * rows * depth * width, bytes_accessed=2 * depth * width, transcendentals=0
        ),
        name="output_project",
    )(me, weight, *lhs)


def swap(block, bit, devices):
    return lax.ppermute(block, AXIS, [(i, i ^ bit) for i in range(devices)])


def exchange(blocks, groups=None):
    return lax.all_to_all(
        blocks, AXIS, split_axis=0, concat_axis=0, tiled=True, axis_index_groups=groups
    )


def local(
    hidden,
    norm_gain,
    query_weight,
    kv_weight,
    out_weight,
    key_factors,
    key_basis,
    value_store,
    lengths,
    block_slot,
    selection,
):
    devices = lax.axis_size(AXIS)
    me = lax.axis_index(AXIS)
    slots_dev, block_len, width = value_store.shape
    seq = key_factors.shape[1]
    pages = block_slot.shape[1]
    model = hidden.shape[2]
    q_cols = query_weight.shape[1]
    k_cols = kv_weight.shape[1]
    fast = devices == 2 * PAIRS and q_cols == 4 * HEAD_DIM and k_cols == HEAD_DIM
    pieces = model // LANES

    me_word = me.astype(jnp.int32).reshape(1)
    block, holder, pair = prepare(
        hidden[:, 0], norm_gain.reshape(pieces, LANES), block_slot, slots_dev, PAIRS if fast else 1
    )
    if fast:
        same_core = [list(range(core, devices, 2)) for core in range(2)]
        block = exchange(block, same_core)
        block, kv_weight = lax.optimization_barrier((block, kv_weight))
        kv_weight = fetch(kv_weight, 50)
        other = swap(block, 1, devices)
        order = None
        x = lax.bitwise_and(lax.shift_right_logical(me_word, 1), 1)
        keep, send = split_values(x, value_store)
        neighbour = swap(send, 2, devices)
    else:
        order = [0]
        bit = devices // 2
        while bit:
            other = swap(block, bit, devices)
            order = order + [k ^ bit for k in order]
            bit //= 2
            if bit:
                block = jnp.concatenate([block, other], axis=0)
        order = tuple(order)
    span = 2 * block_len
    places = (pair[:, None] * span + jnp.arange(span, dtype=jnp.int32)[None, :]).reshape(-1)
    if not fast:
        sent_pages = pick_pages(me_word, block, other, value_store, order)
        block, other, sent_pages = lax.optimization_barrier((block, other, sent_pages))
        fetched = exchange(sent_pages)
    projected = project(
        me_word, block, other, query_weight, kv_weight, order, fast
    )
    if fast:
        projected, rows = projected
        projected, places = lax.optimization_barrier((projected, places))
        columns = exchange(projected)
    else:
        targets = jnp.bitwise_xor(me, jnp.array(order, dtype=jnp.int32))
        columns = exchange(projected.reshape(devices, STEPS, q_cols + k_cols)[targets])
        query = columns[:, :, :q_cols].transpose(1, 0, 2).reshape(STEPS, HEADS // 4, 4, HEAD_DIM)
        query = query.transpose(1, 0, 2, 3).reshape(HEADS // 4, 8, HEAD_DIM)
        fresh = columns[:, :, q_cols:].transpose(1, 0, 2).reshape(STEPS, HEADS // 4, HEAD_DIM)
        fresh = jnp.pad(fresh.transpose(1, 0, 2), ((0, 0), (0, 8 - STEPS), (0, 0)))
        columns = jnp.concatenate([query, fresh], axis=1)

    cosine, sine = turn_tables(places.astype(F32))
    keys = make_keys(pair, key_factors[0], key_basis[0], cosine, sine)
    picked = jnp.any(
        selection[:, 0, :, None] == (places // block_len)[None, None, :], axis=1
    )
    bias = jnp.where(picked & (places < lengths[0])[None, :], 0.0, -1e30).astype(F32)
    new_cos, new_sin = turn_tables(
        (lengths[0] + jnp.arange(STEPS, dtype=jnp.int32)).astype(F32)
    )
    if fast:
        blocks = attend(columns, keys, bias, new_cos, new_sin, None, True)
        blocks, neighbour = lax.optimization_barrier((blocks, neighbour))
        stores = (keep, swap(keep, 1, devices), neighbour, swap(neighbour, 1, devices))
        blocks = exchange(blocks)
        parts = mix(me_word, rows, blocks, stores)
        (*parts, out_weight) = lax.optimization_barrier((*parts, out_weight))
        out_weight = fetch(out_weight, 43)
        lhs = [parts[0]] + [swap(parts[q], q * PLANE, devices) for q in range(1, len(parts))]
    else:
        heads = attend(columns, keys, bias, new_cos, new_sin, fetched, False)
        flat = heads.reshape(HEADS // 4, STEPS, 4 * HEAD_DIM).transpose(1, 0, 2)
        flat = flat.reshape(STEPS, devices, model // devices).transpose(1, 0, 2)
        lhs = [exchange(flat).reshape(devices * STEPS, model // devices)]
    partial = output(me_word, lhs, out_weight, devices * STEPS, fast)
    if fast:
        near, far = partial
        both = near.astype(F32) + swap(far, 1, devices).astype(F32)
        arrived = exchange(both.astype(BF16), same_core)
    else:
        arrived = exchange(partial[0].reshape(devices, STEPS * pieces, LANES))
    total = jnp.sum(arrived.astype(F32), axis=0).astype(BF16)
    return total.reshape(STEPS, 1, model)


def solution(mesh):
    return jax.shard_map(
        local,
        mesh=mesh,
        in_specs=(
            P(None, ("groups", "session"), None),
            P(),
            P(None, "session"),
            P(None, "session"),
            P("session", None),
            P(("groups", "session"), None, None),
            P(("groups", "session"), None, None),
            P(("groups", "session"), None, None),
            P(("groups", "session")),
            P(("groups", "session"), None),
            P(None, ("groups", "session"), None),
        ),
        out_specs=P(None, ("groups", "session"), None),
        check_vma=False,
    )
```

```python
import functools
import math

import jax
import jax.numpy as jnp
from jax import lax
from jax.experimental import pallas as pl
from jax.experimental.pallas import tpu as pltpu
from jax.sharding import PartitionSpec as P

HEADS = 64
KV_HEADS = 8
HEAD_DIM = 128
STEPS = 2
GROUP = HEADS // KV_HEADS
LANES = 128
EXTRA = 16
PLANE = 4
PAIRS = 8
PROJECT_LIMIT = 48 * 2**20
AXIS = "session"
VMEM = pltpu.VMEM
SMEM = pltpu.SMEM
F32 = jnp.float32
BF16 = jnp.bfloat16


def angles(positions):
    half = HEAD_DIM // 2
    frequency = jnp.exp(
        -jnp.arange(half, dtype=F32) * (2.0 * math.log(500000.0) / HEAD_DIM)
    )
    return positions[..., None] * frequency


def turn_tables(positions):
    angle = angles(positions)
    cosine, sine = jnp.cos(angle), jnp.sin(angle)
    return (
        jnp.concatenate([cosine, cosine], axis=-1),
        jnp.concatenate([-sine, sine], axis=-1),
    )


def origin(me, order, j):
    if order is None:
        return 2 * (j % PAIRS) + jnp.bitwise_xor(jnp.bitwise_and(me, 1), j // PAIRS)
    return jnp.bitwise_xor(me, order[j])


def whole(space=VMEM):
    return pl.BlockSpec(memory_space=space)


def prepare_kernel(
    slots_dev, hidden_ref, gain_ref, slots_ref, block_ref, holder_ref, pair_ref, wide_scr
):
    steps, model = hidden_ref.shape
    pieces = model // LANES
    wide = hidden_ref[...].astype(F32)
    scale = lax.rsqrt(jnp.mean(wide * wide, axis=1, keepdims=True) + 1e-05)
    wide = wide * scale
    for step in range(steps):
        for c in range(pieces):
            row = step * pieces + c
            wide_scr[row : row + 1, :] = wide[step : step + 1, c * LANES : (c + 1) * LANES]
    lane = lax.broadcasted_iota(jnp.int32, (EXTRA, LANES), 1)
    parity = lax.broadcasted_iota(jnp.int32, (EXTRA, LANES), 0)
    table = jnp.zeros((EXTRA, LANES), jnp.int32)
    for m in range(holder_ref.shape[0]):
        slot = slots_ref[0, 2 * m]
        holder = lax.div(slot, slots_dev)
        holder_ref[m] = holder
        pair_ref[holder] = m
        base = holder * slots_dev
        pair = jnp.where(parity == 0, slot - base, slots_ref[0, 2 * m + 1] - base)
        table = jnp.where(lane == holder, pair, table)
    wide_scr[steps * pieces :, :] = table.astype(F32)
    gain = gain_ref[...].astype(F32)
    for step in range(steps):
        rows = slice(step * pieces, (step + 1) * pieces)
        wide_scr[rows, :] = wide_scr[rows, :] * gain
    block = wide_scr[...].astype(BF16)
    for copy in range(block_ref.shape[0]):
        block_ref[copy] = block


def prepare(hidden, gain, block_slot, slots_dev, copies):
    assert slots_dev <= 256
    steps, model = hidden.shape
    rows = steps * model // LANES + EXTRA
    return pl.pallas_call(
        functools.partial(prepare_kernel, slots_dev),
        in_specs=[whole(), whole(), whole(SMEM)],
        out_specs=(whole(), whole(SMEM), whole(SMEM)),
        out_shape=(
            jax.ShapeDtypeStruct((copies, rows, LANES), BF16),
            jax.ShapeDtypeStruct((block_slot.shape[1] // 2,), jnp.int32),
            jax.ShapeDtypeStruct((block_slot.shape[1] // 2,), jnp.int32),
        ),
        scratch_shapes=[VMEM((rows, LANES), F32)],
        name="prepare",
    )(hidden, gain, block_slot)


def pick_kernel(order, me_ref, first_ref, second_ref, store_ref, out_ref, table_scr, table_smem, sem):
    block_len = store_ref.shape[1]
    half, rows, _ = first_ref.shape
    for j in range(2 * half):
        source = first_ref if j < half else second_ref
        asked = source[j % half, rows - EXTRA :, :].astype(F32)
        table_scr[j] = asked[:8].astype(jnp.int32)
    copy = pltpu.make_async_copy(table_scr, table_smem, sem)
    copy.start()
    copy.wait()
    me = me_ref[0]
    for j in range(2 * half):
        target = origin(me, order, j)
        for k in range(2):
            out_ref[target, k * block_len : (k + 1) * block_len, :] = store_ref[
                table_smem[j, k, me]
            ]


def pick_pages(me, first, second, store, order):
    count = 2 * first.shape[0]
    _, block_len, width = store.shape
    return pl.pallas_call(
        functools.partial(pick_kernel, order),
        in_specs=[whole(SMEM), whole(), whole(), whole()],
        out_specs=whole(),
        out_shape=jax.ShapeDtypeStruct((count, 2 * block_len, width), store.dtype),
        scratch_shapes=[
            VMEM((count, 8, LANES), jnp.int32),
            SMEM((count, 8, LANES), jnp.int32),
            pltpu.SemaphoreType.DMA(()),
        ],
        compiler_params=pltpu.CompilerParams(vmem_limit_bytes=36 * 2**20),
        name="pick_pages",
    )(me, first, second, store)


def split_kernel(x_ref, store_ref, keep_ref, send_ref):
    slots, block_len, width = store_ref.shape
    for x in range(2):

        @pl.when(x_ref[0] == x)
        def _():
            for head in range(width // LANES):
                target = keep_ref if head % 2 == x else send_ref
                lanes = slice(head // 2 * LANES, (head // 2 + 1) * LANES)
                part = store_ref[:, :, head * LANES : (head + 1) * LANES]
                target[:, lanes] = part.reshape(slots * block_len, LANES)


def split_values(x, store):
    slots, block_len, width = store.shape
    half = jax.ShapeDtypeStruct((slots * block_len, width // 2), store.dtype)
    return pl.pallas_call(
        split_kernel,
        in_specs=[whole(SMEM), whole()],
        out_specs=(whole(), whole()),
        out_shape=(half, half),
        compiler_params=pltpu.CompilerParams(vmem_limit_bytes=16 * 2**20),
        name="split_values",
    )(x, store)


def mix_kernel(me_ref, rows_ref, weights_ref, *rest):
    stores, (values_scr, sum_scr) = rest[:PLANE], rest[-2:]
    out_refs = rest[PLANE:-2]
    me = me_ref[0]
    low = jnp.bitwise_and(me, PLANE - 1)
    z_me = lax.div(me, PLANE)
    sessions = weights_ref.shape[0]
    planes = len(out_refs)
    block_len = values_scr.shape[1] // (2 * PLANE)
    for session in range(sessions):
        for q, store in enumerate(stores):
            device = jnp.bitwise_xor(low, q)
            for k in range(2):
                row = rows_ref[session * (2 * PLANE) + k * PLANE + device]
                source = pl.ds(pl.multiple_of(row * block_len, block_len), block_len)
                target = pl.ds(
                    pl.multiple_of((device * 2 + k) * block_len, block_len), block_len
                )
                values_scr[session, target, :] = store[source, :]
        block = weights_ref[session]
        product = jnp.dot(
            block[: planes * 8], values_scr[session], preferred_element_type=F32
        )
        mine = slice(session * 8, (session + 1) * 8)
        for z in range(planes):
            sum_scr[z, mine, :] = product[z * 8 : (z + 1) * 8, z * LANES : (z + 1) * LANES]
        recent = block[planes * 8 :].astype(F32)
        sum_scr[z_me, mine, :] += recent[:8]
    for q, out_ref in enumerate(out_refs):
        out_ref[...] = sum_scr[jnp.bitwise_xor(z_me, q)].astype(BF16)


def mix(me, rows, weights, stores):
    sessions = weights.shape[0]
    planes = stores[0].shape[1] // LANES
    shape = (planes, sessions * 8, LANES)
    return pl.pallas_call(
        mix_kernel,
        in_specs=[whole(SMEM)] * 2 + [whole()] * (1 + PLANE),
        out_specs=(whole(),) * planes,
        out_shape=(jax.ShapeDtypeStruct(shape[1:], BF16),) * planes,
        scratch_shapes=[VMEM((sessions, LANES, planes * LANES), BF16), VMEM(shape, F32)],
        compiler_params=pltpu.CompilerParams(vmem_limit_bytes=16 * 2**20),
        cost_estimate=pl.CostEstimate(
            flops=2 * sessions * 32 * LANES * planes * LANES,
            bytes_accessed=4 * stores[0].size * PLANE,
            transcendentals=0,
        ),
        name="mix_values",
    )(me, rows, weights, *stores)


def keys_kernel(pair_ref, factors_ref, basis_ref, cos_ref, sin_ref, out_ref, rows_scr):
    span = factors_ref.shape[0] // pair_ref.shape[0]
    count = rows_scr.shape[0] // span
    base = pl.program_id(0) * count
    for p in range(count):
        source = pl.ds(pl.multiple_of(pair_ref[base + p] * span, span), span)
        rows_scr[p * span : (p + 1) * span, :] = factors_ref[source, :]
    product = jnp.dot(rows_scr[...], basis_ref[...], preferred_element_type=F32)
    cosine, sine = cos_ref[...], sin_ref[...]
    for head in range(KV_HEADS):
        lanes = slice(head * HEAD_DIM, (head + 1) * HEAD_DIM)
        part = product[:, lanes]
        turned = part * cosine + pltpu.roll(part, HEAD_DIM // 2, 1) * sine
        out_ref[:, lanes] = turned.astype(BF16)


def make_keys(pair, factors, basis, cosine, sine):
    seq, rank = factors.shape
    width = basis.shape[1]
    rows = min(seq, 512)
    return pl.pallas_call(
        keys_kernel,
        grid=(seq // rows,),
        in_specs=[
            whole(SMEM),
            pl.BlockSpec((seq, rank), lambda i: (0, 0)),
            pl.BlockSpec((rank, width), lambda i: (0, 0)),
            pl.BlockSpec((rows, HEAD_DIM), lambda i: (i, 0)),
            pl.BlockSpec((rows, HEAD_DIM), lambda i: (i, 0)),
        ],
        out_specs=pl.BlockSpec((rows, width), lambda i: (i, 0)),
        out_shape=jax.ShapeDtypeStruct((seq, width), BF16),
        scratch_shapes=[VMEM((rows, rank), BF16)],
        compiler_params=pltpu.CompilerParams(vmem_limit_bytes=32 * 2**20),
        cost_estimate=pl.CostEstimate(
            flops=2 * seq * rank * width, bytes_accessed=4 * seq * width, transcendentals=0
        ),
        name="turned_keys",
    )(pair, factors, basis, cosine, sine)


def fetch_kernel(source_ref, target_ref, sems):
    parts = sems.shape[0]
    span = source_ref.shape[0] // parts
    copies = []
    for part in range(parts):
        rows = pl.ds(part * span, span)
        copies.append(
            pltpu.make_async_copy(source_ref.at[rows, :], target_ref.at[rows, :], sems.at[part])
        )
        copies[-1].start()
    for copy in copies:
        copy.wait()


def fetch(weight, limit):
    return pl.pallas_call(
        fetch_kernel,
        in_specs=[whole(pl.ANY)],
        out_specs=whole(pl.ANY),
        out_shape=jax.ShapeDtypeStruct(weight.shape, weight.dtype),
        scratch_shapes=[pltpu.SemaphoreType.DMA((4,))],
        compiler_params=pltpu.CompilerParams(vmem_limit_bytes=limit * 2**20),
        cost_estimate=pl.CostEstimate(
            flops=0, bytes_accessed=2 * weight.size, transcendentals=0
        ),
        name="fetch_weight",
    )(weight)


def project_kernel(
    order, fast, me_ref, first_ref, second_ref, wq_ref, wk_ref, out_ref, *rest
):
    if fast:
        rows_ref, x_scr, lhs_scr, wq_buf, out_scr, sems, *asked_scr = rest
    else:
        x_scr, lhs_scr, wq_buf, out_scr, sems = rest
    depth, q_cols = wq_ref.shape
    k_cols = wk_ref.shape[1]
    chunks = wq_buf.shape[0]
    span = depth // chunks
    pieces = depth // LANES
    copies = []
    parts = sems.shape[1]
    for i in range(chunks):
        copies.append([])
        for part in range(parts):
            copy = pltpu.make_async_copy(
                wq_ref.at[pl.ds(i * span + part * (span // parts), span // parts), :],
                wq_buf.at[i, pl.ds(part * (span // parts), span // parts), :],
                sems.at[i, part],
            )
            copy.start()
            copies[-1].append(copy)
    half = first_ref.shape[0]
    count = 2 * half * STEPS
    rows = STEPS * pieces
    for j in range(2 * half):
        source = first_ref if j < half else second_ref
        x_scr[j * rows : (j + 1) * rows] = source[j % half, :rows, :].astype(F32)
    if fast:
        table_scr, table_smem, table_sem = asked_scr
        for j in range(2 * half):
            source = first_ref if j < half else second_ref
            asked = source[j % half, rows:, :].astype(F32)
            table_scr[2 * j : 2 * j + 2, :] = asked[:2].astype(jnp.int32)
        table_copy = pltpu.make_async_copy(table_scr, table_smem, table_sem)
        table_copy.start()
    for c in range(pieces):
        part = x_scr[pl.ds(c, count, stride=pieces), :]
        lhs_scr[:, c * LANES : (c + 1) * LANES] = part.astype(BF16)
    if fast:
        me = me_ref[0]
        out_scr[...] = jnp.zeros_like(out_scr)
        table_copy.wait()
        plane = jnp.bitwise_and(me, -PLANE)
        for j in range(2 * half):
            place = origin(me, order, j) * (2 * PLANE)
            for k in range(2):
                for b in range(PLANE):
                    rows_ref[place + k * PLANE + b] = table_smem[2 * j + k, plane + b]
    q_sum = jnp.zeros((count, q_cols), F32)
    k_sum = jnp.zeros((count, k_cols), F32)
    for i in range(chunks):
        for copy in copies[i]:
            copy.wait()
        lhs = lhs_scr[:, i * span : (i + 1) * span]
        q_sum = q_sum + jnp.dot(lhs, wq_buf[i], preferred_element_type=F32)
        k_sum = k_sum + jnp.dot(
            lhs, wk_ref[i * span : (i + 1) * span, :], preferred_element_type=F32
        )
    if not fast:
        out_ref[:, :q_cols] = q_sum.astype(BF16)
        out_ref[:, q_cols:] = k_sum.astype(BF16)
        return
    per = q_cols // LANES
    for j in range(2 * half):
        place = origin(me, order, j)
        for step in range(STEPS):
            row = j * STEPS + step
            for c in range(per):
                out_scr[place, step * per + c : step * per + c + 1, :] = q_sum[
                    row : row + 1, c * LANES : (c + 1) * LANES
                ]
            out_scr[place, STEPS * per + step : STEPS * per + step + 1, :] = k_sum[
                row : row + 1, :
            ]
    out_ref[...] = out_scr[...].astype(BF16)


def project(me, first, second, query_weight, kv_weight, order, fast):
    depth, q_cols = query_weight.shape
    k_cols = kv_weight.shape[1]
    pieces = depth // LANES
    devices = 2 * first.shape[0]
    rows = devices * STEPS
    chunks = 8
    span = depth // chunks
    shape = (devices, 16, LANES) if fast else (rows, q_cols + k_cols)
    return pl.pallas_call(
        functools.partial(project_kernel, order, fast),
        in_specs=[whole(SMEM), whole(), whole(), whole(pl.ANY), whole()],
        out_specs=(whole(), whole(SMEM)) if fast else whole(),
        out_shape=(
            (
                jax.ShapeDtypeStruct(shape, BF16),
                jax.ShapeDtypeStruct((devices * 2 * PLANE,), jnp.int32),
            )
            if fast
            else jax.ShapeDtypeStruct(shape, BF16)
        ),
        scratch_shapes=[
            VMEM((rows * pieces, LANES), F32),
            VMEM((rows, depth), BF16),
            VMEM((chunks, span, q_cols), BF16),
            VMEM((devices, 16, LANES) if fast else (8, LANES), F32),
            pltpu.SemaphoreType.DMA((chunks, 4)),
        ]
        + (
            [
                VMEM((2 * devices, LANES), jnp.int32),
                SMEM((2 * devices, LANES), jnp.int32),
                pltpu.SemaphoreType.DMA(()),
            ]
            if fast
            else []
        ),
        compiler_params=pltpu.CompilerParams(vmem_limit_bytes=PROJECT_LIMIT),
        cost_estimate=pl.CostEstimate(
            flops=2 * rows * depth * (q_cols + k_cols),
            bytes_accessed=2 * depth * (q_cols + k_cols),
            transcendentals=0,
        ),
        name="norm_project",
    )(me, first, second, query_weight, kv_weight)


def attend_kernel(fast, columns_ref, keys_ref, bias_ref, cos_ref, sin_ref, *rest):
    pages_ref, out_ref, out_scr = (None, *rest) if fast else rest
    score_scale = 1.0 / math.sqrt(HEAD_DIM)
    half = HEAD_DIM // 2
    rows = 2 * GROUP
    columns = columns_ref[...].astype(F32)
    count = columns.shape[0]
    query = columns[:, :8, :].reshape(count * 8, HEAD_DIM)
    fresh = columns[:, 8:, :]
    if fast:
        planes = count // PLANE
        out_scr[...] = jnp.zeros_like(out_scr)
    row_step = lax.rem(lax.broadcasted_iota(jnp.int32, (count * 8, 1), 0) // 4, STEPS)
    later = row_step == 1
    cosine = jnp.where(later, cos_ref[1:2, :], cos_ref[0:1, :])
    sine = jnp.where(later, sin_ref[1:2, :], sin_ref[0:1, :])
    turned = (query * cosine + pltpu.roll(query, half, 1) * sine).astype(BF16)
    turned_wide = turned.astype(F32)
    step_later = later[:rows]
    bias = jnp.where(step_later, bias_ref[1:2, :], bias_ref[0:1, :])
    new_keys = []
    for step in range(STEPS):
        part = fresh[:KV_HEADS, step, :]
        new = part * cos_ref[step : step + 1, :] + pltpu.roll(part, half, 1) * sin_ref[step : step + 1, :]
        new_keys.append(new.astype(BF16).astype(F32))
    for head in range(KV_HEADS):
        lanes = slice(head * HEAD_DIM, (head + 1) * HEAD_DIM)
        mine = slice(head * rows, (head + 1) * rows)
        scores = (
            lax.dot_general(
                turned[mine], keys_ref[:, lanes], (((1,), (1,)), ((), ())),
                preferred_element_type=F32,
            )
            * score_scale
            + bias
        )
        recent0 = (
            jnp.sum(turned_wide[mine] * new_keys[0][head : head + 1, :], axis=1, keepdims=True)
            * score_scale
        )
        recent1 = (
            jnp.sum(turned_wide[mine] * new_keys[1][head : head + 1, :], axis=1, keepdims=True)
            * score_scale
        )
        recent1 = jnp.where(step_later, recent1, -1e30)
        largest = jnp.maximum(
            jnp.max(scores, axis=1, keepdims=True), jnp.maximum(recent0, recent1)
        )
        cache_exp = jnp.exp(scores - largest)
        exp0 = jnp.exp(recent0 - largest)
        exp1 = jnp.exp(recent1 - largest)
        denominator = jnp.sum(cache_exp, axis=1, keepdims=True) + (exp0 + exp1)
        weights = (cache_exp / denominator).astype(BF16)
        weight0 = (exp0 / denominator).astype(BF16).astype(F32)
        weight1 = (exp1 / denominator).astype(BF16).astype(F32)
        recent = weight0 * fresh[KV_HEADS + head, 0:1, :]
        recent = recent + weight1 * fresh[KV_HEADS + head, 1:2, :]
        if not fast:
            values = pages_ref[:, :, lanes].reshape(keys_ref.shape[0], HEAD_DIM)
            mixed = jnp.dot(weights, values, preferred_element_type=F32)
            out_ref[mine, :] = (mixed + recent).astype(BF16)
            continue
        weights = weights.astype(F32)
        z, x = divmod(head, 2)
        for c in range(2):
            part = slice(c * 8, (c + 1) * 8)
            for plane in range(planes):
                out_scr[plane * PLANE + 2 * x + c, z * 8 : (z + 1) * 8, :] = weights[
                    part, plane * LANES : (plane + 1) * LANES
                ]
            out_scr[z * PLANE + 2 * x + c, planes * 8 : planes * 8 + 8, :] = recent[part]
    if fast:
        out_ref[...] = out_scr[...].astype(BF16)


def attend(columns, keys, bias, cosine, sine, pages, fast):
    seq, width = keys.shape
    count = columns.shape[0]
    if fast:
        shape = (count, count // PLANE * 8 + 16, LANES)
        scratch = [VMEM(shape, F32)]
        operands = (columns, keys, bias, cosine, sine)
    else:
        shape = (STEPS * HEADS, HEAD_DIM)
        scratch = [VMEM((8, LANES), F32)]
        operands = (columns, keys, bias, cosine, sine, pages)
    return pl.pallas_call(
        functools.partial(attend_kernel, fast),
        in_specs=[whole()] * len(operands),
        out_specs=whole(),
        out_shape=jax.ShapeDtypeStruct(shape, BF16),
        scratch_shapes=scratch,
        compiler_params=pltpu.CompilerParams(vmem_limit_bytes=48 * 2**20),
        cost_estimate=pl.CostEstimate(
            flops=4 * STEPS * HEADS * seq * HEAD_DIM,
            bytes_accessed=4 * seq * width,
            transcendentals=STEPS * HEADS * seq,
        ),
        name="attend",
    )(*operands)


def output_kernel(fast, count, me_ref, weight_ref, *rest):
    lhs_refs, rest = rest[:count], rest[count:]
    out_refs, (out_scr, heads_scr) = rest[:-2], rest[-2:]
    chunks = 8
    span = weight_ref.shape[1] // chunks
    rows = out_scr.shape[0] * LANES // (chunks * span)
    pieces = chunks * span // LANES
    if fast:
        per = heads_scr.shape[0] // rows
        total = lhs_refs[0][...].astype(F32)
        for lhs_ref in lhs_refs[1:]:
            total = total + lhs_ref[...].astype(F32)
        heads_scr[...] = total
        lhs = jnp.concatenate(
            [heads_scr[pl.ds(g, rows, stride=per), :].astype(BF16) for g in range(per)], axis=1
        )
    else:
        lhs = lhs_refs[0][...]
    for i in range(chunks):
        part = jnp.dot(
            lhs, weight_ref[:, i * span : (i + 1) * span], preferred_element_type=F32
        )
        for c in range(span // LANES):
            out_scr[pl.ds(i * (span // LANES) + c, rows, stride=pieces), :] = part[
                :, c * LANES : (c + 1) * LANES
            ]
    if not fast:
        out_refs[0][...] = out_scr[...].astype(BF16)
        return
    low = jnp.bitwise_and(me_ref[0], 1)
    for out_ref, core in zip(out_refs, (low, 1 - low)):
        count, size, _ = out_ref.shape
        for j in range(count):
            part = pl.ds(pl.multiple_of((2 * j + core) * size, size), size)
            out_ref[j] = out_scr[part, :].astype(BF16)


def output(me, lhs, weight, rows, fast):
    depth, width = weight.shape
    if fast:
        shape = (rows // (2 * STEPS), STEPS * width // LANES, LANES)
        shapes = (jax.ShapeDtypeStruct(shape, BF16),) * 2
    else:
        shapes = (jax.ShapeDtypeStruct((rows * width // LANES, LANES), BF16),)
    return pl.pallas_call(
        functools.partial(output_kernel, fast, len(lhs)),
        in_specs=[whole(SMEM)] + [whole()] * (1 + len(lhs)),
        out_specs=(whole(),) * len(shapes),
        out_shape=shapes,
        scratch_shapes=[
            VMEM((rows * width // LANES, LANES), F32),
            VMEM(lhs[0].shape if fast else (8, LANES), F32),
        ],
        compiler_params=pltpu.CompilerParams(vmem_limit_bytes=24 * 2**20),
        cost_estimate=pl.CostEstimate(
            flops=2 * rows * depth * width, bytes_accessed=2 * depth * width, transcendentals=0
        ),
        name="output_project",
    )(me, weight, *lhs)


def swap(block, bit, devices):
    return lax.ppermute(block, AXIS, [(i, i ^ bit) for i in range(devices)])


def exchange(blocks, groups=None):
    return lax.all_to_all(
        blocks, AXIS, split_axis=0, concat_axis=0, tiled=True, axis_index_groups=groups
    )


def local(
    hidden,
    norm_gain,
    query_weight,
    kv_weight,
    out_weight,
    key_factors,
    key_basis,
    value_store,
    lengths,
    block_slot,
    selection,
):
    devices = lax.axis_size(AXIS)
    me = lax.axis_index(AXIS)
    slots_dev, block_len, width = value_store.shape
    seq = key_factors.shape[1]
    pages = block_slot.shape[1]
    model = hidden.shape[2]
    q_cols = query_weight.shape[1]
    k_cols = kv_weight.shape[1]
    fast = devices == 2 * PAIRS and q_cols == 4 * HEAD_DIM and k_cols == HEAD_DIM
    pieces = model // LANES

    me_word = me.astype(jnp.int32).reshape(1)
    block, holder, pair = prepare(
        hidden[:, 0], norm_gain.reshape(pieces, LANES), block_slot, slots_dev, PAIRS if fast else 1
    )
    if fast:
        same_core = [list(range(core, devices, 2)) for core in range(2)]
        block = exchange(block, same_core)
        block, kv_weight = lax.optimization_barrier((block, kv_weight))
        kv_weight = fetch(kv_weight, 50)
        other = swap(block, 1, devices)
        order = None
        x = lax.bitwise_and(lax.shift_right_logical(me_word, 1), 1)
        keep, send = split_values(x, value_store)
        neighbour = swap(send, 2, devices)
    else:
        order = [0]
        bit = devices // 2
        while bit:
            other = swap(block, bit, devices)
            order = order + [k ^ bit for k in order]
            bit //= 2
            if bit:
                block = jnp.concatenate([block, other], axis=0)
        order = tuple(order)
    span = 2 * block_len
    places = (pair[:, None] * span + jnp.arange(span, dtype=jnp.int32)[None, :]).reshape(-1)
    if not fast:
        sent_pages = pick_pages(me_word, block, other, value_store, order)
        block, other, sent_pages = lax.optimization_barrier((block, other, sent_pages))
        fetched = exchange(sent_pages)
    projected = project(
        me_word, block, other, query_weight, kv_weight, order, fast
    )
    if fast:
        projected, rows = projected
        projected, places = lax.optimization_barrier((projected, places))
        columns = exchange(projected)
    else:
        targets = jnp.bitwise_xor(me, jnp.array(order, dtype=jnp.int32))
        columns = exchange(projected.reshape(devices, STEPS, q_cols + k_cols)[targets])
        query = columns[:, :, :q_cols].transpose(1, 0, 2).reshape(STEPS, HEADS // 4, 4, HEAD_DIM)
        query = query.transpose(1, 0, 2, 3).reshape(HEADS // 4, 8, HEAD_DIM)
        fresh = columns[:, :, q_cols:].transpose(1, 0, 2).reshape(STEPS, HEADS // 4, HEAD_DIM)
        fresh = jnp.pad(fresh.transpose(1, 0, 2), ((0, 0), (0, 8 - STEPS), (0, 0)))
        columns = jnp.concatenate([query, fresh], axis=1)

    cosine, sine = turn_tables(places.astype(F32))
    keys = make_keys(pair, key_factors[0], key_basis[0], cosine, sine)
    picked = jnp.any(
        selection[:, 0, :, None] == (places // block_len)[None, None, :], axis=1
    )
    bias = jnp.where(picked & (places < lengths[0])[None, :], 0.0, -1e30).astype(F32)
    new_cos, new_sin = turn_tables(
        (lengths[0] + jnp.arange(STEPS, dtype=jnp.int32)).astype(F32)
    )
    if fast:
        blocks = attend(columns, keys, bias, new_cos, new_sin, None, True)
        blocks, neighbour = lax.optimization_barrier((blocks, neighbour))
        stores = (keep, swap(keep, 1, devices), neighbour, swap(neighbour, 1, devices))
        blocks = exchange(blocks)
        parts = mix(me_word, rows, blocks, stores)
        (*parts, out_weight) = lax.optimization_barrier((*parts, out_weight))
        out_weight = fetch(out_weight, 43)
        lhs = [parts[0]] + [swap(parts[q], q * PLANE, devices) for q in range(1, len(parts))]
    else:
        heads = attend(columns, keys, bias, new_cos, new_sin, fetched, False)
        flat = heads.reshape(HEADS // 4, STEPS, 4 * HEAD_DIM).transpose(1, 0, 2)
        flat = flat.reshape(STEPS, devices, model // devices).transpose(1, 0, 2)
        lhs = [exchange(flat).reshape(devices * STEPS, model // devices)]
    partial = output(me_word, lhs, out_weight, devices * STEPS, fast)
    if fast:
        near, far = partial
        both = near.astype(F32) + swap(far, 1, devices).astype(F32)
        arrived = exchange(both.astype(BF16), same_core)
    else:
        arrived = exchange(partial[0].reshape(devices, STEPS * pieces, LANES))
    total = jnp.sum(arrived.astype(F32), axis=0).astype(BF16)
    return total.reshape(STEPS, 1, model)


def solution(mesh):
    return jax.shard_map(
        local,
        mesh=mesh,
        in_specs=(
            P(None, ("groups", "session"), None),
            P(),
            P(None, "session"),
            P(None, "session"),
            P("session", None),
            P(("groups", "session"), None, None),
            P(("groups", "session"), None, None),
            P(("groups", "session"), None, None),
            P(("groups", "session")),
            P(("groups", "session"), None),
            P(None, ("groups", "session"), None),
        ),
        out_specs=P(None, ("groups", "session"), None),
        check_vma=False,
    )
```

```python
import functools
import math

import jax
import jax.numpy as jnp
from jax import lax
from jax.experimental import pallas as pl
from jax.experimental.pallas import tpu as pltpu
from jax.sharding import PartitionSpec as P

HEADS = 64
KV_HEADS = 8
HEAD_DIM = 128
STEPS = 2
GROUP = HEADS // KV_HEADS
LANES = 128
EXTRA = 16
PLANE = 4
PAIRS = 8
PROJECT_LIMIT = 48 * 2**20
AXIS = "session"
VMEM = pltpu.VMEM
SMEM = pltpu.SMEM
F32 = jnp.float32
BF16 = jnp.bfloat16


def angles(positions):
    half = HEAD_DIM // 2
    frequency = jnp.exp(
        -jnp.arange(half, dtype=F32) * (2.0 * math.log(500000.0) / HEAD_DIM)
    )
    return positions[..., None] * frequency


def turn_tables(positions):
    angle = angles(positions)
    cosine, sine = jnp.cos(angle), jnp.sin(angle)
    return (
        jnp.concatenate([cosine, cosine], axis=-1),
        jnp.concatenate([-sine, sine], axis=-1),
    )


def origin(me, order, j):
    if order is None:
        return 2 * (j % PAIRS) + jnp.bitwise_xor(jnp.bitwise_and(me, 1), j // PAIRS)
    return jnp.bitwise_xor(me, order[j])


def whole(space=VMEM):
    return pl.BlockSpec(memory_space=space)


def prepare_kernel(
    slots_dev, hidden_ref, gain_ref, slots_ref, block_ref, holder_ref, pair_ref, wide_scr
):
    steps, model = hidden_ref.shape
    pieces = model // LANES
    wide = hidden_ref[...].astype(F32)
    scale = lax.rsqrt(jnp.mean(wide * wide, axis=1, keepdims=True) + 1e-05)
    wide = wide * scale
    for step in range(steps):
        for c in range(pieces):
            row = step * pieces + c
            wide_scr[row : row + 1, :] = wide[step : step + 1, c * LANES : (c + 1) * LANES]
    lane = lax.broadcasted_iota(jnp.int32, (EXTRA, LANES), 1)
    parity = lax.broadcasted_iota(jnp.int32, (EXTRA, LANES), 0)
    table = jnp.zeros((EXTRA, LANES), jnp.int32)
    for m in range(holder_ref.shape[0]):
        slot = slots_ref[0, 2 * m]
        holder = lax.div(slot, slots_dev)
        holder_ref[m] = holder
        pair_ref[holder] = m
        base = holder * slots_dev
        pair = jnp.where(parity == 0, slot - base, slots_ref[0, 2 * m + 1] - base)
        table = jnp.where(lane == holder, pair, table)
    wide_scr[steps * pieces :, :] = table.astype(F32)
    gain = gain_ref[...].astype(F32)
    for step in range(steps):
        rows = slice(step * pieces, (step + 1) * pieces)
        wide_scr[rows, :] = wide_scr[rows, :] * gain
    block = wide_scr[...].astype(BF16)
    for copy in range(block_ref.shape[0]):
        block_ref[copy] = block


def prepare(hidden, gain, block_slot, slots_dev, copies):
    assert slots_dev <= 256
    steps, model = hidden.shape
    rows = steps * model // LANES + EXTRA
    return pl.pallas_call(
        functools.partial(prepare_kernel, slots_dev),
        in_specs=[whole(), whole(), whole(SMEM)],
        out_specs=(whole(), whole(SMEM), whole(SMEM)),
        out_shape=(
            jax.ShapeDtypeStruct((copies, rows, LANES), BF16),
            jax.ShapeDtypeStruct((block_slot.shape[1] // 2,), jnp.int32),
            jax.ShapeDtypeStruct((block_slot.shape[1] // 2,), jnp.int32),
        ),
        scratch_shapes=[VMEM((rows, LANES), F32)],
        name="prepare",
    )(hidden, gain, block_slot)


def pick_kernel(order, me_ref, first_ref, second_ref, store_ref, out_ref, table_scr, table_smem, sem):
    block_len = store_ref.shape[1]
    half, rows, _ = first_ref.shape
    for j in range(2 * half):
        source = first_ref if j < half else second_ref
        asked = source[j % half, rows - EXTRA :, :].astype(F32)
        table_scr[j] = asked[:8].astype(jnp.int32)
    copy = pltpu.make_async_copy(table_scr, table_smem, sem)
    copy.start()
    copy.wait()
    me = me_ref[0]
    for j in range(2 * half):
        target = origin(me, order, j)
        for k in range(2):
            out_ref[target, k * block_len : (k + 1) * block_len, :] = store_ref[
                table_smem[j, k, me]
            ]


def pick_pages(me, first, second, store, order):
    count = 2 * first.shape[0]
    _, block_len, width = store.shape
    return pl.pallas_call(
        functools.partial(pick_kernel, order),
        in_specs=[whole(SMEM), whole(), whole(), whole()],
        out_specs=whole(),
        out_shape=jax.ShapeDtypeStruct((count, 2 * block_len, width), store.dtype),
        scratch_shapes=[
            VMEM((count, 8, LANES), jnp.int32),
            SMEM((count, 8, LANES), jnp.int32),
            pltpu.SemaphoreType.DMA(()),
        ],
        compiler_params=pltpu.CompilerParams(vmem_limit_bytes=36 * 2**20),
        name="pick_pages",
    )(me, first, second, store)


def split_kernel(x_ref, store_ref, keep_ref, send_ref):
    slots, block_len, width = store_ref.shape
    for x in range(2):

        @pl.when(x_ref[0] == x)
        def _():
            for head in range(width // LANES):
                target = keep_ref if head % 2 == x else send_ref
                lanes = slice(head // 2 * LANES, (head // 2 + 1) * LANES)
                part = store_ref[:, :, head * LANES : (head + 1) * LANES]
                target[:, lanes] = part.reshape(slots * block_len, LANES)


def split_values(x, store):
    slots, block_len, width = store.shape
    half = jax.ShapeDtypeStruct((slots * block_len, width // 2), store.dtype)
    return pl.pallas_call(
        split_kernel,
        in_specs=[whole(SMEM), whole()],
        out_specs=(whole(), whole()),
        out_shape=(half, half),
        compiler_params=pltpu.CompilerParams(vmem_limit_bytes=16 * 2**20),
        name="split_values",
    )(x, store)


def mix_kernel(me_ref, rows_ref, weights_ref, *rest):
    stores, (values_scr, sum_scr) = rest[:PLANE], rest[-2:]
    out_refs = rest[PLANE:-2]
    me = me_ref[0]
    low = jnp.bitwise_and(me, PLANE - 1)
    z_me = lax.div(me, PLANE)
    sessions = weights_ref.shape[0]
    planes = len(out_refs)
    block_len = values_scr.shape[1] // (2 * PLANE)
    for session in range(sessions):
        for q, store in enumerate(stores):
            device = jnp.bitwise_xor(low, q)
            for k in range(2):
                row = rows_ref[session * (2 * PLANE) + k * PLANE + device]
                source = pl.ds(pl.multiple_of(row * block_len, block_len), block_len)
                target = pl.ds(
                    pl.multiple_of((device * 2 + k) * block_len, block_len), block_len
                )
                values_scr[session, target, :] = store[source, :]
        block = weights_ref[session]
        product = jnp.dot(
            block[: planes * 8], values_scr[session], preferred_element_type=F32
        )
        mine = slice(session * 8, (session + 1) * 8)
        for z in range(planes):
            sum_scr[z, mine, :] = product[z * 8 : (z + 1) * 8, z * LANES : (z + 1) * LANES]
        recent = block[planes * 8 :].astype(F32)
        sum_scr[z_me, mine, :] += recent[:8]
    for q, out_ref in enumerate(out_refs):
        out_ref[...] = sum_scr[jnp.bitwise_xor(z_me, q)].astype(BF16)


def mix(me, rows, weights, stores):
    sessions = weights.shape[0]
    planes = stores[0].shape[1] // LANES
    shape = (planes, sessions * 8, LANES)
    return pl.pallas_call(
        mix_kernel,
        in_specs=[whole(SMEM)] * 2 + [whole()] * (1 + PLANE),
        out_specs=(whole(),) * planes,
        out_shape=(jax.ShapeDtypeStruct(shape[1:], BF16),) * planes,
        scratch_shapes=[VMEM((sessions, LANES, planes * LANES), BF16), VMEM(shape, F32)],
        compiler_params=pltpu.CompilerParams(vmem_limit_bytes=16 * 2**20),
        cost_estimate=pl.CostEstimate(
            flops=2 * sessions * 32 * LANES * planes * LANES,
            bytes_accessed=4 * stores[0].size * PLANE,
            transcendentals=0,
        ),
        name="mix_values",
    )(me, rows, weights, *stores)


def keys_kernel(pair_ref, factors_ref, basis_ref, cos_ref, sin_ref, out_ref, rows_scr):
    span = factors_ref.shape[0] // pair_ref.shape[0]
    count = rows_scr.shape[0] // span
    base = pl.program_id(0) * count
    for p in range(count):
        source = pl.ds(pl.multiple_of(pair_ref[base + p] * span, span), span)
        rows_scr[p * span : (p + 1) * span, :] = factors_ref[source, :]
    product = jnp.dot(rows_scr[...], basis_ref[...], preferred_element_type=F32)
    cosine, sine = cos_ref[...], sin_ref[...]
    for head in range(KV_HEADS):
        lanes = slice(head * HEAD_DIM, (head + 1) * HEAD_DIM)
        part = product[:, lanes]
        turned = part * cosine + pltpu.roll(part, HEAD_DIM // 2, 1) * sine
        out_ref[:, lanes] = turned.astype(BF16)


def make_keys(pair, factors, basis, cosine, sine):
    seq, rank = factors.shape
    width = basis.shape[1]
    rows = min(seq, 512)
    return pl.pallas_call(
        keys_kernel,
        grid=(seq // rows,),
        in_specs=[
            whole(SMEM),
            pl.BlockSpec((seq, rank), lambda i: (0, 0)),
            pl.BlockSpec((rank, width), lambda i: (0, 0)),
            pl.BlockSpec((rows, HEAD_DIM), lambda i: (i, 0)),
            pl.BlockSpec((rows, HEAD_DIM), lambda i: (i, 0)),
        ],
        out_specs=pl.BlockSpec((rows, width), lambda i: (i, 0)),
        out_shape=jax.ShapeDtypeStruct((seq, width), BF16),
        scratch_shapes=[VMEM((rows, rank), BF16)],
        compiler_params=pltpu.CompilerParams(vmem_limit_bytes=32 * 2**20),
        cost_estimate=pl.CostEstimate(
            flops=2 * seq * rank * width, bytes_accessed=4 * seq * width, transcendentals=0
        ),
        name="turned_keys",
    )(pair, factors, basis, cosine, sine)


def fetch_kernel(source_ref, target_ref, sems):
    parts = sems.shape[0]
    span = source_ref.shape[0] // parts
    copies = []
    for part in range(parts):
        rows = pl.ds(part * span, span)
        copies.append(
            pltpu.make_async_copy(source_ref.at[rows, :], target_ref.at[rows, :], sems.at[part])
        )
        copies[-1].start()
    for copy in copies:
        copy.wait()


def fetch(weight, limit):
    return pl.pallas_call(
        fetch_kernel,
        in_specs=[whole(pl.ANY)],
        out_specs=whole(pl.ANY),
        out_shape=jax.ShapeDtypeStruct(weight.shape, weight.dtype),
        scratch_shapes=[pltpu.SemaphoreType.DMA((4,))],
        compiler_params=pltpu.CompilerParams(vmem_limit_bytes=limit * 2**20),
        cost_estimate=pl.CostEstimate(
            flops=0, bytes_accessed=2 * weight.size, transcendentals=0
        ),
        name="fetch_weight",
    )(weight)


def project_kernel(
    order, fast, me_ref, first_ref, second_ref, wq_ref, wk_ref, out_ref, *rest
):
    if fast:
        rows_ref, x_scr, lhs_scr, wq_buf, out_scr, sems, *asked_scr = rest
    else:
        x_scr, lhs_scr, wq_buf, out_scr, sems = rest
    depth, q_cols = wq_ref.shape
    k_cols = wk_ref.shape[1]
    chunks = wq_buf.shape[0]
    span = depth // chunks
    pieces = depth // LANES
    copies = []
    parts = sems.shape[1]
    for i in range(chunks):
        copies.append([])
        for part in range(parts):
            copy = pltpu.make_async_copy(
                wq_ref.at[pl.ds(i * span + part * (span // parts), span // parts), :],
                wq_buf.at[i, pl.ds(part * (span // parts), span // parts), :],
                sems.at[i, part],
            )
            copy.start()
            copies[-1].append(copy)
    half = first_ref.shape[0]
    count = 2 * half * STEPS
    rows = STEPS * pieces
    for j in range(2 * half):
        source = first_ref if j < half else second_ref
        x_scr[j * rows : (j + 1) * rows] = source[j % half, :rows, :].astype(F32)
    if fast:
        table_scr, table_smem, table_sem = asked_scr
        for j in range(2 * half):
            source = first_ref if j < half else second_ref
            asked = source[j % half, rows:, :].astype(F32)
            table_scr[2 * j : 2 * j + 2, :] = asked[:2].astype(jnp.int32)
        table_copy = pltpu.make_async_copy(table_scr, table_smem, table_sem)
        table_copy.start()
    for c in range(pieces):
        part = x_scr[pl.ds(c, count, stride=pieces), :]
        lhs_scr[:, c * LANES : (c + 1) * LANES] = part.astype(BF16)
    if fast:
        me = me_ref[0]
        out_scr[...] = jnp.zeros_like(out_scr)
        table_copy.wait()
        plane = jnp.bitwise_and(me, -PLANE)
        for j in range(2 * half):
            place = origin(me, order, j) * (2 * PLANE)
            for k in range(2):
                for b in range(PLANE):
                    rows_ref[place + k * PLANE + b] = table_smem[2 * j + k, plane + b]
    q_sum = jnp.zeros((count, q_cols), F32)
    k_sum = jnp.zeros((count, k_cols), F32)
    for i in range(chunks):
        for copy in copies[i]:
            copy.wait()
        lhs = lhs_scr[:, i * span : (i + 1) * span]
        q_sum = q_sum + jnp.dot(lhs, wq_buf[i], preferred_element_type=F32)
        k_sum = k_sum + jnp.dot(
            lhs, wk_ref[i * span : (i + 1) * span, :], preferred_element_type=F32
        )
    if not fast:
        out_ref[:, :q_cols] = q_sum.astype(BF16)
        out_ref[:, q_cols:] = k_sum.astype(BF16)
        return
    per = q_cols // LANES
    for j in range(2 * half):
        place = origin(me, order, j)
        for step in range(STEPS):
            row = j * STEPS + step
            for c in range(per):
                out_scr[place, step * per + c : step * per + c + 1, :] = q_sum[
                    row : row + 1, c * LANES : (c + 1) * LANES
                ]
            out_scr[place, STEPS * per + step : STEPS * per + step + 1, :] = k_sum[
                row : row + 1, :
            ]
    out_ref[...] = out_scr[...].astype(BF16)


def project(me, first, second, query_weight, kv_weight, order, fast):
    depth, q_cols = query_weight.shape
    k_cols = kv_weight.shape[1]
    pieces = depth // LANES
    devices = 2 * first.shape[0]
    rows = devices * STEPS
    chunks = 8
    span = depth // chunks
    shape = (devices, 16, LANES) if fast else (rows, q_cols + k_cols)
    return pl.pallas_call(
        functools.partial(project_kernel, order, fast),
        in_specs=[whole(SMEM), whole(), whole(), whole(pl.ANY), whole()],
        out_specs=(whole(), whole(SMEM)) if fast else whole(),
        out_shape=(
            (
                jax.ShapeDtypeStruct(shape, BF16),
                jax.ShapeDtypeStruct((devices * 2 * PLANE,), jnp.int32),
            )
            if fast
            else jax.ShapeDtypeStruct(shape, BF16)
        ),
        scratch_shapes=[
            VMEM((rows * pieces, LANES), F32),
            VMEM((rows, depth), BF16),
            VMEM((chunks, span, q_cols), BF16),
            VMEM((devices, 16, LANES) if fast else (8, LANES), F32),
            pltpu.SemaphoreType.DMA((chunks, 4)),
        ]
        + (
            [
                VMEM((2 * devices, LANES), jnp.int32),
                SMEM((2 * devices, LANES), jnp.int32),
                pltpu.SemaphoreType.DMA(()),
            ]
            if fast
            else []
        ),
        compiler_params=pltpu.CompilerParams(vmem_limit_bytes=PROJECT_LIMIT),
        cost_estimate=pl.CostEstimate(
            flops=2 * rows * depth * (q_cols + k_cols),
            bytes_accessed=2 * depth * (q_cols + k_cols),
            transcendentals=0,
        ),
        name="norm_project",
    )(me, first, second, query_weight, kv_weight)


def attend_kernel(fast, columns_ref, keys_ref, bias_ref, cos_ref, sin_ref, *rest):
    pages_ref, out_ref, out_scr = (None, *rest) if fast else rest
    score_scale = 1.0 / math.sqrt(HEAD_DIM)
    half = HEAD_DIM // 2
    rows = 2 * GROUP
    columns = columns_ref[...].astype(F32)
    count = columns.shape[0]
    query = columns[:, :8, :].reshape(count * 8, HEAD_DIM)
    fresh = columns[:, 8:, :]
    if fast:
        planes = count // PLANE
        out_scr[...] = jnp.zeros_like(out_scr)
    row_step = lax.rem(lax.broadcasted_iota(jnp.int32, (count * 8, 1), 0) // 4, STEPS)
    later = row_step == 1
    cosine = jnp.where(later, cos_ref[1:2, :], cos_ref[0:1, :])
    sine = jnp.where(later, sin_ref[1:2, :], sin_ref[0:1, :])
    turned = (query * cosine + pltpu.roll(query, half, 1) * sine).astype(BF16)
    turned_wide = turned.astype(F32)
    step_later = later[:rows]
    bias = jnp.where(step_later, bias_ref[1:2, :], bias_ref[0:1, :])
    new_keys = []
    for step in range(STEPS):
        part = fresh[:KV_HEADS, step, :]
        new = part * cos_ref[step : step + 1, :] + pltpu.roll(part, half, 1) * sin_ref[step : step + 1, :]
        new_keys.append(new.astype(BF16).astype(F32))
    for head in range(KV_HEADS):
        lanes = slice(head * HEAD_DIM, (head + 1) * HEAD_DIM)
        mine = slice(head * rows, (head + 1) * rows)
        scores = (
            lax.dot_general(
                turned[mine], keys_ref[:, lanes], (((1,), (1,)), ((), ())),
                preferred_element_type=F32,
            )
            * score_scale
            + bias
        )
        recent0 = (
            jnp.sum(turned_wide[mine] * new_keys[0][head : head + 1, :], axis=1, keepdims=True)
            * score_scale
        )
        recent1 = (
            jnp.sum(turned_wide[mine] * new_keys[1][head : head + 1, :], axis=1, keepdims=True)
            * score_scale
        )
        recent1 = jnp.where(step_later, recent1, -1e30)
        largest = jnp.maximum(
            jnp.max(scores, axis=1, keepdims=True), jnp.maximum(recent0, recent1)
        )
        cache_exp = jnp.exp(scores - largest)
        exp0 = jnp.exp(recent0 - largest)
        exp1 = jnp.exp(recent1 - largest)
        denominator = jnp.sum(cache_exp, axis=1, keepdims=True) + (exp0 + exp1)
        weights = (cache_exp / denominator).astype(BF16)
        weight0 = (exp0 / denominator).astype(BF16).astype(F32)
        weight1 = (exp1 / denominator).astype(BF16).astype(F32)
        recent = weight0 * fresh[KV_HEADS + head, 0:1, :]
        recent = recent + weight1 * fresh[KV_HEADS + head, 1:2, :]
        if not fast:
            values = pages_ref[:, :, lanes].reshape(keys_ref.shape[0], HEAD_DIM)
            mixed = jnp.dot(weights, values, preferred_element_type=F32)
            out_ref[mine, :] = (mixed + recent).astype(BF16)
            continue
        weights = weights.astype(F32)
        z, x = divmod(head, 2)
        for c in range(2):
            part = slice(c * 8, (c + 1) * 8)
            for plane in range(planes):
                out_scr[plane * PLANE + 2 * x + c, z * 8 : (z + 1) * 8, :] = weights[
                    part, plane * LANES : (plane + 1) * LANES
                ]
            out_scr[z * PLANE + 2 * x + c, planes * 8 : planes * 8 + 8, :] = recent[part]
    if fast:
        out_ref[...] = out_scr[...].astype(BF16)


def attend(columns, keys, bias, cosine, sine, pages, fast):
    seq, width = keys.shape
    count = columns.shape[0]
    if fast:
        shape = (count, count // PLANE * 8 + 16, LANES)
        scratch = [VMEM(shape, F32)]
        operands = (columns, keys, bias, cosine, sine)
    else:
        shape = (STEPS * HEADS, HEAD_DIM)
        scratch = [VMEM((8, LANES), F32)]
        operands = (columns, keys, bias, cosine, sine, pages)
    return pl.pallas_call(
        functools.partial(attend_kernel, fast),
        in_specs=[whole()] * len(operands),
        out_specs=whole(),
        out_shape=jax.ShapeDtypeStruct(shape, BF16),
        scratch_shapes=scratch,
        compiler_params=pltpu.CompilerParams(vmem_limit_bytes=48 * 2**20),
        cost_estimate=pl.CostEstimate(
            flops=4 * STEPS * HEADS * seq * HEAD_DIM,
            bytes_accessed=4 * seq * width,
            transcendentals=STEPS * HEADS * seq,
        ),
        name="attend",
    )(*operands)


def output_kernel(fast, count, me_ref, weight_ref, *rest):
    lhs_refs, rest = rest[:count], rest[count:]
    out_refs, (out_scr, heads_scr) = rest[:-2], rest[-2:]
    chunks = 8
    span = weight_ref.shape[1] // chunks
    rows = out_scr.shape[0] * LANES // (chunks * span)
    pieces = chunks * span // LANES
    if fast:
        per = heads_scr.shape[0] // rows
        total = lhs_refs[0][...].astype(F32)
        for lhs_ref in lhs_refs[1:]:
            total = total + lhs_ref[...].astype(F32)
        heads_scr[...] = total
        lhs = jnp.concatenate(
            [heads_scr[pl.ds(g, rows, stride=per), :].astype(BF16) for g in range(per)], axis=1
        )
    else:
        lhs = lhs_refs[0][...]
    for i in range(chunks):
        part = jnp.dot(
            lhs, weight_ref[:, i * span : (i + 1) * span], preferred_element_type=F32
        )
        for c in range(span // LANES):
            out_scr[pl.ds(i * (span // LANES) + c, rows, stride=pieces), :] = part[
                :, c * LANES : (c + 1) * LANES
            ]
    if not fast:
        out_refs[0][...] = out_scr[...].astype(BF16)
        return
    low = jnp.bitwise_and(me_ref[0], 1)
    for out_ref, core in zip(out_refs, (low, 1 - low)):
        count, size, _ = out_ref.shape
        for j in range(count):
            part = pl.ds(pl.multiple_of((2 * j + core) * size, size), size)
            out_ref[j] = out_scr[part, :].astype(BF16)


def output(me, lhs, weight, rows, fast):
    depth, width = weight.shape
    if fast:
        shape = (rows // (2 * STEPS), STEPS * width // LANES, LANES)
        shapes = (jax.ShapeDtypeStruct(shape, BF16),) * 2
    else:
        shapes = (jax.ShapeDtypeStruct((rows * width // LANES, LANES), BF16),)
    return pl.pallas_call(
        functools.partial(output_kernel, fast, len(lhs)),
        in_specs=[whole(SMEM)] + [whole()] * (1 + len(lhs)),
        out_specs=(whole(),) * len(shapes),
        out_shape=shapes,
        scratch_shapes=[
            VMEM((rows * width // LANES, LANES), F32),
            VMEM(lhs[0].shape if fast else (8, LANES), F32),
        ],
        compiler_params=pltpu.CompilerParams(vmem_limit_bytes=24 * 2**20),
        cost_estimate=pl.CostEstimate(
            flops=2 * rows * depth * width, bytes_accessed=2 * depth * width, transcendentals=0
        ),
        name="output_project",
    )(me, weight, *lhs)


def swap(block, bit, devices):
    return lax.ppermute(block, AXIS, [(i, i ^ bit) for i in range(devices)])


def exchange(blocks, groups=None):
    return lax.all_to_all(
        blocks, AXIS, split_axis=0, concat_axis=0, tiled=True, axis_index_groups=groups
    )


def local(
    hidden,
    norm_gain,
    query_weight,
    kv_weight,
    out_weight,
    key_factors,
    key_basis,
    value_store,
    lengths,
    block_slot,
    selection,
):
    devices = lax.axis_size(AXIS)
    me = lax.axis_index(AXIS)
    slots_dev, block_len, width = value_store.shape
    seq = key_factors.shape[1]
    pages = block_slot.shape[1]
    model = hidden.shape[2]
    q_cols = query_weight.shape[1]
    k_cols = kv_weight.shape[1]
    fast = devices == 2 * PAIRS and q_cols == 4 * HEAD_DIM and k_cols == HEAD_DIM
    pieces = model // LANES

    me_word = me.astype(jnp.int32).reshape(1)
    block, holder, pair = prepare(
        hidden[:, 0], norm_gain.reshape(pieces, LANES), block_slot, slots_dev, PAIRS if fast else 1
    )
    if fast:
        same_core = [list(range(core, devices, 2)) for core in range(2)]
        block = exchange(block, same_core)
        x = lax.bitwise_and(lax.shift_right_logical(me_word, 1), 1)
        keep, send = split_values(x, value_store)
        block, kv_weight, send = lax.optimization_barrier((block, kv_weight, send))
        kv_weight = fetch(kv_weight, 50)
        other = swap(block, 1, devices)
        order = None
        neighbour = swap(send, 2, devices)
    else:
        order = [0]
        bit = devices // 2
        while bit:
            other = swap(block, bit, devices)
            order = order + [k ^ bit for k in order]
            bit //= 2
            if bit:
                block = jnp.concatenate([block, other], axis=0)
        order = tuple(order)
    span = 2 * block_len
    places = (pair[:, None] * span + jnp.arange(span, dtype=jnp.int32)[None, :]).reshape(-1)
    if not fast:
        sent_pages = pick_pages(me_word, block, other, value_store, order)
        block, other, sent_pages = lax.optimization_barrier((block, other, sent_pages))
        fetched = exchange(sent_pages)
    projected = project(
        me_word, block, other, query_weight, kv_weight, order, fast
    )
    if fast:
        projected, rows = projected
        projected, places = lax.optimization_barrier((projected, places))
        columns = exchange(projected)
    else:
        targets = jnp.bitwise_xor(me, jnp.array(order, dtype=jnp.int32))
        columns = exchange(projected.reshape(devices, STEPS, q_cols + k_cols)[targets])
        query = columns[:, :, :q_cols].transpose(1, 0, 2).reshape(STEPS, HEADS // 4, 4, HEAD_DIM)
        query = query.transpose(1, 0, 2, 3).reshape(HEADS // 4, 8, HEAD_DIM)
        fresh = columns[:, :, q_cols:].transpose(1, 0, 2).reshape(STEPS, HEADS // 4, HEAD_DIM)
        fresh = jnp.pad(fresh.transpose(1, 0, 2), ((0, 0), (0, 8 - STEPS), (0, 0)))
        columns = jnp.concatenate([query, fresh], axis=1)

    cosine, sine = turn_tables(places.astype(F32))
    keys = make_keys(pair, key_factors[0], key_basis[0], cosine, sine)
    picked = jnp.any(
        selection[:, 0, :, None] == (places // block_len)[None, None, :], axis=1
    )
    bias = jnp.where(picked & (places < lengths[0])[None, :], 0.0, -1e30).astype(F32)
    new_cos, new_sin = turn_tables(
        (lengths[0] + jnp.arange(STEPS, dtype=jnp.int32)).astype(F32)
    )
    if fast:
        blocks = attend(columns, keys, bias, new_cos, new_sin, None, True)
        blocks, neighbour = lax.optimization_barrier((blocks, neighbour))
        stores = (keep, swap(keep, 1, devices), neighbour, swap(neighbour, 1, devices))
        blocks = exchange(blocks)
        parts = mix(me_word, rows, blocks, stores)
        (*parts, out_weight) = lax.optimization_barrier((*parts, out_weight))
        out_weight = fetch(out_weight, 43)
        lhs = [parts[0]] + [swap(parts[q], q * PLANE, devices) for q in range(1, len(parts))]
    else:
        heads = attend(columns, keys, bias, new_cos, new_sin, fetched, False)
        flat = heads.reshape(HEADS // 4, STEPS, 4 * HEAD_DIM).transpose(1, 0, 2)
        flat = flat.reshape(STEPS, devices, model // devices).transpose(1, 0, 2)
        lhs = [exchange(flat).reshape(devices * STEPS, model // devices)]
    partial = output(me_word, lhs, out_weight, devices * STEPS, fast)
    if fast:
        near, far = partial
        both = near.astype(F32) + swap(far, 1, devices).astype(F32)
        arrived = exchange(both.astype(BF16), same_core)
    else:
        arrived = exchange(partial[0].reshape(devices, STEPS * pieces, LANES))
    total = jnp.sum(arrived.astype(F32), axis=0).astype(BF16)
    return total.reshape(STEPS, 1, model)


def solution(mesh):
    return jax.shard_map(
        local,
        mesh=mesh,
        in_specs=(
            P(None, ("groups", "session"), None),
            P(),
            P(None, "session"),
            P(None, "session"),
            P("session", None),
            P(("groups", "session"), None, None),
            P(("groups", "session"), None, None),
            P(("groups", "session"), None, None),
            P(("groups", "session")),
            P(("groups", "session"), None),
            P(None, ("groups", "session"), None),
        ),
        out_specs=P(None, ("groups", "session"), None),
        check_vma=False,
    )
```

```python
import functools
import math

import jax
import jax.numpy as jnp
from jax import lax
from jax.experimental import pallas as pl
from jax.experimental.pallas import tpu as pltpu
from jax.sharding import PartitionSpec as P

HEADS = 64
KV_HEADS = 8
HEAD_DIM = 128
STEPS = 2
GROUP = HEADS // KV_HEADS
LANES = 128
EXTRA = 16
PLANE = 4
PAIRS = 8
PROJECT_LIMIT = 48 * 2**20
AXIS = "session"
VMEM = pltpu.VMEM
SMEM = pltpu.SMEM
F32 = jnp.float32
BF16 = jnp.bfloat16


def angles(positions):
    half = HEAD_DIM // 2
    frequency = jnp.exp(
        -jnp.arange(half, dtype=F32) * (2.0 * math.log(500000.0) / HEAD_DIM)
    )
    return positions[..., None] * frequency


def turn_tables(positions):
    angle = angles(positions)
    cosine, sine = jnp.cos(angle), jnp.sin(angle)
    return (
        jnp.concatenate([cosine, cosine], axis=-1),
        jnp.concatenate([-sine, sine], axis=-1),
    )


def origin(me, order, j):
    if order is None:
        return 2 * (j % PAIRS) + jnp.bitwise_xor(jnp.bitwise_and(me, 1), j // PAIRS)
    return jnp.bitwise_xor(me, order[j])


def whole(space=VMEM):
    return pl.BlockSpec(memory_space=space)


def prepare_kernel(
    slots_dev, hidden_ref, gain_ref, slots_ref, block_ref, pair_ref, wide_scr
):
    steps, model = hidden_ref.shape
    pieces = model // LANES
    wide = hidden_ref[...].astype(F32)
    scale = lax.rsqrt(jnp.mean(wide * wide, axis=1, keepdims=True) + 1e-05)
    wide = wide * scale
    for step in range(steps):
        for c in range(pieces):
            row = step * pieces + c
            wide_scr[row : row + 1, :] = wide[step : step + 1, c * LANES : (c + 1) * LANES]
    lane = lax.broadcasted_iota(jnp.int32, (EXTRA, LANES), 1)
    parity = lax.broadcasted_iota(jnp.int32, (EXTRA, LANES), 0)
    table = jnp.zeros((EXTRA, LANES), jnp.int32)
    for m in range(pair_ref.shape[0]):
        slot = slots_ref[0, 2 * m]
        holder = lax.div(slot, slots_dev)
        pair_ref[holder] = m
        base = holder * slots_dev
        pair = jnp.where(parity == 0, slot - base, slots_ref[0, 2 * m + 1] - base)
        table = jnp.where(lane == holder, pair, table)
    wide_scr[steps * pieces :, :] = table.astype(F32)
    gain = gain_ref[...].astype(F32)
    for step in range(steps):
        rows = slice(step * pieces, (step + 1) * pieces)
        wide_scr[rows, :] = wide_scr[rows, :] * gain
    block = wide_scr[...].astype(BF16)
    for copy in range(block_ref.shape[0]):
        block_ref[copy] = block


def prepare(hidden, gain, block_slot, slots_dev, copies):
    assert slots_dev <= 256
    steps, model = hidden.shape
    rows = steps * model // LANES + EXTRA
    return pl.pallas_call(
        functools.partial(prepare_kernel, slots_dev),
        in_specs=[whole(), whole(), whole(SMEM)],
        out_specs=(whole(), whole(SMEM)),
        out_shape=(
            jax.ShapeDtypeStruct((copies, rows, LANES), BF16),
            jax.ShapeDtypeStruct((block_slot.shape[1] // 2,), jnp.int32),
        ),
        scratch_shapes=[VMEM((rows, LANES), F32)],
        name="prepare",
    )(hidden, gain, block_slot)


def pick_kernel(order, me_ref, first_ref, second_ref, store_ref, out_ref, table_scr, table_smem, sem):
    block_len = store_ref.shape[1]
    half, rows, _ = first_ref.shape
    for j in range(2 * half):
        source = first_ref if j < half else second_ref
        asked = source[j % half, rows - EXTRA :, :].astype(F32)
        table_scr[j] = asked[:8].astype(jnp.int32)
    copy = pltpu.make_async_copy(table_scr, table_smem, sem)
    copy.start()
    copy.wait()
    me = me_ref[0]
    for j in range(2 * half):
        target = origin(me, order, j)
        for k in range(2):
            out_ref[target, k * block_len : (k + 1) * block_len, :] = store_ref[
                table_smem[j, k, me]
            ]


def pick_pages(me, first, second, store, order):
    count = 2 * first.shape[0]
    _, block_len, width = store.shape
    return pl.pallas_call(
        functools.partial(pick_kernel, order),
        in_specs=[whole(SMEM), whole(), whole(), whole()],
        out_specs=whole(),
        out_shape=jax.ShapeDtypeStruct((count, 2 * block_len, width), store.dtype),
        scratch_shapes=[
            VMEM((count, 8, LANES), jnp.int32),
            SMEM((count, 8, LANES), jnp.int32),
            pltpu.SemaphoreType.DMA(()),
        ],
        compiler_params=pltpu.CompilerParams(vmem_limit_bytes=36 * 2**20),
        name="pick_pages",
    )(me, first, second, store)


def split_kernel(x_ref, store_ref, keep_ref, send_ref):
    slots, block_len, width = store_ref.shape
    for x in range(2):

        @pl.when(x_ref[0] == x)
        def _():
            for head in range(width // LANES):
                target = keep_ref if head % 2 == x else send_ref
                lanes = slice(head // 2 * LANES, (head // 2 + 1) * LANES)
                part = store_ref[:, :, head * LANES : (head + 1) * LANES]
                target[:, lanes] = part.reshape(slots * block_len, LANES)


def split_values(x, store):
    slots, block_len, width = store.shape
    half = jax.ShapeDtypeStruct((slots * block_len, width // 2), store.dtype)
    return pl.pallas_call(
        split_kernel,
        in_specs=[whole(SMEM), whole()],
        out_specs=(whole(), whole()),
        out_shape=(half, half),
        compiler_params=pltpu.CompilerParams(vmem_limit_bytes=16 * 2**20),
        name="split_values",
    )(x, store)


def mix_kernel(me_ref, rows_ref, weights_ref, *rest):
    stores, (values_scr, sum_scr) = rest[:PLANE], rest[-2:]
    out_refs = rest[PLANE:-2]
    me = me_ref[0]
    low = jnp.bitwise_and(me, PLANE - 1)
    z_me = lax.div(me, PLANE)
    sessions = weights_ref.shape[0]
    planes = len(out_refs)
    block_len = values_scr.shape[1] // (2 * PLANE)
    for session in range(sessions):
        for q, store in enumerate(stores):
            device = jnp.bitwise_xor(low, q)
            for k in range(2):
                row = rows_ref[session * (2 * PLANE) + k * PLANE + device]
                source = pl.ds(pl.multiple_of(row * block_len, block_len), block_len)
                target = pl.ds(
                    pl.multiple_of((device * 2 + k) * block_len, block_len), block_len
                )
                values_scr[session, target, :] = store[source, :]
        block = weights_ref[session]
        product = jnp.dot(
            block[: planes * 8], values_scr[session], preferred_element_type=F32
        )
        mine = slice(session * 8, (session + 1) * 8)
        for z in range(planes):
            sum_scr[z, mine, :] = product[z * 8 : (z + 1) * 8, z * LANES : (z + 1) * LANES]
        recent = block[planes * 8 :].astype(F32)
        sum_scr[z_me, mine, :] += recent[:8]
    for q, out_ref in enumerate(out_refs):
        out_ref[...] = sum_scr[jnp.bitwise_xor(z_me, q)].astype(BF16)


def mix(me, rows, weights, stores):
    sessions = weights.shape[0]
    planes = stores[0].shape[1] // LANES
    shape = (planes, sessions * 8, LANES)
    return pl.pallas_call(
        mix_kernel,
        in_specs=[whole(SMEM)] * 2 + [whole()] * (1 + PLANE),
        out_specs=(whole(),) * planes,
        out_shape=(jax.ShapeDtypeStruct(shape[1:], BF16),) * planes,
        scratch_shapes=[VMEM((sessions, LANES, planes * LANES), BF16), VMEM(shape, F32)],
        compiler_params=pltpu.CompilerParams(vmem_limit_bytes=16 * 2**20),
        cost_estimate=pl.CostEstimate(
            flops=2 * sessions * 32 * LANES * planes * LANES,
            bytes_accessed=4 * stores[0].size * PLANE,
            transcendentals=0,
        ),
        name="mix_values",
    )(me, rows, weights, *stores)


def keys_kernel(pair_ref, factors_ref, basis_ref, cos_ref, sin_ref, out_ref, rows_scr):
    span = factors_ref.shape[0] // pair_ref.shape[0]
    count = rows_scr.shape[0] // span
    base = pl.program_id(0) * count
    for p in range(count):
        source = pl.ds(pl.multiple_of(pair_ref[base + p] * span, span), span)
        rows_scr[p * span : (p + 1) * span, :] = factors_ref[source, :]
    product = jnp.dot(rows_scr[...], basis_ref[...], preferred_element_type=F32)
    cosine, sine = cos_ref[...], sin_ref[...]
    for head in range(KV_HEADS):
        lanes = slice(head * HEAD_DIM, (head + 1) * HEAD_DIM)
        part = product[:, lanes]
        turned = part * cosine + pltpu.roll(part, HEAD_DIM // 2, 1) * sine
        out_ref[:, lanes] = turned.astype(BF16)


def make_keys(pair, factors, basis, cosine, sine):
    seq, rank = factors.shape
    width = basis.shape[1]
    rows = min(seq, 512)
    return pl.pallas_call(
        keys_kernel,
        grid=(seq // rows,),
        in_specs=[
            whole(SMEM),
            pl.BlockSpec((seq, rank), lambda i: (0, 0)),
            pl.BlockSpec((rank, width), lambda i: (0, 0)),
            pl.BlockSpec((rows, HEAD_DIM), lambda i: (i, 0)),
            pl.BlockSpec((rows, HEAD_DIM), lambda i: (i, 0)),
        ],
        out_specs=pl.BlockSpec((rows, width), lambda i: (i, 0)),
        out_shape=jax.ShapeDtypeStruct((seq, width), BF16),
        scratch_shapes=[VMEM((rows, rank), BF16)],
        compiler_params=pltpu.CompilerParams(vmem_limit_bytes=32 * 2**20),
        cost_estimate=pl.CostEstimate(
            flops=2 * seq * rank * width, bytes_accessed=4 * seq * width, transcendentals=0
        ),
        name="turned_keys",
    )(pair, factors, basis, cosine, sine)


def fetch_kernel(source_ref, target_ref, sems):
    parts = sems.shape[0]
    span = source_ref.shape[0] // parts
    copies = []
    for part in range(parts):
        rows = pl.ds(part * span, span)
        copies.append(
            pltpu.make_async_copy(source_ref.at[rows, :], target_ref.at[rows, :], sems.at[part])
        )
        copies[-1].start()
    for copy in copies:
        copy.wait()


def fetch(weight, limit):
    return pl.pallas_call(
        fetch_kernel,
        in_specs=[whole(pl.ANY)],
        out_specs=whole(pl.ANY),
        out_shape=jax.ShapeDtypeStruct(weight.shape, weight.dtype),
        scratch_shapes=[pltpu.SemaphoreType.DMA((4,))],
        compiler_params=pltpu.CompilerParams(vmem_limit_bytes=limit * 2**20),
        cost_estimate=pl.CostEstimate(
            flops=0, bytes_accessed=2 * weight.size, transcendentals=0
        ),
        name="fetch_weight",
    )(weight)


def project_kernel(
    order, fast, me_ref, first_ref, second_ref, wq_ref, wk_ref, out_ref, *rest
):
    if fast:
        rows_ref, x_scr, lhs_scr, wq_buf, out_scr, sems, *asked_scr = rest
    else:
        x_scr, lhs_scr, wq_buf, out_scr, sems = rest
    depth, q_cols = wq_ref.shape
    k_cols = wk_ref.shape[1]
    chunks = wq_buf.shape[0]
    span = depth // chunks
    pieces = depth // LANES
    copies = []
    parts = sems.shape[1]
    for i in range(chunks):
        copies.append([])
        for part in range(parts):
            copy = pltpu.make_async_copy(
                wq_ref.at[pl.ds(i * span + part * (span // parts), span // parts), :],
                wq_buf.at[i, pl.ds(part * (span // parts), span // parts), :],
                sems.at[i, part],
            )
            copy.start()
            copies[-1].append(copy)
    half = first_ref.shape[0]
    count = 2 * half * STEPS
    rows = STEPS * pieces
    for j in range(2 * half):
        source = first_ref if j < half else second_ref
        x_scr[j * rows : (j + 1) * rows] = source[j % half, :rows, :].astype(F32)
    if fast:
        table_scr, table_smem, table_sem = asked_scr
        for j in range(2 * half):
            source = first_ref if j < half else second_ref
            asked = source[j % half, rows:, :].astype(F32)
            table_scr[2 * j : 2 * j + 2, :] = asked[:2].astype(jnp.int32)
        table_copy = pltpu.make_async_copy(table_scr, table_smem, table_sem)
        table_copy.start()
    for c in range(pieces):
        part = x_scr[pl.ds(c, count, stride=pieces), :]
        lhs_scr[:, c * LANES : (c + 1) * LANES] = part.astype(BF16)
    if fast:
        me = me_ref[0]
        out_scr[...] = jnp.zeros_like(out_scr)
        table_copy.wait()
        plane = jnp.bitwise_and(me, -PLANE)
        for j in range(2 * half):
            place = origin(me, order, j) * (2 * PLANE)
            for k in range(2):
                for b in range(PLANE):
                    rows_ref[place + k * PLANE + b] = table_smem[2 * j + k, plane + b]
    q_sum = jnp.zeros((count, q_cols), F32)
    k_sum = jnp.zeros((count, k_cols), F32)
    for i in range(chunks):
        for copy in copies[i]:
            copy.wait()
        lhs = lhs_scr[:, i * span : (i + 1) * span]
        q_sum = q_sum + jnp.dot(lhs, wq_buf[i], preferred_element_type=F32)
        k_sum = k_sum + jnp.dot(
            lhs, wk_ref[i * span : (i + 1) * span, :], preferred_element_type=F32
        )
    if not fast:
        out_ref[:, :q_cols] = q_sum.astype(BF16)
        out_ref[:, q_cols:] = k_sum.astype(BF16)
        return
    per = q_cols // LANES
    for j in range(2 * half):
        place = origin(me, order, j)
        for step in range(STEPS):
            row = j * STEPS + step
            for c in range(per):
                out_scr[place, step * per + c : step * per + c + 1, :] = q_sum[
                    row : row + 1, c * LANES : (c + 1) * LANES
                ]
            out_scr[place, STEPS * per + step : STEPS * per + step + 1, :] = k_sum[
                row : row + 1, :
            ]
    out_ref[...] = out_scr[...].astype(BF16)


def project(me, first, second, query_weight, kv_weight, order, fast):
    depth, q_cols = query_weight.shape
    k_cols = kv_weight.shape[1]
    pieces = depth // LANES
    devices = 2 * first.shape[0]
    rows = devices * STEPS
    chunks = 8
    span = depth // chunks
    shape = (devices, 16, LANES) if fast else (rows, q_cols + k_cols)
    return pl.pallas_call(
        functools.partial(project_kernel, order, fast),
        in_specs=[whole(SMEM), whole(), whole(), whole(pl.ANY), whole()],
        out_specs=(whole(), whole(SMEM)) if fast else whole(),
        out_shape=(
            (
                jax.ShapeDtypeStruct(shape, BF16),
                jax.ShapeDtypeStruct((devices * 2 * PLANE,), jnp.int32),
            )
            if fast
            else jax.ShapeDtypeStruct(shape, BF16)
        ),
        scratch_shapes=[
            VMEM((rows * pieces, LANES), F32),
            VMEM((rows, depth), BF16),
            VMEM((chunks, span, q_cols), BF16),
            VMEM((devices, 16, LANES) if fast else (8, LANES), F32),
            pltpu.SemaphoreType.DMA((chunks, 4)),
        ]
        + (
            [
                VMEM((2 * devices, LANES), jnp.int32),
                SMEM((2 * devices, LANES), jnp.int32),
                pltpu.SemaphoreType.DMA(()),
            ]
            if fast
            else []
        ),
        compiler_params=pltpu.CompilerParams(vmem_limit_bytes=PROJECT_LIMIT),
        cost_estimate=pl.CostEstimate(
            flops=2 * rows * depth * (q_cols + k_cols),
            bytes_accessed=2 * depth * (q_cols + k_cols),
            transcendentals=0,
        ),
        name="norm_project",
    )(me, first, second, query_weight, kv_weight)


def attend_kernel(fast, columns_ref, keys_ref, bias_ref, cos_ref, sin_ref, *rest):
    pages_ref, out_ref, out_scr = (None, *rest) if fast else rest
    score_scale = 1.0 / math.sqrt(HEAD_DIM)
    half = HEAD_DIM // 2
    rows = 2 * GROUP
    columns = columns_ref[...].astype(F32)
    count = columns.shape[0]
    query = columns[:, :8, :].reshape(count * 8, HEAD_DIM)
    fresh = columns[:, 8:, :]
    if fast:
        planes = count // PLANE
        out_scr[...] = jnp.zeros_like(out_scr)
    row_step = lax.rem(lax.broadcasted_iota(jnp.int32, (count * 8, 1), 0) // 4, STEPS)
    later = row_step == 1
    cosine = jnp.where(later, cos_ref[1:2, :], cos_ref[0:1, :])
    sine = jnp.where(later, sin_ref[1:2, :], sin_ref[0:1, :])
    turned = (query * cosine + pltpu.roll(query, half, 1) * sine).astype(BF16)
    turned_wide = turned.astype(F32)
    step_later = later[:rows]
    bias = jnp.where(step_later, bias_ref[1:2, :], bias_ref[0:1, :])
    new_keys = []
    for step in range(STEPS):
        part = fresh[:KV_HEADS, step, :]
        new = part * cos_ref[step : step + 1, :] + pltpu.roll(part, half, 1) * sin_ref[step : step + 1, :]
        new_keys.append(new.astype(BF16).astype(F32))
    for head in range(KV_HEADS):
        lanes = slice(head * HEAD_DIM, (head + 1) * HEAD_DIM)
        mine = slice(head * rows, (head + 1) * rows)
        scores = (
            lax.dot_general(
                turned[mine], keys_ref[:, lanes], (((1,), (1,)), ((), ())),
                preferred_element_type=F32,
            )
            * score_scale
            + bias
        )
        recent0 = (
            jnp.sum(turned_wide[mine] * new_keys[0][head : head + 1, :], axis=1, keepdims=True)
            * score_scale
        )
        recent1 = (
            jnp.sum(turned_wide[mine] * new_keys[1][head : head + 1, :], axis=1, keepdims=True)
            * score_scale
        )
        recent1 = jnp.where(step_later, recent1, -1e30)
        largest = jnp.maximum(
            jnp.max(scores, axis=1, keepdims=True), jnp.maximum(recent0, recent1)
        )
        cache_exp = jnp.exp(scores - largest)
        exp0 = jnp.exp(recent0 - largest)
        exp1 = jnp.exp(recent1 - largest)
        denominator = jnp.sum(cache_exp, axis=1, keepdims=True) + (exp0 + exp1)
        weights = (cache_exp / denominator).astype(BF16)
        weight0 = (exp0 / denominator).astype(BF16).astype(F32)
        weight1 = (exp1 / denominator).astype(BF16).astype(F32)
        recent = weight0 * fresh[KV_HEADS + head, 0:1, :]
        recent = recent + weight1 * fresh[KV_HEADS + head, 1:2, :]
        if not fast:
            values = pages_ref[:, :, lanes].reshape(keys_ref.shape[0], HEAD_DIM)
            mixed = jnp.dot(weights, values, preferred_element_type=F32)
            out_ref[mine, :] = (mixed + recent).astype(BF16)
            continue
        weights = weights.astype(F32)
        z, x = divmod(head, 2)
        for c in range(2):
            part = slice(c * 8, (c + 1) * 8)
            for plane in range(planes):
                out_scr[plane * PLANE + 2 * x + c, z * 8 : (z + 1) * 8, :] = weights[
                    part, plane * LANES : (plane + 1) * LANES
                ]
            out_scr[z * PLANE + 2 * x + c, planes * 8 : planes * 8 + 8, :] = recent[part]
    if fast:
        out_ref[...] = out_scr[...].astype(BF16)


def attend(columns, keys, bias, cosine, sine, pages, fast):
    seq, width = keys.shape
    count = columns.shape[0]
    if fast:
        shape = (count, count // PLANE * 8 + 16, LANES)
        scratch = [VMEM(shape, F32)]
        operands = (columns, keys, bias, cosine, sine)
    else:
        shape = (STEPS * HEADS, HEAD_DIM)
        scratch = [VMEM((8, LANES), F32)]
        operands = (columns, keys, bias, cosine, sine, pages)
    return pl.pallas_call(
        functools.partial(attend_kernel, fast),
        in_specs=[whole()] * len(operands),
        out_specs=whole(),
        out_shape=jax.ShapeDtypeStruct(shape, BF16),
        scratch_shapes=scratch,
        compiler_params=pltpu.CompilerParams(vmem_limit_bytes=48 * 2**20),
        cost_estimate=pl.CostEstimate(
            flops=4 * STEPS * HEADS * seq * HEAD_DIM,
            bytes_accessed=4 * seq * width,
            transcendentals=STEPS * HEADS * seq,
        ),
        name="attend",
    )(*operands)


def output_kernel(fast, count, me_ref, weight_ref, *rest):
    lhs_refs, rest = rest[:count], rest[count:]
    out_refs, (out_scr, heads_scr) = rest[:-2], rest[-2:]
    chunks = 8
    span = weight_ref.shape[1] // chunks
    rows = out_scr.shape[0] * LANES // (chunks * span)
    pieces = chunks * span // LANES
    if fast:
        per = heads_scr.shape[0] // rows
        total = lhs_refs[0][...].astype(F32)
        for lhs_ref in lhs_refs[1:]:
            total = total + lhs_ref[...].astype(F32)
        heads_scr[...] = total
        lhs = jnp.concatenate(
            [heads_scr[pl.ds(g, rows, stride=per), :].astype(BF16) for g in range(per)], axis=1
        )
    else:
        lhs = lhs_refs[0][...]
    for i in range(chunks):
        part = jnp.dot(
            lhs, weight_ref[:, i * span : (i + 1) * span], preferred_element_type=F32
        )
        for c in range(span // LANES):
            out_scr[pl.ds(i * (span // LANES) + c, rows, stride=pieces), :] = part[
                :, c * LANES : (c + 1) * LANES
            ]
    if not fast:
        out_refs[0][...] = out_scr[...].astype(BF16)
        return
    low = jnp.bitwise_and(me_ref[0], 1)
    for out_ref, core in zip(out_refs, (low, 1 - low)):
        count, size, _ = out_ref.shape
        for j in range(count):
            part = pl.ds(pl.multiple_of((2 * j + core) * size, size), size)
            out_ref[j] = out_scr[part, :].astype(BF16)


def output(me, lhs, weight, rows, fast):
    depth, width = weight.shape
    if fast:
        shape = (rows // (2 * STEPS), STEPS * width // LANES, LANES)
        shapes = (jax.ShapeDtypeStruct(shape, BF16),) * 2
    else:
        shapes = (jax.ShapeDtypeStruct((rows * width // LANES, LANES), BF16),)
    return pl.pallas_call(
        functools.partial(output_kernel, fast, len(lhs)),
        in_specs=[whole(SMEM)] + [whole()] * (1 + len(lhs)),
        out_specs=(whole(),) * len(shapes),
        out_shape=shapes,
        scratch_shapes=[
            VMEM((rows * width // LANES, LANES), F32),
            VMEM(lhs[0].shape if fast else (8, LANES), F32),
        ],
        compiler_params=pltpu.CompilerParams(vmem_limit_bytes=24 * 2**20),
        cost_estimate=pl.CostEstimate(
            flops=2 * rows * depth * width, bytes_accessed=2 * depth * width, transcendentals=0
        ),
        name="output_project",
    )(me, weight, *lhs)


def swap(block, bit, devices):
    return lax.ppermute(block, AXIS, [(i, i ^ bit) for i in range(devices)])


def exchange(blocks, groups=None):
    return lax.all_to_all(
        blocks, AXIS, split_axis=0, concat_axis=0, tiled=True, axis_index_groups=groups
    )


def local(
    hidden,
    norm_gain,
    query_weight,
    kv_weight,
    out_weight,
    key_factors,
    key_basis,
    value_store,
    lengths,
    block_slot,
    selection,
):
    devices = lax.axis_size(AXIS)
    me = lax.axis_index(AXIS)
    slots_dev, block_len, width = value_store.shape
    seq = key_factors.shape[1]
    pages = block_slot.shape[1]
    model = hidden.shape[2]
    q_cols = query_weight.shape[1]
    k_cols = kv_weight.shape[1]
    fast = devices == 2 * PAIRS and q_cols == 4 * HEAD_DIM and k_cols == HEAD_DIM
    pieces = model // LANES

    me_word = me.astype(jnp.int32).reshape(1)
    block, pair = prepare(
        hidden[:, 0], norm_gain.reshape(pieces, LANES), block_slot, slots_dev, PAIRS if fast else 1
    )
    if fast:
        same_core = [list(range(core, devices, 2)) for core in range(2)]
        block = exchange(block, same_core)
        block, kv_weight = lax.optimization_barrier((block, kv_weight))
        kv_weight = fetch(kv_weight, 50)
        other = swap(block, 1, devices)
        order = None
        x = lax.bitwise_and(lax.shift_right_logical(me_word, 1), 1)
        keep, send = split_values(x, value_store)
        neighbour = swap(send, 2, devices)
    else:
        order = [0]
        bit = devices // 2
        while bit:
            other = swap(block, bit, devices)
            order = order + [k ^ bit for k in order]
            bit //= 2
            if bit:
                block = jnp.concatenate([block, other], axis=0)
        order = tuple(order)
    span = 2 * block_len
    places = (pair[:, None] * span + jnp.arange(span, dtype=jnp.int32)[None, :]).reshape(-1)
    if not fast:
        sent_pages = pick_pages(me_word, block, other, value_store, order)
        block, other, sent_pages = lax.optimization_barrier((block, other, sent_pages))
        fetched = exchange(sent_pages)
    projected = project(
        me_word, block, other, query_weight, kv_weight, order, fast
    )
    if fast:
        projected, rows = projected
        projected, places = lax.optimization_barrier((projected, places))
        columns = exchange(projected)
    else:
        targets = jnp.bitwise_xor(me, jnp.array(order, dtype=jnp.int32))
        columns = exchange(projected.reshape(devices, STEPS, q_cols + k_cols)[targets])
        query = columns[:, :, :q_cols].transpose(1, 0, 2).reshape(STEPS, HEADS // 4, 4, HEAD_DIM)
        query = query.transpose(1, 0, 2, 3).reshape(HEADS // 4, 8, HEAD_DIM)
        fresh = columns[:, :, q_cols:].transpose(1, 0, 2).reshape(STEPS, HEADS // 4, HEAD_DIM)
        fresh = jnp.pad(fresh.transpose(1, 0, 2), ((0, 0), (0, 8 - STEPS), (0, 0)))
        columns = jnp.concatenate([query, fresh], axis=1)

    cosine, sine = turn_tables(places.astype(F32))
    keys = make_keys(pair, key_factors[0], key_basis[0], cosine, sine)
    picked = jnp.any(
        selection[:, 0, :, None] == (places // block_len)[None, None, :], axis=1
    )
    bias = jnp.where(picked & (places < lengths[0])[None, :], 0.0, -1e30).astype(F32)
    new_cos, new_sin = turn_tables(
        (lengths[0] + jnp.arange(STEPS, dtype=jnp.int32)).astype(F32)
    )
    if fast:
        blocks = attend(columns, keys, bias, new_cos, new_sin, None, True)
        blocks, neighbour = lax.optimization_barrier((blocks, neighbour))
        stores = (keep, swap(keep, 1, devices), neighbour, swap(neighbour, 1, devices))
        blocks = exchange(blocks)
        parts = mix(me_word, rows, blocks, stores)
        (*parts, out_weight) = lax.optimization_barrier((*parts, out_weight))
        out_weight = fetch(out_weight, 43)
        lhs = [parts[0]] + [swap(parts[q], q * PLANE, devices) for q in range(1, len(parts))]
    else:
        heads = attend(columns, keys, bias, new_cos, new_sin, fetched, False)
        flat = heads.reshape(HEADS // 4, STEPS, 4 * HEAD_DIM).transpose(1, 0, 2)
        flat = flat.reshape(STEPS, devices, model // devices).transpose(1, 0, 2)
        lhs = [exchange(flat).reshape(devices * STEPS, model // devices)]
    partial = output(me_word, lhs, out_weight, devices * STEPS, fast)
    if fast:
        near, far = partial
        both = near.astype(F32) + swap(far, 1, devices).astype(F32)
        arrived = exchange(both.astype(BF16), same_core)
    else:
        arrived = exchange(partial[0].reshape(devices, STEPS * pieces, LANES))
    total = jnp.sum(arrived.astype(F32), axis=0).astype(BF16)
    return total.reshape(STEPS, 1, model)


def solution(mesh):
    return jax.shard_map(
        local,
        mesh=mesh,
        in_specs=(
            P(None, ("groups", "session"), None),
            P(),
            P(None, "session"),
            P(None, "session"),
            P("session", None),
            P(("groups", "session"), None, None),
            P(("groups", "session"), None, None),
            P(("groups", "session"), None, None),
            P(("groups", "session")),
            P(("groups", "session"), None),
            P(None, ("groups", "session"), None),
        ),
        out_specs=P(None, ("groups", "session"), None),
        check_vma=False,
    )
```

```python
import functools
import math

import jax
import jax.numpy as jnp
from jax import lax
from jax.experimental import pallas as pl
from jax.experimental.pallas import tpu as pltpu
from jax.sharding import PartitionSpec as P

HEADS = 64
KV_HEADS = 8
HEAD_DIM = 128
STEPS = 2
GROUP = HEADS // KV_HEADS
LANES = 128
EXTRA = 16
PLANE = 4
PAIRS = 8
PROJECT_LIMIT = 48 * 2**20
AXIS = "session"
VMEM = pltpu.VMEM
SMEM = pltpu.SMEM
F32 = jnp.float32
BF16 = jnp.bfloat16


def angles(positions):
    half = HEAD_DIM // 2
    frequency = jnp.exp(
        -jnp.arange(half, dtype=F32) * (2.0 * math.log(500000.0) / HEAD_DIM)
    )
    return positions[..., None] * frequency


def turn_tables(positions):
    angle = angles(positions)
    cosine, sine = jnp.cos(angle), jnp.sin(angle)
    return (
        jnp.concatenate([cosine, cosine], axis=-1),
        jnp.concatenate([-sine, sine], axis=-1),
    )


def origin(me, order, j):
    if order is None:
        return 2 * (j % PAIRS) + jnp.bitwise_xor(jnp.bitwise_and(me, 1), j // PAIRS)
    return jnp.bitwise_xor(me, order[j])


def whole(space=VMEM):
    return pl.BlockSpec(memory_space=space)


def prepare_kernel(
    slots_dev, hidden_ref, gain_ref, slots_ref, block_ref, holder_ref, pair_ref, wide_scr
):
    steps, model = hidden_ref.shape
    pieces = model // LANES
    wide = hidden_ref[...].astype(F32)
    scale = lax.rsqrt(jnp.mean(wide * wide, axis=1, keepdims=True) + 1e-05)
    wide = wide * scale
    for step in range(steps):
        for c in range(pieces):
            row = step * pieces + c
            wide_scr[row : row + 1, :] = wide[step : step + 1, c * LANES : (c + 1) * LANES]
    lane = lax.broadcasted_iota(jnp.int32, (EXTRA, LANES), 1)
    parity = lax.broadcasted_iota(jnp.int32, (EXTRA, LANES), 0)
    table = jnp.zeros((EXTRA, LANES), jnp.int32)
    for m in range(holder_ref.shape[0]):
        slot = slots_ref[0, 2 * m]
        holder = lax.div(slot, slots_dev)
        holder_ref[m] = holder
        pair_ref[holder] = m
        base = holder * slots_dev
        pair = jnp.where(parity == 0, slot - base, slots_ref[0, 2 * m + 1] - base)
        table = jnp.where(lane == holder, pair, table)
    wide_scr[steps * pieces :, :] = table.astype(F32)
    gain = gain_ref[...].astype(F32)
    for step in range(steps):
        rows = slice(step * pieces, (step + 1) * pieces)
        wide_scr[rows, :] = wide_scr[rows, :] * gain
    block = wide_scr[...].astype(BF16)
    for copy in range(block_ref.shape[0]):
        block_ref[copy] = block


def prepare(hidden, gain, block_slot, slots_dev, copies):
    assert slots_dev <= 256
    steps, model = hidden.shape
    rows = steps * model // LANES + EXTRA
    return pl.pallas_call(
        functools.partial(prepare_kernel, slots_dev),
        in_specs=[whole(), whole(), whole(SMEM)],
        out_specs=(whole(), whole(SMEM), whole(SMEM)),
        out_shape=(
            jax.ShapeDtypeStruct((copies, rows, LANES), BF16),
            jax.ShapeDtypeStruct((block_slot.shape[1] // 2,), jnp.int32),
            jax.ShapeDtypeStruct((block_slot.shape[1] // 2,), jnp.int32),
        ),
        scratch_shapes=[VMEM((rows, LANES), F32)],
        name="prepare",
    )(hidden, gain, block_slot)


def pick_kernel(order, me_ref, first_ref, second_ref, store_ref, out_ref, table_scr, table_smem, sem):
    block_len = store_ref.shape[1]
    half, rows, _ = first_ref.shape
    for j in range(2 * half):
        source = first_ref if j < half else second_ref
        asked = source[j % half, rows - EXTRA :, :].astype(F32)
        table_scr[j] = asked[:8].astype(jnp.int32)
    copy = pltpu.make_async_copy(table_scr, table_smem, sem)
    copy.start()
    copy.wait()
    me = me_ref[0]
    for j in range(2 * half):
        target = origin(me, order, j)
        for k in range(2):
            out_ref[target, k * block_len : (k + 1) * block_len, :] = store_ref[
                table_smem[j, k, me]
            ]


def pick_pages(me, first, second, store, order):
    count = 2 * first.shape[0]
    _, block_len, width = store.shape
    return pl.pallas_call(
        functools.partial(pick_kernel, order),
        in_specs=[whole(SMEM), whole(), whole(), whole()],
        out_specs=whole(),
        out_shape=jax.ShapeDtypeStruct((count, 2 * block_len, width), store.dtype),
        scratch_shapes=[
            VMEM((count, 8, LANES), jnp.int32),
            SMEM((count, 8, LANES), jnp.int32),
            pltpu.SemaphoreType.DMA(()),
        ],
        compiler_params=pltpu.CompilerParams(vmem_limit_bytes=36 * 2**20),
        name="pick_pages",
    )(me, first, second, store)


def split_kernel(x_ref, store_ref, keep_ref, send_ref):
    slots, block_len, width = store_ref.shape
    for x in range(2):

        @pl.when(x_ref[0] == x)
        def _():
            for head in range(width // LANES):
                target = keep_ref if head % 2 == x else send_ref
                lanes = slice(head // 2 * LANES, (head // 2 + 1) * LANES)
                part = store_ref[:, :, head * LANES : (head + 1) * LANES]
                target[:, lanes] = part.reshape(slots * block_len, LANES)


def split_values(x, store):
    slots, block_len, width = store.shape
    half = jax.ShapeDtypeStruct((slots * block_len, width // 2), store.dtype)
    return pl.pallas_call(
        split_kernel,
        in_specs=[whole(SMEM), whole()],
        out_specs=(whole(), whole()),
        out_shape=(half, half),
        compiler_params=pltpu.CompilerParams(vmem_limit_bytes=16 * 2**20),
        name="split_values",
    )(x, store)


def mix_kernel(me_ref, rows_ref, weights_ref, *rest):
    stores, (values_scr, sum_scr) = rest[:PLANE], rest[-2:]
    out_refs = rest[PLANE:-2]
    me = me_ref[0]
    low = jnp.bitwise_and(me, PLANE - 1)
    z_me = lax.div(me, PLANE)
    sessions = weights_ref.shape[0]
    planes = len(out_refs)
    block_len = values_scr.shape[1] // (2 * PLANE)
    for session in range(sessions):
        for q, store in enumerate(stores):
            device = jnp.bitwise_xor(low, q)
            for k in range(2):
                row = rows_ref[session * (2 * PLANE) + k * PLANE + device]
                source = pl.ds(pl.multiple_of(row * block_len, block_len), block_len)
                target = pl.ds(
                    pl.multiple_of((device * 2 + k) * block_len, block_len), block_len
                )
                values_scr[session, target, :] = store[source, :]
        block = weights_ref[session]
        product = jnp.dot(
            block[: planes * 8], values_scr[session], preferred_element_type=F32
        )
        mine = slice(session * 8, (session + 1) * 8)
        for z in range(planes):
            sum_scr[z, mine, :] = product[z * 8 : (z + 1) * 8, z * LANES : (z + 1) * LANES]
        recent = block[planes * 8 :].astype(F32)
        sum_scr[z_me, mine, :] += recent[:8]
    for q, out_ref in enumerate(out_refs):
        out_ref[...] = sum_scr[jnp.bitwise_xor(z_me, q)].astype(BF16)


def mix(me, rows, weights, stores):
    sessions = weights.shape[0]
    planes = stores[0].shape[1] // LANES
    shape = (planes, sessions * 8, LANES)
    return pl.pallas_call(
        mix_kernel,
        in_specs=[whole(SMEM)] * 2 + [whole()] * (1 + PLANE),
        out_specs=(whole(),) * planes,
        out_shape=(jax.ShapeDtypeStruct(shape[1:], BF16),) * planes,
        scratch_shapes=[VMEM((sessions, LANES, planes * LANES), BF16), VMEM(shape, F32)],
        compiler_params=pltpu.CompilerParams(vmem_limit_bytes=16 * 2**20),
        cost_estimate=pl.CostEstimate(
            flops=2 * sessions * 32 * LANES * planes * LANES,
            bytes_accessed=4 * stores[0].size * PLANE,
            transcendentals=0,
        ),
        name="mix_values",
    )(me, rows, weights, *stores)


def keys_kernel(pair_ref, factors_ref, basis_ref, cos_ref, sin_ref, out_ref, rows_scr):
    span = factors_ref.shape[0] // pair_ref.shape[0]
    count = rows_scr.shape[0] // span
    base = pl.program_id(0) * count
    for p in range(count):
        source = pl.ds(pl.multiple_of(pair_ref[base + p] * span, span), span)
        rows_scr[p * span : (p + 1) * span, :] = factors_ref[source, :]
    product = jnp.dot(rows_scr[...], basis_ref[...], preferred_element_type=F32)
    cosine, sine = cos_ref[...], sin_ref[...]
    for head in range(KV_HEADS):
        lanes = slice(head * HEAD_DIM, (head + 1) * HEAD_DIM)
        part = product[:, lanes]
        turned = part * cosine + pltpu.roll(part, HEAD_DIM // 2, 1) * sine
        out_ref[:, lanes] = turned.astype(BF16)


def make_keys(pair, factors, basis, cosine, sine):
    seq, rank = factors.shape
    width = basis.shape[1]
    rows = min(seq, 512)
    return pl.pallas_call(
        keys_kernel,
        grid=(seq // rows,),
        in_specs=[
            whole(SMEM),
            pl.BlockSpec((seq, rank), lambda i: (0, 0)),
            pl.BlockSpec((rank, width), lambda i: (0, 0)),
            pl.BlockSpec((rows, HEAD_DIM), lambda i: (i, 0)),
            pl.BlockSpec((rows, HEAD_DIM), lambda i: (i, 0)),
        ],
        out_specs=pl.BlockSpec((rows, width), lambda i: (i, 0)),
        out_shape=jax.ShapeDtypeStruct((seq, width), BF16),
        scratch_shapes=[VMEM((rows, rank), BF16)],
        compiler_params=pltpu.CompilerParams(vmem_limit_bytes=32 * 2**20),
        cost_estimate=pl.CostEstimate(
            flops=2 * seq * rank * width, bytes_accessed=4 * seq * width, transcendentals=0
        ),
        name="turned_keys",
    )(pair, factors, basis, cosine, sine)


def fetch_kernel(source_ref, target_ref, sems):
    parts = sems.shape[0]
    span = source_ref.shape[0] // parts
    copies = []
    for part in range(parts):
        rows = pl.ds(part * span, span)
        copies.append(
            pltpu.make_async_copy(source_ref.at[rows, :], target_ref.at[rows, :], sems.at[part])
        )
        copies[-1].start()
    for copy in copies:
        copy.wait()


def fetch(weight, limit):
    return pl.pallas_call(
        fetch_kernel,
        in_specs=[whole(pl.ANY)],
        out_specs=whole(pl.ANY),
        out_shape=jax.ShapeDtypeStruct(weight.shape, weight.dtype),
        scratch_shapes=[pltpu.SemaphoreType.DMA((16,))],
        compiler_params=pltpu.CompilerParams(vmem_limit_bytes=limit * 2**20),
        cost_estimate=pl.CostEstimate(
            flops=0, bytes_accessed=2 * weight.size, transcendentals=0
        ),
        name="fetch_weight",
    )(weight)


def project_kernel(
    order, fast, me_ref, first_ref, second_ref, wq_ref, wk_ref, out_ref, *rest
):
    if fast:
        rows_ref, x_scr, lhs_scr, wq_buf, out_scr, sems, *asked_scr = rest
    else:
        x_scr, lhs_scr, wq_buf, out_scr, sems = rest
    depth, q_cols = wq_ref.shape
    k_cols = wk_ref.shape[1]
    chunks = wq_buf.shape[0]
    span = depth // chunks
    pieces = depth // LANES
    copies = []
    parts = sems.shape[1]
    for i in range(chunks):
        copies.append([])
        for part in range(parts):
            copy = pltpu.make_async_copy(
                wq_ref.at[pl.ds(i * span + part * (span // parts), span // parts), :],
                wq_buf.at[i, pl.ds(part * (span // parts), span // parts), :],
                sems.at[i, part],
            )
            copy.start()
            copies[-1].append(copy)
    half = first_ref.shape[0]
    count = 2 * half * STEPS
    rows = STEPS * pieces
    for j in range(2 * half):
        source = first_ref if j < half else second_ref
        x_scr[j * rows : (j + 1) * rows] = source[j % half, :rows, :].astype(F32)
    if fast:
        table_scr, table_smem, table_sem = asked_scr
        for j in range(2 * half):
            source = first_ref if j < half else second_ref
            asked = source[j % half, rows:, :].astype(F32)
            table_scr[2 * j : 2 * j + 2, :] = asked[:2].astype(jnp.int32)
        table_copy = pltpu.make_async_copy(table_scr, table_smem, table_sem)
        table_copy.start()
    for c in range(pieces):
        part = x_scr[pl.ds(c, count, stride=pieces), :]
        lhs_scr[:, c * LANES : (c + 1) * LANES] = part.astype(BF16)
    if fast:
        me = me_ref[0]
        out_scr[...] = jnp.zeros_like(out_scr)
        table_copy.wait()
        plane = jnp.bitwise_and(me, -PLANE)
        for j in range(2 * half):
            place = origin(me, order, j) * (2 * PLANE)
            for k in range(2):
                for b in range(PLANE):
                    rows_ref[place + k * PLANE + b] = table_smem[2 * j + k, plane + b]
    q_sum = jnp.zeros((count, q_cols), F32)
    k_sum = jnp.zeros((count, k_cols), F32)
    for i in range(chunks):
        for copy in copies[i]:
            copy.wait()
        lhs = lhs_scr[:, i * span : (i + 1) * span]
        q_sum = q_sum + jnp.dot(lhs, wq_buf[i], preferred_element_type=F32)
        k_sum = k_sum + jnp.dot(
            lhs, wk_ref[i * span : (i + 1) * span, :], preferred_element_type=F32
        )
    if not fast:
        out_ref[:, :q_cols] = q_sum.astype(BF16)
        out_ref[:, q_cols:] = k_sum.astype(BF16)
        return
    per = q_cols // LANES
    for j in range(2 * half):
        place = origin(me, order, j)
        for step in range(STEPS):
            row = j * STEPS + step
            for c in range(per):
                out_scr[place, step * per + c : step * per + c + 1, :] = q_sum[
                    row : row + 1, c * LANES : (c + 1) * LANES
                ]
            out_scr[place, STEPS * per + step : STEPS * per + step + 1, :] = k_sum[
                row : row + 1, :
            ]
    out_ref[...] = out_scr[...].astype(BF16)


def project(me, first, second, query_weight, kv_weight, order, fast):
    depth, q_cols = query_weight.shape
    k_cols = kv_weight.shape[1]
    pieces = depth // LANES
    devices = 2 * first.shape[0]
    rows = devices * STEPS
    chunks = 8
    span = depth // chunks
    shape = (devices, 16, LANES) if fast else (rows, q_cols + k_cols)
    return pl.pallas_call(
        functools.partial(project_kernel, order, fast),
        in_specs=[whole(SMEM), whole(), whole(), whole(pl.ANY), whole()],
        out_specs=(whole(), whole(SMEM)) if fast else whole(),
        out_shape=(
            (
                jax.ShapeDtypeStruct(shape, BF16),
                jax.ShapeDtypeStruct((devices * 2 * PLANE,), jnp.int32),
            )
            if fast
            else jax.ShapeDtypeStruct(shape, BF16)
        ),
        scratch_shapes=[
            VMEM((rows * pieces, LANES), F32),
            VMEM((rows, depth), BF16),
            VMEM((chunks, span, q_cols), BF16),
            VMEM((devices, 16, LANES) if fast else (8, LANES), F32),
            pltpu.SemaphoreType.DMA((chunks, 4)),
        ]
        + (
            [
                VMEM((2 * devices, LANES), jnp.int32),
                SMEM((2 * devices, LANES), jnp.int32),
                pltpu.SemaphoreType.DMA(()),
            ]
            if fast
            else []
        ),
        compiler_params=pltpu.CompilerParams(vmem_limit_bytes=PROJECT_LIMIT),
        cost_estimate=pl.CostEstimate(
            flops=2 * rows * depth * (q_cols + k_cols),
            bytes_accessed=2 * depth * (q_cols + k_cols),
            transcendentals=0,
        ),
        name="norm_project",
    )(me, first, second, query_weight, kv_weight)


def attend_kernel(fast, columns_ref, keys_ref, bias_ref, cos_ref, sin_ref, *rest):
    pages_ref, out_ref, out_scr = (None, *rest) if fast else rest
    score_scale = 1.0 / math.sqrt(HEAD_DIM)
    half = HEAD_DIM // 2
    rows = 2 * GROUP
    columns = columns_ref[...].astype(F32)
    count = columns.shape[0]
    query = columns[:, :8, :].reshape(count * 8, HEAD_DIM)
    fresh = columns[:, 8:, :]
    if fast:
        planes = count // PLANE
        out_scr[...] = jnp.zeros_like(out_scr)
    row_step = lax.rem(lax.broadcasted_iota(jnp.int32, (count * 8, 1), 0) // 4, STEPS)
    later = row_step == 1
    cosine = jnp.where(later, cos_ref[1:2, :], cos_ref[0:1, :])
    sine = jnp.where(later, sin_ref[1:2, :], sin_ref[0:1, :])
    turned = (query * cosine + pltpu.roll(query, half, 1) * sine).astype(BF16)
    turned_wide = turned.astype(F32)
    step_later = later[:rows]
    bias = jnp.where(step_later, bias_ref[1:2, :], bias_ref[0:1, :])
    new_keys = []
    for step in range(STEPS):
        part = fresh[:KV_HEADS, step, :]
        new = part * cos_ref[step : step + 1, :] + pltpu.roll(part, half, 1) * sin_ref[step : step + 1, :]
        new_keys.append(new.astype(BF16).astype(F32))
    for head in range(KV_HEADS):
        lanes = slice(head * HEAD_DIM, (head + 1) * HEAD_DIM)
        mine = slice(head * rows, (head + 1) * rows)
        scores = (
            lax.dot_general(
                turned[mine], keys_ref[:, lanes], (((1,), (1,)), ((), ())),
                preferred_element_type=F32,
            )
            * score_scale
            + bias
        )
        recent0 = (
            jnp.sum(turned_wide[mine] * new_keys[0][head : head + 1, :], axis=1, keepdims=True)
            * score_scale
        )
        recent1 = (
            jnp.sum(turned_wide[mine] * new_keys[1][head : head + 1, :], axis=1, keepdims=True)
            * score_scale
        )
        recent1 = jnp.where(step_later, recent1, -1e30)
        largest = jnp.maximum(
            jnp.max(scores, axis=1, keepdims=True), jnp.maximum(recent0, recent1)
        )
        cache_exp = jnp.exp(scores - largest)
        exp0 = jnp.exp(recent0 - largest)
        exp1 = jnp.exp(recent1 - largest)
        denominator = jnp.sum(cache_exp, axis=1, keepdims=True) + (exp0 + exp1)
        weights = (cache_exp / denominator).astype(BF16)
        weight0 = (exp0 / denominator).astype(BF16).astype(F32)
        weight1 = (exp1 / denominator).astype(BF16).astype(F32)
        recent = weight0 * fresh[KV_HEADS + head, 0:1, :]
        recent = recent + weight1 * fresh[KV_HEADS + head, 1:2, :]
        if not fast:
            values = pages_ref[:, :, lanes].reshape(keys_ref.shape[0], HEAD_DIM)
            mixed = jnp.dot(weights, values, preferred_element_type=F32)
            out_ref[mine, :] = (mixed + recent).astype(BF16)
            continue
        weights = weights.astype(F32)
        z, x = divmod(head, 2)
        for c in range(2):
            part = slice(c * 8, (c + 1) * 8)
            for plane in range(planes):
                out_scr[plane * PLANE + 2 * x + c, z * 8 : (z + 1) * 8, :] = weights[
                    part, plane * LANES : (plane + 1) * LANES
                ]
            out_scr[z * PLANE + 2 * x + c, planes * 8 : planes * 8 + 8, :] = recent[part]
    if fast:
        out_ref[...] = out_scr[...].astype(BF16)


def attend(columns, keys, bias, cosine, sine, pages, fast):
    seq, width = keys.shape
    count = columns.shape[0]
    if fast:
        shape = (count, count // PLANE * 8 + 16, LANES)
        scratch = [VMEM(shape, F32)]
        operands = (columns, keys, bias, cosine, sine)
    else:
        shape = (STEPS * HEADS, HEAD_DIM)
        scratch = [VMEM((8, LANES), F32)]
        operands = (columns, keys, bias, cosine, sine, pages)
    return pl.pallas_call(
        functools.partial(attend_kernel, fast),
        in_specs=[whole()] * len(operands),
        out_specs=whole(),
        out_shape=jax.ShapeDtypeStruct(shape, BF16),
        scratch_shapes=scratch,
        compiler_params=pltpu.CompilerParams(vmem_limit_bytes=48 * 2**20),
        cost_estimate=pl.CostEstimate(
            flops=4 * STEPS * HEADS * seq * HEAD_DIM,
            bytes_accessed=4 * seq * width,
            transcendentals=STEPS * HEADS * seq,
        ),
        name="attend",
    )(*operands)


def output_kernel(fast, count, me_ref, weight_ref, *rest):
    lhs_refs, rest = rest[:count], rest[count:]
    out_refs, (out_scr, heads_scr) = rest[:-2], rest[-2:]
    chunks = 8
    span = weight_ref.shape[1] // chunks
    rows = out_scr.shape[0] * LANES // (chunks * span)
    pieces = chunks * span // LANES
    if fast:
        per = heads_scr.shape[0] // rows
        total = lhs_refs[0][...].astype(F32)
        for lhs_ref in lhs_refs[1:]:
            total = total + lhs_ref[...].astype(F32)
        heads_scr[...] = total
        lhs = jnp.concatenate(
            [heads_scr[pl.ds(g, rows, stride=per), :].astype(BF16) for g in range(per)], axis=1
        )
    else:
        lhs = lhs_refs[0][...]
    for i in range(chunks):
        part = jnp.dot(
            lhs, weight_ref[:, i * span : (i + 1) * span], preferred_element_type=F32
        )
        for c in range(span // LANES):
            out_scr[pl.ds(i * (span // LANES) + c, rows, stride=pieces), :] = part[
                :, c * LANES : (c + 1) * LANES
            ]
    if not fast:
        out_refs[0][...] = out_scr[...].astype(BF16)
        return
    low = jnp.bitwise_and(me_ref[0], 1)
    for out_ref, core in zip(out_refs, (low, 1 - low)):
        count, size, _ = out_ref.shape
        for j in range(count):
            part = pl.ds(pl.multiple_of((2 * j + core) * size, size), size)
            out_ref[j] = out_scr[part, :].astype(BF16)


def output(me, lhs, weight, rows, fast):
    depth, width = weight.shape
    if fast:
        shape = (rows // (2 * STEPS), STEPS * width // LANES, LANES)
        shapes = (jax.ShapeDtypeStruct(shape, BF16),) * 2
    else:
        shapes = (jax.ShapeDtypeStruct((rows * width // LANES, LANES), BF16),)
    return pl.pallas_call(
        functools.partial(output_kernel, fast, len(lhs)),
        in_specs=[whole(SMEM)] + [whole()] * (1 + len(lhs)),
        out_specs=(whole(),) * len(shapes),
        out_shape=shapes,
        scratch_shapes=[
            VMEM((rows * width // LANES, LANES), F32),
            VMEM(lhs[0].shape if fast else (8, LANES), F32),
        ],
        compiler_params=pltpu.CompilerParams(vmem_limit_bytes=24 * 2**20),
        cost_estimate=pl.CostEstimate(
            flops=2 * rows * depth * width, bytes_accessed=2 * depth * width, transcendentals=0
        ),
        name="output_project",
    )(me, weight, *lhs)


def swap(block, bit, devices):
    return lax.ppermute(block, AXIS, [(i, i ^ bit) for i in range(devices)])


def exchange(blocks, groups=None):
    return lax.all_to_all(
        blocks, AXIS, split_axis=0, concat_axis=0, tiled=True, axis_index_groups=groups
    )


def local(
    hidden,
    norm_gain,
    query_weight,
    kv_weight,
    out_weight,
    key_factors,
    key_basis,
    value_store,
    lengths,
    block_slot,
    selection,
):
    devices = lax.axis_size(AXIS)
    me = lax.axis_index(AXIS)
    slots_dev, block_len, width = value_store.shape
    seq = key_factors.shape[1]
    pages = block_slot.shape[1]
    model = hidden.shape[2]
    q_cols = query_weight.shape[1]
    k_cols = kv_weight.shape[1]
    fast = devices == 2 * PAIRS and q_cols == 4 * HEAD_DIM and k_cols == HEAD_DIM
    pieces = model // LANES

    me_word = me.astype(jnp.int32).reshape(1)
    block, holder, pair = prepare(
        hidden[:, 0], norm_gain.reshape(pieces, LANES), block_slot, slots_dev, PAIRS if fast else 1
    )
    if fast:
        same_core = [list(range(core, devices, 2)) for core in range(2)]
        block = exchange(block, same_core)
        block, kv_weight = lax.optimization_barrier((block, kv_weight))
        kv_weight = fetch(kv_weight, 50)
        other = swap(block, 1, devices)
        order = None
        x = lax.bitwise_and(lax.shift_right_logical(me_word, 1), 1)
        keep, send = split_values(x, value_store)
        neighbour = swap(send, 2, devices)
    else:
        order = [0]
        bit = devices // 2
        while bit:
            other = swap(block, bit, devices)
            order = order + [k ^ bit for k in order]
            bit //= 2
            if bit:
                block = jnp.concatenate([block, other], axis=0)
        order = tuple(order)
    span = 2 * block_len
    places = (pair[:, None] * span + jnp.arange(span, dtype=jnp.int32)[None, :]).reshape(-1)
    if not fast:
        sent_pages = pick_pages(me_word, block, other, value_store, order)
        block, other, sent_pages = lax.optimization_barrier((block, other, sent_pages))
        fetched = exchange(sent_pages)
    projected = project(
        me_word, block, other, query_weight, kv_weight, order, fast
    )
    if fast:
        projected, rows = projected
        projected, places = lax.optimization_barrier((projected, places))
        columns = exchange(projected)
    else:
        targets = jnp.bitwise_xor(me, jnp.array(order, dtype=jnp.int32))
        columns = exchange(projected.reshape(devices, STEPS, q_cols + k_cols)[targets])
        query = columns[:, :, :q_cols].transpose(1, 0, 2).reshape(STEPS, HEADS // 4, 4, HEAD_DIM)
        query = query.transpose(1, 0, 2, 3).reshape(HEADS // 4, 8, HEAD_DIM)
        fresh = columns[:, :, q_cols:].transpose(1, 0, 2).reshape(STEPS, HEADS // 4, HEAD_DIM)
        fresh = jnp.pad(fresh.transpose(1, 0, 2), ((0, 0), (0, 8 - STEPS), (0, 0)))
        columns = jnp.concatenate([query, fresh], axis=1)

    cosine, sine = turn_tables(places.astype(F32))
    keys = make_keys(pair, key_factors[0], key_basis[0], cosine, sine)
    picked = jnp.any(
        selection[:, 0, :, None] == (places // block_len)[None, None, :], axis=1
    )
    bias = jnp.where(picked & (places < lengths[0])[None, :], 0.0, -1e30).astype(F32)
    new_cos, new_sin = turn_tables(
        (lengths[0] + jnp.arange(STEPS, dtype=jnp.int32)).astype(F32)
    )
    if fast:
        blocks = attend(columns, keys, bias, new_cos, new_sin, None, True)
        blocks, neighbour = lax.optimization_barrier((blocks, neighbour))
        stores = (keep, swap(keep, 1, devices), neighbour, swap(neighbour, 1, devices))
        blocks = exchange(blocks)
        parts = mix(me_word, rows, blocks, stores)
        (*parts, out_weight) = lax.optimization_barrier((*parts, out_weight))
        out_weight = fetch(out_weight, 43)
        lhs = [parts[0]] + [swap(parts[q], q * PLANE, devices) for q in range(1, len(parts))]
    else:
        heads = attend(columns, keys, bias, new_cos, new_sin, fetched, False)
        flat = heads.reshape(HEADS // 4, STEPS, 4 * HEAD_DIM).transpose(1, 0, 2)
        flat = flat.reshape(STEPS, devices, model // devices).transpose(1, 0, 2)
        lhs = [exchange(flat).reshape(devices * STEPS, model // devices)]
    partial = output(me_word, lhs, out_weight, devices * STEPS, fast)
    if fast:
        near, far = partial
        both = near.astype(F32) + swap(far, 1, devices).astype(F32)
        arrived = exchange(both.astype(BF16), same_core)
    else:
        arrived = exchange(partial[0].reshape(devices, STEPS * pieces, LANES))
    total = jnp.sum(arrived.astype(F32), axis=0).astype(BF16)
    return total.reshape(STEPS, 1, model)


def solution(mesh):
    return jax.shard_map(
        local,
        mesh=mesh,
        in_specs=(
            P(None, ("groups", "session"), None),
            P(),
            P(None, "session"),
            P(None, "session"),
            P("session", None),
            P(("groups", "session"), None, None),
            P(("groups", "session"), None, None),
            P(("groups", "session"), None, None),
            P(("groups", "session")),
            P(("groups", "session"), None),
            P(None, ("groups", "session"), None),
        ),
        out_specs=P(None, ("groups", "session"), None),
        check_vma=False,
    )
```
